32 devices in a mesh: groups: 2 (over y), cells: 4 (over z), nodes: 2 (over x), sub: 2 (over core).
Axes of the slice: x: 2, y: 2, z: 4, core: 2. Of those that a mesh axis runs over, the one named last changes fastest.
Arguments:
- adjoint_start: float32 [4, 5, 16384], P('nodes', None, ('groups', 'cells', 'sub')), parts along dimension 2, may hold values from -6 to 6
- adjoint_rhs: float32 [4, 5, 16384], P('nodes', None, ('groups', 'cells', 'sub')), parts along dimension 2, may hold values from -6 to 6
- off_blocks: bfloat16 [4, 6, 25, 16384], P('nodes', None, None, ('groups', 'cells', 'sub')), parts along dimension 3, may hold values from -0.5 to 0.5
- diag_inverse: float32 [4, 25, 16384], P('nodes', None, ('groups', 'cells', 'sub')), parts along dimension 2, may hold values from -2.4 to 2.4
- neighbours: int32 [6, 8192], P(None, ('cells', 'sub')), may hold values from -1 to 8191, as said below
- node_weights: float32 [4], P('nodes'), may hold values from 0.05 to 0.5
- sens_blocks: bfloat16 [4, 15, 16384], P('nodes', None, ('groups', 'cells', 'sub')), parts along dimension 2, may hold values from -1.796875 to 1.796875
- cell_points: float32 [3, 8192], P(None, ('cells', 'sub')), may hold values from 0 to 1
- base_points: float32 [3, 4096], replicated, may hold values from 0 to 1
- ffd_index: int32 [4096, 8], replicated, may hold values from 0 to 511
- ffd_weight: float32 [4096, 8], replicated, may hold values from 0 to 1
Outputs:
- adjoint: float32 [4, 5, 16384], P('nodes', None, ('groups', 'cells', 'sub')), parts along dimension 2
- control_grad: float32 [6, 512], P('groups'), parts along dimension 0
The draws below stay inside these ranges and needn't reach their ends.
There are 2 independent parts, one for each index of `groups`. The reference program is written for one: setup_inputs(seed, part) draws one part's arguments, and reference() takes and returns one part's arrays. A program takes and returns all parts, laid end to end along the dimension named above; an argument that names none is the same for every part. Nothing has to cross between parts.
Inputs may be any that keep to these rules, and one draw needn't show every extreme that they name: `neighbours`: each entry is -1 (no neighbour) or the index of a cell at most 1024 away from the cell; the distance 1024 occurs.
All inputs are finite; a program needn't handle non-finite values.
Results may differ from the reference program's by a relative error of at most 0.0003.
Values sent between devices are 32-bit elements; how exact they have to be, the bound alone decides.
No kernel may reach another device: no remote copies, remote signals or barrier semaphores. Data moves between devices by JAX's collectives and lax.ppermute only.
A program may use at most 64 MiB of HBM per device.

```python
import math
import jax
import jax.numpy as jnp
from jax import lax

REACH = 1024
NODES = 4
NCELLS = 8192
FACES = 6
SWEEPS = 2
BASE = 4096
FFD = 512


def draw_neighbours(key, part):
    key_dist = jax.random.fold_in(key, 11)
    key_sign = jax.random.fold_in(key, 12)
    key_pad = jax.random.fold_in(key, 13)
    distance = jax.random.randint(key_dist, (FACES, NCELLS), 1, REACH + 1)
    upward = jax.random.randint(key_sign, (FACES, NCELLS), 0, 2)
    offset = jnp.where(upward == 1, distance, -distance)
    target = jnp.arange(NCELLS, dtype=jnp.int32)[None, :] + offset
    padded = jax.random.randint(key_pad, (FACES, NCELLS), 0, 6) == 0
    inside = (target >= 0) & (target < NCELLS)
    result = jnp.where(inside & jnp.logical_not(padded), target, -1).astype(jnp.int32)
    return result.at[0, REACH].set(0)


def touch_ends(values, rng, least, high):
    index_at = [jax.random.randint(jax.random.fold_in(rng, axis), (), 0, length) for axis, length in enumerate(values.shape)]
    main_axis = values.shape.index(max(values.shape))
    neighbour = index_at[:main_axis] + [(index_at[main_axis] + 1) % values.shape[main_axis]] + index_at[main_axis + 1:]
    return values.at[tuple(index_at)].set(least).at[tuple(neighbour)].set(high)


def block_scale(rng, dims, split, low, largest):
    level = 1.0
    for position, shards_of in split:
        steps = jax.random.uniform(jax.random.fold_in(jax.random.fold_in(rng, 6), position), (shards_of,), jnp.float32, low / len(split), largest / len(split))
        level = level * jnp.repeat(jnp.exp(steps), dims[position] // shards_of).reshape((-1,) + (1,) * (len(dims) - 1 - position))
    return level


def centred(stream_key, extent, scale, bound, cuts=(), kind=jnp.bfloat16):
    loudness = block_scale(stream_key, extent, cuts, -0.22, 0.18) if cuts else 1.0
    drawn = jax.random.normal(stream_key, extent, jnp.float32) * scale * loudness
    return jnp.minimum(jnp.maximum(drawn, -bound), bound).astype(kind)


def setup_inputs(seed: int = 0, part: int = 0) -> dict:
    key_of = jax.random.split(jax.random.key(seed), 12)
    part_splits = jax.random.split(jax.random.fold_in(key_of[11], part), 12)
    return {
        "adjoint_start": centred(part_splits[0], (NODES, 5, NCELLS), 1.0, 6.0, ((0, 2), (2, 8)), jnp.float32),
        "adjoint_rhs": centred(part_splits[1], (NODES, 5, NCELLS), 1.0, 6.0, ((0, 2), (2, 8)), jnp.float32),
        "off_blocks": centred(part_splits[2], (NODES, FACES, 25, NCELLS), 0.08, 0.5, ((0, 2), (3, 8))),
        "diag_inverse": centred(part_splits[3], (NODES, 25, NCELLS), 0.4, 2.4, ((0, 2), (2, 8)), jnp.float32),
        "neighbours": draw_neighbours(jax.random.fold_in(key_of[11], 71), part),
        "node_weights": jnp.clip(jnp.exp(math.log(0.5) - 2.3025851 * jax.random.uniform(key_of[5], (NODES,), jnp.float32) ** block_scale(key_of[5], (NODES,), ((0, 2),), -0.2, 0.2)), 0.05, 0.5),
        "sens_blocks": centred(part_splits[6], (NODES, 15, NCELLS), 0.3, 1.796875, ((0, 2), (2, 8))),
        "cell_points": jnp.clip(1.0 * jax.random.uniform(key_of[7], (3, NCELLS), jnp.float32) ** block_scale(key_of[7], (3, NCELLS), ((1, 8),), -0.2, 0.2), 0.0, 1.0),
        "base_points": jnp.clip(jax.random.uniform(key_of[8], (3, BASE), jnp.float32, 0.0, 1.0), 0.0, 1.0),
        "ffd_index": touch_ends(jax.random.randint(key_of[9], (BASE, 8), 0, FFD), jax.random.fold_in(key_of[9], 1), 0, FFD - 1).astype(jnp.int32),
        "ffd_weight": jnp.clip(jax.random.uniform(key_of[10], (BASE, 8), jnp.float32, 0.0, 1.0), 0.0, 1.0),
    }


support_radius = 0.3

def relax(adjoint, adjoint_rhs, off_blocks, diag_inverse, neighbours):
    present = neighbours >= 0
    index_safe = jnp.where(present, neighbours, 0)
    coupled = jnp.zeros(adjoint.shape, jnp.float32)
    node_count = adjoint.shape[0]
    for face_slot in range(FACES):
        beside = jnp.where(present[face_slot][None, None, :], adjoint[:, :, index_safe[face_slot]], 0.0)
        coupling = off_blocks[:, face_slot].astype(jnp.float32).reshape(node_count, 5, 5, -1)
        coupled = coupled + lax.optimization_barrier(jnp.sum(coupling * beside[:, None], axis=2))
    inverse = diag_inverse.reshape(node_count, 5, 5, -1)
    return lax.optimization_barrier(jnp.sum(inverse * (adjoint_rhs - coupled)[:, None], axis=2))

def kernel_sum(sensitivity, points, base):
    squared = jnp.zeros((points.shape[1], base.shape[1]), jnp.float32)
    for axis_slot in range(3):
        squared = squared + (points[axis_slot][:, None] - base[axis_slot][None, :]) ** 2
    ratio = jnp.sqrt(squared) / support_radius
    kernel = jnp.maximum(1.0 - ratio, 0.0) ** 4 * (4.0 * ratio + 1.0)
    return jnp.dot(sensitivity, kernel, precision=lax.Precision.HIGHEST, preferred_element_type=jnp.float32)

def lattice_matrix(lattice_index, lattice_weight, columns):
    matches = lattice_index[:, :, None] == jnp.arange(columns, dtype=jnp.int32)[None, None, :]
    return lax.optimization_barrier(jnp.sum(jnp.where(matches, lattice_weight[:, :, None], 0.0), axis=1))

def reference(adjoint_start, adjoint_rhs, off_blocks, diag_inverse, neighbours, node_weights, sens_blocks, cell_points, base_points, ffd_index, ffd_weight):
    adjoint = adjoint_start
    for sweep_step in range(SWEEPS):
        adjoint = relax(adjoint, adjoint_rhs, off_blocks, diag_inverse, neighbours)
    derive = sens_blocks.astype(jnp.float32).reshape(adjoint.shape[0], 5, 3, -1)
    per_node = lax.optimization_barrier(jnp.sum(adjoint[:, :, None] * derive, axis=1))
    sensitivity = lax.optimization_barrier(jnp.sum(node_weights[:, None, None] * per_node, axis=0))
    cell_block = min(4096, NCELLS)

    def add_block(block_index, carry):
        sens_part = lax.dynamic_slice_in_dim(sensitivity, block_index * cell_block, cell_block, 1)
        point_part = lax.dynamic_slice_in_dim(cell_points, block_index * cell_block, cell_block, 1)
        return carry + kernel_sum(sens_part, point_part, base_points)
    base_grad = lax.fori_loop(0, NCELLS // cell_block, add_block, jnp.zeros((3, BASE), jnp.float32))
    base_grad = base_grad / jnp.sqrt(jnp.float32(NCELLS))
    lattice = lattice_matrix(ffd_index, ffd_weight, FFD)
    control_grad = jnp.dot(base_grad, lattice, precision=lax.Precision.HIGHEST, preferred_element_type=jnp.float32)
    return (adjoint, control_grad)
```

```python
import functools
import math

import jax
import jax.numpy as jnp
from jax import lax
from jax.experimental import pallas as pl
from jax.experimental.pallas import tpu as pltpu
from jax.sharding import PartitionSpec as P

SWEEPS = 2
FFD = 512
SUPPORT_RADIUS = 0.3
LANES = 128
VMEM_LIMIT = 48 * 1024 * 1024

CELL_AXES = ("cells", "sub")
SUM_AXES = ("cells", "nodes", "sub")


def rows_of(array):
    nodes, rows, cells = array.shape
    blocks = cells // LANES
    split = array.reshape(nodes, rows, blocks, LANES)
    return split.transpose(1, 2, 0, 3).reshape(rows * blocks * nodes, LANES)


def from_rows(array, nodes, cells):
    blocks = cells // LANES
    split = array.reshape(-1, blocks, nodes, LANES)
    return split.transpose(2, 0, 1, 3).reshape(nodes, -1, cells)


def spread_neighbours(neigh_ref, first_cell, lane_ref, step_ref, nodes):
    faces, cells = neigh_ref.shape
    blocks = cells // LANES
    per_face = blocks * nodes
    for block in range(blocks):
        index = neigh_ref[:, block * LANES : (block + 1) * LANES]
        local = index - first_cell + cells
        lane = jnp.bitwise_and(local, LANES - 1)
        step = jnp.right_shift(local, 7) - block
        step = jnp.where(index >= 0, step, -1)
        for node in range(nodes):
            rows = pl.ds(block * nodes + node, faces, stride=per_face)
            lane_ref[rows, :] = lane
            step_ref[rows, :] = step


def sweep_rows(window_ref, rhs_ref, off_ref, inverse_ref, lane_ref, step_ref, faces, per, steps, store):
    width = 3 * per
    stride = steps[1]
    for half in range(0, per, 8):
        lanes = [lane_ref[f * per + half : f * per + half + 8, :] for f in range(faces)]
        dist = [step_ref[f * per + half : f * per + half + 8, :] for f in range(faces)]
        beside = [[jnp.zeros((8, LANES), jnp.float32)] * 5 for _ in range(faces)]
        for d in range(steps[0]):
            here = [dist[f] == d for f in range(faces)]
            for b in range(5):
                first = b * width + half + d * stride
                table = window_ref[pl.ds(first, 8), :]
                for f in range(faces):
                    got = jnp.take_along_axis(
                        table, lanes[f], axis=1, mode="promise_in_bounds"
                    )
                    beside[f][b] = jnp.where(here[f], got, beside[f][b])
        remaining = []
        for a in range(5):
            total = rhs_ref[a * per + half : a * per + half + 8, :]
            for f in range(faces):
                for b in range(5):
                    row = (f * 25 + 5 * a + b) * per + half
                    total = total - off_ref[row : row + 8, :] * beside[f][b]
            remaining.append(total)
        for a in range(5):
            total = None
            for b in range(5):
                row = (5 * a + b) * per + half
                term = inverse_ref[row : row + 8, :] * remaining[b]
                total = term if total is None else total + term
            store(a, half, total)


def fill_window(window_ref, before_ref, own_ref, after_ref, per):
    for b in range(5):
        for place, ref in enumerate((before_ref, own_ref, after_ref)):
            window_ref[(3 * b + place) * per : (3 * b + place + 1) * per, :] = ref[
                b * per : (b + 1) * per, :
            ]


def sweep_kernel(
    nodes,
    before_ref,
    own_ref,
    after_ref,
    rhs_ref,
    off_ref,
    inverse_ref,
    neigh_ref,
    out_ref,
    window_ref,
    off32_ref,
    lane_ref,
    step_ref,
):
    faces, cells = neigh_ref.shape
    blocks = cells // LANES
    per = blocks * nodes
    first_cell = lax.axis_index(CELL_AXES) * cells
    spread_neighbours(neigh_ref, first_cell, lane_ref, step_ref, nodes)
    fill_window(window_ref, before_ref, own_ref, after_ref, per)
    off32_ref[...] = off_ref[...].astype(jnp.float32)

    def store(a, half, value):
        out_ref[a * per + half : a * per + half + 8, :] = value

    sweep_rows(
        window_ref, rhs_ref, off32_ref, inverse_ref, lane_ref, step_ref,
        faces, per, (2 * blocks + 1, nodes), store,
    )


def last_sweep_kernel(
    nodes,
    before_ref,
    own_ref,
    after_ref,
    rhs_ref,
    off_ref,
    inverse_ref,
    neigh_ref,
    weight_ref,
    sens_ref,
    out_ref,
    sens_out_ref,
    window_ref,
    off32_ref,
    lane_ref,
    step_ref,
    part_ref,
):
    sweep_kernel(
        nodes, before_ref, own_ref, after_ref, rhs_ref, off_ref, inverse_ref, neigh_ref,
        out_ref, window_ref, off32_ref, lane_ref, step_ref,
    )
    cells = neigh_ref.shape[1]
    blocks = cells // LANES
    per = blocks * nodes
    row_node = lax.rem(lax.broadcasted_iota(jnp.int32, (per, LANES), 0), nodes)
    weights = jnp.zeros((per, LANES), jnp.float32)
    for node in range(nodes):
        weights = jnp.where(row_node == node, weight_ref[node], weights)
    for k in range(3):
        total = None
        for a in range(5):
            row = (3 * a + k) * per
            term = out_ref[a * per : (a + 1) * per, :] * sens_ref[row : row + per, :].astype(
                jnp.float32
            )
            total = term if total is None else total + term
        part_ref[k * per : (k + 1) * per, :] = total * weights
    for block in range(blocks):
        total = None
        for node in range(nodes):
            term = part_ref[pl.ds(block * nodes + node, 3, stride=per), :]
            total = term if total is None else total + term
        sens_out_ref[:, block * LANES : (block + 1) * LANES] = total


def pieces(value, count):
    found = []
    for _ in range(count):
        piece = value.astype(jnp.bfloat16).astype(jnp.float32)
        found.append(piece)
        value = value - piece
    return found


def distance_factors(points, left):
    count = points.shape[1]
    scaled = (points - 0.5) * (1.0 / SUPPORT_RADIUS)
    scaled = jnp.concatenate([scaled, jnp.zeros((5, count), jnp.float32)], axis=0)
    norm = jnp.sum(scaled * scaled, axis=0, keepdims=True)
    norms = pieces(jnp.broadcast_to(norm, (8, count)), 3)
    row = lax.broadcasted_iota(jnp.int32, (8, count), 0)
    norm_block = jnp.zeros((8, count), jnp.float32)
    for place in range(3):
        norm_block = jnp.where(row == place, norms[place], norm_block)
    ones_block = jnp.where(row < 3, 1.0, 0.0)
    first, second, third = pieces(scaled, 3)
    if left:
        dims = [first, first, second, second, first, third]
        dims = [-2.0 * part for part in dims]
        blocks = dims + [norm_block, ones_block]
    else:
        dims = [first, second, first, second, third, first]
        blocks = dims + [ones_block, norm_block]
    return jnp.concatenate(blocks, axis=0)


def response_kernel(
    chunk, cell_ref, base_ref, index_ref, weight_ref, out_ref, left_ref, lattice_ref
):
    cells = cell_ref.shape[1]
    owned = base_ref.shape[1] // lax.axis_size("nodes")
    start = pl.multiple_of(lax.axis_index("nodes") * owned, LANES)
    left_ref[...] = distance_factors(cell_ref[...], True).T.astype(jnp.bfloat16)
    slots = index_ref.shape[0]
    columns = out_ref.shape[1]
    out_ref[...] = jnp.zeros_like(out_ref)

    @pl.loop(0, owned // chunk)
    def _(step):
        here = pl.ds(pl.multiple_of(start + step * chunk, LANES), chunk)
        index = index_ref[:, here]
        weight = weight_ref[:, here]
        combined = []
        for j in range(slots):
            total = weight[j : j + 1]
            for i in range(slots):
                if i != j:
                    total = total + jnp.where(
                        index[i : i + 1] == index[j : j + 1], weight[i : i + 1], 0.0
                    )
            combined.append(total)

        for tile in range(0, columns, 8):
            row = lax.broadcasted_iota(jnp.int32, (8, chunk), 0) + tile
            value = jnp.zeros((8, chunk), jnp.float32)
            for j in range(slots):
                value = jnp.where(index[j : j + 1] == row, combined[j], value)
            lattice_ref[tile : tile + 8, :] = value
        lattice = lattice_ref[...]
        lattice_first = lattice.astype(jnp.bfloat16)
        lattice_rest = (lattice - lattice_first.astype(jnp.float32)).astype(jnp.bfloat16)
        right = distance_factors(base_ref[:, here], False).astype(jnp.bfloat16)
        squared = jnp.dot(left_ref[...], right, preferred_element_type=jnp.float32)
        squared = jnp.maximum(squared, 1e-30)
        near = jnp.maximum(1.0 - squared * lax.rsqrt(squared), 0.0)
        power = near * near
        kernel = power * power * (1.25 - near)
        kernel_first = kernel.astype(jnp.bfloat16)
        kernel_rest = (kernel - kernel_first.astype(jnp.float32)).astype(jnp.bfloat16)
        over = (((1,), (1,)), ((), ()))
        out_ref[...] += lax.dot_general(
            jnp.concatenate([kernel_first, kernel_rest, kernel_first], axis=1),
            jnp.concatenate([lattice_first, lattice_first, lattice_rest], axis=1),
            over,
            preferred_element_type=jnp.float32,
        )


def control_kernel(scale, copies, *refs):
    sens_refs, (response_ref, out_ref) = refs[:-2], refs[-2:]
    total = sens_refs[0][...]
    for ref in sens_refs[1:]:
        total = total + ref[...]
    grad = jnp.dot(
        total * scale,
        response_ref[...],
        precision=lax.Precision.HIGHEST,
        preferred_element_type=jnp.float32,
    )
    for copy in range(copies):
        out_ref[copy] = grad


def vmem(count):
    return [pl.BlockSpec(memory_space=pltpu.VMEM)] * count


def body(
    adjoint_start,
    adjoint_rhs,
    off_blocks,
    diag_inverse,
    neighbours,
    node_weights,
    sens_blocks,
    cell_points,
    base_points,
    ffd_index,
    ffd_weight,
):
    nodes, _, cells = adjoint_start.shape
    faces = off_blocks.shape[1]
    blocks = cells // LANES
    per = blocks * nodes
    params = pltpu.CompilerParams(vmem_limit_bytes=VMEM_LIMIT)

    peers = lax.axis_size(CELL_AXES)
    up = [(i, i + 1) for i in range(peers - 1)]
    down = [(j, i) for i, j in up]
    rhs = rows_of(adjoint_rhs)
    off = rows_of(off_blocks.reshape(nodes, faces * 25, cells))
    inverse = rows_of(diag_inverse)
    sens = rows_of(sens_blocks)
    scratch = [
        pltpu.VMEM((3 * 5 * per, LANES), jnp.float32),
        pltpu.VMEM((faces * 25 * per, LANES), jnp.float32),
        pltpu.VMEM((faces * per, LANES), jnp.int32),
        pltpu.VMEM((faces * per, LANES), jnp.int32),
    ]

    base_count = base_points.shape[1]
    owned = base_count // lax.axis_size("nodes")
    chunk = min(256, owned)
    response = pl.pallas_call(
        functools.partial(response_kernel, chunk),
        out_shape=jax.ShapeDtypeStruct((cells, FFD), jnp.float32),
        in_specs=vmem(4),
        out_specs=pl.BlockSpec(memory_space=pltpu.VMEM),
        scratch_shapes=[
            pltpu.VMEM((cells, 64), jnp.bfloat16),
            pltpu.VMEM((FFD, chunk), jnp.float32),
        ],
        compiler_params=params,
        cost_estimate=pl.CostEstimate(
            flops=2 * 3 * cells * owned * FFD, bytes_accessed=4 * cells * FFD, transcendentals=0
        ),
        name="response",
    )(cell_points, base_points, ffd_index.T, ffd_weight.T)

    adjoint = rows_of(adjoint_start)
    for step in range(SWEEPS):
        before = lax.ppermute(adjoint, CELL_AXES, up)
        after = lax.ppermute(adjoint, CELL_AXES, down)
        common = (before, adjoint, after, rhs, off, inverse, neighbours)
        cost = pl.CostEstimate(
            flops=2 * 10 * 35 * cells, bytes_accessed=2 * faces * 25 * per * LANES, transcendentals=0
        )
        if step < SWEEPS - 1:
            adjoint = pl.pallas_call(
                functools.partial(sweep_kernel, nodes),
                out_shape=jax.ShapeDtypeStruct((5 * per, LANES), jnp.float32),
                in_specs=vmem(7),
                out_specs=pl.BlockSpec(memory_space=pltpu.VMEM),
                scratch_shapes=scratch,
                compiler_params=params,
                cost_estimate=cost,
                name="sweep",
            )(*common)
        else:
            adjoint, part_sens = pl.pallas_call(
                functools.partial(last_sweep_kernel, nodes),
                out_shape=(
                    jax.ShapeDtypeStruct((5 * per, LANES), jnp.float32),
                    jax.ShapeDtypeStruct((3, cells), jnp.float32),
                ),
                in_specs=vmem(7) + [pl.BlockSpec(memory_space=pltpu.SMEM)] + vmem(1),
                out_specs=tuple(vmem(2)),
                scratch_shapes=scratch + [pltpu.VMEM((3 * per, LANES), jnp.float32)],
                compiler_params=params,
                cost_estimate=cost,
                name="last_sweep",
            )(*common, node_weights, sens)

    node_peers = lax.axis_size("nodes")
    all_sens = [part_sens]
    for shift in range(1, node_peers):
        ring = [(i, (i + shift) % node_peers) for i in range(node_peers)]
        all_sens.append(lax.ppermute(part_sens, "nodes", ring))
    holders = lax.axis_size(SUM_AXES)
    scale = 4.0 / math.sqrt(cells * peers)
    copies = pl.pallas_call(
        functools.partial(control_kernel, scale, holders),
        out_shape=jax.ShapeDtypeStruct((holders, 3, FFD), jnp.float32),
        in_specs=vmem(node_peers + 1),
        out_specs=pl.BlockSpec(memory_space=pltpu.VMEM),
        compiler_params=params,
        name="control",
    )(*all_sens, response)
    gathered = lax.all_to_all(copies, SUM_AXES, 0, 0, tiled=True)
    control_grad = jnp.sum(gathered, axis=0)
    return (from_rows(adjoint, nodes, cells), control_grad)


def solution(mesh):
    return jax.shard_map(
        body,
        mesh=mesh,
        in_specs=(
            P("nodes", None, ("groups", "cells", "sub")),
            P("nodes", None, ("groups", "cells", "sub")),
            P("nodes", None, None, ("groups", "cells", "sub")),
            P("nodes", None, ("groups", "cells", "sub")),
            P(None, ("cells", "sub")),
            P("nodes"),
            P("nodes", None, ("groups", "cells", "sub")),
            P(None, ("cells", "sub")),
            P(),
            P(),
            P(),
        ),
        out_specs=(P("nodes", None, ("groups", "cells", "sub")), P("groups", None)),
        check_vma=False,
    )
```

```python
import functools
import math

import jax
import jax.numpy as jnp
from jax import lax
from jax.experimental import pallas as pl
from jax.experimental.pallas import tpu as pltpu
from jax.sharding import PartitionSpec as P

SWEEPS = 2
FFD = 512
SUPPORT_RADIUS = 0.3
LANES = 128
CELL_AXES = ("cells", "sub")
FACTOR_ROWS = 64
PARAMS = pltpu.CompilerParams(vmem_limit_bytes=24 * 1024 * 1024)
VMEM = pl.BlockSpec(memory_space=pltpu.VMEM)
HBM = pl.BlockSpec(memory_space=pltpu.HBM)


def rows_of(array):
    nodes, rows, cells = array.shape
    blocks = cells // LANES
    split = array.reshape(nodes, rows, blocks, LANES)
    return split.transpose(1, 2, 0, 3).reshape(rows * blocks * nodes, LANES)


def from_rows(array, nodes, cells):
    blocks = cells // LANES
    split = array.reshape(-1, blocks, nodes, LANES)
    return split.transpose(2, 0, 1, 3).reshape(nodes, -1, cells)


def in_hbm(*arrays):
    return [pltpu.with_memory_space_constraint(array, pltpu.HBM) for array in arrays]


def prepare_kernel(
    nodes,
    off_in,
    inverse_in,
    rhs_in,
    sens_in,
    neigh_in,
    weight_in,
    index_in,
    spread_in,
    start_in,
    off_ref,
    inverse_ref,
    rhs_ref,
    sens_ref,
    lane_ref,
    step_ref,
    high_ref,
    spread_ref,
    one_hot_ref,
    start_ref,
    off_buf,
    sens_buf,
    neigh_buf,
    weight_buf,
    index_buf,
    sems,
):
    owned = index_buf.shape[1]
    start = pl.multiple_of(lax.axis_index("nodes") * owned, LANES)
    mine = pl.ds(start, owned)
    pairs = (
        (neigh_in, neigh_buf),
        (index_in.at[:, mine], index_buf),
        (off_in, off_buf),
        (weight_in, weight_buf),
        (sens_in, sens_buf),
        (spread_in.at[:, mine], spread_ref),
        (inverse_in, inverse_ref),
        (rhs_in, rhs_ref),
        (start_in, start_ref),
    )
    copies = [pltpu.make_async_copy(a, b, sems.at[i]) for i, (a, b) in enumerate(pairs)]
    for copy in copies:
        copy.start()

    faces, cells = neigh_buf.shape
    blocks = cells // LANES
    per = blocks * nodes
    first_cell = lax.axis_index(CELL_AXES) * cells
    copies[0].wait()
    for block in range(blocks):
        index = neigh_buf[:, block * LANES : (block + 1) * LANES]
        local = index - first_cell + cells
        lane = jnp.bitwise_and(local, LANES - 1)
        step = jnp.right_shift(local, 7) - block
        step = jnp.where(index >= 0, step, -1)
        for node in range(nodes):
            rows = pl.ds(block * nodes + node, faces, stride=per)
            lane_ref[rows, :] = lane
            step_ref[rows, :] = step

    copies[1].wait()
    high_ref[...] = jnp.right_shift(index_buf[...], 7)
    piece = min(512, owned)
    for first in range(0, owned, piece):
        here = slice(first, first + piece)
        low = jnp.bitwise_and(index_buf[:, here], LANES - 1).astype(jnp.float32)
        low = low.astype(jnp.bfloat16)
        row = lax.broadcasted_iota(jnp.int32, (LANES, piece), 0).astype(jnp.float32)
        row = row.astype(jnp.bfloat16)
        for j in range(index_buf.shape[0]):
            hit = jnp.broadcast_to(low[j : j + 1], (LANES, piece)) == row
            one_hot_ref[j * LANES : (j + 1) * LANES, here] = jnp.where(
                hit, jnp.bfloat16(1.0), jnp.bfloat16(0.0)
            )

    copies[2].wait()
    off_ref[...] = off_buf[...].astype(jnp.float32)
    copies[3].wait()
    copies[4].wait()
    row_node = lax.rem(lax.broadcasted_iota(jnp.int32, (per, LANES), 0), nodes)
    weights = jnp.zeros((per, LANES), jnp.float32)
    for node in range(nodes):
        weights = jnp.where(row_node == node, weight_buf[node], weights)
    for row in range(0, sens_buf.shape[0], per):
        here = slice(row, row + per)
        sens_ref[here, :] = sens_buf[here, :].astype(jnp.float32) * weights
    for copy in copies[5:]:
        copy.wait()


def sweep_into(
    blocks, first_ref, second_ref, own_ref, rhs_ref, off_ref, inverse_ref, lane_ref, step_ref,
    out_ref, window_ref,
):
    per = rhs_ref.shape[0] // 5
    nodes = per // blocks
    faces = lane_ref.shape[0] // per
    odd = lax.rem(lax.axis_index(CELL_AXES), 2)
    place = pl.multiple_of((1 - odd) * 2 * per, 8)
    other = pl.multiple_of(odd * 2 * per, 8)
    for b in range(5):
        rows = slice(b * per, (b + 1) * per)
        base = 3 * b * per
        window_ref[pl.ds(base + place, per), :] = first_ref[rows, :]
        window_ref[base + per : base + 2 * per, :] = own_ref[rows, :]
        window_ref[pl.ds(base + other, per), :] = second_ref[rows, :]
    for half in range(0, per, 8):
        lanes = [lane_ref[f * per + half : f * per + half + 8, :] for f in range(faces)]
        dist = [step_ref[f * per + half : f * per + half + 8, :] for f in range(faces)]
        beside = [[jnp.zeros((8, LANES), jnp.float32)] * 5 for _ in range(faces)]
        for d in range(2 * blocks + 1):
            here = [dist[f] == d for f in range(faces)]
            for b in range(5):
                table = window_ref[pl.ds(3 * b * per + half + d * nodes, 8), :]
                for f in range(faces):
                    got = jnp.take_along_axis(
                        table, lanes[f], axis=1, mode="promise_in_bounds"
                    )
                    beside[f][b] = jnp.where(here[f], got, beside[f][b])
        remaining = []
        for a in range(5):
            total = rhs_ref[a * per + half : a * per + half + 8, :]
            for f in range(faces):
                for b in range(5):
                    row = (f * 25 + 5 * a + b) * per + half
                    total = total - off_ref[row : row + 8, :] * beside[f][b]
            remaining.append(total)
        for a in range(5):
            total = None
            for b in range(5):
                row = (5 * a + b) * per + half
                term = inverse_ref[row : row + 8, :] * remaining[b]
                total = term if total is None else total + term
            out_ref[a * per + half : a * per + half + 8, :] = total


def sweep_kernel(blocks, *refs):
    sweep_into(blocks, *refs)


def last_sweep_kernel(blocks, *refs):
    ins, (sens_ref, _, out_ref, sens_out_ref, window_ref, part_ref) = refs[:8], refs[8:]
    sweep_into(blocks, *ins, out_ref, window_ref)
    per = out_ref.shape[0] // 5
    nodes = per // blocks
    for k in range(3):
        total = None
        for a in range(5):
            row = (3 * a + k) * per
            term = out_ref[a * per : (a + 1) * per, :] * sens_ref[row : row + per, :]
            total = term if total is None else total + term
        part_ref[k * per : (k + 1) * per, :] = total
    for block in range(blocks):
        total = None
        for node in range(nodes):
            term = part_ref[pl.ds(block * nodes + node, 3, stride=per), :]
            total = term if total is None else total + term
        sens_out_ref[:, block * LANES : (block + 1) * LANES] = total


def pieces(value, count):
    found = []
    for _ in range(count):
        piece = value.astype(jnp.bfloat16).astype(jnp.float32)
        found.append(piece)
        value = value - piece
    return found


def distance_factors(points, left):
    count = points.shape[1]
    scaled = (points - 0.5) * (1.0 / SUPPORT_RADIUS)
    scaled = jnp.concatenate([scaled, jnp.zeros((5, count), jnp.float32)], axis=0)
    norm = jnp.sum(scaled * scaled, axis=0, keepdims=True)
    norms = pieces(jnp.broadcast_to(norm, (8, count)), 3)
    row = lax.broadcasted_iota(jnp.int32, (8, count), 0)
    norm_block = jnp.zeros((8, count), jnp.float32)
    for place in range(3):
        norm_block = jnp.where(row == place, norms[place], norm_block)
    ones_block = jnp.where(row < 3, 1.0, 0.0)
    first, second, third = pieces(scaled, 3)
    if left:
        dims = [first, first, second, second, first, third]
        dims = [-2.0 * part for part in dims]
        blocks = dims + [norm_block, ones_block]
    else:
        dims = [first, second, first, second, third, first]
        blocks = dims + [ones_block, norm_block]
    return jnp.concatenate(blocks, axis=0)


def wendland_kernel(
    cell_in, base_in, _, kernel_ref, token_ref, cell_buf, base_buf, left_ref, right_ref, sems
):
    cells, owned = kernel_ref.shape
    start = pl.multiple_of(lax.axis_index("nodes") * owned, LANES)
    copies = [
        pltpu.make_async_copy(cell_in, cell_buf, sems.at[0]),
        pltpu.make_async_copy(base_in.at[:, pl.ds(start, owned)], base_buf, sems.at[1]),
    ]
    for copy in copies:
        copy.start()
    token_ref[...] = jnp.zeros_like(token_ref)
    copies[0].wait()
    left_ref[...] = distance_factors(cell_buf[...], True).T.astype(jnp.bfloat16)
    copies[1].wait()
    right_ref[...] = distance_factors(base_buf[...], False).astype(jnp.bfloat16)
    tile, wide = 64, min(256, owned)

    @pl.loop(0, cells // tile)
    def _(step):
        rows = pl.ds(pl.multiple_of(step * tile, tile), tile)
        left = left_ref[rows, :]
        for first in range(0, owned, wide):
            here = slice(first, first + wide)
            squared = jnp.dot(left, right_ref[:, here], preferred_element_type=jnp.float32)
            squared = jnp.maximum(squared, 1e-30)
            near = jnp.maximum(1.0 - squared * lax.rsqrt(squared), 0.0)
            power = near * near
            kernel_ref[rows, here] = power * power * (1.25 - near)


def control_kernel(scale, *refs):
    sens_refs = refs[:-7]
    kernel_ref, high_ref, spread_ref, one_hot_ref, out_ref, sens_buf, part_ref = refs[-7:]
    cells, owned = kernel_ref.shape
    slots = high_ref.shape[0]
    groups = FFD // LANES
    total = sens_refs[0][...]
    for ref in sens_refs[1:]:
        total = total + ref[...]
    total = jnp.concatenate([total * scale, jnp.zeros((5, cells), jnp.float32)], axis=0).T
    for k in range(3):
        sens_buf[k * cells : (k + 1) * cells, :] = jnp.broadcast_to(
            total[:, k : k + 1], (cells, LANES)
        )
    part_ref[...] = jnp.zeros_like(part_ref)
    wide = min(4 * LANES, owned)
    tile = 64
    for first in range(0, owned, wide):

        def add(step, sums):
            sums = list(sums)
            for inner in range(0, tile, 8):
                row = pl.multiple_of(step * tile, tile) + inner
                value = [
                    kernel_ref[pl.ds(row, 8), first + lane : first + lane + LANES]
                    for lane in range(0, wide, LANES)
                ]
                for k in range(3):
                    sens = sens_buf[pl.ds(k * cells + row, 8), :]
                    for place in range(len(value)):
                        at = k * len(value) + place
                        sums[at] = sums[at] + value[place] * sens
            return tuple(sums)

        count = wide // LANES
        zero = jnp.zeros((8, LANES), jnp.float32)
        sums = lax.fori_loop(0, cells // tile, add, (zero,) * (3 * count))
        for k in range(3):
            for place in range(count):
                lane = first + place * LANES
                grad = jnp.sum(sums[k * count + place], axis=0, keepdims=True)
                grad = grad * spread_ref[:, lane : lane + LANES]
                high = high_ref[:, lane : lane + LANES]
                for group in range(groups):
                    row = lane // LANES * slots * 16 + k * groups + group
                    part_ref[pl.ds(row, slots, stride=16), :] = jnp.where(
                        high == group, grad, 0.0
                    )
    result = jnp.zeros((32, LANES), jnp.float32)
    over = (((1,), (1,)), ((), ()))
    for j in range(slots):
        part = jnp.concatenate(
            [
                part_ref[(block * slots + j) * 16 : (block * slots + j + 1) * 16, :]
                for block in range(owned // LANES)
            ],
            axis=1,
        )
        part_first = part.astype(jnp.bfloat16)
        part_rest = (part - part_first.astype(jnp.float32)).astype(jnp.bfloat16)
        result = result + lax.dot_general(
            jnp.concatenate([part_first, part_rest], axis=0),
            one_hot_ref[j * LANES : (j + 1) * LANES, :],
            over,
            preferred_element_type=jnp.float32,
        )
    out_ref[...] = result[:16] + result[16:]


def tree(values):
    while len(values) > 1:
        values = [a + b for a, b in zip(values[::2], values[1::2])]
    return values[0]


def add_kernel(*refs):
    refs[-1][...] = tree([ref[...] for ref in refs[:-1]])


def finish_kernel(*refs):
    total = tree([ref[...] for ref in refs[:-1]])
    groups = FFD // LANES
    for k in range(3):
        for group in range(groups):
            row = k * groups + group
            refs[-1][k : k + 1, group * LANES : (group + 1) * LANES] = total[row : row + 1]


def exchanged(value, axes):
    peers = lax.axis_size(axes)
    if peers > 8 or peers & (peers - 1):
        return [lax.psum(value, axes)]
    return [value] + [
        lax.ppermute(value, axes, [(i, i ^ shift) for i in range(peers)])
        for shift in range(1, peers)
    ]


def body(
    adjoint_start,
    adjoint_rhs,
    off_blocks,
    diag_inverse,
    neighbours,
    node_weights,
    sens_blocks,
    cell_points,
    base_points,
    ffd_index,
    ffd_weight,
):
    nodes, _, cells = adjoint_start.shape
    faces = off_blocks.shape[1]
    blocks = cells // LANES
    per = blocks * nodes
    slots = ffd_index.shape[1]
    owned = base_points.shape[1] // lax.axis_size("nodes")
    peers = lax.axis_size(CELL_AXES)
    f32, i32, bf16 = jnp.float32, jnp.int32, jnp.bfloat16

    def shape(dims, dtype=f32):
        return jax.ShapeDtypeStruct(dims, dtype)

    def cost(flops, moved):
        return pl.CostEstimate(flops=flops, bytes_accessed=moved, transcendentals=0)

    def swaps(array):
        first = [(i, i ^ 1) for i in range(peers) if i ^ 1 < peers]
        second = [(i, i + 1 if i % 2 else i - 1) for i in range(peers)]
        second = [(i, j) for i, j in second if 0 <= j < peers]
        far = lax.ppermute(array, CELL_AXES, second)
        close = lax.ppermute(array, CELL_AXES, first)
        return far, close

    adjoint = rows_of(adjoint_start)
    far, close = swaps(adjoint)
    prepared = pl.pallas_call(
        functools.partial(prepare_kernel, nodes),
        out_shape=(
            shape((faces * 25 * per, LANES)),
            shape((25 * per, LANES)),
            shape((5 * per, LANES)),
            shape((15 * per, LANES)),
            shape((faces * per, LANES), i32),
            shape((faces * per, LANES), i32),
            shape((slots, owned), i32),
            shape((slots, owned)),
            shape((slots * LANES, owned), bf16),
            shape((5 * per, LANES)),
        ),
        in_specs=[HBM] * 9,
        out_specs=(VMEM,) * 10,
        scratch_shapes=[
            pltpu.VMEM((faces * 25 * per, LANES), bf16),
            pltpu.VMEM((15 * per, LANES), bf16),
            pltpu.VMEM((faces, cells), i32),
            pltpu.SMEM((nodes,), f32),
            pltpu.VMEM((slots, owned), i32),
            pltpu.SemaphoreType.DMA((9,)),
        ],
        compiler_params=PARAMS,
        cost_estimate=cost(10**9, 10**7),
        name="prepare",
    )(
        *in_hbm(
            rows_of(off_blocks.reshape(nodes, faces * 25, cells)),
            rows_of(diag_inverse),
            rows_of(adjoint_rhs),
            rows_of(sens_blocks),
            neighbours,
            node_weights,
            ffd_index.T,
            ffd_weight.T,
            adjoint,
        )
    )
    off, inverse, rhs, sens, lane, step, high, spread, one_hot, adjoint = prepared
    window = pltpu.VMEM((3 * 5 * per, LANES), f32)
    sweep_cost = cost(2 * 10 * 35 * cells, 4 * faces * 25 * per * LANES)

    for _ in range(SWEEPS - 1):
        adjoint = pl.pallas_call(
            functools.partial(sweep_kernel, blocks),
            out_shape=shape((5 * per, LANES)),
            in_specs=[VMEM] * 8,
            out_specs=VMEM,
            scratch_shapes=[window],
            compiler_params=PARAMS,
            cost_estimate=sweep_cost,
            name="sweep",
        )(close, far, adjoint, rhs, off, inverse, lane, step)
        far, close = swaps(adjoint)

    kernel, token = pl.pallas_call(
        wendland_kernel,
        out_shape=(shape((cells, owned)), shape((8, LANES))),
        in_specs=[HBM, HBM, VMEM],
        out_specs=(VMEM, VMEM),
        scratch_shapes=[
            pltpu.VMEM((3, cells), f32),
            pltpu.VMEM((3, owned), f32),
            pltpu.VMEM((cells, FACTOR_ROWS), bf16),
            pltpu.VMEM((FACTOR_ROWS, owned), bf16),
            pltpu.SemaphoreType.DMA((2,)),
        ],
        compiler_params=PARAMS,
        cost_estimate=cost(10**9, 10**7),
        name="wendland",
    )(*in_hbm(cell_points, base_points), adjoint)

    adjoint, part_sens = pl.pallas_call(
        functools.partial(last_sweep_kernel, blocks),
        out_shape=(shape((5 * per, LANES)), shape((3, cells))),
        in_specs=[VMEM] * 10,
        out_specs=(VMEM, VMEM),
        scratch_shapes=[window, pltpu.VMEM((3 * per, LANES), f32)],
        compiler_params=PARAMS,
        cost_estimate=sweep_cost,
        name="last_sweep",
    )(close, far, adjoint, rhs, off, inverse, lane, step, sens, token)

    all_sens = exchanged(part_sens, "nodes")
    scale = 4.0 / math.sqrt(cells * peers)
    partial = pl.pallas_call(
        functools.partial(control_kernel, scale),
        out_shape=shape((16, LANES)),
        in_specs=[VMEM] * (len(all_sens) + 4),
        out_specs=VMEM,
        scratch_shapes=[
            pltpu.VMEM((3 * cells, LANES), f32),
            pltpu.VMEM((owned // LANES * slots * 16, LANES), f32),
        ],
        compiler_params=PARAMS,
        name="control",
    )(*all_sens, kernel, high, spread, one_hot)

    close_parts = exchanged(partial, ("nodes", "sub"))
    partial = pl.pallas_call(
        add_kernel, out_shape=shape((16, LANES)), name="add", compiler_params=PARAMS
    )(*close_parts)
    control_grad = pl.pallas_call(
        finish_kernel, out_shape=shape((3, FFD)), name="finish", compiler_params=PARAMS
    )(*exchanged(partial, "cells"))
    return (from_rows(adjoint, nodes, cells), control_grad)


def solution(mesh):
    return jax.shard_map(
        body,
        mesh=mesh,
        in_specs=(
            P("nodes", None, ("groups", "cells", "sub")),
            P("nodes", None, ("groups", "cells", "sub")),
            P("nodes", None, None, ("groups", "cells", "sub")),
            P("nodes", None, ("groups", "cells", "sub")),
            P(None, ("cells", "sub")),
            P("nodes"),
            P("nodes", None, ("groups", "cells", "sub")),
            P(None, ("cells", "sub")),
            P(),
            P(),
            P(),
        ),
        out_specs=(P("nodes", None, ("groups", "cells", "sub")), P("groups", None)),
        check_vma=False,
    )
```

```python
import functools
import math

import jax
import jax.numpy as jnp
from jax import lax
from jax.experimental import pallas as pl
from jax.experimental.pallas import tpu as pltpu
from jax.sharding import PartitionSpec as P

SWEEPS = 2
FFD = 512
SUPPORT_RADIUS = 0.3
LANES = 128
CELL_AXES = ("cells", "sub")
FACTOR_ROWS = 64
PARAMS = pltpu.CompilerParams(vmem_limit_bytes=24 * 1024 * 1024)
VMEM = pl.BlockSpec(memory_space=pltpu.VMEM)
HBM = pl.BlockSpec(memory_space=pltpu.HBM)


def rows_of(array):
    nodes, rows, cells = array.shape
    blocks = cells // LANES
    split = array.reshape(nodes, rows, blocks, LANES)
    return split.transpose(1, 2, 0, 3).reshape(rows * blocks * nodes, LANES)


def from_rows(array, nodes, cells):
    blocks = cells // LANES
    split = array.reshape(-1, blocks, nodes, LANES)
    return split.transpose(2, 0, 1, 3).reshape(nodes, -1, cells)


def in_hbm(*arrays):
    return [pltpu.with_memory_space_constraint(array, pltpu.HBM) for array in arrays]


def prepare_kernel(
    nodes,
    off_in,
    inverse_in,
    rhs_in,
    sens_in,
    neigh_in,
    weight_in,
    index_in,
    spread_in,
    start_in,
    cell_in,
    base_in,
    off_ref,
    inverse_ref,
    rhs_ref,
    sens_ref,
    lane_ref,
    step_ref,
    spread_ref,
    one_hot_ref,
    start_ref,
    left_ref,
    right_ref,
    off_buf,
    sens_buf,
    neigh_buf,
    weight_buf,
    index_buf,
    spread_buf,
    cell_buf,
    base_buf,
    sems,
):
    slots, owned = index_buf.shape
    start = pl.multiple_of(lax.axis_index("nodes") * owned, LANES)
    mine = pl.ds(start, owned)
    pairs = (
        (neigh_in, neigh_buf),
        (index_in.at[:, mine], index_buf),
        (spread_in.at[:, mine], spread_buf),
        (cell_in, cell_buf),
        (base_in.at[:, mine], base_buf),
        (off_in, off_buf),
        (weight_in, weight_buf),
        (sens_in, sens_buf),
        (inverse_in, inverse_ref),
        (rhs_in, rhs_ref),
        (start_in, start_ref),
    )
    copies = [pltpu.make_async_copy(a, b, sems.at[i]) for i, (a, b) in enumerate(pairs)]
    for copy in copies:
        copy.start()

    faces, cells = neigh_buf.shape
    blocks = cells // LANES
    per = blocks * nodes
    first_cell = lax.axis_index(CELL_AXES) * cells
    copies[0].wait()
    for block in range(blocks):
        index = neigh_buf[:, block * LANES : (block + 1) * LANES]
        local = index - first_cell + cells
        lane = jnp.bitwise_and(local, LANES - 1)
        step = jnp.right_shift(local, 7) - block
        step = jnp.where(index >= 0, step, -1)
        for node in range(nodes):
            rows = pl.ds(block * nodes + node, faces, stride=per)
            lane_ref[rows, :] = lane
            step_ref[rows, :] = step

    copies[1].wait()
    copies[2].wait()
    groups = FFD // LANES
    piece = min(512, owned)
    for first in range(0, owned, piece):
        here = slice(first, first + piece)
        low = jnp.bitwise_and(index_buf[:, here], LANES - 1).astype(jnp.float32)
        low = low.astype(jnp.bfloat16)
        high = jnp.right_shift(index_buf[:, here], 7)
        row = lax.broadcasted_iota(jnp.int32, (LANES, piece), 0).astype(jnp.float32)
        row = row.astype(jnp.bfloat16)
        part = lax.broadcasted_iota(jnp.int32, (16, piece), 0)
        part = jnp.where(part < 3 * groups, lax.rem(part, groups), -1)
        for j in range(slots):
            hit = jnp.broadcast_to(low[j : j + 1], (LANES, piece)) == row
            one_hot_ref[j * LANES : (j + 1) * LANES, here] = jnp.where(
                hit, jnp.bfloat16(1.0), jnp.bfloat16(0.0)
            )
            spread_ref[j * 16 : (j + 1) * 16, here] = jnp.where(
                high[j : j + 1] == part, spread_buf[j : j + 1, here], 0.0
            )

    copies[3].wait()
    left_ref[...] = distance_factors(cell_buf[...], True).T.astype(jnp.bfloat16)
    copies[4].wait()
    right_ref[...] = distance_factors(base_buf[...], False).astype(jnp.bfloat16)

    copies[5].wait()
    off_ref[...] = off_buf[...].astype(jnp.float32)
    copies[6].wait()
    copies[7].wait()
    row_node = lax.rem(lax.broadcasted_iota(jnp.int32, (per, LANES), 0), nodes)
    weights = jnp.zeros((per, LANES), jnp.float32)
    for node in range(nodes):
        weights = jnp.where(row_node == node, weight_buf[node], weights)
    for row in range(0, sens_buf.shape[0], per):
        here = slice(row, row + per)
        sens_ref[here, :] = sens_buf[here, :].astype(jnp.float32) * weights
    for copy in copies[8:]:
        copy.wait()


def sweep_into(
    blocks, first_ref, second_ref, own_ref, rhs_ref, off_ref, inverse_ref, lane_ref, step_ref,
    out_ref, window_ref, table_ref,
):
    per = rhs_ref.shape[0] // 5
    nodes = per // blocks
    faces = lane_ref.shape[0] // per
    odd = lax.rem(lax.axis_index(CELL_AXES), 2)
    place = pl.multiple_of((1 - odd) * 2 * per, 8)
    other = pl.multiple_of(odd * 2 * per, 8)
    width = 3 * per
    for b in range(5):
        rows = slice(b * per, (b + 1) * per)
        base = b * width
        window_ref[pl.ds(base + place, per), :] = first_ref[rows, :]
        window_ref[base + per : base + 2 * per, :] = own_ref[rows, :]
        window_ref[pl.ds(base + other, per), :] = second_ref[rows, :]
    for shift in range(8 // nodes):
        for b in range(5):
            for tile in range(0, width - (8 if shift else 0), 8):
                to = (shift * 5 + b) * width + tile
                table_ref[to : to + 8, :] = window_ref[
                    pl.ds(b * width + tile + shift * nodes, 8), :
                ]
    for half in range(0, per, 8):
        remaining = [rhs_ref[a * per + half : a * per + half + 8, :] for a in range(5)]
        for f in range(faces):
            lanes = lane_ref[f * per + half : f * per + half + 8, :]
            dist = step_ref[f * per + half : f * per + half + 8, :]
            beside = [jnp.zeros((8, LANES), jnp.float32)] * 5
            for d in range(2 * blocks + 1):
                here = dist == d
                first = half + d * nodes
                for b in range(5):
                    at = ((first % 8) // nodes * 5 + b) * width + first // 8 * 8
                    got = jnp.take_along_axis(
                        table_ref[at : at + 8, :], lanes, axis=1, mode="promise_in_bounds"
                    )
                    beside[b] = jnp.where(here, got, beside[b])
            for a in range(5):
                for b in range(5):
                    row = (f * 25 + 5 * a + b) * per + half
                    remaining[a] = remaining[a] - off_ref[row : row + 8, :] * beside[b]
        for a in range(5):
            total = None
            for b in range(5):
                row = (5 * a + b) * per + half
                term = inverse_ref[row : row + 8, :] * remaining[b]
                total = term if total is None else total + term
            out_ref[a * per + half : a * per + half + 8, :] = total


def sweep_kernel(blocks, *refs):
    sweep_into(blocks, *refs)


def last_sweep_kernel(blocks, *refs):
    ins, rest = refs[:8], refs[8:]
    sens_ref, _, out_ref, sens_out_ref, window_ref, table_ref, part_ref = rest
    sweep_into(blocks, *ins, out_ref, window_ref, table_ref)
    per = out_ref.shape[0] // 5
    nodes = per // blocks
    for k in range(3):
        total = None
        for a in range(5):
            row = (3 * a + k) * per
            term = out_ref[a * per : (a + 1) * per, :] * sens_ref[row : row + per, :]
            total = term if total is None else total + term
        part_ref[k * per : (k + 1) * per, :] = total
    for block in range(blocks):
        total = None
        for node in range(nodes):
            term = part_ref[pl.ds(block * nodes + node, 3, stride=per), :]
            total = term if total is None else total + term
        sens_out_ref[:, block * LANES : (block + 1) * LANES] = total


def pieces(value, count):
    found = []
    for _ in range(count):
        piece = value.astype(jnp.bfloat16).astype(jnp.float32)
        found.append(piece)
        value = value - piece
    return found


def distance_factors(points, left):
    count = points.shape[1]
    scaled = (points - 0.5) * (1.0 / SUPPORT_RADIUS)
    scaled = jnp.concatenate([scaled, jnp.zeros((5, count), jnp.float32)], axis=0)
    norm = jnp.sum(scaled * scaled, axis=0, keepdims=True)
    norms = pieces(jnp.broadcast_to(norm, (8, count)), 3)
    row = lax.broadcasted_iota(jnp.int32, (8, count), 0)
    norm_block = jnp.zeros((8, count), jnp.float32)
    for place in range(3):
        norm_block = jnp.where(row == place, norms[place], norm_block)
    ones_block = jnp.where(row < 3, 1.0, 0.0)
    first, second, third = pieces(scaled, 3)
    if left:
        dims = [first, first, second, second, first, third]
        dims = [-2.0 * part for part in dims]
        blocks = dims + [norm_block, ones_block]
    else:
        dims = [first, second, first, second, third, first]
        blocks = dims + [ones_block, norm_block]
    return jnp.concatenate(blocks, axis=0)


def wendland_kernel(first_cell, left_ref, right_ref, _, first_ref, rest_ref):
    cells, owned = first_ref.shape
    tile, wide = min(128, cells), min(256, owned)

    @pl.loop(0, cells // tile)
    def _(step):
        row = pl.multiple_of(step * tile, tile)
        left = left_ref[pl.ds(row + first_cell, tile), :]
        for lane in range(0, owned, wide):
            here = slice(lane, lane + wide)
            squared = jnp.dot(left, right_ref[:, here], preferred_element_type=jnp.float32)
            squared = jnp.maximum(squared, 1e-30)
            near = jnp.maximum(1.0 - squared * lax.rsqrt(squared), 0.0)
            power = near * near
            kernel = power * power * (1.25 - near)
            first = kernel.astype(jnp.bfloat16)
            first_ref[pl.ds(row, tile), here] = first
            rest_ref[pl.ds(row, tile), here] = (kernel - first.astype(jnp.float32)).astype(
                jnp.bfloat16
            )


def control_kernel(scale, *refs):
    (*sens_refs, near_first, near_rest, far_first, far_rest, spread_ref, one_hot_ref, out_ref) = refs
    cells = sens_refs[0].shape[1]
    half = near_first.shape[0]
    slots = spread_ref.shape[0] // 16
    groups = FFD // LANES
    total = sens_refs[0][...]
    for ref in sens_refs[1:]:
        total = total + ref[...]
    total = total * scale
    row = lax.broadcasted_iota(jnp.int32, (16, cells), 0)
    sens = jnp.zeros((16, cells), jnp.float32)
    for k in range(3):
        mine = jnp.logical_and(row >= k * groups, row < (k + 1) * groups)
        sens = jnp.where(mine, total[k : k + 1], sens)

    def halves(value):
        first = value.astype(jnp.bfloat16)
        rest = (value - first.astype(jnp.float32)).astype(jnp.bfloat16)
        return jnp.concatenate([first, rest], axis=0)

    sens = halves(sens)
    grad = None
    for part, ref in (
        (sens[:, :half], near_first),
        (sens[:, :half], near_rest),
        (sens[:, half:], far_first),
        (sens[:, half:], far_rest),
    ):
        term = jnp.dot(part, ref[...], preferred_element_type=jnp.float32)
        grad = term if grad is None else grad + term
    grad = grad[:16] + grad[16:]
    over = (((1,), (1,)), ((), ()))
    result = None
    for j in range(slots):
        term = lax.dot_general(
            halves(grad * spread_ref[j * 16 : (j + 1) * 16, :]),
            one_hot_ref[j * LANES : (j + 1) * LANES, :],
            over,
            preferred_element_type=jnp.float32,
        )
        result = term if result is None else result + term
    out_ref[...] = result[:16] + result[16:]


def tree(values):
    while len(values) > 1:
        values = [a + b for a, b in zip(values[::2], values[1::2])]
    return values[0]


def add_kernel(*refs):
    refs[-1][...] = tree([ref[...] for ref in refs[:-1]])


def finish_kernel(*refs):
    total = tree([ref[...] for ref in refs[:-1]])
    groups = FFD // LANES
    for k in range(3):
        for group in range(groups):
            row = k * groups + group
            refs[-1][k : k + 1, group * LANES : (group + 1) * LANES] = total[row : row + 1]


def exchanged(value, axes):
    peers = lax.axis_size(axes)
    if peers > 8 or peers & (peers - 1):
        return [lax.psum(value, axes)]
    return [value] + [
        lax.ppermute(value, axes, [(i, i ^ shift) for i in range(peers)])
        for shift in range(1, peers)
    ]


def body(
    adjoint_start,
    adjoint_rhs,
    off_blocks,
    diag_inverse,
    neighbours,
    node_weights,
    sens_blocks,
    cell_points,
    base_points,
    ffd_index,
    ffd_weight,
):
    nodes, _, cells = adjoint_start.shape
    faces = off_blocks.shape[1]
    blocks = cells // LANES
    per = blocks * nodes
    slots = ffd_index.shape[1]
    owned = base_points.shape[1] // lax.axis_size("nodes")
    peers = lax.axis_size(CELL_AXES)
    f32, i32, bf16 = jnp.float32, jnp.int32, jnp.bfloat16

    def shape(dims, dtype=f32):
        return jax.ShapeDtypeStruct(dims, dtype)

    def cost(flops, moved):
        return pl.CostEstimate(flops=flops, bytes_accessed=moved, transcendentals=0)

    def swaps(array):
        first = [(i, i ^ 1) for i in range(peers) if i ^ 1 < peers]
        second = [(i, i + 1 if i % 2 else i - 1) for i in range(peers)]
        second = [(i, j) for i, j in second if 0 <= j < peers]
        far = lax.ppermute(array, CELL_AXES, second)
        close = lax.ppermute(array, CELL_AXES, first)
        return far, close

    adjoint = rows_of(adjoint_start)
    far, close = swaps(adjoint)
    prepared = pl.pallas_call(
        functools.partial(prepare_kernel, nodes),
        out_shape=(
            shape((faces * 25 * per, LANES)),
            shape((25 * per, LANES)),
            shape((5 * per, LANES)),
            shape((15 * per, LANES)),
            shape((faces * per, LANES), i32),
            shape((faces * per, LANES), i32),
            shape((slots * 16, owned)),
            shape((slots * LANES, owned), bf16),
            shape((5 * per, LANES)),
            shape((cells, FACTOR_ROWS), bf16),
            shape((FACTOR_ROWS, owned), bf16),
        ),
        in_specs=[HBM] * 11,
        out_specs=(VMEM,) * 11,
        scratch_shapes=[
            pltpu.VMEM((faces * 25 * per, LANES), bf16),
            pltpu.VMEM((15 * per, LANES), bf16),
            pltpu.VMEM((faces, cells), i32),
            pltpu.SMEM((nodes,), f32),
            pltpu.VMEM((slots, owned), i32),
            pltpu.VMEM((slots, owned), f32),
            pltpu.VMEM((3, cells), f32),
            pltpu.VMEM((3, owned), f32),
            pltpu.SemaphoreType.DMA((11,)),
        ],
        compiler_params=PARAMS,
        cost_estimate=cost(10**9, 10**7),
        name="prepare",
    )(
        *in_hbm(
            rows_of(off_blocks.reshape(nodes, faces * 25, cells)),
            rows_of(diag_inverse),
            rows_of(adjoint_rhs),
            rows_of(sens_blocks),
            neighbours,
            node_weights,
            ffd_index.T,
            ffd_weight.T,
            adjoint,
            cell_points,
            base_points,
        )
    )
    off, inverse, rhs, sens, lane, step, spread, one_hot, adjoint, left, right = prepared
    scratch = [
        pltpu.VMEM((3 * 5 * per, LANES), f32),
        pltpu.VMEM((8 // nodes * 3 * 5 * per, LANES), f32),
    ]
    sweep_cost = cost(2 * 10 * 35 * cells, 4 * faces * 25 * per * LANES)

    for _ in range(SWEEPS - 1):
        adjoint = pl.pallas_call(
            functools.partial(sweep_kernel, blocks),
            out_shape=shape((5 * per, LANES)),
            in_specs=[VMEM] * 8,
            out_specs=VMEM,
            scratch_shapes=scratch,
            compiler_params=PARAMS,
            cost_estimate=sweep_cost,
            name="sweep",
        )(close, far, adjoint, rhs, off, inverse, lane, step)
        far, close = swaps(adjoint)

    def wendland(first_cell, count, behind):
        return pl.pallas_call(
            functools.partial(wendland_kernel, first_cell),
            out_shape=(shape((count, owned), bf16), shape((count, owned), bf16)),
            in_specs=[VMEM] * 3,
            out_specs=(VMEM, VMEM),
            compiler_params=PARAMS,
            cost_estimate=cost(10**9, 10**7),
            name="wendland",
        )(left, right, behind)

    half = cells // 2
    near_first, near_rest = wendland(0, half, adjoint)
    adjoint, part_sens = pl.pallas_call(
        functools.partial(last_sweep_kernel, blocks),
        out_shape=(shape((5 * per, LANES)), shape((3, cells))),
        in_specs=[VMEM] * 9 + [pl.BlockSpec(memory_space=pl.ANY)],
        out_specs=(VMEM, VMEM),
        scratch_shapes=scratch + [pltpu.VMEM((3 * per, LANES), f32)],
        compiler_params=PARAMS,
        cost_estimate=sweep_cost,
        name="last_sweep",
    )(close, far, adjoint, rhs, off, inverse, lane, step, sens, near_first)

    all_sens = exchanged(part_sens, "nodes")
    far_first, far_rest = wendland(half, cells - half, part_sens)
    scale = 4.0 / math.sqrt(cells * peers)
    partial = pl.pallas_call(
        functools.partial(control_kernel, scale),
        out_shape=shape((16, LANES)),
        in_specs=[VMEM] * (len(all_sens) + 6),
        out_specs=VMEM,
        compiler_params=PARAMS,
        name="control",
    )(*all_sens, near_first, near_rest, far_first, far_rest, spread, one_hot)

    close_parts = exchanged(partial, ("nodes", "sub"))
    partial = pl.pallas_call(
        add_kernel, out_shape=shape((16, LANES)), name="add", compiler_params=PARAMS
    )(*close_parts)
    control_grad = pl.pallas_call(
        finish_kernel, out_shape=shape((3, FFD)), name="finish", compiler_params=PARAMS
    )(*exchanged(partial, "cells"))
    return (from_rows(adjoint, nodes, cells), control_grad)


def solution(mesh):
    return jax.shard_map(
        body,
        mesh=mesh,
        in_specs=(
            P("nodes", None, ("groups", "cells", "sub")),
            P("nodes", None, ("groups", "cells", "sub")),
            P("nodes", None, None, ("groups", "cells", "sub")),
            P("nodes", None, ("groups", "cells", "sub")),
            P(None, ("cells", "sub")),
            P("nodes"),
            P("nodes", None, ("groups", "cells", "sub")),
            P(None, ("cells", "sub")),
            P(),
            P(),
            P(),
        ),
        out_specs=(P("nodes", None, ("groups", "cells", "sub")), P("groups", None)),
        check_vma=False,
    )
```

```python
import functools
import math

import jax
import jax.numpy as jnp
from jax import lax
from jax.experimental import pallas as pl
from jax.experimental.pallas import tpu as pltpu
from jax.sharding import PartitionSpec as P

SWEEPS = 2
FFD = 512
SUPPORT_RADIUS = 0.3
LANES = 128
CELL_AXES = ("cells", "sub")
FACTOR_ROWS = 64
PARAMS = pltpu.CompilerParams(vmem_limit_bytes=24 * 1024 * 1024)
VMEM = pl.BlockSpec(memory_space=pltpu.VMEM)
HBM = pl.BlockSpec(memory_space=pltpu.HBM)


def rows_of(array):
    nodes, rows, cells = array.shape
    blocks = cells // LANES
    split = array.reshape(nodes, rows, blocks, LANES)
    return split.transpose(1, 2, 0, 3).reshape(rows * blocks * nodes, LANES)


def from_rows(array, nodes, cells):
    blocks = cells // LANES
    split = array.reshape(-1, blocks, nodes, LANES)
    return split.transpose(2, 0, 1, 3).reshape(nodes, -1, cells)


def in_hbm(*arrays):
    return [pltpu.with_memory_space_constraint(array, pltpu.HBM) for array in arrays]


def prepare_kernel(
    nodes,
    off_in,
    inverse_in,
    rhs_in,
    sens_in,
    neigh_in,
    weight_in,
    index_in,
    spread_in,
    start_in,
    cell_in,
    base_in,
    off_ref,
    inverse_ref,
    rhs_ref,
    sens_ref,
    lane_ref,
    step_ref,
    spread_ref,
    one_hot_ref,
    start_ref,
    left_ref,
    right_ref,
    off_buf,
    sens_buf,
    neigh_buf,
    weight_buf,
    index_buf,
    spread_buf,
    cell_buf,
    base_buf,
    sems,
):
    slots, owned = index_buf.shape
    start = pl.multiple_of(lax.axis_index("nodes") * owned, LANES)
    mine = pl.ds(start, owned)
    pairs = (
        (neigh_in, neigh_buf),
        (index_in.at[:, mine], index_buf),
        (spread_in.at[:, mine], spread_buf),
        (cell_in, cell_buf),
        (base_in.at[:, mine], base_buf),
        (off_in, off_buf),
        (weight_in, weight_buf),
        (sens_in, sens_buf),
        (inverse_in, inverse_ref),
        (rhs_in, rhs_ref),
        (start_in, start_ref),
    )
    copies = [pltpu.make_async_copy(a, b, sems.at[i]) for i, (a, b) in enumerate(pairs)]
    for copy in copies:
        copy.start()

    faces, cells = neigh_buf.shape
    blocks = cells // LANES
    per = blocks * nodes
    first_cell = lax.axis_index(CELL_AXES) * cells
    copies[0].wait()
    for block in range(blocks):
        index = neigh_buf[:, block * LANES : (block + 1) * LANES]
        local = index - first_cell + cells
        lane = jnp.bitwise_and(local, LANES - 1)
        step = jnp.right_shift(local, 7) - block
        step = jnp.where(index >= 0, step, -1)
        for node in range(nodes):
            rows = pl.ds(block * nodes + node, faces, stride=per)
            lane_ref[rows, :] = lane
            step_ref[rows, :] = step

    copies[1].wait()
    copies[2].wait()
    groups = FFD // LANES
    piece = min(512, owned)
    for first in range(0, owned, piece):
        here = slice(first, first + piece)
        low = jnp.bitwise_and(index_buf[:, here], LANES - 1).astype(jnp.float32).T
        low = low.astype(jnp.bfloat16)
        high = jnp.right_shift(index_buf[:, here], 7)
        lane = lax.broadcasted_iota(jnp.int32, (piece, LANES), 1).astype(jnp.float32)
        lane = lane.astype(jnp.bfloat16)
        part = lax.broadcasted_iota(jnp.int32, (16, piece), 0)
        part = jnp.where(part < 3 * groups, lax.rem(part, groups), -1)
        for j in range(slots):
            hit = jnp.broadcast_to(low[:, j : j + 1], (piece, LANES)) == lane
            one_hot_ref[j * owned + first : j * owned + first + piece, :] = jnp.where(
                hit, jnp.bfloat16(1.0), jnp.bfloat16(0.0)
            )
            spread_ref[j * 16 : (j + 1) * 16, here] = jnp.where(
                high[j : j + 1] == part, spread_buf[j : j + 1, here], 0.0
            )

    copies[3].wait()
    left_ref[...] = distance_factors(cell_buf[...], True).T.astype(jnp.bfloat16)
    copies[4].wait()
    right_ref[...] = distance_factors(base_buf[...], False).astype(jnp.bfloat16)

    copies[5].wait()
    off_ref[...] = off_buf[...].astype(jnp.float32)
    copies[6].wait()
    copies[7].wait()
    row_node = lax.rem(lax.broadcasted_iota(jnp.int32, (per, LANES), 0), nodes)
    weights = jnp.zeros((per, LANES), jnp.float32)
    for node in range(nodes):
        weights = jnp.where(row_node == node, weight_buf[node], weights)
    for row in range(0, sens_buf.shape[0], per):
        here = slice(row, row + per)
        sens_ref[here, :] = sens_buf[here, :].astype(jnp.float32) * weights
    for copy in copies[8:]:
        copy.wait()


def sweep_into(
    blocks, first_ref, second_ref, own_ref, rhs_ref, off_ref, inverse_ref, lane_ref, step_ref,
    out_ref, window_ref, table_ref,
):
    per = rhs_ref.shape[0] // 5
    nodes = per // blocks
    faces = lane_ref.shape[0] // per
    odd = lax.rem(lax.axis_index(CELL_AXES), 2)
    place = pl.multiple_of((1 - odd) * 2 * per, 8)
    other = pl.multiple_of(odd * 2 * per, 8)
    width = 3 * per
    for b in range(5):
        rows = slice(b * per, (b + 1) * per)
        base = b * width
        window_ref[pl.ds(base + place, per), :] = first_ref[rows, :]
        window_ref[base + per : base + 2 * per, :] = own_ref[rows, :]
        window_ref[pl.ds(base + other, per), :] = second_ref[rows, :]
    for shift in range(8 // nodes):
        for b in range(5):
            for tile in range(0, width - (8 if shift else 0), 8):
                to = (shift * 5 + b) * width + tile
                table_ref[to : to + 8, :] = window_ref[
                    pl.ds(b * width + tile + shift * nodes, 8), :
                ]
    for half in range(0, per, 8):
        remaining = [rhs_ref[a * per + half : a * per + half + 8, :] for a in range(5)]
        for f in range(faces):
            lanes = lane_ref[f * per + half : f * per + half + 8, :]
            dist = step_ref[f * per + half : f * per + half + 8, :]
            beside = [jnp.zeros((8, LANES), jnp.float32)] * 5
            for d in range(2 * blocks + 1):
                here = dist == d
                first = half + d * nodes
                for b in range(5):
                    at = ((first % 8) // nodes * 5 + b) * width + first // 8 * 8
                    got = jnp.take_along_axis(
                        table_ref[at : at + 8, :], lanes, axis=1, mode="promise_in_bounds"
                    )
                    beside[b] = jnp.where(here, got, beside[b])
            for a in range(5):
                for b in range(5):
                    row = (f * 25 + 5 * a + b) * per + half
                    remaining[a] = remaining[a] - off_ref[row : row + 8, :] * beside[b]
        for a in range(5):
            total = None
            for b in range(5):
                row = (5 * a + b) * per + half
                term = inverse_ref[row : row + 8, :] * remaining[b]
                total = term if total is None else total + term
            out_ref[a * per + half : a * per + half + 8, :] = total


def sweep_kernel(blocks, *refs):
    sweep_into(blocks, *refs)


def last_sweep_kernel(blocks, *refs):
    ins, rest = refs[:8], refs[8:]
    sens_ref, _, out_ref, sens_out_ref, window_ref, table_ref, part_ref = rest
    sweep_into(blocks, *ins, out_ref, window_ref, table_ref)
    per = out_ref.shape[0] // 5
    nodes = per // blocks
    for k in range(3):
        total = None
        for a in range(5):
            row = (3 * a + k) * per
            term = out_ref[a * per : (a + 1) * per, :] * sens_ref[row : row + per, :]
            total = term if total is None else total + term
        part_ref[k * per : (k + 1) * per, :] = total
    for block in range(blocks):
        total = None
        for node in range(nodes):
            term = part_ref[pl.ds(block * nodes + node, 3, stride=per), :]
            total = term if total is None else total + term
        sens_out_ref[:, block * LANES : (block + 1) * LANES] = total


def pieces(value, count):
    found = []
    for _ in range(count):
        piece = value.astype(jnp.bfloat16).astype(jnp.float32)
        found.append(piece)
        value = value - piece
    return found


def distance_factors(points, left):
    count = points.shape[1]
    scaled = (points - 0.5) * (1.0 / SUPPORT_RADIUS)
    scaled = jnp.concatenate([scaled, jnp.zeros((5, count), jnp.float32)], axis=0)
    norm = jnp.sum(scaled * scaled, axis=0, keepdims=True)
    norms = pieces(jnp.broadcast_to(norm, (8, count)), 3)
    row = lax.broadcasted_iota(jnp.int32, (8, count), 0)
    norm_block = jnp.zeros((8, count), jnp.float32)
    for place in range(3):
        norm_block = jnp.where(row == place, norms[place], norm_block)
    ones_block = jnp.where(row < 3, 1.0, 0.0)
    first, second, third = pieces(scaled, 3)
    if left:
        dims = [first, first, second, second, first, third]
        dims = [-2.0 * part for part in dims]
        blocks = dims + [norm_block, ones_block]
    else:
        dims = [first, second, first, second, third, first]
        blocks = dims + [ones_block, norm_block]
    return jnp.concatenate(blocks, axis=0)


def wendland_kernel(first_cell, left_ref, right_ref, _, first_ref, rest_ref):
    cells, owned = first_ref.shape
    tile, wide = min(128, cells), min(256, owned)

    @pl.loop(0, cells // tile)
    def _(step):
        row = pl.multiple_of(step * tile, tile)
        left = left_ref[pl.ds(row + first_cell, tile), :]
        for lane in range(0, owned, wide):
            here = slice(lane, lane + wide)
            squared = jnp.dot(left, right_ref[:, here], preferred_element_type=jnp.float32)
            squared = jnp.maximum(squared, 1e-30)
            near = jnp.maximum(1.0 - squared * lax.rsqrt(squared), 0.0)
            power = near * near
            kernel = power * power * (1.25 - near)
            first = kernel.astype(jnp.bfloat16)
            first_ref[pl.ds(row, tile), here] = first
            rest_ref[pl.ds(row, tile), here] = (kernel - first.astype(jnp.float32)).astype(
                jnp.bfloat16
            )


def control_kernel(scale, *refs):
    (*sens_refs, near_first, near_rest, far_first, far_rest, spread_ref, one_hot_ref, out_ref) = refs
    cells = sens_refs[0].shape[1]
    half = near_first.shape[0]
    slots = spread_ref.shape[0] // 16
    groups = FFD // LANES
    total = sens_refs[0][...]
    for ref in sens_refs[1:]:
        total = total + ref[...]
    total = total * scale
    row = lax.broadcasted_iota(jnp.int32, (16, cells), 0)
    sens = jnp.zeros((16, cells), jnp.float32)
    for k in range(3):
        mine = jnp.logical_and(row >= k * groups, row < (k + 1) * groups)
        sens = jnp.where(mine, total[k : k + 1], sens)

    def halves(value):
        first = value.astype(jnp.bfloat16)
        rest = (value - first.astype(jnp.float32)).astype(jnp.bfloat16)
        return jnp.concatenate([first, rest], axis=0)

    sens = halves(sens)
    grad = None
    for part, ref in (
        (sens[:, :half], near_first),
        (sens[:, :half], near_rest),
        (sens[:, half:], far_first),
        (sens[:, half:], far_rest),
    ):
        term = jnp.dot(part, ref[...], preferred_element_type=jnp.float32)
        grad = term if grad is None else grad + term
    grad = grad[:16] + grad[16:]
    owned = grad.shape[1]
    result = None
    for j in range(slots):
        term = jnp.dot(
            halves(grad * spread_ref[j * 16 : (j + 1) * 16, :]),
            one_hot_ref[j * owned : (j + 1) * owned, :],
            preferred_element_type=jnp.float32,
        )
        result = term if result is None else result + term
    result = result[:16] + result[16:]
    for copy in range(out_ref.shape[0]):
        out_ref[copy] = result


def tree(values):
    while len(values) > 1:
        values = [sum(values[i : i + 2]) for i in range(0, len(values), 2)]
    return values[0]


def add_kernel(in_ref, out_ref):
    total = tree([in_ref[i] for i in range(in_ref.shape[0])])
    for copy in range(out_ref.shape[0]):
        out_ref[copy] = total


def finish_kernel(in_ref, out_ref):
    total = tree([in_ref[i] for i in range(in_ref.shape[0])])
    groups = FFD // LANES
    for k in range(3):
        for group in range(groups):
            row = k * groups + group
            out_ref[k : k + 1, group * LANES : (group + 1) * LANES] = total[row : row + 1]


def exchanged(value, axes):
    peers = lax.axis_size(axes)
    if peers > 8 or peers & (peers - 1):
        return [lax.psum(value, axes)]
    return [value] + [
        lax.ppermute(value, axes, [(i, i ^ shift) for i in range(peers)])
        for shift in range(1, peers)
    ]


def body(
    adjoint_start,
    adjoint_rhs,
    off_blocks,
    diag_inverse,
    neighbours,
    node_weights,
    sens_blocks,
    cell_points,
    base_points,
    ffd_index,
    ffd_weight,
):
    nodes, _, cells = adjoint_start.shape
    faces = off_blocks.shape[1]
    blocks = cells // LANES
    per = blocks * nodes
    slots = ffd_index.shape[1]
    owned = base_points.shape[1] // lax.axis_size("nodes")
    peers = lax.axis_size(CELL_AXES)
    f32, i32, bf16 = jnp.float32, jnp.int32, jnp.bfloat16

    def shape(dims, dtype=f32):
        return jax.ShapeDtypeStruct(dims, dtype)

    def cost(flops, moved):
        return pl.CostEstimate(flops=flops, bytes_accessed=moved, transcendentals=0)

    def swaps(array):
        first = [(i, i ^ 1) for i in range(peers) if i ^ 1 < peers]
        second = [(i, i + 1 if i % 2 else i - 1) for i in range(peers)]
        second = [(i, j) for i, j in second if 0 <= j < peers]
        far = lax.ppermute(array, CELL_AXES, second)
        close = lax.ppermute(array, CELL_AXES, first)
        return far, close

    adjoint = rows_of(adjoint_start)
    far, close = swaps(adjoint)
    prepared = pl.pallas_call(
        functools.partial(prepare_kernel, nodes),
        out_shape=(
            shape((faces * 25 * per, LANES)),
            shape((25 * per, LANES)),
            shape((5 * per, LANES)),
            shape((15 * per, LANES)),
            shape((faces * per, LANES), i32),
            shape((faces * per, LANES), i32),
            shape((slots * 16, owned)),
            shape((slots * owned, LANES), bf16),
            shape((5 * per, LANES)),
            shape((cells, FACTOR_ROWS), bf16),
            shape((FACTOR_ROWS, owned), bf16),
        ),
        in_specs=[HBM] * 11,
        out_specs=(VMEM,) * 11,
        scratch_shapes=[
            pltpu.VMEM((faces * 25 * per, LANES), bf16),
            pltpu.VMEM((15 * per, LANES), bf16),
            pltpu.VMEM((faces, cells), i32),
            pltpu.SMEM((nodes,), f32),
            pltpu.VMEM((slots, owned), i32),
            pltpu.VMEM((slots, owned), f32),
            pltpu.VMEM((3, cells), f32),
            pltpu.VMEM((3, owned), f32),
            pltpu.SemaphoreType.DMA((11,)),
        ],
        compiler_params=PARAMS,
        cost_estimate=cost(10**9, 10**7),
        name="prepare",
    )(
        *in_hbm(
            rows_of(off_blocks.reshape(nodes, faces * 25, cells)),
            rows_of(diag_inverse),
            rows_of(adjoint_rhs),
            rows_of(sens_blocks),
            neighbours,
            node_weights,
            ffd_index.T,
            ffd_weight.T,
            adjoint,
            cell_points,
            base_points,
        )
    )
    off, inverse, rhs, sens, lane, step, spread, one_hot, adjoint, left, right = prepared
    scratch = [
        pltpu.VMEM((3 * 5 * per, LANES), f32),
        pltpu.VMEM((8 // nodes * 3 * 5 * per, LANES), f32),
    ]
    sweep_cost = cost(2 * 10 * 35 * cells, 4 * faces * 25 * per * LANES)

    for _ in range(SWEEPS - 1):
        adjoint = pl.pallas_call(
            functools.partial(sweep_kernel, blocks),
            out_shape=shape((5 * per, LANES)),
            in_specs=[VMEM] * 8,
            out_specs=VMEM,
            scratch_shapes=scratch,
            compiler_params=PARAMS,
            cost_estimate=sweep_cost,
            name="sweep",
        )(close, far, adjoint, rhs, off, inverse, lane, step)
        far, close = swaps(adjoint)

    def wendland(first_cell, count, behind):
        return pl.pallas_call(
            functools.partial(wendland_kernel, first_cell),
            out_shape=(shape((count, owned), bf16), shape((count, owned), bf16)),
            in_specs=[VMEM] * 3,
            out_specs=(VMEM, VMEM),
            compiler_params=PARAMS,
            cost_estimate=cost(10**9, 10**7),
            name="wendland",
        )(left, right, behind)

    half = cells // 2
    near_first, near_rest = wendland(0, half, adjoint)
    adjoint, part_sens = pl.pallas_call(
        functools.partial(last_sweep_kernel, blocks),
        out_shape=(shape((5 * per, LANES)), shape((3, cells))),
        in_specs=[VMEM] * 9 + [pl.BlockSpec(memory_space=pl.ANY)],
        out_specs=(VMEM, VMEM),
        scratch_shapes=scratch + [pltpu.VMEM((3 * per, LANES), f32)],
        compiler_params=PARAMS,
        cost_estimate=sweep_cost,
        name="last_sweep",
    )(close, far, adjoint, rhs, off, inverse, lane, step, sens, near_first)

    all_sens = exchanged(part_sens, "nodes")
    far_first, far_rest = wendland(half, cells - half, part_sens)
    scale = 4.0 / math.sqrt(cells * peers)
    chip_peers = lax.axis_size(("nodes", "sub"))
    row_peers = lax.axis_size("cells")
    copies = pl.pallas_call(
        functools.partial(control_kernel, scale),
        out_shape=shape((chip_peers, 16, LANES)),
        in_specs=[VMEM] * (len(all_sens) + 6),
        out_specs=VMEM,
        compiler_params=PARAMS,
        name="control",
    )(*all_sens, near_first, near_rest, far_first, far_rest, spread, one_hot)

    gathered = lax.all_to_all(copies, ("nodes", "sub"), 0, 0, tiled=True)
    copies = pl.pallas_call(
        add_kernel, out_shape=shape((row_peers, 16, LANES)), name="add", compiler_params=PARAMS
    )(gathered)
    gathered = lax.all_to_all(copies, "cells", 0, 0, tiled=True)
    control_grad = pl.pallas_call(
        finish_kernel, out_shape=shape((3, FFD)), name="finish", compiler_params=PARAMS
    )(gathered)
    return (from_rows(adjoint, nodes, cells), control_grad)


def solution(mesh):
    return jax.shard_map(
        body,
        mesh=mesh,
        in_specs=(
            P("nodes", None, ("groups", "cells", "sub")),
            P("nodes", None, ("groups", "cells", "sub")),
            P("nodes", None, None, ("groups", "cells", "sub")),
            P("nodes", None, ("groups", "cells", "sub")),
            P(None, ("cells", "sub")),
            P("nodes"),
            P("nodes", None, ("groups", "cells", "sub")),
            P(None, ("cells", "sub")),
            P(),
            P(),
            P(),
        ),
        out_specs=(P("nodes", None, ("groups", "cells", "sub")), P("groups", None)),
        check_vma=False,
    )
```

```python
import functools
import math

import jax
import jax.numpy as jnp
from jax import lax
from jax.experimental import pallas as pl
from jax.experimental.pallas import tpu as pltpu
from jax.sharding import PartitionSpec as P

SWEEPS = 2
FFD = 512
SUPPORT_RADIUS = 0.3
LANES = 128
CELL_AXES = ("cells", "sub")
FACTOR_ROWS = 64
PARAMS = pltpu.CompilerParams(vmem_limit_bytes=24 * 1024 * 1024)
VMEM = pl.BlockSpec(memory_space=pltpu.VMEM)
HBM = pl.BlockSpec(memory_space=pltpu.HBM)


def rows_of(array):
    nodes, rows, cells = array.shape
    blocks = cells // LANES
    split = array.reshape(nodes, rows, blocks, LANES)
    return split.transpose(1, 2, 0, 3).reshape(rows * blocks * nodes, LANES)


def from_rows(array, nodes, cells):
    blocks = cells // LANES
    split = array.reshape(-1, blocks, nodes, LANES)
    return split.transpose(2, 0, 1, 3).reshape(nodes, -1, cells)


def in_hbm(*arrays):
    return [pltpu.with_memory_space_constraint(array, pltpu.HBM) for array in arrays]


def prepare_kernel(
    nodes,
    off_in,
    inverse_in,
    rhs_in,
    sens_in,
    neigh_in,
    weight_in,
    index_in,
    spread_in,
    start_in,
    cell_in,
    base_in,
    off_ref,
    inverse_ref,
    rhs_ref,
    sens_ref,
    lane_ref,
    step_ref,
    spread_ref,
    one_hot_ref,
    start_ref,
    left_ref,
    right_ref,
    off_buf,
    sens_buf,
    neigh_buf,
    weight_buf,
    index_buf,
    spread_buf,
    cell_buf,
    base_buf,
    sems,
):
    slots, owned = index_buf.shape
    start = pl.multiple_of(lax.axis_index("nodes") * owned, LANES)
    mine = pl.ds(start, owned)
    pairs = (
        (neigh_in, neigh_buf),
        (index_in.at[:, mine], index_buf),
        (spread_in.at[:, mine], spread_buf),
        (cell_in, cell_buf),
        (base_in.at[:, mine], base_buf),
        (off_in, off_buf),
        (weight_in, weight_buf),
        (sens_in, sens_buf),
        (inverse_in, inverse_ref),
        (rhs_in, rhs_ref),
        (start_in, start_ref),
    )
    copies = [pltpu.make_async_copy(a, b, sems.at[i]) for i, (a, b) in enumerate(pairs)]
    for copy in copies:
        copy.start()

    faces, cells = neigh_buf.shape
    blocks = cells // LANES
    per = blocks * nodes
    first_cell = lax.axis_index(CELL_AXES) * cells
    copies[0].wait()
    for block in range(blocks):
        index = neigh_buf[:, block * LANES : (block + 1) * LANES]
        local = index - first_cell + cells
        lane = jnp.bitwise_and(local, LANES - 1)
        step = jnp.right_shift(local, 7) - block
        step = jnp.where(index >= 0, step, -1)
        for node in range(nodes):
            rows = pl.ds(block * nodes + node, faces, stride=per)
            lane_ref[rows, :] = lane
            step_ref[rows, :] = step

    copies[1].wait()
    copies[2].wait()
    groups = FFD // LANES
    piece = min(512, owned)
    for first in range(0, owned, piece):
        here = slice(first, first + piece)
        low = jnp.bitwise_and(index_buf[:, here], LANES - 1).astype(jnp.float32).T
        low = low.astype(jnp.bfloat16)
        high = jnp.right_shift(index_buf[:, here], 7)
        lane = lax.broadcasted_iota(jnp.int32, (piece, LANES), 1).astype(jnp.float32)
        lane = lane.astype(jnp.bfloat16)
        part = lax.broadcasted_iota(jnp.int32, (16, piece), 0)
        part = jnp.where(part < 3 * groups, lax.rem(part, groups), -1)
        for j in range(slots):
            hit = jnp.broadcast_to(low[:, j : j + 1], (piece, LANES)) == lane
            one_hot_ref[j * owned + first : j * owned + first + piece, :] = jnp.where(
                hit, jnp.bfloat16(1.0), jnp.bfloat16(0.0)
            )
            spread_ref[j * 16 : (j + 1) * 16, here] = jnp.where(
                high[j : j + 1] == part, spread_buf[j : j + 1, here], 0.0
            )

    copies[3].wait()
    left_ref[...] = distance_factors(cell_buf[...], True).T.astype(jnp.bfloat16)
    copies[4].wait()
    right_ref[...] = distance_factors(base_buf[...], False).astype(jnp.bfloat16)

    copies[5].wait()
    off_ref[...] = off_buf[...].astype(jnp.float32)
    copies[6].wait()
    copies[7].wait()
    row_node = lax.rem(lax.broadcasted_iota(jnp.int32, (per, LANES), 0), nodes)
    weights = jnp.zeros((per, LANES), jnp.float32)
    for node in range(nodes):
        weights = jnp.where(row_node == node, weight_buf[node], weights)
    for row in range(0, sens_buf.shape[0], per):
        here = slice(row, row + per)
        sens_ref[here, :] = sens_buf[here, :].astype(jnp.float32) * weights
    for copy in copies[8:]:
        copy.wait()


def sweep_into(
    blocks, first_ref, second_ref, own_ref, rhs_ref, off_ref, inverse_ref, lane_ref, step_ref,
    out_ref, window_ref, table_ref,
):
    per = rhs_ref.shape[0] // 5
    nodes = per // blocks
    faces = lane_ref.shape[0] // per
    odd = lax.rem(lax.axis_index(CELL_AXES), 2)
    place = pl.multiple_of((1 - odd) * 2 * per, 8)
    other = pl.multiple_of(odd * 2 * per, 8)
    width = 3 * per
    for b in range(5):
        rows = slice(b * per, (b + 1) * per)
        base = b * width
        window_ref[pl.ds(base + place, per), :] = first_ref[rows, :]
        window_ref[base + per : base + 2 * per, :] = own_ref[rows, :]
        window_ref[pl.ds(base + other, per), :] = second_ref[rows, :]
    for shift in range(8 // nodes):
        for b in range(5):
            for tile in range(0, width - (8 if shift else 0), 8):
                to = (shift * 5 + b) * width + tile
                table_ref[to : to + 8, :] = window_ref[
                    pl.ds(b * width + tile + shift * nodes, 8), :
                ]
    for half in range(0, per, 8):
        remaining = [rhs_ref[a * per + half : a * per + half + 8, :] for a in range(5)]
        for f in range(faces):
            lanes = lane_ref[f * per + half : f * per + half + 8, :]
            dist = step_ref[f * per + half : f * per + half + 8, :]
            beside = [jnp.zeros((8, LANES), jnp.float32)] * 5
            for d in range(2 * blocks + 1):
                here = dist == d
                first = half + d * nodes
                for b in range(5):
                    at = ((first % 8) // nodes * 5 + b) * width + first // 8 * 8
                    got = jnp.take_along_axis(
                        table_ref[at : at + 8, :], lanes, axis=1, mode="promise_in_bounds"
                    )
                    beside[b] = jnp.where(here, got, beside[b])
            for a in range(5):
                for b in range(5):
                    row = (f * 25 + 5 * a + b) * per + half
                    remaining[a] = remaining[a] - off_ref[row : row + 8, :] * beside[b]
        for a in range(5):
            total = None
            for b in range(5):
                row = (5 * a + b) * per + half
                term = inverse_ref[row : row + 8, :] * remaining[b]
                total = term if total is None else total + term
            out_ref[a * per + half : a * per + half + 8, :] = total


def sweep_kernel(blocks, *refs):
    sweep_into(blocks, *refs)


def last_sweep_kernel(blocks, *refs):
    ins, rest = refs[:8], refs[8:]
    sens_ref, _, out_ref, sens_out_ref, window_ref, table_ref, part_ref = rest
    sweep_into(blocks, *ins, out_ref, window_ref, table_ref)
    per = out_ref.shape[0] // 5
    nodes = per // blocks
    for k in range(3):
        total = None
        for a in range(5):
            row = (3 * a + k) * per
            term = out_ref[a * per : (a + 1) * per, :] * sens_ref[row : row + per, :]
            total = term if total is None else total + term
        part_ref[k * per : (k + 1) * per, :] = total
    for block in range(blocks):
        total = None
        for node in range(nodes):
            term = part_ref[pl.ds(block * nodes + node, 3, stride=per), :]
            total = term if total is None else total + term
        sens_out_ref[:, block * LANES : (block + 1) * LANES] = total


def pieces(value, count):
    found = []
    for _ in range(count):
        piece = value.astype(jnp.bfloat16).astype(jnp.float32)
        found.append(piece)
        value = value - piece
    return found


def distance_factors(points, left):
    count = points.shape[1]
    scaled = (points - 0.5) * (1.0 / SUPPORT_RADIUS)
    scaled = jnp.concatenate([scaled, jnp.zeros((5, count), jnp.float32)], axis=0)
    norm = jnp.sum(scaled * scaled, axis=0, keepdims=True)
    norms = pieces(jnp.broadcast_to(norm, (8, count)), 3)
    row = lax.broadcasted_iota(jnp.int32, (8, count), 0)
    norm_block = jnp.zeros((8, count), jnp.float32)
    for place in range(3):
        norm_block = jnp.where(row == place, norms[place], norm_block)
    ones_block = jnp.where(row < 3, 1.0, 0.0)
    first, second, third = pieces(scaled, 3)
    if left:
        dims = [first, first, second, second, first, third]
        dims = [-2.0 * part for part in dims]
        blocks = dims + [norm_block, ones_block]
    else:
        dims = [first, second, first, second, third, first]
        blocks = dims + [ones_block, norm_block]
    return jnp.concatenate(blocks, axis=0)


def wendland_kernel(first_cell, left_ref, right_ref, _, first_ref, rest_ref):
    cells, owned = first_ref.shape
    tile, wide = min(64, cells), min(256, owned)
    for row in range(0, cells, tile):
        left = left_ref[first_cell + row : first_cell + row + tile, :]
        for lane in range(0, owned, wide):
            here = slice(lane, lane + wide)
            squared = jnp.dot(left, right_ref[:, here], preferred_element_type=jnp.float32)
            squared = jnp.maximum(squared, 1e-30)
            near = jnp.maximum(1.0 - squared * lax.rsqrt(squared), 0.0)
            power = near * near
            kernel = power * power * (1.25 - near)
            first = kernel.astype(jnp.bfloat16)
            first_ref[row : row + tile, here] = first
            rest_ref[row : row + tile, here] = (kernel - first.astype(jnp.float32)).astype(
                jnp.bfloat16
            )


def wendland_and_write_kernel(first_cell, left_ref, right_ref, after, adjoint_ref, *rest):
    first_ref, rest_ref, result_ref, sem = rest
    copy = pltpu.make_async_copy(adjoint_ref, result_ref, sem)
    copy.start()
    wendland_kernel(first_cell, left_ref, right_ref, after, first_ref, rest_ref)
    copy.wait()


def control_kernel(scale, *refs):
    (*sens_refs, near_first, near_rest, far_first, far_rest, spread_ref, one_hot_ref, out_ref) = refs
    cells = sens_refs[0].shape[1]
    half = near_first.shape[0]
    slots = spread_ref.shape[0] // 16
    groups = FFD // LANES
    total = sens_refs[0][...]
    for ref in sens_refs[1:]:
        total = total + ref[...]
    total = total * scale
    row = lax.broadcasted_iota(jnp.int32, (16, cells), 0)
    sens = jnp.zeros((16, cells), jnp.float32)
    for k in range(3):
        mine = jnp.logical_and(row >= k * groups, row < (k + 1) * groups)
        sens = jnp.where(mine, total[k : k + 1], sens)

    def halves(value):
        first = value.astype(jnp.bfloat16)
        rest = (value - first.astype(jnp.float32)).astype(jnp.bfloat16)
        return jnp.concatenate([first, rest], axis=0)

    sens = halves(sens)
    grad = None
    for part, ref in (
        (sens[:, :half], near_first),
        (sens[:, :half], near_rest),
        (sens[:, half:], far_first),
        (sens[:, half:], far_rest),
    ):
        term = jnp.dot(part, ref[...], preferred_element_type=jnp.float32)
        grad = term if grad is None else grad + term
    grad = grad[:16] + grad[16:]
    owned = grad.shape[1]
    result = None
    for j in range(slots):
        term = jnp.dot(
            halves(grad * spread_ref[j * 16 : (j + 1) * 16, :]),
            one_hot_ref[j * owned : (j + 1) * owned, :],
            preferred_element_type=jnp.float32,
        )
        result = term if result is None else result + term
    result = result[:16] + result[16:]
    out_ref[...] = result


def add_kernel(own_ref, other_ref, out_ref):
    out_ref[...] = own_ref[...] + other_ref[...]


def finish_kernel(*refs):
    total = sum(ref[...] for ref in refs[:-1])
    groups = FFD // LANES
    for k in range(3):
        for group in range(groups):
            row = k * groups + group
            refs[-1][k : k + 1, group * LANES : (group + 1) * LANES] = total[row : row + 1]


def steps_of_sum(axes):
    for axis in axes:
        peers = lax.axis_size(axis)
        shift = 1
        while shift < peers:
            yield axis, [(i, i ^ shift) for i in range(peers)]
            shift *= 2


def body(
    adjoint_start,
    adjoint_rhs,
    off_blocks,
    diag_inverse,
    neighbours,
    node_weights,
    sens_blocks,
    cell_points,
    base_points,
    ffd_index,
    ffd_weight,
):
    nodes, _, cells = adjoint_start.shape
    faces = off_blocks.shape[1]
    blocks = cells // LANES
    per = blocks * nodes
    slots = ffd_index.shape[1]
    owned = base_points.shape[1] // lax.axis_size("nodes")
    peers = lax.axis_size(CELL_AXES)
    f32, i32, bf16 = jnp.float32, jnp.int32, jnp.bfloat16

    def shape(dims, dtype=f32):
        return jax.ShapeDtypeStruct(dims, dtype)

    def cost(flops, moved):
        return pl.CostEstimate(flops=flops, bytes_accessed=moved, transcendentals=0)

    def swaps(array):
        first = [(i, i ^ 1) for i in range(peers)]
        second = [(i, i + 1 if i % 2 else i - 1) for i in range(peers)]
        second = [(i, j if 0 <= j < peers else i) for i, j in second]
        far = lax.ppermute(array, CELL_AXES, second)
        close = lax.ppermute(array, CELL_AXES, first)
        return far, close

    adjoint = rows_of(adjoint_start)
    far, close = swaps(adjoint)
    prepared = pl.pallas_call(
        functools.partial(prepare_kernel, nodes),
        out_shape=(
            shape((faces * 25 * per, LANES)),
            shape((25 * per, LANES)),
            shape((5 * per, LANES)),
            shape((15 * per, LANES)),
            shape((faces * per, LANES), i32),
            shape((faces * per, LANES), i32),
            shape((slots * 16, owned)),
            shape((slots * owned, LANES), bf16),
            shape((5 * per, LANES)),
            shape((cells, FACTOR_ROWS), bf16),
            shape((FACTOR_ROWS, owned), bf16),
        ),
        in_specs=[HBM] * 11,
        out_specs=(VMEM,) * 11,
        scratch_shapes=[
            pltpu.VMEM((faces * 25 * per, LANES), bf16),
            pltpu.VMEM((15 * per, LANES), bf16),
            pltpu.VMEM((faces, cells), i32),
            pltpu.SMEM((nodes,), f32),
            pltpu.VMEM((slots, owned), i32),
            pltpu.VMEM((slots, owned), f32),
            pltpu.VMEM((3, cells), f32),
            pltpu.VMEM((3, owned), f32),
            pltpu.SemaphoreType.DMA((11,)),
        ],
        compiler_params=PARAMS,
        cost_estimate=cost(10**9, 10**7),
        name="prepare",
    )(
        *in_hbm(
            rows_of(off_blocks.reshape(nodes, faces * 25, cells)),
            rows_of(diag_inverse),
            rows_of(adjoint_rhs),
            rows_of(sens_blocks),
            neighbours,
            node_weights,
            ffd_index.T,
            ffd_weight.T,
            adjoint,
            cell_points,
            base_points,
        )
    )
    off, inverse, rhs, sens, lane, step, spread, one_hot, adjoint, left, right = prepared
    scratch = [
        pltpu.VMEM((3 * 5 * per, LANES), f32),
        pltpu.VMEM((8 // nodes * 3 * 5 * per, LANES), f32),
    ]
    sweep_cost = cost(2 * 10 * 35 * cells, 4 * faces * 25 * per * LANES)

    for _ in range(SWEEPS - 1):
        adjoint = pl.pallas_call(
            functools.partial(sweep_kernel, blocks),
            out_shape=shape((5 * per, LANES)),
            in_specs=[VMEM] * 8,
            out_specs=VMEM,
            scratch_shapes=scratch,
            compiler_params=PARAMS,
            cost_estimate=sweep_cost,
            name="sweep",
        )(close, far, adjoint, rhs, off, inverse, lane, step)
        far, close = swaps(adjoint)

    half = cells // 2
    wendland_cost = cost(10**9, 10**7)
    kernel_shape = shape((half, owned), bf16)
    near_first, near_rest = pl.pallas_call(
        functools.partial(wendland_kernel, 0),
        out_shape=(kernel_shape, kernel_shape),
        in_specs=[VMEM] * 3,
        out_specs=(VMEM, VMEM),
        compiler_params=PARAMS,
        cost_estimate=wendland_cost,
        name="near_wendland",
    )(left, right, adjoint)
    adjoint, part_sens = pl.pallas_call(
        functools.partial(last_sweep_kernel, blocks),
        out_shape=(shape((5 * per, LANES)), shape((3, cells))),
        in_specs=[VMEM] * 9 + [pl.BlockSpec(memory_space=pl.ANY)],
        out_specs=(VMEM, VMEM),
        scratch_shapes=scratch + [pltpu.VMEM((3 * per, LANES), f32)],
        compiler_params=PARAMS,
        cost_estimate=sweep_cost,
        name="last_sweep",
    )(close, far, adjoint, rhs, off, inverse, lane, step, sens, near_first)

    all_sens = [part_sens]
    node_peers = lax.axis_size("nodes")
    for shift in range(1, node_peers):
        ring = [(i, (i + shift) % node_peers) for i in range(node_peers)]
        all_sens.append(lax.ppermute(part_sens, "nodes", ring))
    far_first, far_rest, adjoint = pl.pallas_call(
        functools.partial(wendland_and_write_kernel, half),
        out_shape=(kernel_shape, kernel_shape, shape((5 * per, LANES))),
        in_specs=[VMEM] * 4,
        out_specs=(VMEM, VMEM, HBM),
        scratch_shapes=[pltpu.SemaphoreType.DMA],
        compiler_params=PARAMS,
        cost_estimate=wendland_cost,
        name="far_wendland",
    )(left, right, part_sens, adjoint)
    scale = 4.0 / math.sqrt(cells * peers)
    terms = [
        pl.pallas_call(
            functools.partial(control_kernel, scale),
            out_shape=shape((16, LANES)),
            in_specs=[VMEM] * (len(all_sens) + 6),
            out_specs=VMEM,
            compiler_params=PARAMS,
            name="control",
        )(*all_sens, near_first, near_rest, far_first, far_rest, spread, one_hot)
    ]
    for axis, partners in steps_of_sum(("sub", "nodes", "cells")):
        partial = terms[0]
        if len(terms) > 1:
            partial = pl.pallas_call(
                add_kernel, out_shape=shape((16, LANES)), name="add", compiler_params=PARAMS
            )(*terms)
        terms = [partial, lax.ppermute(partial, axis, partners)]
    control_grad = pl.pallas_call(
        finish_kernel, out_shape=shape((3, FFD)), name="finish", compiler_params=PARAMS
    )(*terms)
    return (from_rows(adjoint, nodes, cells), control_grad)


def solution(mesh):
    return jax.shard_map(
        body,
        mesh=mesh,
        in_specs=(
            P("nodes", None, ("groups", "cells", "sub")),
            P("nodes", None, ("groups", "cells", "sub")),
            P("nodes", None, None, ("groups", "cells", "sub")),
            P("nodes", None, ("groups", "cells", "sub")),
            P(None, ("cells", "sub")),
            P("nodes"),
            P("nodes", None, ("groups", "cells", "sub")),
            P(None, ("cells", "sub")),
            P(),
            P(),
            P(),
        ),
        out_specs=(P("nodes", None, ("groups", "cells", "sub")), P("groups", None)),
        check_vma=False,
    )
```

```python
import functools
import math

import jax
import jax.numpy as jnp
from jax import lax
from jax.experimental import pallas as pl
from jax.experimental.pallas import tpu as pltpu
from jax.sharding import PartitionSpec as P

SWEEPS = 2
FFD = 512
SUPPORT_RADIUS = 0.3
LANES = 128
CELL_AXES = ("cells", "sub")
SUM_AXES = ("cells", "nodes", "sub")
FACTOR_ROWS = 64
PARAMS = pltpu.CompilerParams(vmem_limit_bytes=24 * 1024 * 1024)
VMEM = pl.BlockSpec(memory_space=pltpu.VMEM)
HBM = pl.BlockSpec(memory_space=pltpu.HBM)


def rows_of(array):
    nodes, rows, cells = array.shape
    blocks = cells // LANES
    split = array.reshape(nodes, rows, blocks, LANES)
    return split.transpose(1, 2, 0, 3).reshape(rows * blocks * nodes, LANES)


def from_rows(array, nodes, cells):
    blocks = cells // LANES
    split = array.reshape(-1, blocks, nodes, LANES)
    return split.transpose(2, 0, 1, 3).reshape(nodes, -1, cells)


def in_hbm(*arrays):
    return [pltpu.with_memory_space_constraint(array, pltpu.HBM) for array in arrays]


def prepare_kernel(
    nodes,
    off_in,
    inverse_in,
    rhs_in,
    sens_in,
    neigh_in,
    weight_in,
    index_in,
    spread_in,
    start_in,
    cell_in,
    base_in,
    _,
    off_ref,
    inverse_ref,
    rhs_ref,
    sens_ref,
    lane_ref,
    step_ref,
    spread_ref,
    one_hot_ref,
    start_ref,
    left_ref,
    right_ref,
    off_buf,
    sens_buf,
    neigh_buf,
    weight_buf,
    index_buf,
    spread_buf,
    cell_buf,
    base_buf,
    sems,
):
    slots, owned = index_buf.shape
    start = pl.multiple_of(lax.axis_index("nodes") * owned, LANES)
    mine = pl.ds(start, owned)
    pairs = (
        (neigh_in, neigh_buf),
        (index_in.at[:, mine], index_buf),
        (spread_in.at[:, mine], spread_buf),
        (cell_in, cell_buf),
        (base_in.at[:, mine], base_buf),
        (off_in, off_buf),
        (weight_in, weight_buf),
        (sens_in, sens_buf),
        (inverse_in, inverse_ref),
        (rhs_in, rhs_ref),
        (start_in, start_ref),
    )
    copies = [pltpu.make_async_copy(a, b, sems.at[i]) for i, (a, b) in enumerate(pairs)]
    for copy in copies:
        copy.start()

    faces, cells = neigh_buf.shape
    blocks = cells // LANES
    per = blocks * nodes
    first_cell = lax.axis_index(CELL_AXES) * cells
    copies[0].wait()
    for block in range(blocks):
        index = neigh_buf[:, block * LANES : (block + 1) * LANES]
        local = index - first_cell + cells
        lane = jnp.bitwise_and(local, LANES - 1)
        step = jnp.right_shift(local, 7) - block
        step = jnp.where(index >= 0, step, -1)
        for node in range(nodes):
            rows = pl.ds(block * nodes + node, faces, stride=per)
            lane_ref[rows, :] = lane
            step_ref[rows, :] = step

    copies[1].wait()
    copies[2].wait()
    groups = FFD // LANES
    piece = min(512, owned)
    for first in range(0, owned, piece):
        here = slice(first, first + piece)
        low = jnp.bitwise_and(index_buf[:, here], LANES - 1).astype(jnp.float32).T
        low = low.astype(jnp.bfloat16)
        high = jnp.right_shift(index_buf[:, here], 7)
        lane = lax.broadcasted_iota(jnp.int32, (piece, LANES), 1).astype(jnp.float32)
        lane = lane.astype(jnp.bfloat16)
        part = lax.broadcasted_iota(jnp.int32, (16, piece), 0)
        part = jnp.where(part < 3 * groups, lax.rem(part, groups), -1)
        for j in range(slots):
            hit = jnp.broadcast_to(low[:, j : j + 1], (piece, LANES)) == lane
            one_hot_ref[j * owned + first : j * owned + first + piece, :] = jnp.where(
                hit, jnp.bfloat16(1.0), jnp.bfloat16(0.0)
            )
            spread_ref[j * 16 : (j + 1) * 16, here] = jnp.where(
                high[j : j + 1] == part, spread_buf[j : j + 1, here], 0.0
            )

    copies[3].wait()
    left_ref[...] = distance_factors(cell_buf[...], True).T.astype(jnp.bfloat16)
    copies[4].wait()
    right_ref[...] = distance_factors(base_buf[...], False).astype(jnp.bfloat16)

    copies[5].wait()
    off_ref[...] = off_buf[...].astype(jnp.float32)
    copies[6].wait()
    copies[7].wait()
    row_node = lax.rem(lax.broadcasted_iota(jnp.int32, (per, LANES), 0), nodes)
    weights = jnp.zeros((per, LANES), jnp.float32)
    for node in range(nodes):
        weights = jnp.where(row_node == node, weight_buf[node], weights)
    for row in range(0, sens_buf.shape[0], per):
        here = slice(row, row + per)
        sens_ref[here, :] = sens_buf[here, :].astype(jnp.float32) * weights
    for copy in copies[8:]:
        copy.wait()


def sweep_into(
    blocks, first_ref, second_ref, own_ref, rhs_ref, off_ref, inverse_ref, lane_ref, step_ref,
    out_ref, window_ref, table_ref,
):
    per = rhs_ref.shape[0] // 5
    nodes = per // blocks
    faces = lane_ref.shape[0] // per
    odd = lax.rem(lax.axis_index(CELL_AXES), 2)
    place = pl.multiple_of((1 - odd) * 2 * per, 8)
    other = pl.multiple_of(odd * 2 * per, 8)
    width = 3 * per
    for b in range(5):
        rows = slice(b * per, (b + 1) * per)
        base = b * width
        window_ref[pl.ds(base + place, per), :] = first_ref[rows, :]
        window_ref[base + per : base + 2 * per, :] = own_ref[rows, :]
        window_ref[pl.ds(base + other, per), :] = second_ref[rows, :]
    for shift in range(8 // nodes):
        for b in range(5):
            for tile in range(0, width - (8 if shift else 0), 8):
                to = (shift * 5 + b) * width + tile
                table_ref[to : to + 8, :] = window_ref[
                    pl.ds(b * width + tile + shift * nodes, 8), :
                ]
    for half in range(0, per, 8):
        remaining = [rhs_ref[a * per + half : a * per + half + 8, :] for a in range(5)]
        for f in range(faces):
            lanes = lane_ref[f * per + half : f * per + half + 8, :]
            dist = step_ref[f * per + half : f * per + half + 8, :]
            beside = [jnp.zeros((8, LANES), jnp.float32)] * 5
            for d in range(2 * blocks + 1):
                here = dist == d
                first = half + d * nodes
                for b in range(5):
                    at = ((first % 8) // nodes * 5 + b) * width + first // 8 * 8
                    got = jnp.take_along_axis(
                        table_ref[at : at + 8, :], lanes, axis=1, mode="promise_in_bounds"
                    )
                    beside[b] = jnp.where(here, got, beside[b])
            for a in range(5):
                for b in range(5):
                    row = (f * 25 + 5 * a + b) * per + half
                    remaining[a] = remaining[a] - off_ref[row : row + 8, :] * beside[b]
        for a in range(5):
            total = None
            for b in range(5):
                row = (5 * a + b) * per + half
                term = inverse_ref[row : row + 8, :] * remaining[b]
                total = term if total is None else total + term
            out_ref[a * per + half : a * per + half + 8, :] = total


def sweep_kernel(blocks, *refs):
    sweep_into(blocks, *refs)


def last_sweep_kernel(blocks, *refs):
    ins, rest = refs[:8], refs[8:]
    sens_ref, _, out_ref, sens_out_ref, window_ref, table_ref, part_ref = rest
    sweep_into(blocks, *ins, out_ref, window_ref, table_ref)
    per = out_ref.shape[0] // 5
    nodes = per // blocks
    for k in range(3):
        total = None
        for a in range(5):
            row = (3 * a + k) * per
            term = out_ref[a * per : (a + 1) * per, :] * sens_ref[row : row + per, :]
            total = term if total is None else total + term
        part_ref[k * per : (k + 1) * per, :] = total
    for block in range(blocks):
        total = None
        for node in range(nodes):
            term = part_ref[pl.ds(block * nodes + node, 3, stride=per), :]
            total = term if total is None else total + term
        sens_out_ref[:, block * LANES : (block + 1) * LANES] = total


def pieces(value, count):
    found = []
    for _ in range(count):
        piece = value.astype(jnp.bfloat16).astype(jnp.float32)
        found.append(piece)
        value = value - piece
    return found


def distance_factors(points, left):
    count = points.shape[1]
    scaled = (points - 0.5) * (1.0 / SUPPORT_RADIUS)
    scaled = jnp.concatenate([scaled, jnp.zeros((5, count), jnp.float32)], axis=0)
    norm = jnp.sum(scaled * scaled, axis=0, keepdims=True)
    norms = pieces(jnp.broadcast_to(norm, (8, count)), 3)
    row = lax.broadcasted_iota(jnp.int32, (8, count), 0)
    norm_block = jnp.zeros((8, count), jnp.float32)
    for place in range(3):
        norm_block = jnp.where(row == place, norms[place], norm_block)
    ones_block = jnp.where(row < 3, 1.0, 0.0)
    first, second, third = pieces(scaled, 3)
    if left:
        dims = [first, first, second, second, first, third]
        dims = [-2.0 * part for part in dims]
        blocks = dims + [norm_block, ones_block]
    else:
        dims = [first, second, first, second, third, first]
        blocks = dims + [ones_block, norm_block]
    return jnp.concatenate(blocks, axis=0)


def wendland_kernel(first_cell, left_ref, right_ref, _, first_ref, rest_ref):
    cells, owned = first_ref.shape
    tile, wide = min(64, cells), min(256, owned)
    for row in range(0, cells, tile):
        left = left_ref[first_cell + row : first_cell + row + tile, :]
        for lane in range(0, owned, wide):
            here = slice(lane, lane + wide)
            squared = jnp.dot(left, right_ref[:, here], preferred_element_type=jnp.float32)
            squared = jnp.maximum(squared, 1e-30)
            near = jnp.maximum(1.0 - squared * lax.rsqrt(squared), 0.0)
            power = near * near
            kernel = power * power * (1.25 - near)
            first = kernel.astype(jnp.bfloat16)
            first_ref[row : row + tile, here] = first
            rest_ref[row : row + tile, here] = (kernel - first.astype(jnp.float32)).astype(
                jnp.bfloat16
            )


def wendland_and_write_kernel(first_cell, left_ref, right_ref, after, adjoint_ref, *rest):
    first_ref, rest_ref, result_ref, sem = rest
    copy = pltpu.make_async_copy(adjoint_ref, result_ref, sem)
    copy.start()
    wendland_kernel(first_cell, left_ref, right_ref, after, first_ref, rest_ref)
    copy.wait()


def control_kernel(scale, *refs):
    (*sens_refs, near_first, near_rest, far_first, far_rest, spread_ref, one_hot_ref, out_ref) = refs
    cells = sens_refs[0].shape[1]
    half = near_first.shape[0]
    slots = spread_ref.shape[0] // 16
    groups = FFD // LANES
    total = sens_refs[0][...]
    for ref in sens_refs[1:]:
        total = total + ref[...]
    total = total * scale
    row = lax.broadcasted_iota(jnp.int32, (16, cells), 0)
    sens = jnp.zeros((16, cells), jnp.float32)
    for k in range(3):
        mine = jnp.logical_and(row >= k * groups, row < (k + 1) * groups)
        sens = jnp.where(mine, total[k : k + 1], sens)

    def halves(value):
        first = value.astype(jnp.bfloat16)
        rest = (value - first.astype(jnp.float32)).astype(jnp.bfloat16)
        return jnp.concatenate([first, rest], axis=0)

    sens = halves(sens)
    grad = None
    for part, ref in (
        (sens[:, :half], near_first),
        (sens[:, :half], near_rest),
        (sens[:, half:], far_first),
        (sens[:, half:], far_rest),
    ):
        term = jnp.dot(part, ref[...], preferred_element_type=jnp.float32)
        grad = term if grad is None else grad + term
    grad = grad[:16] + grad[16:]
    owned = grad.shape[1]
    result = None
    for j in range(slots):
        term = jnp.dot(
            halves(grad * spread_ref[j * 16 : (j + 1) * 16, :]),
            one_hot_ref[j * owned : (j + 1) * owned, :],
            preferred_element_type=jnp.float32,
        )
        result = term if result is None else result + term
    result = result[:16] + result[16:]
    out_ref[...] = result


def add_kernel(own_ref, other_ref, out_ref):
    out_ref[...] = own_ref[...] + other_ref[...]


def line_kernel(own_ref, *refs):
    received, out_ref = [ref[...] for ref in refs[:-1]], refs[-1]
    core = lax.axis_index("sub")
    values = [jnp.where(core == 0, own_ref[...], received[0])] + received[1:]
    while len(values) > 1:
        values = [a + b for a, b in zip(values[::2], values[1::2])]
    out_ref[...] = values[0]


def finish_kernel(own_ref, other_ref, out_ref):
    total = own_ref[...] + other_ref[...]
    groups = FFD // LANES
    for k in range(3):
        for group in range(groups):
            row = k * groups + group
            out_ref[k : k + 1, group * LANES : (group + 1) * LANES] = total[row : row + 1]


def small_call(kernel, name, *arrays):
    shape = jax.ShapeDtypeStruct(arrays[0].shape, arrays[0].dtype)
    return pl.pallas_call(kernel, out_shape=shape, name=name, compiler_params=PARAMS)(*arrays)


def last_terms(value):
    lines, nodes, cores = (lax.axis_size(axis) for axis in SUM_AXES)

    def swap(array, axis, shift):
        pairs = [(i, i ^ shift) for i in range(lax.axis_size(axis))]
        return lax.ppermute(array, axis, pairs)

    if (nodes, cores) == (2, 2) and lines in (2, 4):
        chip = small_call(add_kernel, "add", value, swap(value, "sub", 1))
        received = []
        for shift in range(lines):
            pairs = []
            for line in range(lines):
                for node in range(2):
                    for core in range(2):
                        other = node ^ 1 if core or not shift else node
                        pairs.append(
                            (
                                (line * 2 + node) * 2 + core,
                                ((line ^ shift) * 2 + other) * 2 + core,
                            )
                        )
            received.append(lax.ppermute(chip, SUM_AXES, pairs))
        total = small_call(line_kernel, "line", chip, *received)
        return total, swap(total, "sub", 1)

    terms = (value,)
    for axis in ("sub", "nodes", "cells"):
        shift = 1
        while shift < lax.axis_size(axis):
            total = small_call(add_kernel, "add", *terms) if len(terms) > 1 else value
            terms = (total, swap(total, axis, shift))
            shift *= 2
    return terms


def body(
    adjoint_start,
    adjoint_rhs,
    off_blocks,
    diag_inverse,
    neighbours,
    node_weights,
    sens_blocks,
    cell_points,
    base_points,
    ffd_index,
    ffd_weight,
):
    nodes, _, cells = adjoint_start.shape
    faces = off_blocks.shape[1]
    blocks = cells // LANES
    per = blocks * nodes
    slots = ffd_index.shape[1]
    owned = base_points.shape[1] // lax.axis_size("nodes")
    peers = lax.axis_size(CELL_AXES)
    f32, i32, bf16 = jnp.float32, jnp.int32, jnp.bfloat16

    def shape(dims, dtype=f32):
        return jax.ShapeDtypeStruct(dims, dtype)

    def cost(flops, moved):
        return pl.CostEstimate(flops=flops, bytes_accessed=moved, transcendentals=0)

    def halo(array):
        close = lax.ppermute(array, CELL_AXES, [(i, i ^ 1) for i in range(peers)])
        onward = [(i, i - 2 if i % 2 else i + 2) for i in range(peers)]
        onward = [(i, j) for i, j in onward if 0 <= j < peers]
        return lax.ppermute(close, CELL_AXES, onward), close

    adjoint = rows_of(adjoint_start)
    far, close = halo(adjoint)
    prepared = pl.pallas_call(
        functools.partial(prepare_kernel, nodes),
        out_shape=(
            shape((faces * 25 * per, LANES)),
            shape((25 * per, LANES)),
            shape((5 * per, LANES)),
            shape((15 * per, LANES)),
            shape((faces * per, LANES), i32),
            shape((faces * per, LANES), i32),
            shape((slots * 16, owned)),
            shape((slots * owned, LANES), bf16),
            shape((5 * per, LANES)),
            shape((cells, FACTOR_ROWS), bf16),
            shape((FACTOR_ROWS, owned), bf16),
        ),
        in_specs=[HBM] * 11 + [VMEM],
        out_specs=(VMEM,) * 11,
        scratch_shapes=[
            pltpu.VMEM((faces * 25 * per, LANES), bf16),
            pltpu.VMEM((15 * per, LANES), bf16),
            pltpu.VMEM((faces, cells), i32),
            pltpu.SMEM((nodes,), f32),
            pltpu.VMEM((slots, owned), i32),
            pltpu.VMEM((slots, owned), f32),
            pltpu.VMEM((3, cells), f32),
            pltpu.VMEM((3, owned), f32),
            pltpu.SemaphoreType.DMA((11,)),
        ],
        compiler_params=PARAMS,
        cost_estimate=cost(10**9, 10**7),
        name="prepare",
    )(
        *in_hbm(
            rows_of(off_blocks.reshape(nodes, faces * 25, cells)),
            rows_of(diag_inverse),
            rows_of(adjoint_rhs),
            rows_of(sens_blocks),
            neighbours,
            node_weights,
            ffd_index.T,
            ffd_weight.T,
            adjoint,
            cell_points,
            base_points,
        ),
        close,
    )
    off, inverse, rhs, sens, lane, step, spread, one_hot, adjoint, left, right = prepared
    scratch = [
        pltpu.VMEM((3 * 5 * per, LANES), f32),
        pltpu.VMEM((8 // nodes * 3 * 5 * per, LANES), f32),
    ]
    sweep_cost = cost(2 * 10 * 35 * cells, 4 * faces * 25 * per * LANES)

    for _ in range(SWEEPS - 1):
        adjoint = pl.pallas_call(
            functools.partial(sweep_kernel, blocks),
            out_shape=shape((5 * per, LANES)),
            in_specs=[VMEM] * 8,
            out_specs=VMEM,
            scratch_shapes=scratch,
            compiler_params=PARAMS,
            cost_estimate=sweep_cost,
            name="sweep",
        )(close, far, adjoint, rhs, off, inverse, lane, step)
        far, close = halo(adjoint)

    half = cells // 2
    wendland_cost = cost(10**9, 10**7)
    kernel_shape = shape((half, owned), bf16)
    near_first, near_rest = pl.pallas_call(
        functools.partial(wendland_kernel, 0),
        out_shape=(kernel_shape, kernel_shape),
        in_specs=[VMEM] * 3,
        out_specs=(VMEM, VMEM),
        compiler_params=PARAMS,
        cost_estimate=wendland_cost,
        name="near_wendland",
    )(left, right, close)
    adjoint, part_sens = pl.pallas_call(
        functools.partial(last_sweep_kernel, blocks),
        out_shape=(shape((5 * per, LANES)), shape((3, cells))),
        in_specs=[VMEM] * 9 + [pl.BlockSpec(memory_space=pl.ANY)],
        out_specs=(VMEM, VMEM),
        scratch_shapes=scratch + [pltpu.VMEM((3 * per, LANES), f32)],
        compiler_params=PARAMS,
        cost_estimate=sweep_cost,
        name="last_sweep",
    )(close, far, adjoint, rhs, off, inverse, lane, step, sens, near_first)

    all_sens = [part_sens]
    node_peers = lax.axis_size("nodes")
    for shift in range(1, node_peers):
        ring = [(i, (i + shift) % node_peers) for i in range(node_peers)]
        all_sens.append(lax.ppermute(part_sens, "nodes", ring))
    far_first, far_rest, adjoint = pl.pallas_call(
        functools.partial(wendland_and_write_kernel, half),
        out_shape=(kernel_shape, kernel_shape, shape((5 * per, LANES))),
        in_specs=[VMEM] * 4,
        out_specs=(VMEM, VMEM, HBM),
        scratch_shapes=[pltpu.SemaphoreType.DMA],
        compiler_params=PARAMS,
        cost_estimate=wendland_cost,
        name="far_wendland",
    )(left, right, part_sens, adjoint)
    scale = 4.0 / math.sqrt(cells * peers)
    partial = pl.pallas_call(
        functools.partial(control_kernel, scale),
        out_shape=shape((16, LANES)),
        in_specs=[VMEM] * (len(all_sens) + 6),
        out_specs=VMEM,
        compiler_params=PARAMS,
        name="control",
    )(*all_sens, near_first, near_rest, far_first, far_rest, spread, one_hot)
    control_grad = pl.pallas_call(
        finish_kernel, out_shape=shape((3, FFD)), name="finish", compiler_params=PARAMS
    )(*last_terms(partial))
    return (from_rows(adjoint, nodes, cells), control_grad)


def solution(mesh):
    return jax.shard_map(
        body,
        mesh=mesh,
        in_specs=(
            P("nodes", None, ("groups", "cells", "sub")),
            P("nodes", None, ("groups", "cells", "sub")),
            P("nodes", None, None, ("groups", "cells", "sub")),
            P("nodes", None, ("groups", "cells", "sub")),
            P(None, ("cells", "sub")),
            P("nodes"),
            P("nodes", None, ("groups", "cells", "sub")),
            P(None, ("cells", "sub")),
            P(),
            P(),
            P(),
        ),
        out_specs=(P("nodes", None, ("groups", "cells", "sub")), P("groups", None)),
        check_vma=False,
    )
```

```python
import functools
import math

import jax
import jax.numpy as jnp
from jax import lax
from jax.experimental import pallas as pl
from jax.experimental.pallas import tpu as pltpu
from jax.sharding import PartitionSpec as P

SWEEPS = 2
FFD = 512
SUPPORT_RADIUS = 0.3
LANES = 128
CELL_AXES = ("cells", "sub")
FACTOR_ROWS = 64
PARAMS = pltpu.CompilerParams(vmem_limit_bytes=24 * 1024 * 1024)
VMEM = pl.BlockSpec(memory_space=pltpu.VMEM)
HBM = pl.BlockSpec(memory_space=pltpu.HBM)


def rows_of(array):
    nodes, rows, cells = array.shape
    blocks = cells // LANES
    split = array.reshape(nodes, rows, blocks, LANES)
    return split.transpose(1, 2, 0, 3).reshape(rows * blocks * nodes, LANES)


def from_rows(array, nodes, cells):
    blocks = cells // LANES
    split = array.reshape(-1, blocks, nodes, LANES)
    return split.transpose(2, 0, 1, 3).reshape(nodes, -1, cells)


def in_hbm(*arrays):
    return [pltpu.with_memory_space_constraint(array, pltpu.HBM) for array in arrays]


def prepare_kernel(
    nodes,
    off_in,
    inverse_in,
    rhs_in,
    sens_in,
    neigh_in,
    weight_in,
    index_in,
    spread_in,
    start_in,
    cell_in,
    base_in,
    off_ref,
    inverse_ref,
    rhs_ref,
    sens_ref,
    lane_ref,
    step_ref,
    spread_ref,
    one_hot_ref,
    start_ref,
    left_ref,
    right_ref,
    off_buf,
    sens_buf,
    neigh_buf,
    weight_buf,
    index_buf,
    spread_buf,
    cell_buf,
    base_buf,
    sems,
):
    slots, owned = index_buf.shape
    start = pl.multiple_of(lax.axis_index("nodes") * owned, LANES)
    mine = pl.ds(start, owned)
    pairs = (
        (neigh_in, neigh_buf),
        (index_in.at[:, mine], index_buf),
        (spread_in.at[:, mine], spread_buf),
        (cell_in, cell_buf),
        (base_in.at[:, mine], base_buf),
        (off_in, off_buf),
        (weight_in, weight_buf),
        (sens_in, sens_buf),
        (inverse_in, inverse_ref),
        (rhs_in, rhs_ref),
        (start_in, start_ref),
    )
    copies = [pltpu.make_async_copy(a, b, sems.at[i]) for i, (a, b) in enumerate(pairs)]
    for copy in copies:
        copy.start()

    faces, cells = neigh_buf.shape
    blocks = cells // LANES
    per = blocks * nodes
    first_cell = lax.axis_index(CELL_AXES) * cells
    copies[0].wait()
    for block in range(blocks):
        index = neigh_buf[:, block * LANES : (block + 1) * LANES]
        local = index - first_cell + cells
        lane = jnp.bitwise_and(local, LANES - 1)
        step = jnp.right_shift(local, 7) - block
        step = jnp.where(index >= 0, step, -1)
        for node in range(nodes):
            rows = pl.ds(block * nodes + node, faces, stride=per)
            lane_ref[rows, :] = lane
            step_ref[rows, :] = step

    copies[1].wait()
    copies[2].wait()
    groups = FFD // LANES
    piece = min(512, owned)
    for first in range(0, owned, piece):
        here = slice(first, first + piece)
        low = jnp.bitwise_and(index_buf[:, here], LANES - 1).astype(jnp.float32).T
        low = low.astype(jnp.bfloat16)
        high = jnp.right_shift(index_buf[:, here], 7)
        lane = lax.broadcasted_iota(jnp.int32, (piece, LANES), 1).astype(jnp.float32)
        lane = lane.astype(jnp.bfloat16)
        part = lax.broadcasted_iota(jnp.int32, (16, piece), 0)
        part = jnp.where(part < 3 * groups, lax.rem(part, groups), -1)
        for j in range(slots):
            hit = jnp.broadcast_to(low[:, j : j + 1], (piece, LANES)) == lane
            one_hot_ref[j * owned + first : j * owned + first + piece, :] = jnp.where(
                hit, jnp.bfloat16(1.0), jnp.bfloat16(0.0)
            )
            spread_ref[j * 16 : (j + 1) * 16, here] = jnp.where(
                high[j : j + 1] == part, spread_buf[j : j + 1, here], 0.0
            )

    copies[3].wait()
    left_ref[...] = distance_factors(cell_buf[...], True).T.astype(jnp.bfloat16)
    copies[4].wait()
    right_ref[...] = distance_factors(base_buf[...], False).astype(jnp.bfloat16)

    copies[5].wait()
    off_ref[...] = off_buf[...].astype(jnp.float32)
    copies[6].wait()
    copies[7].wait()
    row_node = lax.rem(lax.broadcasted_iota(jnp.int32, (per, LANES), 0), nodes)
    weights = jnp.zeros((per, LANES), jnp.float32)
    for node in range(nodes):
        weights = jnp.where(row_node == node, weight_buf[node], weights)
    for row in range(0, sens_buf.shape[0], per):
        here = slice(row, row + per)
        sens_ref[here, :] = sens_buf[here, :].astype(jnp.float32) * weights
    for copy in copies[8:]:
        copy.wait()


def sweep_into(
    blocks, first_ref, second_ref, own_ref, rhs_ref, off_ref, inverse_ref, lane_ref, step_ref,
    out_ref, window_ref, table_ref,
):
    per = rhs_ref.shape[0] // 5
    nodes = per // blocks
    faces = lane_ref.shape[0] // per
    odd = lax.rem(lax.axis_index(CELL_AXES), 2)
    place = pl.multiple_of((1 - odd) * 2 * per, 8)
    other = pl.multiple_of(odd * 2 * per, 8)
    width = 3 * per
    for b in range(5):
        rows = slice(b * per, (b + 1) * per)
        base = b * width
        window_ref[pl.ds(base + place, per), :] = first_ref[rows, :]
        window_ref[base + per : base + 2 * per, :] = own_ref[rows, :]
        window_ref[pl.ds(base + other, per), :] = second_ref[rows, :]
    for shift in range(8 // nodes):
        for b in range(5):
            for tile in range(0, width - (8 if shift else 0), 8):
                to = (shift * 5 + b) * width + tile
                table_ref[to : to + 8, :] = window_ref[
                    pl.ds(b * width + tile + shift * nodes, 8), :
                ]
    for half in range(0, per, 8):
        remaining = [rhs_ref[a * per + half : a * per + half + 8, :] for a in range(5)]
        for f in range(faces):
            lanes = lane_ref[f * per + half : f * per + half + 8, :]
            dist = step_ref[f * per + half : f * per + half + 8, :]
            beside = [jnp.zeros((8, LANES), jnp.float32)] * 5
            for d in range(2 * blocks + 1):
                here = dist == d
                first = half + d * nodes
                for b in range(5):
                    at = ((first % 8) // nodes * 5 + b) * width + first // 8 * 8
                    got = jnp.take_along_axis(
                        table_ref[at : at + 8, :], lanes, axis=1, mode="promise_in_bounds"
                    )
                    beside[b] = jnp.where(here, got, beside[b])
            for a in range(5):
                for b in range(5):
                    row = (f * 25 + 5 * a + b) * per + half
                    remaining[a] = remaining[a] - off_ref[row : row + 8, :] * beside[b]
        for a in range(5):
            total = None
            for b in range(5):
                row = (5 * a + b) * per + half
                term = inverse_ref[row : row + 8, :] * remaining[b]
                total = term if total is None else total + term
            out_ref[a * per + half : a * per + half + 8, :] = total


def sweep_kernel(blocks, *refs):
    sweep_into(blocks, *refs)


def last_sweep_kernel(blocks, *refs):
    ins, rest = refs[:8], refs[8:]
    sens_ref, _, out_ref, sens_out_ref, window_ref, table_ref, part_ref = rest
    sweep_into(blocks, *ins, out_ref, window_ref, table_ref)
    per = out_ref.shape[0] // 5
    nodes = per // blocks
    for k in range(3):
        total = None
        for a in range(5):
            row = (3 * a + k) * per
            term = out_ref[a * per : (a + 1) * per, :] * sens_ref[row : row + per, :]
            total = term if total is None else total + term
        part_ref[k * per : (k + 1) * per, :] = total
    for block in range(blocks):
        total = None
        for node in range(nodes):
            term = part_ref[pl.ds(block * nodes + node, 3, stride=per), :]
            total = term if total is None else total + term
        sens_out_ref[pl.ds(block, 3, stride=blocks), :] = total


def pieces(value, count):
    found = []
    for _ in range(count):
        piece = value.astype(jnp.bfloat16).astype(jnp.float32)
        found.append(piece)
        value = value - piece
    return found


def distance_factors(points, left):
    count = points.shape[1]
    scaled = (points - 0.5) * (1.0 / SUPPORT_RADIUS)
    scaled = jnp.concatenate([scaled, jnp.zeros((5, count), jnp.float32)], axis=0)
    norm = jnp.sum(scaled * scaled, axis=0, keepdims=True)
    norms = pieces(jnp.broadcast_to(norm, (8, count)), 3)
    row = lax.broadcasted_iota(jnp.int32, (8, count), 0)
    norm_block = jnp.zeros((8, count), jnp.float32)
    for place in range(3):
        norm_block = jnp.where(row == place, norms[place], norm_block)
    ones_block = jnp.where(row < 3, 1.0, 0.0)
    first, second, third = pieces(scaled, 3)
    if left:
        dims = [first, first, second, second, first, third]
        dims = [-2.0 * part for part in dims]
        blocks = dims + [norm_block, ones_block]
    else:
        dims = [first, second, first, second, third, first]
        blocks = dims + [ones_block, norm_block]
    return jnp.concatenate(blocks, axis=0)


def wendland_kernel(first_cell, left_ref, right_ref, _, first_ref, rest_ref):
    cells, owned = first_ref.shape
    tile, wide = min(64, cells), min(256, owned)
    for row in range(0, cells, tile):
        left = left_ref[first_cell + row : first_cell + row + tile, :]
        for lane in range(0, owned, wide):
            here = slice(lane, lane + wide)
            squared = jnp.dot(left, right_ref[:, here], preferred_element_type=jnp.float32)
            squared = jnp.maximum(squared, 1e-30)
            near = jnp.maximum(1.0 - squared * lax.rsqrt(squared), 0.0)
            power = near * near
            kernel = power * power * (1.25 - near)
            first = kernel.astype(jnp.bfloat16)
            first_ref[row : row + tile, here] = first
            rest_ref[row : row + tile, here] = (kernel - first.astype(jnp.float32)).astype(
                jnp.bfloat16
            )


def wendland_and_write_kernel(first_cell, left_ref, right_ref, after, adjoint_ref, *rest):
    first_ref, rest_ref, result_ref, sem = rest
    copy = pltpu.make_async_copy(adjoint_ref, result_ref, sem)
    copy.start()
    wendland_kernel(first_cell, left_ref, right_ref, after, first_ref, rest_ref)
    copy.wait()


def control_kernel(scale, *refs):
    (*sens_refs, near_first, near_rest, far_first, far_rest, spread_ref, one_hot_ref, out_ref) = refs
    blocks = sens_refs[0].shape[0] // 3
    cells = blocks * LANES
    half = near_first.shape[0]
    slots = spread_ref.shape[0] // 16
    groups = FFD // LANES
    total = sens_refs[0][...]
    for ref in sens_refs[1:]:
        total = total + ref[...]
    total = total * scale
    row = lax.broadcasted_iota(jnp.int32, (16, LANES), 0)
    wide = []
    for block in range(blocks):
        sens = jnp.zeros((16, LANES), jnp.float32)
        for k in range(3):
            mine = jnp.logical_and(row >= k * groups, row < (k + 1) * groups)
            sens = jnp.where(mine, total[k * blocks + block : k * blocks + block + 1], sens)
        wide.append(sens)
    sens = jnp.concatenate(wide, axis=1)

    def halves(value):
        first = value.astype(jnp.bfloat16)
        rest = (value - first.astype(jnp.float32)).astype(jnp.bfloat16)
        return jnp.concatenate([first, rest], axis=0)

    sens = halves(sens)
    grad = None
    for part, ref in (
        (sens[:, :half], near_first),
        (sens[:, :half], near_rest),
        (sens[:, half:], far_first),
        (sens[:, half:], far_rest),
    ):
        term = jnp.dot(part, ref[...], preferred_element_type=jnp.float32)
        grad = term if grad is None else grad + term
    grad = grad[:16] + grad[16:]
    owned = grad.shape[1]
    result = None
    for j in range(slots):
        term = jnp.dot(
            halves(grad * spread_ref[j * 16 : (j + 1) * 16, :]),
            one_hot_ref[j * owned : (j + 1) * owned, :],
            preferred_element_type=jnp.float32,
        )
        result = term if result is None else result + term
    result = result[:16] + result[16:]
    out_ref[...] = result[: 3 * groups]


def chip_kernel(own_ref, other_ref, out_ref):
    total = own_ref[...] + other_ref[...]
    for copy in range(out_ref.shape[0]):
        out_ref[copy] = total


def finish_kernel(in_ref, out_ref):
    values = [in_ref[i] for i in range(in_ref.shape[0])]
    while len(values) > 1:
        values = [sum(values[i : i + 2]) for i in range(0, len(values), 2)]
    groups = out_ref.shape[1] // LANES
    for k in range(3):
        for group in range(groups):
            row = k * groups + group
            out_ref[k : k + 1, group * LANES : (group + 1) * LANES] = values[0][row : row + 1]


def body(
    adjoint_start,
    adjoint_rhs,
    off_blocks,
    diag_inverse,
    neighbours,
    node_weights,
    sens_blocks,
    cell_points,
    base_points,
    ffd_index,
    ffd_weight,
):
    nodes, _, cells = adjoint_start.shape
    faces = off_blocks.shape[1]
    blocks = cells // LANES
    per = blocks * nodes
    slots = ffd_index.shape[1]
    owned = base_points.shape[1] // lax.axis_size("nodes")
    peers = lax.axis_size(CELL_AXES)
    f32, i32, bf16 = jnp.float32, jnp.int32, jnp.bfloat16

    def shape(dims, dtype=f32):
        return jax.ShapeDtypeStruct(dims, dtype)

    def cost(flops, moved):
        return pl.CostEstimate(flops=flops, bytes_accessed=moved, transcendentals=0)

    def swaps(array):
        first = [(i, i ^ 1) for i in range(peers)]
        second = [(i, i + 1 if i % 2 else i - 1) for i in range(peers)]
        second = [(i, j if 0 <= j < peers else i) for i, j in second]
        far = lax.ppermute(array, CELL_AXES, second)
        close = lax.ppermute(array, CELL_AXES, first)
        return far, close

    adjoint = rows_of(adjoint_start)
    far, close = swaps(adjoint)
    prepared = pl.pallas_call(
        functools.partial(prepare_kernel, nodes),
        out_shape=(
            shape((faces * 25 * per, LANES)),
            shape((25 * per, LANES)),
            shape((5 * per, LANES)),
            shape((15 * per, LANES)),
            shape((faces * per, LANES), i32),
            shape((faces * per, LANES), i32),
            shape((slots * 16, owned)),
            shape((slots * owned, LANES), bf16),
            shape((5 * per, LANES)),
            shape((cells, FACTOR_ROWS), bf16),
            shape((FACTOR_ROWS, owned), bf16),
        ),
        in_specs=[HBM] * 11,
        out_specs=(VMEM,) * 11,
        scratch_shapes=[
            pltpu.VMEM((faces * 25 * per, LANES), bf16),
            pltpu.VMEM((15 * per, LANES), bf16),
            pltpu.VMEM((faces, cells), i32),
            pltpu.SMEM((nodes,), f32),
            pltpu.VMEM((slots, owned), i32),
            pltpu.VMEM((slots, owned), f32),
            pltpu.VMEM((3, cells), f32),
            pltpu.VMEM((3, owned), f32),
            pltpu.SemaphoreType.DMA((11,)),
        ],
        compiler_params=PARAMS,
        cost_estimate=cost(10**9, 10**7),
        name="prepare",
    )(
        *in_hbm(
            rows_of(off_blocks.reshape(nodes, faces * 25, cells)),
            rows_of(diag_inverse),
            rows_of(adjoint_rhs),
            rows_of(sens_blocks),
            neighbours,
            node_weights,
            ffd_index.T,
            ffd_weight.T,
            adjoint,
            cell_points,
            base_points,
        )
    )
    off, inverse, rhs, sens, lane, step, spread, one_hot, adjoint, left, right = prepared
    scratch = [
        pltpu.VMEM((3 * 5 * per, LANES), f32),
        pltpu.VMEM((8 // nodes * 3 * 5 * per, LANES), f32),
    ]
    sweep_cost = cost(2 * 10 * 35 * cells, 4 * faces * 25 * per * LANES)

    for _ in range(SWEEPS - 1):
        adjoint = pl.pallas_call(
            functools.partial(sweep_kernel, blocks),
            out_shape=shape((5 * per, LANES)),
            in_specs=[VMEM] * 8,
            out_specs=VMEM,
            scratch_shapes=scratch,
            compiler_params=PARAMS,
            cost_estimate=sweep_cost,
            name="sweep",
        )(close, far, adjoint, rhs, off, inverse, lane, step)
        far, close = swaps(adjoint)

    half = cells * 5 // 8 // LANES * LANES
    wendland_cost = cost(10**9, 10**7)
    near_shape, far_shape = shape((half, owned), bf16), shape((cells - half, owned), bf16)
    near_first, near_rest = pl.pallas_call(
        functools.partial(wendland_kernel, 0),
        out_shape=(near_shape, near_shape),
        in_specs=[VMEM] * 3,
        out_specs=(VMEM, VMEM),
        compiler_params=PARAMS,
        cost_estimate=wendland_cost,
        name="near_wendland",
    )(left, right, adjoint)
    adjoint, part_sens = pl.pallas_call(
        functools.partial(last_sweep_kernel, blocks),
        out_shape=(shape((5 * per, LANES)), shape((3 * blocks, LANES))),
        in_specs=[VMEM] * 9 + [pl.BlockSpec(memory_space=pl.ANY)],
        out_specs=(VMEM, VMEM),
        scratch_shapes=scratch + [pltpu.VMEM((3 * per, LANES), f32)],
        compiler_params=PARAMS,
        cost_estimate=sweep_cost,
        name="last_sweep",
    )(close, far, adjoint, rhs, off, inverse, lane, step, sens, near_first)

    all_sens = [part_sens]
    node_peers = lax.axis_size("nodes")
    for shift in range(1, node_peers):
        ring = [(i, (i + shift) % node_peers) for i in range(node_peers)]
        all_sens.append(lax.ppermute(part_sens, "nodes", ring))
    far_first, far_rest, adjoint = pl.pallas_call(
        functools.partial(wendland_and_write_kernel, half),
        out_shape=(far_shape, far_shape, shape((5 * per, LANES))),
        in_specs=[VMEM] * 4,
        out_specs=(VMEM, VMEM, HBM),
        scratch_shapes=[pltpu.SemaphoreType.DMA],
        compiler_params=PARAMS,
        cost_estimate=wendland_cost,
        name="far_wendland",
    )(left, right, part_sens, adjoint)
    scale = 4.0 / math.sqrt(cells * peers)
    rows = 3 * FFD // LANES
    partial = pl.pallas_call(
        functools.partial(control_kernel, scale),
        out_shape=shape((rows, LANES)),
        in_specs=[VMEM] * (len(all_sens) + 6),
        out_specs=VMEM,
        compiler_params=PARAMS,
        name="control",
    )(*all_sens, near_first, near_rest, far_first, far_rest, spread, one_hot)
    cores = lax.axis_size("sub")
    other = lax.ppermute(partial, "sub", [(i, cores - 1 - i) for i in range(cores)])
    copies = pl.pallas_call(
        chip_kernel,
        out_shape=shape((lax.axis_size(("cells", "nodes")), rows, LANES)),
        in_specs=[VMEM] * 2,
        out_specs=VMEM,
        name="chip",
        compiler_params=PARAMS,
    )(partial, other)
    gathered = lax.all_to_all(copies, ("cells", "nodes"), 0, 0, tiled=True)
    control_grad = pl.pallas_call(
        finish_kernel, out_shape=shape((3, FFD)), name="finish", compiler_params=PARAMS
    )(gathered)
    return (from_rows(adjoint, nodes, cells), control_grad)


def solution(mesh):
    return jax.shard_map(
        body,
        mesh=mesh,
        in_specs=(
            P("nodes", None, ("groups", "cells", "sub")),
            P("nodes", None, ("groups", "cells", "sub")),
            P("nodes", None, None, ("groups", "cells", "sub")),
            P("nodes", None, ("groups", "cells", "sub")),
            P(None, ("cells", "sub")),
            P("nodes"),
            P("nodes", None, ("groups", "cells", "sub")),
            P(None, ("cells", "sub")),
            P(),
            P(),
            P(),
        ),
        out_specs=(P("nodes", None, ("groups", "cells", "sub")), P("groups", None)),
        check_vma=False,
    )
```

```python
import functools
import math

import jax
import jax.numpy as jnp
from jax import lax
from jax.experimental import pallas as pl
from jax.experimental.pallas import tpu as pltpu
from jax.sharding import PartitionSpec as P

SWEEPS = 2
FFD = 512
SUPPORT_RADIUS = 0.3
LANES = 128
CELL_AXES = ("cells", "sub")
FACTOR_ROWS = 64
PARAMS = pltpu.CompilerParams(vmem_limit_bytes=24 * 1024 * 1024)
VMEM = pl.BlockSpec(memory_space=pltpu.VMEM)
HBM = pl.BlockSpec(memory_space=pltpu.HBM)


def rows_of(array):
    nodes, rows, cells = array.shape
    blocks = cells // LANES
    split = array.reshape(nodes, rows, blocks, LANES)
    return split.transpose(1, 2, 0, 3).reshape(rows * blocks * nodes, LANES)


def from_rows(array, nodes, cells):
    blocks = cells // LANES
    split = array.reshape(-1, blocks, nodes, LANES)
    return split.transpose(2, 0, 1, 3).reshape(nodes, -1, cells)


def in_hbm(*arrays):
    return [pltpu.with_memory_space_constraint(array, pltpu.HBM) for array in arrays]


def write_one_hot(low_ref, one_hot_ref, first_slot):
    owned = low_ref.shape[1]
    piece = min(512, owned)
    lane = lax.broadcasted_iota(jnp.int32, (piece, LANES), 1).astype(jnp.float32)
    lane = lane.astype(jnp.bfloat16)
    for first in range(0, owned, piece):
        low = low_ref[:, first : first + piece].T.astype(jnp.bfloat16)
        for j in range(one_hot_ref.shape[0] // owned):
            column = low[:, first_slot + j : first_slot + j + 1]
            hit = jnp.broadcast_to(column, (piece, LANES)) == lane
            one_hot_ref[j * owned + first : j * owned + first + piece, :] = jnp.where(
                hit, jnp.bfloat16(1.0), jnp.bfloat16(0.0)
            )


def prepare_kernel(
    nodes,
    off_in,
    inverse_in,
    rhs_in,
    sens_in,
    neigh_in,
    weight_in,
    index_in,
    spread_in,
    start_in,
    cell_in,
    base_in,
    off_ref,
    inverse_ref,
    rhs_ref,
    sens_ref,
    lane_ref,
    step_ref,
    spread_ref,
    low_ref,
    one_hot_ref,
    start_ref,
    left_ref,
    right_ref,
    off_buf,
    sens_buf,
    neigh_buf,
    weight_buf,
    index_buf,
    spread_buf,
    cell_buf,
    base_buf,
    sems,
):
    slots, owned = index_buf.shape
    start = pl.multiple_of(lax.axis_index("nodes") * owned, LANES)
    mine = pl.ds(start, owned)
    pairs = (
        (neigh_in, neigh_buf),
        (index_in.at[:, mine], index_buf),
        (spread_in.at[:, mine], spread_buf),
        (cell_in, cell_buf),
        (base_in.at[:, mine], base_buf),
        (off_in, off_buf),
        (weight_in, weight_buf),
        (sens_in, sens_buf),
        (inverse_in, inverse_ref),
        (rhs_in, rhs_ref),
        (start_in, start_ref),
    )
    copies = [pltpu.make_async_copy(a, b, sems.at[i]) for i, (a, b) in enumerate(pairs)]
    for copy in copies:
        copy.start()

    faces, cells = neigh_buf.shape
    blocks = cells // LANES
    per = blocks * nodes
    first_cell = lax.axis_index(CELL_AXES) * cells
    copies[0].wait()
    for block in range(blocks):
        index = neigh_buf[:, block * LANES : (block + 1) * LANES]
        local = index - first_cell + cells
        lane = jnp.bitwise_and(local, LANES - 1)
        step = jnp.right_shift(local, 7) - block
        step = jnp.where(index >= 0, step, -1)
        for node in range(nodes):
            rows = pl.ds(block * nodes + node, faces, stride=per)
            lane_ref[rows, :] = lane
            step_ref[rows, :] = step

    copies[1].wait()
    copies[2].wait()
    groups = FFD // LANES
    piece = min(512, owned)
    for first in range(0, owned, piece):
        here = slice(first, first + piece)
        high = jnp.right_shift(index_buf[:, here], 7)
        part = lax.broadcasted_iota(jnp.int32, (16, piece), 0)
        part = jnp.where(part < 3 * groups, lax.rem(part, groups), -1)
        for j in range(slots):
            spread_ref[j * 16 : (j + 1) * 16, here] = jnp.where(
                high[j : j + 1] == part, spread_buf[j : j + 1, here], 0.0
            )

    low_ref[...] = jnp.bitwise_and(index_buf[...], LANES - 1).astype(jnp.float32)
    write_one_hot(low_ref, one_hot_ref, 0)

    copies[3].wait()
    left_ref[...] = distance_factors(cell_buf[...], True).T.astype(jnp.bfloat16)
    copies[4].wait()
    right_ref[...] = distance_factors(base_buf[...], False).astype(jnp.bfloat16)

    copies[5].wait()
    off_ref[...] = off_buf[...].astype(jnp.float32)
    copies[6].wait()
    copies[7].wait()
    row_node = lax.rem(lax.broadcasted_iota(jnp.int32, (per, LANES), 0), nodes)
    weights = jnp.zeros((per, LANES), jnp.float32)
    for node in range(nodes):
        weights = jnp.where(row_node == node, weight_buf[node], weights)
    for row in range(0, sens_buf.shape[0], per):
        here = slice(row, row + per)
        sens_ref[here, :] = sens_buf[here, :].astype(jnp.float32) * weights
    for copy in copies[8:]:
        copy.wait()


def sweep_into(
    blocks, first_ref, second_ref, own_ref, rhs_ref, off_ref, inverse_ref, lane_ref, step_ref,
    out_ref, window_ref, table_ref,
):
    per = rhs_ref.shape[0] // 5
    nodes = per // blocks
    faces = lane_ref.shape[0] // per
    odd = lax.rem(lax.axis_index(CELL_AXES), 2)
    place = pl.multiple_of((1 - odd) * 2 * per, 8)
    other = pl.multiple_of(odd * 2 * per, 8)
    width = 3 * per
    for b in range(5):
        rows = slice(b * per, (b + 1) * per)
        base = b * width
        window_ref[pl.ds(base + place, per), :] = first_ref[rows, :]
        window_ref[base + per : base + 2 * per, :] = own_ref[rows, :]
        window_ref[pl.ds(base + other, per), :] = second_ref[rows, :]
    for shift in range(8 // nodes):
        for b in range(5):
            for tile in range(0, width - (8 if shift else 0), 8):
                to = (shift * 5 + b) * width + tile
                table_ref[to : to + 8, :] = window_ref[
                    pl.ds(b * width + tile + shift * nodes, 8), :
                ]
    for half in range(0, per, 8):
        remaining = [rhs_ref[a * per + half : a * per + half + 8, :] for a in range(5)]
        for f in range(faces):
            lanes = lane_ref[f * per + half : f * per + half + 8, :]
            dist = step_ref[f * per + half : f * per + half + 8, :]
            beside = [jnp.zeros((8, LANES), jnp.float32)] * 5
            for d in range(2 * blocks + 1):
                here = dist == d
                first = half + d * nodes
                for b in range(5):
                    at = ((first % 8) // nodes * 5 + b) * width + first // 8 * 8
                    got = jnp.take_along_axis(
                        table_ref[at : at + 8, :], lanes, axis=1, mode="promise_in_bounds"
                    )
                    beside[b] = jnp.where(here, got, beside[b])
            for a in range(5):
                for b in range(5):
                    row = (f * 25 + 5 * a + b) * per + half
                    remaining[a] = remaining[a] - off_ref[row : row + 8, :] * beside[b]
        for a in range(5):
            total = None
            for b in range(5):
                row = (5 * a + b) * per + half
                term = inverse_ref[row : row + 8, :] * remaining[b]
                total = term if total is None else total + term
            out_ref[a * per + half : a * per + half + 8, :] = total


def sweep_kernel(blocks, *refs):
    sweep_into(blocks, *refs)


def last_sweep_kernel(blocks, *refs):
    ins, rest = refs[:8], refs[8:]
    sens_ref, _, out_ref, sens_out_ref, window_ref, table_ref, part_ref = rest
    sweep_into(blocks, *ins, out_ref, window_ref, table_ref)
    per = out_ref.shape[0] // 5
    nodes = per // blocks
    for k in range(3):
        total = None
        for a in range(5):
            row = (3 * a + k) * per
            term = out_ref[a * per : (a + 1) * per, :] * sens_ref[row : row + per, :]
            total = term if total is None else total + term
        part_ref[k * per : (k + 1) * per, :] = total
    for block in range(blocks):
        total = None
        for node in range(nodes):
            term = part_ref[pl.ds(block * nodes + node, 3, stride=per), :]
            total = term if total is None else total + term
        sens_out_ref[pl.ds(block, 3, stride=blocks), :] = total


def pieces(value, count):
    found = []
    for _ in range(count):
        piece = value.astype(jnp.bfloat16).astype(jnp.float32)
        found.append(piece)
        value = value - piece
    return found


def distance_factors(points, left):
    count = points.shape[1]
    scaled = (points - 0.5) * (1.0 / SUPPORT_RADIUS)
    scaled = jnp.concatenate([scaled, jnp.zeros((5, count), jnp.float32)], axis=0)
    norm = jnp.sum(scaled * scaled, axis=0, keepdims=True)
    norms = pieces(jnp.broadcast_to(norm, (8, count)), 3)
    row = lax.broadcasted_iota(jnp.int32, (8, count), 0)
    norm_block = jnp.zeros((8, count), jnp.float32)
    for place in range(3):
        norm_block = jnp.where(row == place, norms[place], norm_block)
    ones_block = jnp.where(row < 3, 1.0, 0.0)
    first, second, third = pieces(scaled, 3)
    if left:
        dims = [first, first, second, second, first, third]
        dims = [-2.0 * part for part in dims]
        blocks = dims + [norm_block, ones_block]
    else:
        dims = [first, second, first, second, third, first]
        blocks = dims + [ones_block, norm_block]
    return jnp.concatenate(blocks, axis=0)


def wendland_kernel(first_cell, left_ref, right_ref, _, first_ref, rest_ref):
    cells, owned = first_ref.shape
    tile, wide = min(64, cells), min(256, owned)
    for row in range(0, cells, tile):
        left = left_ref[first_cell + row : first_cell + row + tile, :]
        for lane in range(0, owned, wide):
            here = slice(lane, lane + wide)
            squared = jnp.dot(left, right_ref[:, here], preferred_element_type=jnp.float32)
            squared = jnp.maximum(squared, 1e-30)
            near = jnp.maximum(1.0 - squared * lax.rsqrt(squared), 0.0)
            power = near * near
            kernel = power * power * (1.25 - near)
            first = kernel.astype(jnp.bfloat16)
            first_ref[row : row + tile, here] = first
            rest_ref[row : row + tile, here] = (kernel - first.astype(jnp.float32)).astype(
                jnp.bfloat16
            )


def far_wendland_kernel(
    first_cell, left_ref, right_ref, after, adjoint_ref, low_ref, *rest
):
    first_ref, rest_ref, one_hot_ref, result_ref, sem = rest
    copy = pltpu.make_async_copy(adjoint_ref, result_ref, sem)
    copy.start()
    owned = low_ref.shape[1]
    write_one_hot(low_ref, one_hot_ref, low_ref.shape[0] - one_hot_ref.shape[0] // owned)
    wendland_kernel(first_cell, left_ref, right_ref, after, first_ref, rest_ref)
    copy.wait()


def control_kernel(scale, *refs):
    *sens_refs, near_first, near_rest, far_first, far_rest = refs[:-4]
    spread_ref, near_hot, far_hot, out_ref = refs[-4:]
    blocks = sens_refs[0].shape[0] // 3
    cells = blocks * LANES
    half = near_first.shape[0]
    groups = FFD // LANES
    total = sens_refs[0][...]
    for ref in sens_refs[1:]:
        total = total + ref[...]
    total = total * scale
    row = lax.broadcasted_iota(jnp.int32, (16, LANES), 0)
    wide = []
    for block in range(blocks):
        sens = jnp.zeros((16, LANES), jnp.float32)
        for k in range(3):
            mine = jnp.logical_and(row >= k * groups, row < (k + 1) * groups)
            sens = jnp.where(mine, total[k * blocks + block : k * blocks + block + 1], sens)
        wide.append(sens)
    sens = jnp.concatenate(wide, axis=1)

    def halves(value):
        first = value.astype(jnp.bfloat16)
        rest = (value - first.astype(jnp.float32)).astype(jnp.bfloat16)
        return jnp.concatenate([first, rest], axis=0)

    sens = halves(sens)
    grad = None
    for part, ref in (
        (sens[:, :half], near_first),
        (sens[:, :half], near_rest),
        (sens[:, half:], far_first),
        (sens[:, half:], far_rest),
    ):
        term = jnp.dot(part, ref[...], preferred_element_type=jnp.float32)
        grad = term if grad is None else grad + term
    grad = grad[:16] + grad[16:]
    owned = grad.shape[1]
    result = None
    places = [
        (ref, first) for ref in (near_hot, far_hot) for first in range(0, ref.shape[0], owned)
    ]
    for j, (ref, first) in enumerate(places):
        term = jnp.dot(
            halves(grad * spread_ref[j * 16 : (j + 1) * 16, :]),
            ref[first : first + owned, :],
            preferred_element_type=jnp.float32,
        )
        result = term if result is None else result + term
    result = result[:16] + result[16:]
    out_ref[...] = result[: 3 * groups]


def tree(values):
    while len(values) > 1:
        values = [sum(values[i : i + 2]) for i in range(0, len(values), 2)]
    return values[0]


def add_kernel(*refs):
    refs[-1][...] = tree([ref[...] for ref in refs[:-1]])


def finish_kernel(*refs):
    total, out_ref = tree([ref[...] for ref in refs[:-1]]), refs[-1]
    groups = out_ref.shape[1] // LANES
    for k in range(3):
        for group in range(groups):
            row = k * groups + group
            out_ref[k : k + 1, group * LANES : (group + 1) * LANES] = total[row : row + 1]


def exchanged(value, axes):
    peers = lax.axis_size(axes)
    if peers > 8 or peers & (peers - 1):
        return [lax.psum(value, axes)]
    return [value] + [
        lax.ppermute(value, axes, [(i, i ^ shift) for i in range(peers)])
        for shift in range(1, peers)
    ]


def body(
    adjoint_start,
    adjoint_rhs,
    off_blocks,
    diag_inverse,
    neighbours,
    node_weights,
    sens_blocks,
    cell_points,
    base_points,
    ffd_index,
    ffd_weight,
):
    nodes, _, cells = adjoint_start.shape
    faces = off_blocks.shape[1]
    blocks = cells // LANES
    per = blocks * nodes
    slots = ffd_index.shape[1]
    owned = base_points.shape[1] // lax.axis_size("nodes")
    peers = lax.axis_size(CELL_AXES)
    f32, i32, bf16 = jnp.float32, jnp.int32, jnp.bfloat16

    def shape(dims, dtype=f32):
        return jax.ShapeDtypeStruct(dims, dtype)

    def cost(flops, moved):
        return pl.CostEstimate(flops=flops, bytes_accessed=moved, transcendentals=0)

    def swaps(array):
        first = [(i, i ^ 1) for i in range(peers)]
        second = [(i, i + 1 if i % 2 else i - 1) for i in range(peers)]
        second = [(i, j if 0 <= j < peers else i) for i, j in second]
        far = lax.ppermute(array, CELL_AXES, second)
        close = lax.ppermute(array, CELL_AXES, first)
        return far, close

    adjoint = rows_of(adjoint_start)
    far, close = swaps(adjoint)
    prepared = pl.pallas_call(
        functools.partial(prepare_kernel, nodes),
        out_shape=(
            shape((faces * 25 * per, LANES)),
            shape((25 * per, LANES)),
            shape((5 * per, LANES)),
            shape((15 * per, LANES)),
            shape((faces * per, LANES), i32),
            shape((faces * per, LANES), i32),
            shape((slots * 16, owned)),
            shape((slots, owned)),
            shape((slots // 2 * owned, LANES), bf16),
            shape((5 * per, LANES)),
            shape((cells, FACTOR_ROWS), bf16),
            shape((FACTOR_ROWS, owned), bf16),
        ),
        in_specs=[HBM] * 11,
        out_specs=(VMEM,) * 12,
        scratch_shapes=[
            pltpu.VMEM((faces * 25 * per, LANES), bf16),
            pltpu.VMEM((15 * per, LANES), bf16),
            pltpu.VMEM((faces, cells), i32),
            pltpu.SMEM((nodes,), f32),
            pltpu.VMEM((slots, owned), i32),
            pltpu.VMEM((slots, owned), f32),
            pltpu.VMEM((3, cells), f32),
            pltpu.VMEM((3, owned), f32),
            pltpu.SemaphoreType.DMA((11,)),
        ],
        compiler_params=PARAMS,
        cost_estimate=cost(10**9, 10**7),
        name="prepare",
    )(
        *in_hbm(
            rows_of(off_blocks.reshape(nodes, faces * 25, cells)),
            rows_of(diag_inverse),
            rows_of(adjoint_rhs),
            rows_of(sens_blocks),
            neighbours,
            node_weights,
            ffd_index.T,
            ffd_weight.T,
            adjoint,
            cell_points,
            base_points,
        )
    )
    off, inverse, rhs, sens, lane, step, spread, low, near_hot, adjoint, left, right = prepared
    scratch = [
        pltpu.VMEM((3 * 5 * per, LANES), f32),
        pltpu.VMEM((8 // nodes * 3 * 5 * per, LANES), f32),
    ]
    sweep_cost = cost(2 * 10 * 35 * cells, 4 * faces * 25 * per * LANES)

    for _ in range(SWEEPS - 1):
        adjoint = pl.pallas_call(
            functools.partial(sweep_kernel, blocks),
            out_shape=shape((5 * per, LANES)),
            in_specs=[VMEM] * 8,
            out_specs=VMEM,
            scratch_shapes=scratch,
            compiler_params=PARAMS,
            cost_estimate=sweep_cost,
            name="sweep",
        )(close, far, adjoint, rhs, off, inverse, lane, step)
        far, close = swaps(adjoint)

    half = cells * 5 // 8 // LANES * LANES
    wendland_cost = cost(10**9, 10**7)
    near_shape, far_shape = shape((half, owned), bf16), shape((cells - half, owned), bf16)
    near_first, near_rest = pl.pallas_call(
        functools.partial(wendland_kernel, 0),
        out_shape=(near_shape, near_shape),
        in_specs=[VMEM] * 3,
        out_specs=(VMEM, VMEM),
        compiler_params=PARAMS,
        cost_estimate=wendland_cost,
        name="near_wendland",
    )(left, right, adjoint)
    adjoint, part_sens = pl.pallas_call(
        functools.partial(last_sweep_kernel, blocks),
        out_shape=(shape((5 * per, LANES)), shape((3 * blocks, LANES))),
        in_specs=[VMEM] * 9 + [pl.BlockSpec(memory_space=pl.ANY)],
        out_specs=(VMEM, VMEM),
        scratch_shapes=scratch + [pltpu.VMEM((3 * per, LANES), f32)],
        compiler_params=PARAMS,
        cost_estimate=sweep_cost,
        name="last_sweep",
    )(close, far, adjoint, rhs, off, inverse, lane, step, sens, near_first)

    all_sens = [part_sens]
    node_peers = lax.axis_size("nodes")
    for shift in range(1, node_peers):
        ring = [(i, (i + shift) % node_peers) for i in range(node_peers)]
        all_sens.append(lax.ppermute(part_sens, "nodes", ring))
    hot_shape = shape(((slots - slots // 2) * owned, LANES), bf16)
    far_first, far_rest, far_hot, adjoint = pl.pallas_call(
        functools.partial(far_wendland_kernel, half),
        out_shape=(far_shape, far_shape, hot_shape, shape((5 * per, LANES))),
        in_specs=[VMEM] * 5,
        out_specs=(VMEM, VMEM, VMEM, HBM),
        scratch_shapes=[pltpu.SemaphoreType.DMA],
        compiler_params=PARAMS,
        cost_estimate=wendland_cost,
        name="far_wendland",
    )(left, right, part_sens, adjoint, low)
    scale = 4.0 / math.sqrt(cells * peers)
    rows = 3 * FFD // LANES
    partial = pl.pallas_call(
        functools.partial(control_kernel, scale),
        out_shape=shape((rows, LANES)),
        in_specs=[VMEM] * (len(all_sens) + 7),
        out_specs=VMEM,
        compiler_params=PARAMS,
        name="control",
    )(*all_sens, near_first, near_rest, far_first, far_rest, spread, near_hot, far_hot)
    partial = pl.pallas_call(
        add_kernel, out_shape=shape((rows, LANES)), name="add", compiler_params=PARAMS
    )(*exchanged(partial, ("nodes", "sub")))
    control_grad = pl.pallas_call(
        finish_kernel, out_shape=shape((3, FFD)), name="finish", compiler_params=PARAMS
    )(*exchanged(partial, "cells"))
    return (from_rows(adjoint, nodes, cells), control_grad)


def solution(mesh):
    return jax.shard_map(
        body,
        mesh=mesh,
        in_specs=(
            P("nodes", None, ("groups", "cells", "sub")),
            P("nodes", None, ("groups", "cells", "sub")),
            P("nodes", None, None, ("groups", "cells", "sub")),
            P("nodes", None, ("groups", "cells", "sub")),
            P(None, ("cells", "sub")),
            P("nodes"),
            P("nodes", None, ("groups", "cells", "sub")),
            P(None, ("cells", "sub")),
            P(),
            P(),
            P(),
        ),
        out_specs=(P("nodes", None, ("groups", "cells", "sub")), P("groups", None)),
        check_vma=False,
    )
```

```python
import functools
import math

import jax
import jax.numpy as jnp
from jax import lax
from jax.experimental import pallas as pl
from jax.experimental.pallas import tpu as pltpu
from jax.sharding import PartitionSpec as P

SWEEPS = 2
FFD = 512
SUPPORT_RADIUS = 0.3
LANES = 128
CELL_AXES = ("cells", "sub")
SUM_AXES = ("cells", "nodes", "sub")
FACTOR_ROWS = 64
PARAMS = pltpu.CompilerParams(vmem_limit_bytes=24 * 1024 * 1024)
VMEM = pl.BlockSpec(memory_space=pltpu.VMEM)
HBM = pl.BlockSpec(memory_space=pltpu.HBM)


def rows_of(array):
    nodes, rows, cells = array.shape
    blocks = cells // LANES
    split = array.reshape(nodes, rows, blocks, LANES)
    return split.transpose(1, 2, 0, 3).reshape(rows * blocks * nodes, LANES)


def from_rows(array, nodes, cells):
    blocks = cells // LANES
    split = array.reshape(-1, blocks, nodes, LANES)
    return split.transpose(2, 0, 1, 3).reshape(nodes, -1, cells)


def in_hbm(*arrays):
    return [pltpu.with_memory_space_constraint(array, pltpu.HBM) for array in arrays]


def write_one_hot(low_ref, one_hot_ref, first_slot):
    owned = low_ref.shape[1]
    piece = min(512, owned)
    lane = lax.broadcasted_iota(jnp.int32, (piece, LANES), 1).astype(jnp.float32)
    lane = lane.astype(jnp.bfloat16)
    for first in range(0, owned, piece):
        low = low_ref[:, first : first + piece].T.astype(jnp.bfloat16)
        for j in range(one_hot_ref.shape[0] // owned):
            column = low[:, first_slot + j : first_slot + j + 1]
            hit = jnp.broadcast_to(column, (piece, LANES)) == lane
            one_hot_ref[j * owned + first : j * owned + first + piece, :] = jnp.where(
                hit, jnp.bfloat16(1.0), jnp.bfloat16(0.0)
            )


def prepare_kernel(
    nodes,
    off_in,
    inverse_in,
    rhs_in,
    sens_in,
    neigh_in,
    weight_in,
    index_in,
    spread_in,
    start_in,
    cell_in,
    base_in,
    off_ref,
    inverse_ref,
    rhs_ref,
    sens_ref,
    lane_ref,
    step_ref,
    spread_ref,
    low_ref,
    one_hot_ref,
    start_ref,
    left_ref,
    right_ref,
    off_buf,
    sens_buf,
    neigh_buf,
    weight_buf,
    index_buf,
    spread_buf,
    cell_buf,
    base_buf,
    sems,
):
    slots, owned = index_buf.shape
    start = pl.multiple_of(lax.axis_index("nodes") * owned, LANES)
    mine = pl.ds(start, owned)
    pairs = (
        (neigh_in, neigh_buf),
        (index_in.at[:, mine], index_buf),
        (spread_in.at[:, mine], spread_buf),
        (cell_in, cell_buf),
        (base_in.at[:, mine], base_buf),
        (off_in, off_buf),
        (weight_in, weight_buf),
        (sens_in, sens_buf),
        (inverse_in, inverse_ref),
        (rhs_in, rhs_ref),
        (start_in, start_ref),
    )
    copies = [pltpu.make_async_copy(a, b, sems.at[i]) for i, (a, b) in enumerate(pairs)]
    for copy in copies:
        copy.start()

    faces, cells = neigh_buf.shape
    blocks = cells // LANES
    per = blocks * nodes
    first_cell = lax.axis_index(CELL_AXES) * cells
    copies[0].wait()
    for block in range(blocks):
        index = neigh_buf[:, block * LANES : (block + 1) * LANES]
        local = index - first_cell + cells
        lane = jnp.bitwise_and(local, LANES - 1)
        step = jnp.right_shift(local, 7) - block
        step = jnp.where(index >= 0, step, -1)
        for node in range(nodes):
            rows = pl.ds(block * nodes + node, faces, stride=per)
            lane_ref[rows, :] = lane
            step_ref[rows, :] = step

    copies[1].wait()
    copies[2].wait()
    groups = FFD // LANES
    piece = min(512, owned)
    for first in range(0, owned, piece):
        here = slice(first, first + piece)
        high = jnp.right_shift(index_buf[:, here], 7)
        part = lax.broadcasted_iota(jnp.int32, (16, piece), 0)
        part = jnp.where(part < 3 * groups, lax.rem(part, groups), -1)
        for j in range(slots):
            spread_ref[j * 16 : (j + 1) * 16, here] = jnp.where(
                high[j : j + 1] == part, spread_buf[j : j + 1, here], 0.0
            )

    low_ref[...] = jnp.bitwise_and(index_buf[...], LANES - 1).astype(jnp.float32)
    write_one_hot(low_ref, one_hot_ref, 0)

    copies[3].wait()
    left_ref[...] = distance_factors(cell_buf[...], True).T.astype(jnp.bfloat16)
    copies[4].wait()
    right_ref[...] = distance_factors(base_buf[...], False).astype(jnp.bfloat16)

    copies[5].wait()
    off_ref[...] = off_buf[...].astype(jnp.float32)
    copies[6].wait()
    copies[7].wait()
    row_node = lax.rem(lax.broadcasted_iota(jnp.int32, (per, LANES), 0), nodes)
    weights = jnp.zeros((per, LANES), jnp.float32)
    for node in range(nodes):
        weights = jnp.where(row_node == node, weight_buf[node], weights)
    for row in range(0, sens_buf.shape[0], per):
        here = slice(row, row + per)
        sens_ref[here, :] = sens_buf[here, :].astype(jnp.float32) * weights
    for copy in copies[8:]:
        copy.wait()


def sweep_into(
    blocks, first_ref, second_ref, own_ref, rhs_ref, off_ref, inverse_ref, lane_ref, step_ref,
    out_ref, window_ref, table_ref,
):
    per = rhs_ref.shape[0] // 5
    nodes = per // blocks
    faces = lane_ref.shape[0] // per
    odd = lax.rem(lax.axis_index(CELL_AXES), 2)
    place = pl.multiple_of((1 - odd) * 2 * per, 8)
    other = pl.multiple_of(odd * 2 * per, 8)
    width = 3 * per
    for b in range(5):
        rows = slice(b * per, (b + 1) * per)
        base = b * width
        window_ref[pl.ds(base + place, per), :] = first_ref[rows, :]
        window_ref[base + per : base + 2 * per, :] = own_ref[rows, :]
        window_ref[pl.ds(base + other, per), :] = second_ref[rows, :]
    for shift in range(8 // nodes):
        for b in range(5):
            for tile in range(0, width - (8 if shift else 0), 8):
                to = (shift * 5 + b) * width + tile
                table_ref[to : to + 8, :] = window_ref[
                    pl.ds(b * width + tile + shift * nodes, 8), :
                ]
    for half in range(0, per, 8):
        remaining = [rhs_ref[a * per + half : a * per + half + 8, :] for a in range(5)]
        for f in range(faces):
            lanes = lane_ref[f * per + half : f * per + half + 8, :]
            dist = step_ref[f * per + half : f * per + half + 8, :]
            beside = [jnp.zeros((8, LANES), jnp.float32)] * 5
            for d in range(2 * blocks + 1):
                here = dist == d
                first = half + d * nodes
                for b in range(5):
                    at = ((first % 8) // nodes * 5 + b) * width + first // 8 * 8
                    got = jnp.take_along_axis(
                        table_ref[at : at + 8, :], lanes, axis=1, mode="promise_in_bounds"
                    )
                    beside[b] = jnp.where(here, got, beside[b])
            for a in range(5):
                for b in range(5):
                    row = (f * 25 + 5 * a + b) * per + half
                    remaining[a] = remaining[a] - off_ref[row : row + 8, :] * beside[b]
        for a in range(5):
            total = None
            for b in range(5):
                row = (5 * a + b) * per + half
                term = inverse_ref[row : row + 8, :] * remaining[b]
                total = term if total is None else total + term
            out_ref[a * per + half : a * per + half + 8, :] = total


def sweep_kernel(blocks, *refs):
    sweep_into(blocks, *refs)


def last_sweep_kernel(blocks, *refs):
    ins, rest = refs[:8], refs[8:]
    sens_ref, _, out_ref, sens_out_ref, window_ref, table_ref, part_ref = rest
    sweep_into(blocks, *ins, out_ref, window_ref, table_ref)
    per = out_ref.shape[0] // 5
    nodes = per // blocks
    for k in range(3):
        total = None
        for a in range(5):
            row = (3 * a + k) * per
            term = out_ref[a * per : (a + 1) * per, :] * sens_ref[row : row + per, :]
            total = term if total is None else total + term
        part_ref[k * per : (k + 1) * per, :] = total
    for block in range(blocks):
        total = None
        for node in range(nodes):
            term = part_ref[pl.ds(block * nodes + node, 3, stride=per), :]
            total = term if total is None else total + term
        sens_out_ref[pl.ds(block, 3, stride=blocks), :] = total


def pieces(value, count):
    found = []
    for _ in range(count):
        piece = value.astype(jnp.bfloat16).astype(jnp.float32)
        found.append(piece)
        value = value - piece
    return found


def distance_factors(points, left):
    count = points.shape[1]
    scaled = (points - 0.5) * (1.0 / SUPPORT_RADIUS)
    scaled = jnp.concatenate([scaled, jnp.zeros((5, count), jnp.float32)], axis=0)
    norm = jnp.sum(scaled * scaled, axis=0, keepdims=True)
    norms = pieces(jnp.broadcast_to(norm, (8, count)), 3)
    row = lax.broadcasted_iota(jnp.int32, (8, count), 0)
    norm_block = jnp.zeros((8, count), jnp.float32)
    for place in range(3):
        norm_block = jnp.where(row == place, norms[place], norm_block)
    ones_block = jnp.where(row < 3, 1.0, 0.0)
    first, second, third = pieces(scaled, 3)
    if left:
        dims = [first, first, second, second, first, third]
        dims = [-2.0 * part for part in dims]
        blocks = dims + [norm_block, ones_block]
    else:
        dims = [first, second, first, second, third, first]
        blocks = dims + [ones_block, norm_block]
    return jnp.concatenate(blocks, axis=0)


def wendland_kernel(first_cell, left_ref, right_ref, _, kernel_ref):
    cells, owned = kernel_ref.shape[0] // 2, kernel_ref.shape[1]
    tile, wide = min(64, cells), min(256, owned)
    for row in range(0, cells, tile):
        left = left_ref[first_cell + row : first_cell + row + tile, :]
        for lane in range(0, owned, wide):
            here = slice(lane, lane + wide)
            squared = jnp.dot(left, right_ref[:, here], preferred_element_type=jnp.float32)
            squared = jnp.maximum(squared, 1e-30)
            near = jnp.maximum(1.0 - squared * lax.rsqrt(squared), 0.0)
            power = near * near
            kernel = power * power * (1.25 - near)
            first = kernel.astype(jnp.bfloat16)
            rest = (kernel - first.astype(jnp.float32)).astype(jnp.bfloat16)
            kernel_ref[row : row + tile, here] = first
            kernel_ref[cells + row : cells + row + tile, here] = rest


def far_wendland_kernel(
    first_cell, left_ref, right_ref, after, adjoint_ref, low_ref, *rest
):
    kernel_ref, one_hot_ref, result_ref, sem = rest
    copy = pltpu.make_async_copy(adjoint_ref, result_ref, sem)
    copy.start()
    owned = low_ref.shape[1]
    write_one_hot(low_ref, one_hot_ref, low_ref.shape[0] - one_hot_ref.shape[0] // owned)
    wendland_kernel(first_cell, left_ref, right_ref, after, kernel_ref)
    copy.wait()


def control_kernel(scale, *refs):
    *sens_refs, near_ref, far_ref = refs[:-4]
    spread_ref, near_hot, far_hot, out_ref = refs[-4:]
    blocks = sens_refs[0].shape[0] // 3
    half = near_ref.shape[0] // 2
    groups = FFD // LANES
    total = sens_refs[0][...]
    for ref in sens_refs[1:]:
        total = total + ref[...]
    total = total * scale

    def halves(value):
        first = value.astype(jnp.bfloat16)
        rest = (value - first.astype(jnp.float32)).astype(jnp.bfloat16)
        return first, rest

    row = lax.broadcasted_iota(jnp.int32, (8, LANES), 0)
    wide = []
    for block in range(blocks):
        sens = jnp.zeros((8, LANES), jnp.float32)
        for k in range(3):
            sens = jnp.where(row == k, total[k * blocks + block : k * blocks + block + 1], sens)
        first = sens.astype(jnp.bfloat16).astype(jnp.float32)
        wide.append(jnp.concatenate([first, sens - first], axis=0))
    sens = jnp.concatenate(wide, axis=1).astype(jnp.bfloat16)
    grad = None
    for part, ref in ((sens[:, :half], near_ref), (sens[:, half:], far_ref)):
        both = jnp.concatenate([part, part], axis=1)
        term = jnp.dot(both, ref[...], preferred_element_type=jnp.float32)
        grad = term if grad is None else grad + term
    grad = grad[:8] + grad[8:]
    row = lax.broadcasted_iota(jnp.int32, (16, grad.shape[1]), 0)
    wide = jnp.zeros(row.shape, jnp.float32)
    for k in range(3):
        mine = jnp.logical_and(row >= k * groups, row < (k + 1) * groups)
        wide = jnp.where(mine, grad[k : k + 1], wide)
    grad = wide
    owned = grad.shape[1]
    result = None
    places = [
        (ref, first) for ref in (near_hot, far_hot) for first in range(0, ref.shape[0], owned)
    ]
    for j, (ref, first) in enumerate(places):
        term = jnp.dot(
            jnp.concatenate(halves(grad * spread_ref[j * 16 : (j + 1) * 16, :]), axis=0),
            ref[first : first + owned, :],
            preferred_element_type=jnp.float32,
        )
        result = term if result is None else result + term
    result = result[:16] + result[16:]
    out_ref[...] = result[: 3 * groups]


def tree(values):
    while len(values) > 1:
        values = [sum(values[i : i + 2]) for i in range(0, len(values), 2)]
    return values[0]


def add_kernel(*refs):
    refs[-1][...] = tree([ref[...] for ref in refs[:-1]])


def finish_kernel(own_ref, other_ref, out_ref):
    last = lax.axis_size("sub") - 1
    total = jnp.where(lax.axis_index("sub") == last, own_ref[...], other_ref[...])
    groups = out_ref.shape[1] // LANES
    for k in range(3):
        for group in range(groups):
            row = k * groups + group
            out_ref[k : k + 1, group * LANES : (group + 1) * LANES] = total[row : row + 1]


def add(*arrays):
    shape = jax.ShapeDtypeStruct(arrays[0].shape, arrays[0].dtype)
    return pl.pallas_call(add_kernel, out_shape=shape, name="add", compiler_params=PARAMS)(*arrays)


def sum_on_last_cores(value):
    cores = lax.axis_size("sub")
    received = [
        lax.ppermute(value, "sub", [(i, (i + shift) % cores) for i in range(cores)])
        for shift in range(1, cores)
    ]
    value = add(value, *received)
    for axis, other, major in (("nodes", "cells", False), ("cells", "nodes", True)):
        peers, others = lax.axis_size(axis), lax.axis_size(other)

        def swap(array, shift):
            pairs = []
            for mine in range(peers):
                for beside in range(others):
                    ends = [
                        at * others + beside if major else beside * peers + at
                        for at in (mine, mine ^ shift)
                    ]
                    pairs.append(tuple(end * cores + cores - 1 for end in ends))
            return lax.ppermute(array, SUM_AXES, pairs)

        if peers <= 4:
            value = add(value, *[swap(value, shift) for shift in range(1, peers)])
        else:
            shift = 1
            while shift < peers:
                value = add(value, swap(value, shift))
                shift *= 2
    return value


def body(
    adjoint_start,
    adjoint_rhs,
    off_blocks,
    diag_inverse,
    neighbours,
    node_weights,
    sens_blocks,
    cell_points,
    base_points,
    ffd_index,
    ffd_weight,
):
    nodes, _, cells = adjoint_start.shape
    faces = off_blocks.shape[1]
    blocks = cells // LANES
    per = blocks * nodes
    slots = ffd_index.shape[1]
    owned = base_points.shape[1] // lax.axis_size("nodes")
    peers = lax.axis_size(CELL_AXES)
    f32, i32, bf16 = jnp.float32, jnp.int32, jnp.bfloat16

    def shape(dims, dtype=f32):
        return jax.ShapeDtypeStruct(dims, dtype)

    def cost(flops, moved):
        return pl.CostEstimate(flops=flops, bytes_accessed=moved, transcendentals=0)

    def swaps(array):
        first = [(i, i ^ 1) for i in range(peers)]
        second = [(i, i + 1 if i % 2 else i - 1) for i in range(peers)]
        second = [(i, j if 0 <= j < peers else i) for i, j in second]
        far = lax.ppermute(array, CELL_AXES, second)
        close = lax.ppermute(array, CELL_AXES, first)
        return far, close

    adjoint = rows_of(adjoint_start)
    far, close = swaps(adjoint)
    prepared = pl.pallas_call(
        functools.partial(prepare_kernel, nodes),
        out_shape=(
            shape((faces * 25 * per, LANES)),
            shape((25 * per, LANES)),
            shape((5 * per, LANES)),
            shape((15 * per, LANES)),
            shape((faces * per, LANES), i32),
            shape((faces * per, LANES), i32),
            shape((slots * 16, owned)),
            shape((slots, owned)),
            shape((slots // 2 * owned, LANES), bf16),
            shape((5 * per, LANES)),
            shape((cells, FACTOR_ROWS), bf16),
            shape((FACTOR_ROWS, owned), bf16),
        ),
        in_specs=[HBM] * 11,
        out_specs=(VMEM,) * 12,
        scratch_shapes=[
            pltpu.VMEM((faces * 25 * per, LANES), bf16),
            pltpu.VMEM((15 * per, LANES), bf16),
            pltpu.VMEM((faces, cells), i32),
            pltpu.SMEM((nodes,), f32),
            pltpu.VMEM((slots, owned), i32),
            pltpu.VMEM((slots, owned), f32),
            pltpu.VMEM((3, cells), f32),
            pltpu.VMEM((3, owned), f32),
            pltpu.SemaphoreType.DMA((11,)),
        ],
        compiler_params=PARAMS,
        cost_estimate=cost(10**9, 10**7),
        name="prepare",
    )(
        *in_hbm(
            rows_of(off_blocks.reshape(nodes, faces * 25, cells)),
            rows_of(diag_inverse),
            rows_of(adjoint_rhs),
            rows_of(sens_blocks),
            neighbours,
            node_weights,
            ffd_index.T,
            ffd_weight.T,
            adjoint,
            cell_points,
            base_points,
        )
    )
    off, inverse, rhs, sens, lane, step, spread, low, near_hot, adjoint, left, right = prepared
    scratch = [
        pltpu.VMEM((3 * 5 * per, LANES), f32),
        pltpu.VMEM((8 // nodes * 3 * 5 * per, LANES), f32),
    ]
    sweep_cost = cost(2 * 10 * 35 * cells, 4 * faces * 25 * per * LANES)

    for _ in range(SWEEPS - 1):
        adjoint = pl.pallas_call(
            functools.partial(sweep_kernel, blocks),
            out_shape=shape((5 * per, LANES)),
            in_specs=[VMEM] * 8,
            out_specs=VMEM,
            scratch_shapes=scratch,
            compiler_params=PARAMS,
            cost_estimate=sweep_cost,
            name="sweep",
        )(close, far, adjoint, rhs, off, inverse, lane, step)
        far, close = swaps(adjoint)

    half = cells * 5 // 8 // LANES * LANES
    wendland_cost = cost(10**9, 10**7)
    near_shape = shape((2 * half, owned), bf16)
    far_shape = shape((2 * (cells - half), owned), bf16)
    near_kernel = pl.pallas_call(
        functools.partial(wendland_kernel, 0),
        out_shape=near_shape,
        in_specs=[VMEM] * 3,
        out_specs=VMEM,
        compiler_params=PARAMS,
        cost_estimate=wendland_cost,
        name="near_wendland",
    )(left, right, adjoint)
    adjoint, part_sens = pl.pallas_call(
        functools.partial(last_sweep_kernel, blocks),
        out_shape=(shape((5 * per, LANES)), shape((3 * blocks, LANES))),
        in_specs=[VMEM] * 9 + [pl.BlockSpec(memory_space=pl.ANY)],
        out_specs=(VMEM, VMEM),
        scratch_shapes=scratch + [pltpu.VMEM((3 * per, LANES), f32)],
        compiler_params=PARAMS,
        cost_estimate=sweep_cost,
        name="last_sweep",
    )(close, far, adjoint, rhs, off, inverse, lane, step, sens, near_kernel)

    all_sens = [part_sens]
    node_peers = lax.axis_size("nodes")
    for shift in range(1, node_peers):
        ring = [(i, (i + shift) % node_peers) for i in range(node_peers)]
        all_sens.append(lax.ppermute(part_sens, "nodes", ring))
    hot_shape = shape(((slots - slots // 2) * owned, LANES), bf16)
    far_kernel, far_hot, adjoint = pl.pallas_call(
        functools.partial(far_wendland_kernel, half),
        out_shape=(far_shape, hot_shape, shape((5 * per, LANES))),
        in_specs=[VMEM] * 5,
        out_specs=(VMEM, VMEM, HBM),
        scratch_shapes=[pltpu.SemaphoreType.DMA],
        compiler_params=PARAMS,
        cost_estimate=wendland_cost,
        name="far_wendland",
    )(left, right, part_sens, adjoint, low)
    scale = 4.0 / math.sqrt(cells * peers)
    rows = 3 * FFD // LANES
    partial = pl.pallas_call(
        functools.partial(control_kernel, scale),
        out_shape=shape((rows, LANES)),
        in_specs=[VMEM] * (len(all_sens) + 5),
        out_specs=VMEM,
        compiler_params=PARAMS,
        name="control",
    )(*all_sens, near_kernel, far_kernel, spread, near_hot, far_hot)
    total = sum_on_last_cores(partial)
    last = lax.axis_size("sub") - 1
    control_grad = pl.pallas_call(
        finish_kernel, out_shape=shape((3, FFD)), name="finish", compiler_params=PARAMS
    )(total, lax.ppermute(total, "sub", [(last, i) for i in range(1)]))
    return (from_rows(adjoint, nodes, cells), control_grad)


def solution(mesh):
    return jax.shard_map(
        body,
        mesh=mesh,
        in_specs=(
            P("nodes", None, ("groups", "cells", "sub")),
            P("nodes", None, ("groups", "cells", "sub")),
            P("nodes", None, None, ("groups", "cells", "sub")),
            P("nodes", None, ("groups", "cells", "sub")),
            P(None, ("cells", "sub")),
            P("nodes"),
            P("nodes", None, ("groups", "cells", "sub")),
            P(None, ("cells", "sub")),
            P(),
            P(),
            P(),
        ),
        out_specs=(P("nodes", None, ("groups", "cells", "sub")), P("groups", None)),
        check_vma=False,
    )
```

```python
import functools
import math

import jax
import jax.numpy as jnp
from jax import lax
from jax.experimental import pallas as pl
from jax.experimental.pallas import tpu as pltpu
from jax.sharding import PartitionSpec as P

SWEEPS = 2
FFD = 512
SUPPORT_RADIUS = 0.3
LANES = 128
CELL_AXES = ("cells", "sub")
SUM_AXES = ("cells", "nodes", "sub")
FACTOR_ROWS = 64
PARAMS = pltpu.CompilerParams(vmem_limit_bytes=24 * 1024 * 1024)
VMEM = pl.BlockSpec(memory_space=pltpu.VMEM)
HBM = pl.BlockSpec(memory_space=pltpu.HBM)


def rows_of(array):
    nodes, rows, cells = array.shape
    blocks = cells // LANES
    split = array.reshape(nodes, rows, blocks, LANES)
    return split.transpose(1, 2, 0, 3).reshape(rows * blocks * nodes, LANES)


def from_rows(array, nodes, cells):
    blocks = cells // LANES
    split = array.reshape(-1, blocks, nodes, LANES)
    return split.transpose(2, 0, 1, 3).reshape(nodes, -1, cells)


def in_hbm(*arrays):
    return [pltpu.with_memory_space_constraint(array, pltpu.HBM) for array in arrays]


def write_one_hot(low_ref, one_hot_ref, first_slot):
    owned = low_ref.shape[1]
    piece = min(512, owned)
    lane = lax.broadcasted_iota(jnp.int32, (piece, LANES), 1).astype(jnp.float32)
    lane = lane.astype(jnp.bfloat16)
    for first in range(0, owned, piece):
        low = low_ref[:, first : first + piece].T.astype(jnp.bfloat16)
        for j in range(one_hot_ref.shape[0] // owned):
            column = low[:, first_slot + j : first_slot + j + 1]
            hit = jnp.broadcast_to(column, (piece, LANES)) == lane
            one_hot_ref[j * owned + first : j * owned + first + piece, :] = jnp.where(
                hit, jnp.bfloat16(1.0), jnp.bfloat16(0.0)
            )


def prepare_kernel(
    nodes,
    off_in,
    inverse_in,
    rhs_in,
    sens_in,
    neigh_in,
    weight_in,
    index_in,
    spread_in,
    start_in,
    cell_in,
    base_in,
    off_ref,
    inverse_ref,
    rhs_ref,
    sens_ref,
    lane_ref,
    step_ref,
    spread_ref,
    low_ref,
    one_hot_ref,
    start_ref,
    left_ref,
    right_ref,
    off_buf,
    sens_buf,
    neigh_buf,
    weight_buf,
    index_buf,
    spread_buf,
    cell_buf,
    base_buf,
    sems,
):
    slots, owned = index_buf.shape
    start = pl.multiple_of(lax.axis_index("nodes") * owned, LANES)
    mine = pl.ds(start, owned)
    pairs = (
        (neigh_in, neigh_buf),
        (index_in.at[:, mine], index_buf),
        (spread_in.at[:, mine], spread_buf),
        (cell_in, cell_buf),
        (base_in.at[:, mine], base_buf),
        (off_in, off_buf),
        (weight_in, weight_buf),
        (sens_in, sens_buf),
        (inverse_in, inverse_ref),
        (rhs_in, rhs_ref),
        (start_in, start_ref),
    )
    copies = [pltpu.make_async_copy(a, b, sems.at[i]) for i, (a, b) in enumerate(pairs)]
    for copy in copies:
        copy.start()

    faces, cells = neigh_buf.shape
    blocks = cells // LANES
    per = blocks * nodes
    first_cell = lax.axis_index(CELL_AXES) * cells
    copies[0].wait()
    for block in range(blocks):
        index = neigh_buf[:, block * LANES : (block + 1) * LANES]
        local = index - first_cell + cells
        lane = jnp.bitwise_and(local, LANES - 1)
        step = jnp.right_shift(local, 7) - block
        step = jnp.where(index >= 0, step, -1)
        for node in range(nodes):
            rows = pl.ds(block * nodes + node, faces, stride=per)
            lane_ref[rows, :] = lane
            step_ref[rows, :] = step

    copies[1].wait()
    copies[2].wait()
    groups = FFD // LANES
    piece = min(512, owned)
    for first in range(0, owned, piece):
        here = slice(first, first + piece)
        high = jnp.right_shift(index_buf[:, here], 7)
        part = lax.broadcasted_iota(jnp.int32, (16, piece), 0)
        part = jnp.where(part < 3 * groups, lax.rem(part, groups), -1)
        for j in range(slots):
            spread_ref[j * 16 : (j + 1) * 16, here] = jnp.where(
                high[j : j + 1] == part, spread_buf[j : j + 1, here], 0.0
            )

    low_ref[...] = jnp.bitwise_and(index_buf[...], LANES - 1).astype(jnp.float32)
    write_one_hot(low_ref, one_hot_ref, 0)

    copies[3].wait()
    left_ref[...] = distance_factors(cell_buf[...], True).T.astype(jnp.bfloat16)
    copies[4].wait()
    right_ref[...] = distance_factors(base_buf[...], False).astype(jnp.bfloat16)

    copies[5].wait()
    off_ref[...] = off_buf[...].astype(jnp.float32)
    copies[6].wait()
    copies[7].wait()
    row_node = lax.rem(lax.broadcasted_iota(jnp.int32, (per, LANES), 0), nodes)
    weights = jnp.zeros((per, LANES), jnp.float32)
    for node in range(nodes):
        weights = jnp.where(row_node == node, weight_buf[node], weights)
    for row in range(0, sens_buf.shape[0], per):
        here = slice(row, row + per)
        sens_ref[here, :] = sens_buf[here, :].astype(jnp.float32) * weights
    for copy in copies[8:]:
        copy.wait()


def sweep_into(
    blocks, first_ref, second_ref, own_ref, rhs_ref, off_ref, inverse_ref, lane_ref, step_ref,
    out_ref, window_ref, table_ref,
):
    per = rhs_ref.shape[0] // 5
    nodes = per // blocks
    faces = lane_ref.shape[0] // per
    odd = lax.rem(lax.axis_index(CELL_AXES), 2)
    place = pl.multiple_of((1 - odd) * 2 * per, 8)
    other = pl.multiple_of(odd * 2 * per, 8)
    width = 3 * per
    for b in range(5):
        rows = slice(b * per, (b + 1) * per)
        base = b * width
        window_ref[pl.ds(base + place, per), :] = first_ref[rows, :]
        window_ref[base + per : base + 2 * per, :] = own_ref[rows, :]
        window_ref[pl.ds(base + other, per), :] = second_ref[rows, :]
    for shift in range(8 // nodes):
        for b in range(5):
            for tile in range(0, width - (8 if shift else 0), 8):
                to = (shift * 5 + b) * width + tile
                table_ref[to : to + 8, :] = window_ref[
                    pl.ds(b * width + tile + shift * nodes, 8), :
                ]
    for half in range(0, per, 8):
        remaining = [rhs_ref[a * per + half : a * per + half + 8, :] for a in range(5)]
        for f in range(faces):
            lanes = lane_ref[f * per + half : f * per + half + 8, :]
            dist = step_ref[f * per + half : f * per + half + 8, :]
            beside = [jnp.zeros((8, LANES), jnp.float32)] * 5
            for d in range(2 * blocks + 1):
                here = dist == d
                first = half + d * nodes
                for b in range(5):
                    at = ((first % 8) // nodes * 5 + b) * width + first // 8 * 8
                    got = jnp.take_along_axis(
                        table_ref[at : at + 8, :], lanes, axis=1, mode="promise_in_bounds"
                    )
                    beside[b] = jnp.where(here, got, beside[b])
            for a in range(5):
                for b in range(5):
                    row = (f * 25 + 5 * a + b) * per + half
                    remaining[a] = remaining[a] - off_ref[row : row + 8, :] * beside[b]
        for a in range(5):
            total = None
            for b in range(5):
                row = (5 * a + b) * per + half
                term = inverse_ref[row : row + 8, :] * remaining[b]
                total = term if total is None else total + term
            out_ref[a * per + half : a * per + half + 8, :] = total


def sweep_kernel(blocks, *refs):
    sweep_into(blocks, *refs)


def last_sweep_kernel(blocks, *refs):
    ins, rest = refs[:8], refs[8:]
    sens_ref, _, out_ref, sens_out_ref, window_ref, table_ref, part_ref = rest
    sweep_into(blocks, *ins, out_ref, window_ref, table_ref)
    per = out_ref.shape[0] // 5
    nodes = per // blocks
    for k in range(3):
        total = None
        for a in range(5):
            row = (3 * a + k) * per
            term = out_ref[a * per : (a + 1) * per, :] * sens_ref[row : row + per, :]
            total = term if total is None else total + term
        part_ref[k * per : (k + 1) * per, :] = total
    for block in range(blocks):
        total = None
        for node in range(nodes):
            term = part_ref[pl.ds(block * nodes + node, 3, stride=per), :]
            total = term if total is None else total + term
        sens_out_ref[pl.ds(block, 3, stride=blocks), :] = total


def pieces(value, count):
    found = []
    for _ in range(count):
        piece = value.astype(jnp.bfloat16).astype(jnp.float32)
        found.append(piece)
        value = value - piece
    return found


def distance_factors(points, left):
    count = points.shape[1]
    scaled = (points - 0.5) * (1.0 / SUPPORT_RADIUS)
    scaled = jnp.concatenate([scaled, jnp.zeros((5, count), jnp.float32)], axis=0)
    norm = jnp.sum(scaled * scaled, axis=0, keepdims=True)
    norms = pieces(jnp.broadcast_to(norm, (8, count)), 3)
    row = lax.broadcasted_iota(jnp.int32, (8, count), 0)
    norm_block = jnp.zeros((8, count), jnp.float32)
    for place in range(3):
        norm_block = jnp.where(row == place, norms[place], norm_block)
    ones_block = jnp.where(row < 3, 1.0, 0.0)
    first, second, third = pieces(scaled, 3)
    if left:
        dims = [first, first, second, second, first, third]
        dims = [-2.0 * part for part in dims]
        blocks = dims + [norm_block, ones_block]
    else:
        dims = [first, second, first, second, third, first]
        blocks = dims + [ones_block, norm_block]
    return jnp.concatenate(blocks, axis=0)


def wendland_kernel(first_cell, left_ref, right_ref, _, kernel_ref):
    cells, owned = kernel_ref.shape[0] // 2, kernel_ref.shape[1]
    tile, wide = min(64, cells), min(256, owned)
    for row in range(0, cells, tile):
        left = left_ref[first_cell + row : first_cell + row + tile, :]
        for lane in range(0, owned, wide):
            here = slice(lane, lane + wide)
            squared = jnp.dot(left, right_ref[:, here], preferred_element_type=jnp.float32)
            squared = jnp.maximum(squared, 1e-30)
            near = jnp.maximum(1.0 - squared * lax.rsqrt(squared), 0.0)
            power = near * near
            kernel = power * power * (1.25 - near)
            first = kernel.astype(jnp.bfloat16)
            rest = (kernel - first.astype(jnp.float32)).astype(jnp.bfloat16)
            kernel_ref[row : row + tile, here] = first
            kernel_ref[cells + row : cells + row + tile, here] = rest


def far_wendland_kernel(
    first_cell, left_ref, right_ref, after, adjoint_ref, low_ref, *rest
):
    kernel_ref, one_hot_ref, result_ref, sem = rest
    copy = pltpu.make_async_copy(adjoint_ref, result_ref, sem)
    copy.start()
    owned = low_ref.shape[1]
    write_one_hot(low_ref, one_hot_ref, low_ref.shape[0] - one_hot_ref.shape[0] // owned)
    wendland_kernel(first_cell, left_ref, right_ref, after, kernel_ref)
    copy.wait()


def control_kernel(scale, *refs):
    *sens_refs, near_ref, far_ref = refs[:-4]
    spread_ref, near_hot, far_hot, out_ref = refs[-4:]
    blocks = sens_refs[0].shape[0] // 3
    half = near_ref.shape[0] // 2
    groups = FFD // LANES
    total = sens_refs[0][...]
    for ref in sens_refs[1:]:
        total = total + ref[...]
    total = total * scale

    def halves(value):
        first = value.astype(jnp.bfloat16)
        rest = (value - first.astype(jnp.float32)).astype(jnp.bfloat16)
        return first, rest

    row = lax.broadcasted_iota(jnp.int32, (8, LANES), 0)
    wide = []
    for block in range(blocks):
        sens = jnp.zeros((8, LANES), jnp.float32)
        for k in range(3):
            sens = jnp.where(row == k, total[k * blocks + block : k * blocks + block + 1], sens)
        first = sens.astype(jnp.bfloat16).astype(jnp.float32)
        wide.append(jnp.concatenate([first, sens - first], axis=0))
    sens = jnp.concatenate(wide, axis=1).astype(jnp.bfloat16)
    grad = None
    for part, ref in ((sens[:, :half], near_ref), (sens[:, half:], far_ref)):
        both = jnp.concatenate([part, part], axis=1)
        term = jnp.dot(both, ref[...], preferred_element_type=jnp.float32)
        grad = term if grad is None else grad + term
    grad = grad[:8] + grad[8:]
    row = lax.broadcasted_iota(jnp.int32, (16, grad.shape[1]), 0)
    wide = jnp.zeros(row.shape, jnp.float32)
    for k in range(3):
        mine = jnp.logical_and(row >= k * groups, row < (k + 1) * groups)
        wide = jnp.where(mine, grad[k : k + 1], wide)
    grad = wide
    owned = grad.shape[1]
    result = None
    places = [
        (ref, first) for ref in (near_hot, far_hot) for first in range(0, ref.shape[0], owned)
    ]
    for j, (ref, first) in enumerate(places):
        term = jnp.dot(
            jnp.concatenate(halves(grad * spread_ref[j * 16 : (j + 1) * 16, :]), axis=0),
            ref[first : first + owned, :],
            preferred_element_type=jnp.float32,
        )
        result = term if result is None else result + term
    result = result[:16] + result[16:]
    out_ref[...] = result[: 3 * groups]


def tree(values):
    while len(values) > 1:
        values = [sum(values[i : i + 2]) for i in range(0, len(values), 2)]
    return values[0]


def add_kernel(*refs):
    refs[-1][...] = tree([ref[...] for ref in refs[:-1]])


def finish_kernel(*refs):
    total, out_ref = tree([ref[...] for ref in refs[:-1]]), refs[-1]
    groups = out_ref.shape[1] // LANES
    for k in range(3):
        for group in range(groups):
            row = k * groups + group
            out_ref[k : k + 1, group * LANES : (group + 1) * LANES] = total[row : row + 1]


def exchanged(value, axes):
    peers = lax.axis_size(axes)
    if peers > 8 or peers & (peers - 1):
        return [lax.psum(value, axes)]
    return [value] + [
        lax.ppermute(value, axes, [(i, i ^ shift) for i in range(peers)])
        for shift in range(1, peers)
    ]


def body(
    adjoint_start,
    adjoint_rhs,
    off_blocks,
    diag_inverse,
    neighbours,
    node_weights,
    sens_blocks,
    cell_points,
    base_points,
    ffd_index,
    ffd_weight,
):
    nodes, _, cells = adjoint_start.shape
    faces = off_blocks.shape[1]
    blocks = cells // LANES
    per = blocks * nodes
    slots = ffd_index.shape[1]
    owned = base_points.shape[1] // lax.axis_size("nodes")
    peers = lax.axis_size(CELL_AXES)
    cores = lax.axis_size("sub")
    node_peers = lax.axis_size("nodes")
    f32, i32, bf16 = jnp.float32, jnp.int32, jnp.bfloat16

    def shape(dims, dtype=f32):
        return jax.ShapeDtypeStruct(dims, dtype)

    def cost(flops, moved):
        return pl.CostEstimate(flops=flops, bytes_accessed=moved, transcendentals=0)

    def swaps(array):
        close = lax.ppermute(array, CELL_AXES, [(i, i ^ 1) for i in range(peers)])
        pairs = []
        for i in range(peers):
            line, core = divmod(i, cores)
            for node in range(node_peers):
                j, beside = (i + 1 if i % 2 else i - 1), node
                if not 0 <= j < peers:
                    j, beside = i, (node ^ 1 if node_peers % 2 == 0 else node)
                to_line, to_core = divmod(j, cores)
                pairs.append(
                    (
                        (line * node_peers + node) * cores + core,
                        (to_line * node_peers + beside) * cores + to_core,
                    )
                )
        return lax.ppermute(array, SUM_AXES, pairs), close

    adjoint = rows_of(adjoint_start)
    far, close = swaps(adjoint)
    prepared = pl.pallas_call(
        functools.partial(prepare_kernel, nodes),
        out_shape=(
            shape((faces * 25 * per, LANES)),
            shape((25 * per, LANES)),
            shape((5 * per, LANES)),
            shape((15 * per, LANES)),
            shape((faces * per, LANES), i32),
            shape((faces * per, LANES), i32),
            shape((slots * 16, owned)),
            shape((slots, owned)),
            shape((slots // 2 * owned, LANES), bf16),
            shape((5 * per, LANES)),
            shape((cells, FACTOR_ROWS), bf16),
            shape((FACTOR_ROWS, owned), bf16),
        ),
        in_specs=[HBM] * 11,
        out_specs=(VMEM,) * 12,
        scratch_shapes=[
            pltpu.VMEM((faces * 25 * per, LANES), bf16),
            pltpu.VMEM((15 * per, LANES), bf16),
            pltpu.VMEM((faces, cells), i32),
            pltpu.SMEM((nodes,), f32),
            pltpu.VMEM((slots, owned), i32),
            pltpu.VMEM((slots, owned), f32),
            pltpu.VMEM((3, cells), f32),
            pltpu.VMEM((3, owned), f32),
            pltpu.SemaphoreType.DMA((11,)),
        ],
        compiler_params=PARAMS,
        cost_estimate=cost(10**9, 10**7),
        name="prepare",
    )(
        *in_hbm(
            rows_of(off_blocks.reshape(nodes, faces * 25, cells)),
            rows_of(diag_inverse),
            rows_of(adjoint_rhs),
            rows_of(sens_blocks),
            neighbours,
            node_weights,
            ffd_index.T,
            ffd_weight.T,
            adjoint,
            cell_points,
            base_points,
        )
    )
    off, inverse, rhs, sens, lane, step, spread, low, near_hot, adjoint, left, right = prepared
    scratch = [
        pltpu.VMEM((3 * 5 * per, LANES), f32),
        pltpu.VMEM((8 // nodes * 3 * 5 * per, LANES), f32),
    ]
    sweep_cost = cost(2 * 10 * 35 * cells, 4 * faces * 25 * per * LANES)

    for _ in range(SWEEPS - 1):
        adjoint = pl.pallas_call(
            functools.partial(sweep_kernel, blocks),
            out_shape=shape((5 * per, LANES)),
            in_specs=[VMEM] * 8,
            out_specs=VMEM,
            scratch_shapes=scratch,
            compiler_params=PARAMS,
            cost_estimate=sweep_cost,
            name="sweep",
        )(close, far, adjoint, rhs, off, inverse, lane, step)
        far, close = swaps(adjoint)

    half = cells * 5 // 8 // LANES * LANES
    wendland_cost = cost(10**9, 10**7)
    near_shape = shape((2 * half, owned), bf16)
    far_shape = shape((2 * (cells - half), owned), bf16)
    near_kernel = pl.pallas_call(
        functools.partial(wendland_kernel, 0),
        out_shape=near_shape,
        in_specs=[VMEM] * 3,
        out_specs=VMEM,
        compiler_params=PARAMS,
        cost_estimate=wendland_cost,
        name="near_wendland",
    )(left, right, adjoint)
    adjoint, part_sens = pl.pallas_call(
        functools.partial(last_sweep_kernel, blocks),
        out_shape=(shape((5 * per, LANES)), shape((3 * blocks, LANES))),
        in_specs=[VMEM] * 9 + [pl.BlockSpec(memory_space=pl.ANY)],
        out_specs=(VMEM, VMEM),
        scratch_shapes=scratch + [pltpu.VMEM((3 * per, LANES), f32)],
        compiler_params=PARAMS,
        cost_estimate=sweep_cost,
        name="last_sweep",
    )(close, far, adjoint, rhs, off, inverse, lane, step, sens, near_kernel)

    all_sens = [part_sens]
    for shift in range(1, node_peers):
        ring = [(i, (i + shift) % node_peers) for i in range(node_peers)]
        all_sens.append(lax.ppermute(part_sens, "nodes", ring))
    hot_shape = shape(((slots - slots // 2) * owned, LANES), bf16)
    far_kernel, far_hot, adjoint = pl.pallas_call(
        functools.partial(far_wendland_kernel, half),
        out_shape=(far_shape, hot_shape, shape((5 * per, LANES))),
        in_specs=[VMEM] * 5,
        out_specs=(VMEM, VMEM, HBM),
        scratch_shapes=[pltpu.SemaphoreType.DMA],
        compiler_params=PARAMS,
        cost_estimate=wendland_cost,
        name="far_wendland",
    )(left, right, part_sens, adjoint, low)
    scale = 4.0 / math.sqrt(cells * peers)
    rows = 3 * FFD // LANES
    partial = pl.pallas_call(
        functools.partial(control_kernel, scale),
        out_shape=shape((rows, LANES)),
        in_specs=[VMEM] * (len(all_sens) + 5),
        out_specs=VMEM,
        compiler_params=PARAMS,
        name="control",
    )(*all_sens, near_kernel, far_kernel, spread, near_hot, far_hot)
    partial = pl.pallas_call(
        add_kernel, out_shape=shape((rows, LANES)), name="add", compiler_params=PARAMS
    )(*exchanged(partial, ("nodes", "sub")))
    control_grad = pl.pallas_call(
        finish_kernel, out_shape=shape((3, FFD)), name="finish", compiler_params=PARAMS
    )(*exchanged(partial, "cells"))
    return (from_rows(adjoint, nodes, cells), control_grad)


def solution(mesh):
    return jax.shard_map(
        body,
        mesh=mesh,
        in_specs=(
            P("nodes", None, ("groups", "cells", "sub")),
            P("nodes", None, ("groups", "cells", "sub")),
            P("nodes", None, None, ("groups", "cells", "sub")),
            P("nodes", None, ("groups", "cells", "sub")),
            P(None, ("cells", "sub")),
            P("nodes"),
            P("nodes", None, ("groups", "cells", "sub")),
            P(None, ("cells", "sub")),
            P(),
            P(),
            P(),
        ),
        out_specs=(P("nodes", None, ("groups", "cells", "sub")), P("groups", None)),
        check_vma=False,
    )
```

```python
import functools
import math

import jax
import jax.numpy as jnp
from jax import lax
from jax.experimental import pallas as pl
from jax.experimental.pallas import tpu as pltpu
from jax.sharding import PartitionSpec as P

SWEEPS = 2
FFD = 512
SUPPORT_RADIUS = 0.3
LANES = 128
CELL_AXES = ("cells", "sub")
SUM_AXES = ("cells", "nodes", "sub")
FACTOR_ROWS = 64
PARAMS = pltpu.CompilerParams(vmem_limit_bytes=24 * 1024 * 1024)
VMEM = pl.BlockSpec(memory_space=pltpu.VMEM)
HBM = pl.BlockSpec(memory_space=pltpu.HBM)


def rows_of(array):
    nodes, rows, cells = array.shape
    blocks = cells // LANES
    split = array.reshape(nodes, rows, blocks, LANES)
    return split.transpose(1, 2, 0, 3).reshape(rows * blocks * nodes, LANES)


def from_rows(array, nodes, cells):
    blocks = cells // LANES
    split = array.reshape(-1, blocks, nodes, LANES)
    return split.transpose(2, 0, 1, 3).reshape(nodes, -1, cells)


def in_hbm(*arrays):
    return [pltpu.with_memory_space_constraint(array, pltpu.HBM) for array in arrays]


def write_one_hot(low_ref, one_hot_ref, first_slot):
    owned = low_ref.shape[1]
    piece = min(512, owned)
    lane = lax.broadcasted_iota(jnp.int32, (piece, LANES), 1).astype(jnp.float32)
    lane = lane.astype(jnp.bfloat16)
    for first in range(0, owned, piece):
        low = low_ref[:, first : first + piece].T.astype(jnp.bfloat16)
        for j in range(one_hot_ref.shape[0] // owned):
            column = low[:, first_slot + j : first_slot + j + 1]
            hit = jnp.broadcast_to(column, (piece, LANES)) == lane
            one_hot_ref[j * owned + first : j * owned + first + piece, :] = jnp.where(
                hit, jnp.bfloat16(1.0), jnp.bfloat16(0.0)
            )


def prepare_kernel(
    nodes,
    off_in,
    inverse_in,
    rhs_in,
    sens_in,
    neigh_in,
    weight_in,
    index_in,
    spread_in,
    start_in,
    cell_in,
    base_in,
    off_ref,
    inverse_ref,
    rhs_ref,
    sens_ref,
    lane_ref,
    step_ref,
    spread_ref,
    low_ref,
    one_hot_ref,
    start_ref,
    left_ref,
    right_ref,
    off_buf,
    sens_buf,
    neigh_buf,
    weight_buf,
    index_buf,
    spread_buf,
    cell_buf,
    base_buf,
    sems,
):
    slots, owned = index_buf.shape
    start = pl.multiple_of(lax.axis_index("nodes") * owned, LANES)
    mine = pl.ds(start, owned)
    pairs = (
        (neigh_in, neigh_buf),
        (index_in.at[:, mine], index_buf),
        (spread_in.at[:, mine], spread_buf),
        (cell_in, cell_buf),
        (base_in.at[:, mine], base_buf),
        (off_in, off_buf),
        (weight_in, weight_buf),
        (sens_in, sens_buf),
        (inverse_in, inverse_ref),
        (rhs_in, rhs_ref),
        (start_in, start_ref),
    )
    copies = [pltpu.make_async_copy(a, b, sems.at[i]) for i, (a, b) in enumerate(pairs)]
    for copy in copies:
        copy.start()

    faces, cells = neigh_buf.shape
    blocks = cells // LANES
    per = blocks * nodes
    first_cell = lax.axis_index(CELL_AXES) * cells
    copies[0].wait()
    for block in range(blocks):
        index = neigh_buf[:, block * LANES : (block + 1) * LANES]
        local = index - first_cell + cells
        lane = jnp.bitwise_and(local, LANES - 1)
        step = jnp.right_shift(local, 7) - block
        step = jnp.where(index >= 0, step, -1)
        for node in range(nodes):
            rows = pl.ds(block * nodes + node, faces, stride=per)
            lane_ref[rows, :] = lane
            step_ref[rows, :] = step

    copies[1].wait()
    copies[2].wait()
    groups = FFD // LANES
    piece = min(512, owned)
    for first in range(0, owned, piece):
        here = slice(first, first + piece)
        high = jnp.right_shift(index_buf[:, here], 7)
        part = lax.broadcasted_iota(jnp.int32, (16, piece), 0)
        part = jnp.where(part < 3 * groups, lax.rem(part, groups), -1)
        for j in range(slots):
            spread_ref[j * 16 : (j + 1) * 16, here] = jnp.where(
                high[j : j + 1] == part, spread_buf[j : j + 1, here], 0.0
            )

    low_ref[...] = jnp.bitwise_and(index_buf[...], LANES - 1).astype(jnp.float32)
    write_one_hot(low_ref, one_hot_ref, 0)

    copies[3].wait()
    left_ref[...] = distance_factors(cell_buf[...], True).T.astype(jnp.bfloat16)
    copies[4].wait()
    right_ref[...] = distance_factors(base_buf[...], False).astype(jnp.bfloat16)

    copies[5].wait()
    off_ref[...] = off_buf[...].astype(jnp.float32)
    copies[6].wait()
    copies[7].wait()
    row_node = lax.rem(lax.broadcasted_iota(jnp.int32, (per, LANES), 0), nodes)
    weights = jnp.zeros((per, LANES), jnp.float32)
    for node in range(nodes):
        weights = jnp.where(row_node == node, weight_buf[node], weights)
    for row in range(0, sens_buf.shape[0], per):
        here = slice(row, row + per)
        sens_ref[here, :] = sens_buf[here, :].astype(jnp.float32) * weights
    for copy in copies[8:]:
        copy.wait()


def sweep_into(
    blocks, first_ref, second_ref, own_ref, rhs_ref, off_ref, inverse_ref, lane_ref, step_ref,
    out_ref, window_ref, table_ref,
):
    per = rhs_ref.shape[0] // 5
    nodes = per // blocks
    faces = lane_ref.shape[0] // per
    odd = lax.rem(lax.axis_index(CELL_AXES), 2)
    place = pl.multiple_of((1 - odd) * 2 * per, 8)
    other = pl.multiple_of(odd * 2 * per, 8)
    width = 3 * per
    for b in range(5):
        rows = slice(b * per, (b + 1) * per)
        base = b * width
        window_ref[pl.ds(base + place, per), :] = first_ref[rows, :]
        window_ref[base + per : base + 2 * per, :] = own_ref[rows, :]
        window_ref[pl.ds(base + other, per), :] = second_ref[rows, :]
    for shift in range(1, 8 // nodes):
        for b in range(5):
            for tile in range(0, width - 8, 8):
                to = ((shift - 1) * 5 + b) * width + tile
                table_ref[to : to + 8, :] = window_ref[
                    pl.ds(b * width + tile + shift * nodes, 8), :
                ]
    for half in range(0, per, 8):
        remaining = [rhs_ref[a * per + half : a * per + half + 8, :] for a in range(5)]
        for f in range(faces):
            lanes = lane_ref[f * per + half : f * per + half + 8, :]
            dist = step_ref[f * per + half : f * per + half + 8, :]
            beside = [jnp.zeros((8, LANES), jnp.float32)] * 5
            for d in range(2 * blocks + 1):
                here = dist == d
                first = half + d * nodes
                for b in range(5):
                    shift, at = first % 8 // nodes, b * width + first // 8 * 8
                    if shift:
                        at = at + (shift - 1) * 5 * width
                        table = table_ref[at : at + 8, :]
                    else:
                        table = window_ref[at : at + 8, :]
                    got = jnp.take_along_axis(
                        table, lanes, axis=1, mode="promise_in_bounds"
                    )
                    beside[b] = jnp.where(here, got, beside[b])
            for a in range(5):
                for b in range(5):
                    row = (f * 25 + 5 * a + b) * per + half
                    remaining[a] = remaining[a] - off_ref[row : row + 8, :] * beside[b]
        for a in range(5):
            total = None
            for b in range(5):
                row = (5 * a + b) * per + half
                term = inverse_ref[row : row + 8, :] * remaining[b]
                total = term if total is None else total + term
            out_ref[a * per + half : a * per + half + 8, :] = total


def sweep_kernel(blocks, *refs):
    sweep_into(blocks, *refs)


def last_sweep_kernel(blocks, *refs):
    ins, rest = refs[:8], refs[8:]
    sens_ref, _, out_ref, sens_out_ref, window_ref, table_ref, part_ref = rest
    sweep_into(blocks, *ins, out_ref, window_ref, table_ref)
    per = out_ref.shape[0] // 5
    nodes = per // blocks
    for k in range(3):
        total = None
        for a in range(5):
            row = (3 * a + k) * per
            term = out_ref[a * per : (a + 1) * per, :] * sens_ref[row : row + per, :]
            total = term if total is None else total + term
        part_ref[k * per : (k + 1) * per, :] = total
    for block in range(blocks):
        total = None
        for node in range(nodes):
            term = part_ref[pl.ds(block * nodes + node, 3, stride=per), :]
            total = term if total is None else total + term
        sens_out_ref[pl.ds(block, 3, stride=blocks), :] = total


def pieces(value, count):
    found = []
    for _ in range(count):
        piece = value.astype(jnp.bfloat16).astype(jnp.float32)
        found.append(piece)
        value = value - piece
    return found


def distance_factors(points, left):
    count = points.shape[1]
    scaled = (points - 0.5) * (1.0 / SUPPORT_RADIUS)
    scaled = jnp.concatenate([scaled, jnp.zeros((5, count), jnp.float32)], axis=0)
    norm = jnp.sum(scaled * scaled, axis=0, keepdims=True)
    norms = pieces(jnp.broadcast_to(norm, (8, count)), 3)
    row = lax.broadcasted_iota(jnp.int32, (8, count), 0)
    norm_block = jnp.zeros((8, count), jnp.float32)
    for place in range(3):
        norm_block = jnp.where(row == place, norms[place], norm_block)
    ones_block = jnp.where(row < 3, 1.0, 0.0)
    first, second, third = pieces(scaled, 3)
    if left:
        dims = [first, first, second, second, first, third]
        dims = [-2.0 * part for part in dims]
        blocks = dims + [norm_block, ones_block]
    else:
        dims = [first, second, first, second, third, first]
        blocks = dims + [ones_block, norm_block]
    return jnp.concatenate(blocks, axis=0)


def wendland_kernel(first_cell, left_ref, right_ref, _, kernel_ref):
    cells, owned = kernel_ref.shape[0] // 2, kernel_ref.shape[1]
    tile, wide = min(64, cells), min(256, owned)
    for row in range(0, cells, tile):
        left = left_ref[first_cell + row : first_cell + row + tile, :]
        for lane in range(0, owned, wide):
            here = slice(lane, lane + wide)
            squared = jnp.dot(left, right_ref[:, here], preferred_element_type=jnp.float32)
            squared = jnp.maximum(squared, 1e-30)
            near = jnp.maximum(1.0 - squared * lax.rsqrt(squared), 0.0)
            power = near * near
            kernel = power * power * (1.25 - near)
            first = kernel.astype(jnp.bfloat16)
            rest = (kernel - first.astype(jnp.float32)).astype(jnp.bfloat16)
            kernel_ref[row : row + tile, here] = first
            kernel_ref[cells + row : cells + row + tile, here] = rest


def far_wendland_kernel(
    first_cell, left_ref, right_ref, after, adjoint_ref, low_ref, *rest
):
    kernel_ref, one_hot_ref, result_ref, sem = rest
    copy = pltpu.make_async_copy(adjoint_ref, result_ref, sem)
    copy.start()
    owned = low_ref.shape[1]
    write_one_hot(low_ref, one_hot_ref, low_ref.shape[0] - one_hot_ref.shape[0] // owned)
    wendland_kernel(first_cell, left_ref, right_ref, after, kernel_ref)
    copy.wait()


def control_kernel(scale, *refs):
    *sens_refs, near_ref, far_ref = refs[:-4]
    spread_ref, near_hot, far_hot, out_ref = refs[-4:]
    blocks = sens_refs[0].shape[0] // 3
    half = near_ref.shape[0] // 2
    groups = FFD // LANES
    total = sens_refs[0][...]
    for ref in sens_refs[1:]:
        total = total + ref[...]
    total = total * scale

    def halves(value):
        first = value.astype(jnp.bfloat16)
        rest = (value - first.astype(jnp.float32)).astype(jnp.bfloat16)
        return first, rest

    row = lax.broadcasted_iota(jnp.int32, (8, LANES), 0)
    wide = []
    for block in range(blocks):
        sens = jnp.zeros((8, LANES), jnp.float32)
        for k in range(3):
            sens = jnp.where(row == k, total[k * blocks + block : k * blocks + block + 1], sens)
        first = sens.astype(jnp.bfloat16).astype(jnp.float32)
        wide.append(jnp.concatenate([first, sens - first], axis=0))
    sens = jnp.concatenate(wide, axis=1).astype(jnp.bfloat16)
    grad = None
    for part, ref in ((sens[:, :half], near_ref), (sens[:, half:], far_ref)):
        both = jnp.concatenate([part, part], axis=1)
        term = jnp.dot(both, ref[...], preferred_element_type=jnp.float32)
        grad = term if grad is None else grad + term
    grad = grad[:8] + grad[8:]
    row = lax.broadcasted_iota(jnp.int32, (16, grad.shape[1]), 0)
    wide = jnp.zeros(row.shape, jnp.float32)
    for k in range(3):
        mine = jnp.logical_and(row >= k * groups, row < (k + 1) * groups)
        wide = jnp.where(mine, grad[k : k + 1], wide)
    grad = wide
    owned = grad.shape[1]
    result = None
    places = [
        (ref, first) for ref in (near_hot, far_hot) for first in range(0, ref.shape[0], owned)
    ]
    for j, (ref, first) in enumerate(places):
        term = jnp.dot(
            jnp.concatenate(halves(grad * spread_ref[j * 16 : (j + 1) * 16, :]), axis=0),
            ref[first : first + owned, :],
            preferred_element_type=jnp.float32,
        )
        result = term if result is None else result + term
    result = result[:16] + result[16:]
    out_ref[...] = result[: 3 * groups]


def tree(values):
    while len(values) > 1:
        values = [sum(values[i : i + 2]) for i in range(0, len(values), 2)]
    return values[0]


def add_kernel(*refs):
    refs[-1][...] = tree([ref[...] for ref in refs[:-1]])


def finish_kernel(*refs):
    total, out_ref = tree([ref[...] for ref in refs[:-1]]), refs[-1]
    groups = out_ref.shape[1] // LANES
    for k in range(3):
        for group in range(groups):
            row = k * groups + group
            out_ref[k : k + 1, group * LANES : (group + 1) * LANES] = total[row : row + 1]


def sum_rounds():
    lines, nodes, cores = (lax.axis_size(axis) for axis in SUM_AXES)
    if any(size & (size - 1) for size in (lines, nodes, cores)):
        return None
    near = [cores >> 1 >> i for i in range(cores.bit_length() - 1)]
    node_bits = [cores << i for i in range(nodes.bit_length() - 1)]
    line_bits = [cores * nodes << i for i in range(lines.bit_length() - 1)]
    bits = near + line_bits[:1] + node_bits[:1] + line_bits[1:] + node_bits[1:]
    rounds = []
    for first in range(0, len(bits), 2):
        masks = bits[first : first + 2]
        if len(masks) == 2:
            masks = masks + [masks[0] | masks[1]]
        rounds.append([mask | (cores - 1) for mask in masks] if first else masks)
    return rounds


def exchanged(value, masks):
    peers = lax.axis_size(SUM_AXES)
    return [value] + [
        lax.ppermute(value, SUM_AXES, [(i, i ^ mask) for i in range(peers)]) for mask in masks
    ]


def body(
    adjoint_start,
    adjoint_rhs,
    off_blocks,
    diag_inverse,
    neighbours,
    node_weights,
    sens_blocks,
    cell_points,
    base_points,
    ffd_index,
    ffd_weight,
):
    nodes, _, cells = adjoint_start.shape
    faces = off_blocks.shape[1]
    blocks = cells // LANES
    per = blocks * nodes
    slots = ffd_index.shape[1]
    owned = base_points.shape[1] // lax.axis_size("nodes")
    peers = lax.axis_size(CELL_AXES)
    cores = lax.axis_size("sub")
    node_peers = lax.axis_size("nodes")
    f32, i32, bf16 = jnp.float32, jnp.int32, jnp.bfloat16

    def shape(dims, dtype=f32):
        return jax.ShapeDtypeStruct(dims, dtype)

    def cost(flops, moved):
        return pl.CostEstimate(flops=flops, bytes_accessed=moved, transcendentals=0)

    def swaps(array):
        close = lax.ppermute(array, CELL_AXES, [(i, i ^ 1) for i in range(peers)])
        pairs = []
        for i in range(peers):
            line, core = divmod(i, cores)
            for node in range(node_peers):
                j, beside = (i + 1 if i % 2 else i - 1), node
                if not 0 <= j < peers:
                    j, beside = i, (node ^ 1 if node_peers % 2 == 0 else node)
                to_line, to_core = divmod(j, cores)
                pairs.append(
                    (
                        (line * node_peers + node) * cores + core,
                        (to_line * node_peers + beside) * cores + to_core,
                    )
                )
        return lax.ppermute(array, SUM_AXES, pairs), close

    adjoint = rows_of(adjoint_start)
    far, close = swaps(adjoint)
    prepared = pl.pallas_call(
        functools.partial(prepare_kernel, nodes),
        out_shape=(
            shape((faces * 25 * per, LANES)),
            shape((25 * per, LANES)),
            shape((5 * per, LANES)),
            shape((15 * per, LANES)),
            shape((faces * per, LANES), i32),
            shape((faces * per, LANES), i32),
            shape((slots * 16, owned)),
            shape((slots, owned)),
            shape((slots // 2 * owned, LANES), bf16),
            shape((5 * per, LANES)),
            shape((cells, FACTOR_ROWS), bf16),
            shape((FACTOR_ROWS, owned), bf16),
        ),
        in_specs=[HBM] * 11,
        out_specs=(VMEM,) * 12,
        scratch_shapes=[
            pltpu.VMEM((faces * 25 * per, LANES), bf16),
            pltpu.VMEM((15 * per, LANES), bf16),
            pltpu.VMEM((faces, cells), i32),
            pltpu.SMEM((nodes,), f32),
            pltpu.VMEM((slots, owned), i32),
            pltpu.VMEM((slots, owned), f32),
            pltpu.VMEM((3, cells), f32),
            pltpu.VMEM((3, owned), f32),
            pltpu.SemaphoreType.DMA((11,)),
        ],
        compiler_params=PARAMS,
        cost_estimate=cost(10**9, 10**7),
        name="prepare",
    )(
        *in_hbm(
            rows_of(off_blocks.reshape(nodes, faces * 25, cells)),
            rows_of(diag_inverse),
            rows_of(adjoint_rhs),
            rows_of(sens_blocks),
            neighbours,
            node_weights,
            ffd_index.T,
            ffd_weight.T,
            adjoint,
            cell_points,
            base_points,
        )
    )
    off, inverse, rhs, sens, lane, step, spread, low, near_hot, adjoint, left, right = prepared
    scratch = [
        pltpu.VMEM((3 * 5 * per, LANES), f32),
        pltpu.VMEM((max(8 // nodes - 1, 1) * 3 * 5 * per, LANES), f32),
    ]
    sweep_cost = cost(2 * 10 * 35 * cells, 4 * faces * 25 * per * LANES)

    for _ in range(SWEEPS - 1):
        adjoint = pl.pallas_call(
            functools.partial(sweep_kernel, blocks),
            out_shape=shape((5 * per, LANES)),
            in_specs=[VMEM] * 8,
            out_specs=VMEM,
            scratch_shapes=scratch,
            compiler_params=PARAMS,
            cost_estimate=sweep_cost,
            name="sweep",
        )(close, far, adjoint, rhs, off, inverse, lane, step)
        far, close = swaps(adjoint)

    half = cells * 5 // 8 // LANES * LANES
    wendland_cost = cost(10**9, 10**7)
    near_shape = shape((2 * half, owned), bf16)
    far_shape = shape((2 * (cells - half), owned), bf16)
    near_kernel = pl.pallas_call(
        functools.partial(wendland_kernel, 0),
        out_shape=near_shape,
        in_specs=[VMEM] * 3,
        out_specs=VMEM,
        compiler_params=PARAMS,
        cost_estimate=wendland_cost,
        name="near_wendland",
    )(left, right, adjoint)
    adjoint, part_sens = pl.pallas_call(
        functools.partial(last_sweep_kernel, blocks),
        out_shape=(shape((5 * per, LANES)), shape((3 * blocks, LANES))),
        in_specs=[VMEM] * 9 + [pl.BlockSpec(memory_space=pl.ANY)],
        out_specs=(VMEM, VMEM),
        scratch_shapes=scratch + [pltpu.VMEM((3 * per, LANES), f32)],
        compiler_params=PARAMS,
        cost_estimate=sweep_cost,
        name="last_sweep",
    )(close, far, adjoint, rhs, off, inverse, lane, step, sens, near_kernel)

    all_sens = [part_sens]
    for shift in range(1, node_peers):
        ring = [(i, (i + shift) % node_peers) for i in range(node_peers)]
        all_sens.append(lax.ppermute(part_sens, "nodes", ring))
    hot_shape = shape(((slots - slots // 2) * owned, LANES), bf16)
    far_kernel, far_hot, adjoint = pl.pallas_call(
        functools.partial(far_wendland_kernel, half),
        out_shape=(far_shape, hot_shape, shape((5 * per, LANES))),
        in_specs=[VMEM] * 5,
        out_specs=(VMEM, VMEM, HBM),
        scratch_shapes=[pltpu.SemaphoreType.DMA],
        compiler_params=PARAMS,
        cost_estimate=wendland_cost,
        name="far_wendland",
    )(left, right, part_sens, adjoint, low)
    scale = 4.0 / math.sqrt(cells * peers)
    rows = 3 * FFD // LANES
    partial = pl.pallas_call(
        functools.partial(control_kernel, scale),
        out_shape=shape((rows, LANES)),
        in_specs=[VMEM] * (len(all_sens) + 5),
        out_specs=VMEM,
        compiler_params=PARAMS,
        name="control",
    )(*all_sens, near_kernel, far_kernel, spread, near_hot, far_hot)
    rounds = sum_rounds()
    terms = [partial] if rounds else [lax.psum(partial, SUM_AXES)]
    for masks in rounds or ():
        if len(terms) > 1:
            partial = pl.pallas_call(
                add_kernel, out_shape=shape((rows, LANES)), name="add", compiler_params=PARAMS
            )(*terms)
        terms = exchanged(partial, masks)
    control_grad = pl.pallas_call(
        finish_kernel, out_shape=shape((3, FFD)), name="finish", compiler_params=PARAMS
    )(*terms)
    return (from_rows(adjoint, nodes, cells), control_grad)


def solution(mesh):
    return jax.shard_map(
        body,
        mesh=mesh,
        in_specs=(
            P("nodes", None, ("groups", "cells", "sub")),
            P("nodes", None, ("groups", "cells", "sub")),
            P("nodes", None, None, ("groups", "cells", "sub")),
            P("nodes", None, ("groups", "cells", "sub")),
            P(None, ("cells", "sub")),
            P("nodes"),
            P("nodes", None, ("groups", "cells", "sub")),
            P(None, ("cells", "sub")),
            P(),
            P(),
            P(),
        ),
        out_specs=(P("nodes", None, ("groups", "cells", "sub")), P("groups", None)),
        check_vma=False,
    )
```

```python
import functools
import math

import jax
import jax.numpy as jnp
from jax import lax
from jax.experimental import pallas as pl
from jax.experimental.pallas import tpu as pltpu
from jax.sharding import PartitionSpec as P

SWEEPS = 2
FFD = 512
SUPPORT_RADIUS = 0.3
LANES = 128
CELL_AXES = ("cells", "sub")
SUM_AXES = ("cells", "nodes", "sub")
FACTOR_ROWS = 64
PARAMS = pltpu.CompilerParams(vmem_limit_bytes=24 * 1024 * 1024)
VMEM = pl.BlockSpec(memory_space=pltpu.VMEM)
HBM = pl.BlockSpec(memory_space=pltpu.HBM)


def rows_of(array):
    nodes, rows, cells = array.shape
    blocks = cells // LANES
    split = array.reshape(nodes, rows, blocks, LANES)
    return split.transpose(1, 2, 0, 3).reshape(rows * blocks * nodes, LANES)


def from_rows(array, nodes, cells):
    blocks = cells // LANES
    split = array.reshape(-1, blocks, nodes, LANES)
    return split.transpose(2, 0, 1, 3).reshape(nodes, -1, cells)


def in_hbm(*arrays):
    return [pltpu.with_memory_space_constraint(array, pltpu.HBM) for array in arrays]


def write_one_hot(low_ref, one_hot_ref, first_slot):
    owned = low_ref.shape[1]
    piece = min(512, owned)
    lane = lax.broadcasted_iota(jnp.int32, (piece, LANES), 1).astype(jnp.float32)
    lane = lane.astype(jnp.bfloat16)
    for first in range(0, owned, piece):
        low = low_ref[:, first : first + piece].T.astype(jnp.bfloat16)
        for j in range(one_hot_ref.shape[0] // owned):
            column = low[:, first_slot + j : first_slot + j + 1]
            hit = jnp.broadcast_to(column, (piece, LANES)) == lane
            one_hot_ref[j * owned + first : j * owned + first + piece, :] = jnp.where(
                hit, jnp.bfloat16(1.0), jnp.bfloat16(0.0)
            )


def prepare_kernel(
    nodes,
    off_in,
    inverse_in,
    rhs_in,
    sens_in,
    neigh_in,
    weight_in,
    index_in,
    spread_in,
    start_in,
    cell_in,
    base_in,
    off_ref,
    inverse_ref,
    rhs_ref,
    sens_ref,
    lane_ref,
    step_ref,
    spread_ref,
    low_ref,
    one_hot_ref,
    start_ref,
    left_ref,
    right_ref,
    off_buf,
    sens_buf,
    neigh_buf,
    weight_buf,
    index_buf,
    spread_buf,
    cell_buf,
    base_buf,
    sems,
):
    slots, owned = index_buf.shape
    start = pl.multiple_of(lax.axis_index("nodes") * owned, LANES)
    mine = pl.ds(start, owned)
    pairs = (
        (neigh_in, neigh_buf),
        (index_in.at[:, mine], index_buf),
        (spread_in.at[:, mine], spread_buf),
        (cell_in, cell_buf),
        (base_in.at[:, mine], base_buf),
        (off_in, off_buf),
        (weight_in, weight_buf),
        (sens_in, sens_buf),
        (inverse_in, inverse_ref),
        (rhs_in, rhs_ref),
        (start_in, start_ref),
    )
    copies = [pltpu.make_async_copy(a, b, sems.at[i]) for i, (a, b) in enumerate(pairs)]
    for copy in copies:
        copy.start()

    faces, cells = neigh_buf.shape
    blocks = cells // LANES
    per = blocks * nodes
    first_cell = lax.axis_index(CELL_AXES) * cells
    copies[0].wait()
    for block in range(blocks):
        index = neigh_buf[:, block * LANES : (block + 1) * LANES]
        local = index - first_cell + cells
        lane = jnp.bitwise_and(local, LANES - 1)
        step = jnp.right_shift(local, 7) - block
        step = jnp.where(index >= 0, step, -1)
        for node in range(nodes):
            rows = pl.ds(block * nodes + node, faces, stride=per)
            lane_ref[rows, :] = lane
            step_ref[rows, :] = step

    copies[1].wait()
    copies[2].wait()
    groups = FFD // LANES
    piece = min(512, owned)
    for first in range(0, owned, piece):
        here = slice(first, first + piece)
        high = jnp.right_shift(index_buf[:, here], 7)
        part = lax.broadcasted_iota(jnp.int32, (16, piece), 0)
        part = jnp.where(part < 3 * groups, lax.rem(part, groups), -1)
        for j in range(slots):
            spread_ref[j * 16 : (j + 1) * 16, here] = jnp.where(
                high[j : j + 1] == part, spread_buf[j : j + 1, here], 0.0
            )

    low_ref[...] = jnp.bitwise_and(index_buf[...], LANES - 1).astype(jnp.float32)
    write_one_hot(low_ref, one_hot_ref, 0)

    copies[3].wait()
    left_ref[...] = distance_factors(cell_buf[...], True).T.astype(jnp.bfloat16)
    copies[4].wait()
    right_ref[...] = distance_factors(base_buf[...], False).astype(jnp.bfloat16)

    copies[5].wait()
    off_ref[...] = off_buf[...].astype(jnp.float32)
    copies[6].wait()
    copies[7].wait()
    row_node = lax.rem(lax.broadcasted_iota(jnp.int32, (per, LANES), 0), nodes)
    weights = jnp.zeros((per, LANES), jnp.float32)
    for node in range(nodes):
        weights = jnp.where(row_node == node, weight_buf[node], weights)
    for row in range(0, sens_buf.shape[0], per):
        here = slice(row, row + per)
        sens_ref[here, :] = sens_buf[here, :].astype(jnp.float32) * weights
    for copy in copies[8:]:
        copy.wait()


def take_lanes(table, lanes):
    numbers = lax.GatherDimensionNumbers(
        offset_dims=(),
        collapsed_slice_dims=(1,),
        start_index_map=(1,),
        operand_batching_dims=(0,),
        start_indices_batching_dims=(0,),
    )
    return lax.gather(
        table,
        lanes[..., None],
        numbers,
        slice_sizes=(1, 1),
        mode=lax.GatherScatterMode.PROMISE_IN_BOUNDS,
    )


def sweep_into(
    blocks, first_ref, second_ref, own_ref, rhs_ref, off_ref, inverse_ref, lane_ref, step_ref,
    out_ref, window_ref, table_ref,
):
    per = rhs_ref.shape[0] // 5
    nodes = per // blocks
    faces = lane_ref.shape[0] // per
    odd = lax.rem(lax.axis_index(CELL_AXES), 2)
    place = pl.multiple_of((1 - odd) * 2 * per, 8)
    other = pl.multiple_of(odd * 2 * per, 8)
    width = 3 * per
    for b in range(5):
        rows = slice(b * per, (b + 1) * per)
        base = b * width
        window_ref[pl.ds(base + place, per), :] = first_ref[rows, :]
        window_ref[base + per : base + 2 * per, :] = own_ref[rows, :]
        window_ref[pl.ds(base + other, per), :] = second_ref[rows, :]
    for shift in range(1, 8 // nodes):
        for b in range(5):
            for tile in range(0, width - 8, 8):
                to = ((shift - 1) * 5 + b) * width + tile
                table_ref[to : to + 8, :] = window_ref[
                    pl.ds(b * width + tile + shift * nodes, 8), :
                ]
    for half in range(0, per, 8):
        remaining = [rhs_ref[a * per + half : a * per + half + 8, :] for a in range(5)]
        for f in range(faces):
            lanes = lane_ref[f * per + half : f * per + half + 8, :]
            dist = step_ref[f * per + half : f * per + half + 8, :]
            beside = [jnp.zeros((8, LANES), jnp.float32)] * 5
            for d in range(2 * blocks + 1):
                here = dist == d
                first = half + d * nodes
                for b in range(5):
                    shift, at = first % 8 // nodes, b * width + first // 8 * 8
                    if shift:
                        at = at + (shift - 1) * 5 * width
                        table = table_ref[at : at + 8, :]
                    else:
                        table = window_ref[at : at + 8, :]
                    beside[b] = jnp.where(here, take_lanes(table, lanes), beside[b])
            for a in range(5):
                for b in range(5):
                    row = (f * 25 + 5 * a + b) * per + half
                    remaining[a] = remaining[a] - off_ref[row : row + 8, :] * beside[b]
        for a in range(5):
            total = None
            for b in range(5):
                row = (5 * a + b) * per + half
                term = inverse_ref[row : row + 8, :] * remaining[b]
                total = term if total is None else total + term
            out_ref[a * per + half : a * per + half + 8, :] = total


def sweep_kernel(blocks, *refs):
    sweep_into(blocks, *refs)


def last_sweep_kernel(blocks, *refs):
    ins, rest = refs[:8], refs[8:]
    sens_ref, _, out_ref, sens_out_ref, window_ref, table_ref, part_ref = rest
    sweep_into(blocks, *ins, out_ref, window_ref, table_ref)
    per = out_ref.shape[0] // 5
    nodes = per // blocks
    for k in range(3):
        total = None
        for a in range(5):
            row = (3 * a + k) * per
            term = out_ref[a * per : (a + 1) * per, :] * sens_ref[row : row + per, :]
            total = term if total is None else total + term
        part_ref[k * per : (k + 1) * per, :] = total
    for block in range(blocks):
        total = None
        for node in range(nodes):
            term = part_ref[pl.ds(block * nodes + node, 3, stride=per), :]
            total = term if total is None else total + term
        sens_out_ref[pl.ds(block, 3, stride=blocks), :] = total


def pieces(value, count):
    found = []
    for _ in range(count):
        piece = value.astype(jnp.bfloat16).astype(jnp.float32)
        found.append(piece)
        value = value - piece
    return found


def distance_factors(points, left):
    count = points.shape[1]
    scaled = (points - 0.5) * (1.0 / SUPPORT_RADIUS)
    scaled = jnp.concatenate([scaled, jnp.zeros((5, count), jnp.float32)], axis=0)
    norm = jnp.sum(scaled * scaled, axis=0, keepdims=True)
    norms = pieces(jnp.broadcast_to(norm, (8, count)), 3)
    row = lax.broadcasted_iota(jnp.int32, (8, count), 0)
    norm_block = jnp.zeros((8, count), jnp.float32)
    for place in range(3):
        norm_block = jnp.where(row == place, norms[place], norm_block)
    ones_block = jnp.where(row < 3, 1.0, 0.0)
    first, second, third = pieces(scaled, 3)
    if left:
        dims = [first, first, second, second, first, third]
        dims = [-2.0 * part for part in dims]
        blocks = dims + [norm_block, ones_block]
    else:
        dims = [first, second, first, second, third, first]
        blocks = dims + [ones_block, norm_block]
    return jnp.concatenate(blocks, axis=0)


def wendland_kernel(first_cell, left_ref, right_ref, _, kernel_ref):
    cells, owned = kernel_ref.shape[0] // 2, kernel_ref.shape[1]
    tile, wide = min(128, cells), min(256, owned)
    for row in range(0, cells, tile):
        left = left_ref[first_cell + row : first_cell + row + tile, :]
        for lane in range(0, owned, wide):
            here = slice(lane, lane + wide)
            squared = jnp.dot(left, right_ref[:, here], preferred_element_type=jnp.float32)
            squared = jnp.maximum(squared, 1e-30)
            near = jnp.maximum(1.0 - squared * lax.rsqrt(squared), 0.0)
            power = near * near
            kernel = power * power * (1.25 - near)
            first = kernel.astype(jnp.bfloat16)
            rest = (kernel - first.astype(jnp.float32)).astype(jnp.bfloat16)
            kernel_ref[row : row + tile, here] = first
            kernel_ref[cells + row : cells + row + tile, here] = rest


def far_wendland_kernel(
    first_cell, left_ref, right_ref, after, adjoint_ref, low_ref, *rest
):
    kernel_ref, one_hot_ref, result_ref, sem = rest
    copy = pltpu.make_async_copy(adjoint_ref, result_ref, sem)
    copy.start()
    owned = low_ref.shape[1]
    write_one_hot(low_ref, one_hot_ref, low_ref.shape[0] - one_hot_ref.shape[0] // owned)
    wendland_kernel(first_cell, left_ref, right_ref, after, kernel_ref)
    copy.wait()


def control_kernel(scale, *refs):
    *sens_refs, near_ref, far_ref = refs[:-4]
    spread_ref, near_hot, far_hot, out_ref = refs[-4:]
    blocks = sens_refs[0].shape[0] // 3
    half = near_ref.shape[0] // 2
    groups = FFD // LANES
    total = sens_refs[0][...]
    for ref in sens_refs[1:]:
        total = total + ref[...]
    total = total * scale

    def halves(value):
        first = value.astype(jnp.bfloat16)
        rest = (value - first.astype(jnp.float32)).astype(jnp.bfloat16)
        return first, rest

    row = lax.broadcasted_iota(jnp.int32, (8, LANES), 0)
    wide = []
    for block in range(blocks):
        sens = jnp.zeros((8, LANES), jnp.float32)
        for k in range(3):
            sens = jnp.where(row == k, total[k * blocks + block : k * blocks + block + 1], sens)
        first = sens.astype(jnp.bfloat16).astype(jnp.float32)
        wide.append(jnp.concatenate([first, sens - first], axis=0))
    sens = jnp.concatenate(wide, axis=1).astype(jnp.bfloat16)
    grad = None
    for part, ref in ((sens[:, :half], near_ref), (sens[:, half:], far_ref)):
        both = jnp.concatenate([part, part], axis=1)
        term = jnp.dot(both, ref[...], preferred_element_type=jnp.float32)
        grad = term if grad is None else grad + term
    grad = grad[:8] + grad[8:]
    row = lax.broadcasted_iota(jnp.int32, (16, grad.shape[1]), 0)
    wide = jnp.zeros(row.shape, jnp.float32)
    for k in range(3):
        mine = jnp.logical_and(row >= k * groups, row < (k + 1) * groups)
        wide = jnp.where(mine, grad[k : k + 1], wide)
    grad = wide
    owned = grad.shape[1]
    result = None
    places = [
        (ref, first) for ref in (near_hot, far_hot) for first in range(0, ref.shape[0], owned)
    ]
    for j, (ref, first) in enumerate(places):
        term = jnp.dot(
            jnp.concatenate(halves(grad * spread_ref[j * 16 : (j + 1) * 16, :]), axis=0),
            ref[first : first + owned, :],
            preferred_element_type=jnp.float32,
        )
        result = term if result is None else result + term
    result = result[:16] + result[16:]
    out_ref[...] = result[: 3 * groups]


def tree(values):
    while len(values) > 1:
        values = [sum(values[i : i + 2]) for i in range(0, len(values), 2)]
    return values[0]


def add_kernel(*refs):
    refs[-1][...] = tree([ref[...] for ref in refs[:-1]])


def finish_kernel(*refs):
    total, out_ref = tree([ref[...] for ref in refs[:-1]]), refs[-1]
    groups = out_ref.shape[1] // LANES
    for k in range(3):
        for group in range(groups):
            row = k * groups + group
            out_ref[k : k + 1, group * LANES : (group + 1) * LANES] = total[row : row + 1]


def sum_rounds():
    lines, nodes, cores = (lax.axis_size(axis) for axis in SUM_AXES)
    if any(size & (size - 1) for size in (lines, nodes, cores)):
        return None
    near = [cores >> 1 >> i for i in range(cores.bit_length() - 1)]
    node_bits = [cores << i for i in range(nodes.bit_length() - 1)]
    line_bits = [cores * nodes << i for i in range(lines.bit_length() - 1)]
    bits = near + line_bits[:1] + node_bits[:1] + line_bits[1:] + node_bits[1:]
    rounds = []
    for first in range(0, len(bits), 2):
        masks = bits[first : first + 2]
        if len(masks) == 2:
            masks = masks + [masks[0] | masks[1]]
        rounds.append([mask | (cores - 1) for mask in masks] if first else masks)
    return rounds


def exchanged(value, masks):
    peers = lax.axis_size(SUM_AXES)
    return [value] + [
        lax.ppermute(value, SUM_AXES, [(i, i ^ mask) for i in range(peers)]) for mask in masks
    ]


def body(
    adjoint_start,
    adjoint_rhs,
    off_blocks,
    diag_inverse,
    neighbours,
    node_weights,
    sens_blocks,
    cell_points,
    base_points,
    ffd_index,
    ffd_weight,
):
    nodes, _, cells = adjoint_start.shape
    faces = off_blocks.shape[1]
    blocks = cells // LANES
    per = blocks * nodes
    slots = ffd_index.shape[1]
    owned = base_points.shape[1] // lax.axis_size("nodes")
    peers = lax.axis_size(CELL_AXES)
    cores = lax.axis_size("sub")
    node_peers = lax.axis_size("nodes")
    f32, i32, bf16 = jnp.float32, jnp.int32, jnp.bfloat16

    def shape(dims, dtype=f32):
        return jax.ShapeDtypeStruct(dims, dtype)

    def cost(flops, moved):
        return pl.CostEstimate(flops=flops, bytes_accessed=moved, transcendentals=0)

    def swaps(array):
        close = lax.ppermute(array, CELL_AXES, [(i, i ^ 1) for i in range(peers)])
        pairs = []
        for i in range(peers):
            line, core = divmod(i, cores)
            for node in range(node_peers):
                j, beside = (i + 1 if i % 2 else i - 1), node
                if not 0 <= j < peers:
                    j, beside = i, (node ^ 1 if node_peers % 2 == 0 else node)
                to_line, to_core = divmod(j, cores)
                pairs.append(
                    (
                        (line * node_peers + node) * cores + core,
                        (to_line * node_peers + beside) * cores + to_core,
                    )
                )
        return lax.ppermute(array, SUM_AXES, pairs), close

    adjoint = rows_of(adjoint_start)
    far, close = swaps(adjoint)
    prepared = pl.pallas_call(
        functools.partial(prepare_kernel, nodes),
        out_shape=(
            shape((faces * 25 * per, LANES)),
            shape((25 * per, LANES)),
            shape((5 * per, LANES)),
            shape((15 * per, LANES)),
            shape((faces * per, LANES), i32),
            shape((faces * per, LANES), i32),
            shape((slots * 16, owned)),
            shape((slots, owned)),
            shape((slots // 2 * owned, LANES), bf16),
            shape((5 * per, LANES)),
            shape((cells, FACTOR_ROWS), bf16),
            shape((FACTOR_ROWS, owned), bf16),
        ),
        in_specs=[HBM] * 11,
        out_specs=(VMEM,) * 12,
        scratch_shapes=[
            pltpu.VMEM((faces * 25 * per, LANES), bf16),
            pltpu.VMEM((15 * per, LANES), bf16),
            pltpu.VMEM((faces, cells), i32),
            pltpu.SMEM((nodes,), f32),
            pltpu.VMEM((slots, owned), i32),
            pltpu.VMEM((slots, owned), f32),
            pltpu.VMEM((3, cells), f32),
            pltpu.VMEM((3, owned), f32),
            pltpu.SemaphoreType.DMA((11,)),
        ],
        compiler_params=PARAMS,
        cost_estimate=cost(10**9, 10**7),
        name="prepare",
    )(
        *in_hbm(
            rows_of(off_blocks.reshape(nodes, faces * 25, cells)),
            rows_of(diag_inverse),
            rows_of(adjoint_rhs),
            rows_of(sens_blocks),
            neighbours,
            node_weights,
            ffd_index.T,
            ffd_weight.T,
            adjoint,
            cell_points,
            base_points,
        )
    )
    off, inverse, rhs, sens, lane, step, spread, low, near_hot, adjoint, left, right = prepared
    scratch = [
        pltpu.VMEM((3 * 5 * per, LANES), f32),
        pltpu.VMEM((max(8 // nodes - 1, 1) * 3 * 5 * per, LANES), f32),
    ]
    sweep_cost = cost(2 * 10 * 35 * cells, 4 * faces * 25 * per * LANES)

    for _ in range(SWEEPS - 1):
        adjoint = pl.pallas_call(
            functools.partial(sweep_kernel, blocks),
            out_shape=shape((5 * per, LANES)),
            in_specs=[VMEM] * 8,
            out_specs=VMEM,
            scratch_shapes=scratch,
            compiler_params=PARAMS,
            cost_estimate=sweep_cost,
            name="sweep",
        )(close, far, adjoint, rhs, off, inverse, lane, step)
        far, close = swaps(adjoint)

    half = cells * 5 // 8 // LANES * LANES
    wendland_cost = cost(10**9, 10**7)
    near_shape = shape((2 * half, owned), bf16)
    far_shape = shape((2 * (cells - half), owned), bf16)
    near_kernel = pl.pallas_call(
        functools.partial(wendland_kernel, 0),
        out_shape=near_shape,
        in_specs=[VMEM] * 3,
        out_specs=VMEM,
        compiler_params=PARAMS,
        cost_estimate=wendland_cost,
        name="near_wendland",
    )(left, right, adjoint)
    adjoint, part_sens = pl.pallas_call(
        functools.partial(last_sweep_kernel, blocks),
        out_shape=(shape((5 * per, LANES)), shape((3 * blocks, LANES))),
        in_specs=[VMEM] * 9 + [pl.BlockSpec(memory_space=pl.ANY)],
        out_specs=(VMEM, VMEM),
        scratch_shapes=scratch + [pltpu.VMEM((3 * per, LANES), f32)],
        compiler_params=PARAMS,
        cost_estimate=sweep_cost,
        name="last_sweep",
    )(close, far, adjoint, rhs, off, inverse, lane, step, sens, near_kernel)

    all_sens = [part_sens]
    for shift in range(1, node_peers):
        ring = [(i, (i + shift) % node_peers) for i in range(node_peers)]
        all_sens.append(lax.ppermute(part_sens, "nodes", ring))
    hot_shape = shape(((slots - slots // 2) * owned, LANES), bf16)
    far_kernel, far_hot, adjoint = pl.pallas_call(
        functools.partial(far_wendland_kernel, half),
        out_shape=(far_shape, hot_shape, shape((5 * per, LANES))),
        in_specs=[VMEM] * 5,
        out_specs=(VMEM, VMEM, HBM),
        scratch_shapes=[pltpu.SemaphoreType.DMA],
        compiler_params=PARAMS,
        cost_estimate=wendland_cost,
        name="far_wendland",
    )(left, right, part_sens, adjoint, low)
    scale = 4.0 / math.sqrt(cells * peers)
    rows = 3 * FFD // LANES
    partial = pl.pallas_call(
        functools.partial(control_kernel, scale),
        out_shape=shape((rows, LANES)),
        in_specs=[VMEM] * (len(all_sens) + 5),
        out_specs=VMEM,
        compiler_params=PARAMS,
        name="control",
    )(*all_sens, near_kernel, far_kernel, spread, near_hot, far_hot)
    rounds = sum_rounds()
    terms = [partial] if rounds else [lax.psum(partial, SUM_AXES)]
    for masks in rounds or ():
        if len(terms) > 1:
            partial = pl.pallas_call(
                add_kernel, out_shape=shape((rows, LANES)), name="add", compiler_params=PARAMS
            )(*terms)
        terms = exchanged(partial, masks)
    control_grad = pl.pallas_call(
        finish_kernel, out_shape=shape((3, FFD)), name="finish", compiler_params=PARAMS
    )(*terms)
    return (from_rows(adjoint, nodes, cells), control_grad)


def solution(mesh):
    return jax.shard_map(
        body,
        mesh=mesh,
        in_specs=(
            P("nodes", None, ("groups", "cells", "sub")),
            P("nodes", None, ("groups", "cells", "sub")),
            P("nodes", None, None, ("groups", "cells", "sub")),
            P("nodes", None, ("groups", "cells", "sub")),
            P(None, ("cells", "sub")),
            P("nodes"),
            P("nodes", None, ("groups", "cells", "sub")),
            P(None, ("cells", "sub")),
            P(),
            P(),
            P(),
        ),
        out_specs=(P("nodes", None, ("groups", "cells", "sub")), P("groups", None)),
        check_vma=False,
    )
```

```python
import functools
import math

import jax
import jax.numpy as jnp
from jax import lax
from jax.experimental import pallas as pl
from jax.experimental.pallas import tpu as pltpu
from jax.sharding import PartitionSpec as P

SWEEPS = 2
FFD = 512
SUPPORT_RADIUS = 0.3
LANES = 128
CELL_AXES = ("cells", "sub")
SUM_AXES = ("cells", "nodes", "sub")
FACTOR_ROWS = 64
PARAMS = pltpu.CompilerParams(vmem_limit_bytes=24 * 1024 * 1024)
VMEM = pl.BlockSpec(memory_space=pltpu.VMEM)
HBM = pl.BlockSpec(memory_space=pltpu.HBM)


def rows_of(array):
    nodes, rows, cells = array.shape
    blocks = cells // LANES
    split = array.reshape(nodes, rows, blocks, LANES)
    return split.transpose(1, 2, 0, 3).reshape(rows * blocks * nodes, LANES)


def from_rows(array, nodes, cells):
    blocks = cells // LANES
    split = array.reshape(-1, blocks, nodes, LANES)
    return split.transpose(2, 0, 1, 3).reshape(nodes, -1, cells)


def in_hbm(*arrays):
    return [pltpu.with_memory_space_constraint(array, pltpu.HBM) for array in arrays]


def write_one_hot(low_ref, one_hot_ref, first_slot):
    owned = low_ref.shape[1]
    piece = min(512, owned)
    lane = lax.broadcasted_iota(jnp.int32, (piece, LANES), 1).astype(jnp.float32)
    lane = lane.astype(jnp.bfloat16)
    for first in range(0, owned, piece):
        low = low_ref[:, first : first + piece].T.astype(jnp.bfloat16)
        for j in range(one_hot_ref.shape[0] // owned):
            column = low[:, first_slot + j : first_slot + j + 1]
            hit = jnp.broadcast_to(column, (piece, LANES)) == lane
            one_hot_ref[j * owned + first : j * owned + first + piece, :] = jnp.where(
                hit, jnp.bfloat16(1.0), jnp.bfloat16(0.0)
            )


def prepare_kernel(
    nodes,
    off_in,
    inverse_in,
    rhs_in,
    sens_in,
    neigh_in,
    weight_in,
    index_in,
    spread_in,
    start_in,
    cell_in,
    base_in,
    off_ref,
    inverse_ref,
    rhs_ref,
    sens_ref,
    lane_ref,
    step_ref,
    spread_ref,
    low_ref,
    one_hot_ref,
    start_ref,
    left_ref,
    right_ref,
    off_buf,
    sens_buf,
    neigh_buf,
    weight_buf,
    index_buf,
    spread_buf,
    cell_buf,
    base_buf,
    sems,
):
    slots, owned = index_buf.shape
    start = pl.multiple_of(lax.axis_index("nodes") * owned, LANES)
    mine = pl.ds(start, owned)
    pairs = (
        (neigh_in, neigh_buf),
        (index_in.at[:, mine], index_buf),
        (spread_in.at[:, mine], spread_buf),
        (cell_in, cell_buf),
        (base_in.at[:, mine], base_buf),
        (off_in, off_buf),
        (weight_in, weight_buf),
        (sens_in, sens_buf),
        (inverse_in, inverse_ref),
        (rhs_in, rhs_ref),
        (start_in, start_ref),
    )
    copies = [pltpu.make_async_copy(a, b, sems.at[i]) for i, (a, b) in enumerate(pairs)]
    for copy in copies:
        copy.start()

    faces, cells = neigh_buf.shape
    blocks = cells // LANES
    per = blocks * nodes
    first_cell = lax.axis_index(CELL_AXES) * cells
    copies[0].wait()
    for block in range(blocks):
        index = neigh_buf[:, block * LANES : (block + 1) * LANES]
        local = index - first_cell + cells
        lane = jnp.bitwise_and(local, LANES - 1)
        step = jnp.right_shift(local, 7) - block
        step = jnp.where(index >= 0, step, -1)
        for node in range(nodes):
            rows = pl.ds(block * nodes + node, faces, stride=per)
            lane_ref[rows, :] = lane
            step_ref[rows, :] = step

    copies[1].wait()
    copies[2].wait()
    groups = FFD // LANES
    piece = min(512, owned)
    for first in range(0, owned, piece):
        here = slice(first, first + piece)
        high = jnp.right_shift(index_buf[:, here], 7)
        part = lax.broadcasted_iota(jnp.int32, (16, piece), 0)
        part = jnp.where(part < 3 * groups, lax.rem(part, groups), -1)
        for j in range(slots):
            spread_ref[j * 16 : (j + 1) * 16, here] = jnp.where(
                high[j : j + 1] == part, spread_buf[j : j + 1, here], 0.0
            )

    low_ref[...] = jnp.bitwise_and(index_buf[...], LANES - 1).astype(jnp.float32)
    write_one_hot(low_ref, one_hot_ref, 0)

    copies[3].wait()
    left_ref[...] = distance_factors(cell_buf[...], True).T.astype(jnp.bfloat16)
    copies[4].wait()
    right_ref[...] = distance_factors(base_buf[...], False).astype(jnp.bfloat16)

    copies[5].wait()
    off_ref[...] = off_buf[...].astype(jnp.float32)
    copies[6].wait()
    copies[7].wait()
    row_node = lax.rem(lax.broadcasted_iota(jnp.int32, (per, LANES), 0), nodes)
    weights = jnp.zeros((per, LANES), jnp.float32)
    for node in range(nodes):
        weights = jnp.where(row_node == node, weight_buf[node], weights)
    for row in range(0, sens_buf.shape[0], per):
        here = slice(row, row + per)
        sens_ref[here, :] = sens_buf[here, :].astype(jnp.float32) * weights
    for copy in copies[8:]:
        copy.wait()


def take_lanes(table, lanes):
    numbers = lax.GatherDimensionNumbers(
        offset_dims=(),
        collapsed_slice_dims=(1,),
        start_index_map=(1,),
        operand_batching_dims=(0,),
        start_indices_batching_dims=(0,),
    )
    return lax.gather(
        table,
        lanes[..., None],
        numbers,
        slice_sizes=(1, 1),
        mode=lax.GatherScatterMode.PROMISE_IN_BOUNDS,
    )


def sweep_into(
    blocks, first_ref, second_ref, own_ref, rhs_ref, off_ref, inverse_ref, lane_ref, step_ref,
    out_ref, window_ref, table_ref,
):
    per = rhs_ref.shape[0] // 5
    nodes = per // blocks
    faces = lane_ref.shape[0] // per
    odd = lax.rem(lax.axis_index(CELL_AXES), 2)
    place = pl.multiple_of((1 - odd) * 2 * per, 8)
    other = pl.multiple_of(odd * 2 * per, 8)
    width = 3 * per
    for b in range(5):
        rows = slice(b * per, (b + 1) * per)
        base = b * width
        window_ref[pl.ds(base + place, per), :] = first_ref[rows, :]
        window_ref[base + per : base + 2 * per, :] = own_ref[rows, :]
        window_ref[pl.ds(base + other, per), :] = second_ref[rows, :]
    for shift in range(1, 8 // nodes):
        for b in range(5):
            for tile in range(0, width - 8, 8):
                to = ((shift - 1) * 5 + b) * width + tile
                table_ref[to : to + 8, :] = window_ref[
                    pl.ds(b * width + tile + shift * nodes, 8), :
                ]
    for half in range(0, per, 8):
        remaining = [rhs_ref[a * per + half : a * per + half + 8, :] for a in range(5)]
        for f in range(faces):
            lanes = lane_ref[f * per + half : f * per + half + 8, :]
            dist = step_ref[f * per + half : f * per + half + 8, :]
            beside = [jnp.zeros((8, LANES), jnp.float32)] * 5
            for d in range(2 * blocks + 1):
                here = dist == d
                first = half + d * nodes
                for b in range(5):
                    shift, at = first % 8 // nodes, b * width + first // 8 * 8
                    if shift:
                        at = at + (shift - 1) * 5 * width
                        table = table_ref[at : at + 8, :]
                    else:
                        table = window_ref[at : at + 8, :]
                    beside[b] = jnp.where(here, take_lanes(table, lanes), beside[b])
            for a in range(5):
                for b in range(5):
                    row = (f * 25 + 5 * a + b) * per + half
                    remaining[a] = remaining[a] - off_ref[row : row + 8, :] * beside[b]
        for a in range(5):
            total = None
            for b in range(5):
                row = (5 * a + b) * per + half
                term = inverse_ref[row : row + 8, :] * remaining[b]
                total = term if total is None else total + term
            out_ref[a * per + half : a * per + half + 8, :] = total


def sweep_kernel(blocks, *refs):
    sweep_into(blocks, *refs)


def last_sweep_kernel(blocks, *refs):
    ins, rest = refs[:8], refs[8:]
    sens_ref, _, out_ref, sens_out_ref, window_ref, table_ref, part_ref = rest
    sweep_into(blocks, *ins, out_ref, window_ref, table_ref)
    per = out_ref.shape[0] // 5
    nodes = per // blocks
    for k in range(3):
        total = None
        for a in range(5):
            row = (3 * a + k) * per
            term = out_ref[a * per : (a + 1) * per, :] * sens_ref[row : row + per, :]
            total = term if total is None else total + term
        part_ref[k * per : (k + 1) * per, :] = total
    for block in range(blocks):
        total = None
        for node in range(nodes):
            term = part_ref[pl.ds(block * nodes + node, 3, stride=per), :]
            total = term if total is None else total + term
        sens_out_ref[pl.ds(block, 3, stride=blocks), :] = total


def pieces(value, count):
    found = []
    for _ in range(count):
        piece = value.astype(jnp.bfloat16).astype(jnp.float32)
        found.append(piece)
        value = value - piece
    return found


def distance_factors(points, left):
    count = points.shape[1]
    scaled = (points - 0.5) * (1.0 / SUPPORT_RADIUS)
    scaled = jnp.concatenate([scaled, jnp.zeros((5, count), jnp.float32)], axis=0)
    norm = jnp.sum(scaled * scaled, axis=0, keepdims=True)
    norms = pieces(jnp.broadcast_to(norm, (8, count)), 3)
    row = lax.broadcasted_iota(jnp.int32, (8, count), 0)
    norm_block = jnp.zeros((8, count), jnp.float32)
    for place in range(3):
        norm_block = jnp.where(row == place, norms[place], norm_block)
    ones_block = jnp.where(row < 3, 1.0, 0.0)
    first, second, third = pieces(scaled, 3)
    if left:
        dims = [first, first, second, second, first, third]
        dims = [-2.0 * part for part in dims]
        blocks = dims + [norm_block, ones_block]
    else:
        dims = [first, second, first, second, third, first]
        blocks = dims + [ones_block, norm_block]
    return jnp.concatenate(blocks, axis=0)


def wendland_kernel(first_cell, left_ref, right_ref, _, kernel_ref):
    cells, owned = kernel_ref.shape[0] // 2, kernel_ref.shape[1]
    tile, wide = min(128, cells), min(256, owned)

    def squares(row, lane):
        left = left_ref[first_cell + row : first_cell + row + tile, :]
        right = right_ref[:, lane : lane + wide]
        return jnp.dot(left, right, preferred_element_type=jnp.float32)

    places = [(row, lane) for lane in range(0, owned, wide) for row in range(0, cells, tile)]
    following = squares(*places[0])
    for at, (row, lane) in enumerate(places):
        squared = jnp.maximum(following, 1e-30)
        if at + 1 < len(places):
            following = squares(*places[at + 1])
        near = jnp.maximum(1.0 - squared * lax.rsqrt(squared), 0.0)
        power = near * near
        kernel = power * power * (1.25 - near)
        first = kernel.astype(jnp.bfloat16)
        rest = (kernel - first.astype(jnp.float32)).astype(jnp.bfloat16)
        here = slice(lane, lane + wide)
        kernel_ref[row : row + tile, here] = first
        kernel_ref[cells + row : cells + row + tile, here] = rest


def far_wendland_kernel(
    first_cell, left_ref, right_ref, after, adjoint_ref, low_ref, *rest
):
    kernel_ref, one_hot_ref, result_ref, sem = rest
    copy = pltpu.make_async_copy(adjoint_ref, result_ref, sem)
    copy.start()
    owned = low_ref.shape[1]
    write_one_hot(low_ref, one_hot_ref, low_ref.shape[0] - one_hot_ref.shape[0] // owned)
    wendland_kernel(first_cell, left_ref, right_ref, after, kernel_ref)
    copy.wait()


def control_kernel(scale, *refs):
    *sens_refs, near_ref, far_ref = refs[:-4]
    spread_ref, near_hot, far_hot, out_ref = refs[-4:]
    blocks = sens_refs[0].shape[0] // 3
    half = near_ref.shape[0] // 2
    groups = FFD // LANES
    total = sens_refs[0][...]
    for ref in sens_refs[1:]:
        total = total + ref[...]
    total = total * scale

    def halves(value):
        first = value.astype(jnp.bfloat16)
        rest = (value - first.astype(jnp.float32)).astype(jnp.bfloat16)
        return first, rest

    row = lax.broadcasted_iota(jnp.int32, (8, LANES), 0)
    wide = []
    for block in range(blocks):
        sens = jnp.zeros((8, LANES), jnp.float32)
        for k in range(3):
            sens = jnp.where(row == k, total[k * blocks + block : k * blocks + block + 1], sens)
        first = sens.astype(jnp.bfloat16).astype(jnp.float32)
        wide.append(jnp.concatenate([first, sens - first], axis=0))
    sens = jnp.concatenate(wide, axis=1).astype(jnp.bfloat16)
    grad = None
    for part, ref in ((sens[:, :half], near_ref), (sens[:, half:], far_ref)):
        both = jnp.concatenate([part, part], axis=1)
        term = jnp.dot(both, ref[...], preferred_element_type=jnp.float32)
        grad = term if grad is None else grad + term
    grad = grad[:8] + grad[8:]
    row = lax.broadcasted_iota(jnp.int32, (16, grad.shape[1]), 0)
    wide = jnp.zeros(row.shape, jnp.float32)
    for k in range(3):
        mine = jnp.logical_and(row >= k * groups, row < (k + 1) * groups)
        wide = jnp.where(mine, grad[k : k + 1], wide)
    grad = wide
    owned = grad.shape[1]
    result = None
    places = [
        (ref, first) for ref in (near_hot, far_hot) for first in range(0, ref.shape[0], owned)
    ]
    for j, (ref, first) in enumerate(places):
        term = jnp.dot(
            jnp.concatenate(halves(grad * spread_ref[j * 16 : (j + 1) * 16, :]), axis=0),
            ref[first : first + owned, :],
            preferred_element_type=jnp.float32,
        )
        result = term if result is None else result + term
    result = result[:16] + result[16:]
    out_ref[...] = result[: 3 * groups]


def tree(values):
    while len(values) > 1:
        values = [sum(values[i : i + 2]) for i in range(0, len(values), 2)]
    return values[0]


def add_kernel(*refs):
    refs[-1][...] = tree([ref[...] for ref in refs[:-1]])


def finish_kernel(*refs):
    total, out_ref = tree([ref[...] for ref in refs[:-1]]), refs[-1]
    groups = out_ref.shape[1] // LANES
    for k in range(3):
        for group in range(groups):
            row = k * groups + group
            out_ref[k : k + 1, group * LANES : (group + 1) * LANES] = total[row : row + 1]


def sum_rounds():
    lines, nodes, cores = (lax.axis_size(axis) for axis in SUM_AXES)
    if any(size & (size - 1) for size in (lines, nodes, cores)):
        return None
    near = [cores >> 1 >> i for i in range(cores.bit_length() - 1)]
    node_bits = [cores << i for i in range(nodes.bit_length() - 1)]
    line_bits = [cores * nodes << i for i in range(lines.bit_length() - 1)]
    bits = near + line_bits[:2] + node_bits[:1] + line_bits[2:] + node_bits[1:]
    rounds = []
    for first in range(0, len(bits), 2):
        masks = bits[first : first + 2]
        if len(masks) == 2:
            masks = masks + [masks[0] | masks[1]]
        rounds.append([mask | (cores - 1) for mask in masks] if first else masks)
    return rounds


def exchanged(value, masks):
    peers = lax.axis_size(SUM_AXES)
    return [value] + [
        lax.ppermute(value, SUM_AXES, [(i, i ^ mask) for i in range(peers)]) for mask in masks
    ]


def body(
    adjoint_start,
    adjoint_rhs,
    off_blocks,
    diag_inverse,
    neighbours,
    node_weights,
    sens_blocks,
    cell_points,
    base_points,
    ffd_index,
    ffd_weight,
):
    nodes, _, cells = adjoint_start.shape
    faces = off_blocks.shape[1]
    blocks = cells // LANES
    per = blocks * nodes
    slots = ffd_index.shape[1]
    far_slots = max(1, slots * 3 // 8)
    owned = base_points.shape[1] // lax.axis_size("nodes")
    peers = lax.axis_size(CELL_AXES)
    cores = lax.axis_size("sub")
    node_peers = lax.axis_size("nodes")
    f32, i32, bf16 = jnp.float32, jnp.int32, jnp.bfloat16

    def shape(dims, dtype=f32):
        return jax.ShapeDtypeStruct(dims, dtype)

    def cost(flops, moved):
        return pl.CostEstimate(flops=flops, bytes_accessed=moved, transcendentals=0)

    def swaps(array):
        close = lax.ppermute(array, CELL_AXES, [(i, i ^ 1) for i in range(peers)])
        pairs = []
        for i in range(peers):
            line, core = divmod(i, cores)
            for node in range(node_peers):
                j, beside = (i + 1 if i % 2 else i - 1), node
                if not 0 <= j < peers:
                    j, beside = i, (node ^ 1 if node_peers % 2 == 0 else node)
                to_line, to_core = divmod(j, cores)
                pairs.append(
                    (
                        (line * node_peers + node) * cores + core,
                        (to_line * node_peers + beside) * cores + to_core,
                    )
                )
        return lax.ppermute(array, SUM_AXES, pairs), close

    adjoint = rows_of(adjoint_start)
    far, close = swaps(adjoint)
    prepared = pl.pallas_call(
        functools.partial(prepare_kernel, nodes),
        out_shape=(
            shape((faces * 25 * per, LANES)),
            shape((25 * per, LANES)),
            shape((5 * per, LANES)),
            shape((15 * per, LANES)),
            shape((faces * per, LANES), i32),
            shape((faces * per, LANES), i32),
            shape((slots * 16, owned)),
            shape((slots, owned)),
            shape(((slots - far_slots) * owned, LANES), bf16),
            shape((5 * per, LANES)),
            shape((cells, FACTOR_ROWS), bf16),
            shape((FACTOR_ROWS, owned), bf16),
        ),
        in_specs=[HBM] * 11,
        out_specs=(VMEM,) * 12,
        scratch_shapes=[
            pltpu.VMEM((faces * 25 * per, LANES), bf16),
            pltpu.VMEM((15 * per, LANES), bf16),
            pltpu.VMEM((faces, cells), i32),
            pltpu.SMEM((nodes,), f32),
            pltpu.VMEM((slots, owned), i32),
            pltpu.VMEM((slots, owned), f32),
            pltpu.VMEM((3, cells), f32),
            pltpu.VMEM((3, owned), f32),
            pltpu.SemaphoreType.DMA((11,)),
        ],
        compiler_params=PARAMS,
        cost_estimate=cost(10**9, 10**7),
        name="prepare",
    )(
        *in_hbm(
            rows_of(off_blocks.reshape(nodes, faces * 25, cells)),
            rows_of(diag_inverse),
            rows_of(adjoint_rhs),
            rows_of(sens_blocks),
            neighbours,
            node_weights,
            ffd_index.T,
            ffd_weight.T,
            adjoint,
            cell_points,
            base_points,
        )
    )
    off, inverse, rhs, sens, lane, step, spread, low, near_hot, adjoint, left, right = prepared
    scratch = [
        pltpu.VMEM((3 * 5 * per, LANES), f32),
        pltpu.VMEM((max(8 // nodes - 1, 1) * 3 * 5 * per, LANES), f32),
    ]
    sweep_cost = cost(2 * 10 * 35 * cells, 4 * faces * 25 * per * LANES)

    for _ in range(SWEEPS - 1):
        adjoint = pl.pallas_call(
            functools.partial(sweep_kernel, blocks),
            out_shape=shape((5 * per, LANES)),
            in_specs=[VMEM] * 8,
            out_specs=VMEM,
            scratch_shapes=scratch,
            compiler_params=PARAMS,
            cost_estimate=sweep_cost,
            name="sweep",
        )(close, far, adjoint, rhs, off, inverse, lane, step)
        far, close = swaps(adjoint)

    half = cells * 5 // 8 // LANES * LANES
    wendland_cost = cost(10**9, 10**7)
    near_shape = shape((2 * half, owned), bf16)
    far_shape = shape((2 * (cells - half), owned), bf16)
    near_kernel = pl.pallas_call(
        functools.partial(wendland_kernel, 0),
        out_shape=near_shape,
        in_specs=[VMEM] * 3,
        out_specs=VMEM,
        compiler_params=PARAMS,
        cost_estimate=wendland_cost,
        name="near_wendland",
    )(left, right, adjoint)
    adjoint, part_sens = pl.pallas_call(
        functools.partial(last_sweep_kernel, blocks),
        out_shape=(shape((5 * per, LANES)), shape((3 * blocks, LANES))),
        in_specs=[VMEM] * 9 + [pl.BlockSpec(memory_space=pl.ANY)],
        out_specs=(VMEM, VMEM),
        scratch_shapes=scratch + [pltpu.VMEM((3 * per, LANES), f32)],
        compiler_params=PARAMS,
        cost_estimate=sweep_cost,
        name="last_sweep",
    )(close, far, adjoint, rhs, off, inverse, lane, step, sens, near_kernel)

    all_sens = [part_sens]
    for shift in range(1, node_peers):
        ring = [(i, (i + shift) % node_peers) for i in range(node_peers)]
        all_sens.append(lax.ppermute(part_sens, "nodes", ring))
    hot_shape = shape((far_slots * owned, LANES), bf16)
    far_kernel, far_hot, adjoint = pl.pallas_call(
        functools.partial(far_wendland_kernel, half),
        out_shape=(far_shape, hot_shape, shape((5 * per, LANES))),
        in_specs=[VMEM] * 5,
        out_specs=(VMEM, VMEM, HBM),
        scratch_shapes=[pltpu.SemaphoreType.DMA],
        compiler_params=PARAMS,
        cost_estimate=wendland_cost,
        name="far_wendland",
    )(left, right, part_sens, adjoint, low)
    scale = 4.0 / math.sqrt(cells * peers)
    rows = 3 * FFD // LANES
    partial = pl.pallas_call(
        functools.partial(control_kernel, scale),
        out_shape=shape((rows, LANES)),
        in_specs=[VMEM] * (len(all_sens) + 5),
        out_specs=VMEM,
        compiler_params=PARAMS,
        name="control",
    )(*all_sens, near_kernel, far_kernel, spread, near_hot, far_hot)
    rounds = sum_rounds()
    terms = [partial] if rounds else [lax.psum(partial, SUM_AXES)]
    for masks in rounds or ():
        if len(terms) > 1:
            partial = pl.pallas_call(
                add_kernel, out_shape=shape((rows, LANES)), name="add", compiler_params=PARAMS
            )(*terms)
        terms = exchanged(partial, masks)
    control_grad = pl.pallas_call(
        finish_kernel, out_shape=shape((3, FFD)), name="finish", compiler_params=PARAMS
    )(*terms)
    return (from_rows(adjoint, nodes, cells), control_grad)


def solution(mesh):
    return jax.shard_map(
        body,
        mesh=mesh,
        in_specs=(
            P("nodes", None, ("groups", "cells", "sub")),
            P("nodes", None, ("groups", "cells", "sub")),
            P("nodes", None, None, ("groups", "cells", "sub")),
            P("nodes", None, ("groups", "cells", "sub")),
            P(None, ("cells", "sub")),
            P("nodes"),
            P("nodes", None, ("groups", "cells", "sub")),
            P(None, ("cells", "sub")),
            P(),
            P(),
            P(),
        ),
        out_specs=(P("nodes", None, ("groups", "cells", "sub")), P("groups", None)),
        check_vma=False,
    )
```

```python
import functools
import math

import jax
import jax.numpy as jnp
from jax import lax
from jax.experimental import pallas as pl
from jax.experimental.pallas import tpu as pltpu
from jax.sharding import PartitionSpec as P

SWEEPS = 2
FFD = 512
SUPPORT_RADIUS = 0.3
LANES = 128
CELL_AXES = ("cells", "sub")
SUM_AXES = ("cells", "nodes", "sub")
FACTOR_ROWS = 64
PARAMS = pltpu.CompilerParams(vmem_limit_bytes=24 * 1024 * 1024)
VMEM = pl.BlockSpec(memory_space=pltpu.VMEM)
HBM = pl.BlockSpec(memory_space=pltpu.HBM)


def rows_of(array):
    nodes, rows, cells = array.shape
    blocks = cells // LANES
    split = array.reshape(nodes, rows, blocks, LANES)
    return split.transpose(1, 2, 0, 3).reshape(rows * blocks * nodes, LANES)


def from_rows(array, nodes, cells):
    blocks = cells // LANES
    split = array.reshape(-1, blocks, nodes, LANES)
    return split.transpose(2, 0, 1, 3).reshape(nodes, -1, cells)


def in_hbm(*arrays):
    return [pltpu.with_memory_space_constraint(array, pltpu.HBM) for array in arrays]


def write_one_hot(low_ref, one_hot_ref, first_slot):
    owned = low_ref.shape[1]
    piece = min(512, owned)
    lane = lax.broadcasted_iota(jnp.int32, (piece, LANES), 1).astype(jnp.float32)
    lane = lane.astype(jnp.bfloat16)
    for first in range(0, owned, piece):
        low = low_ref[:, first : first + piece].T.astype(jnp.bfloat16)
        for j in range(one_hot_ref.shape[0] // owned):
            column = low[:, first_slot + j : first_slot + j + 1]
            hit = jnp.broadcast_to(column, (piece, LANES)) == lane
            one_hot_ref[j * owned + first : j * owned + first + piece, :] = jnp.where(
                hit, jnp.bfloat16(1.0), jnp.bfloat16(0.0)
            )


def prepare_kernel(
    nodes,
    off_in,
    inverse_in,
    rhs_in,
    sens_in,
    neigh_in,
    weight_in,
    index_in,
    spread_in,
    start_in,
    cell_in,
    base_in,
    off_ref,
    inverse_ref,
    rhs_ref,
    sens_ref,
    lane_ref,
    step_ref,
    spread_ref,
    low_ref,
    one_hot_ref,
    start_ref,
    left_ref,
    right_ref,
    off_buf,
    sens_buf,
    neigh_buf,
    weight_buf,
    index_buf,
    spread_buf,
    cell_buf,
    base_buf,
    sems,
):
    slots, owned = index_buf.shape
    start = pl.multiple_of(lax.axis_index("nodes") * owned, LANES)
    mine = pl.ds(start, owned)
    pairs = (
        (neigh_in, neigh_buf),
        (index_in.at[:, mine], index_buf),
        (spread_in.at[:, mine], spread_buf),
        (cell_in, cell_buf),
        (base_in.at[:, mine], base_buf),
        (off_in, off_buf),
        (weight_in, weight_buf),
        (sens_in, sens_buf),
        (inverse_in, inverse_ref),
        (rhs_in, rhs_ref),
        (start_in, start_ref),
    )
    copies = [pltpu.make_async_copy(a, b, sems.at[i]) for i, (a, b) in enumerate(pairs)]
    for copy in copies:
        copy.start()

    faces, cells = neigh_buf.shape
    blocks = cells // LANES
    per = blocks * nodes
    first_cell = lax.axis_index(CELL_AXES) * cells
    copies[0].wait()
    for block in range(blocks):
        index = neigh_buf[:, block * LANES : (block + 1) * LANES]
        local = index - first_cell + cells
        lane = jnp.bitwise_and(local, LANES - 1)
        step = jnp.right_shift(local, 7) - block
        step = jnp.where(index >= 0, step, -1)
        for node in range(nodes):
            rows = pl.ds(block * nodes + node, faces, stride=per)
            lane_ref[rows, :] = lane
            step_ref[rows, :] = step

    copies[1].wait()
    copies[2].wait()
    groups = FFD // LANES
    piece = min(512, owned)
    for first in range(0, owned, piece):
        here = slice(first, first + piece)
        high = jnp.right_shift(index_buf[:, here], 7)
        part = lax.broadcasted_iota(jnp.int32, (16, piece), 0)
        part = jnp.where(part < 3 * groups, lax.rem(part, groups), -1)
        for j in range(slots):
            spread_ref[j * 16 : (j + 1) * 16, here] = jnp.where(
                high[j : j + 1] == part, spread_buf[j : j + 1, here], 0.0
            )

    low_ref[...] = jnp.bitwise_and(index_buf[...], LANES - 1).astype(jnp.float32)
    write_one_hot(low_ref, one_hot_ref, 0)

    copies[3].wait()
    left_ref[...] = distance_factors(cell_buf[...], True).T.astype(jnp.bfloat16)
    copies[4].wait()
    right_ref[...] = distance_factors(base_buf[...], False).astype(jnp.bfloat16)

    copies[5].wait()
    off_ref[...] = off_buf[...].astype(jnp.float32)
    copies[6].wait()
    copies[7].wait()
    row_node = lax.rem(lax.broadcasted_iota(jnp.int32, (per, LANES), 0), nodes)
    weights = jnp.zeros((per, LANES), jnp.float32)
    for node in range(nodes):
        weights = jnp.where(row_node == node, weight_buf[node], weights)
    for row in range(0, sens_buf.shape[0], per):
        here = slice(row, row + per)
        sens_ref[here, :] = sens_buf[here, :].astype(jnp.float32) * weights
    for copy in copies[8:]:
        copy.wait()


def take_lanes(table, lanes):
    numbers = lax.GatherDimensionNumbers(
        offset_dims=(),
        collapsed_slice_dims=(1,),
        start_index_map=(1,),
        operand_batching_dims=(0,),
        start_indices_batching_dims=(0,),
    )
    return lax.gather(
        table,
        lanes[..., None],
        numbers,
        slice_sizes=(1, 1),
        mode=lax.GatherScatterMode.PROMISE_IN_BOUNDS,
    )


def sweep_into(
    blocks, far_ref, close_ref, own_ref, rhs_ref, off_ref, inverse_ref, lane_ref, step_ref,
    out_ref, window_ref, table_ref,
):
    per = rhs_ref.shape[0] // 5
    nodes = per // blocks
    faces = lane_ref.shape[0] // per
    odd = lax.rem(lax.axis_index(CELL_AXES), 2)
    place = pl.multiple_of((1 - odd) * 2 * per, 8)
    other = pl.multiple_of(odd * 2 * per, 8)
    width = 3 * per
    for b in range(5):
        rows = slice(b * per, (b + 1) * per)
        base = b * width
        window_ref[pl.ds(base + place, per), :] = close_ref[rows, :]
        window_ref[base + per : base + 2 * per, :] = own_ref[rows, :]
        window_ref[pl.ds(base + other, per), :] = far_ref[rows, :]
    for shift in range(1, 8 // nodes):
        for b in range(5):
            for tile in range(0, width - 8, 8):
                to = ((shift - 1) * 5 + b) * width + tile
                table_ref[to : to + 8, :] = window_ref[
                    pl.ds(b * width + tile + shift * nodes, 8), :
                ]
    for half in range(0, per, 8):
        remaining = [rhs_ref[a * per + half : a * per + half + 8, :] for a in range(5)]
        for f in range(faces):
            lanes = lane_ref[f * per + half : f * per + half + 8, :]
            dist = step_ref[f * per + half : f * per + half + 8, :]
            beside = [jnp.zeros((8, LANES), jnp.float32)] * 5
            for d in range(2 * blocks + 1):
                here = dist == d
                first = half + d * nodes
                for b in range(5):
                    shift, at = first % 8 // nodes, b * width + first // 8 * 8
                    if shift:
                        at = at + (shift - 1) * 5 * width
                        table = table_ref[at : at + 8, :]
                    else:
                        table = window_ref[at : at + 8, :]
                    beside[b] = jnp.where(here, take_lanes(table, lanes), beside[b])
            for a in range(5):
                for b in range(5):
                    row = (f * 25 + 5 * a + b) * per + half
                    remaining[a] = remaining[a] - off_ref[row : row + 8, :] * beside[b]
        for a in range(5):
            total = None
            for b in range(5):
                row = (5 * a + b) * per + half
                term = inverse_ref[row : row + 8, :] * remaining[b]
                total = term if total is None else total + term
            out_ref[a * per + half : a * per + half + 8, :] = total


def sweep_kernel(blocks, *refs):
    sweep_into(blocks, *refs)


def last_sweep_kernel(blocks, *refs):
    ins, rest = refs[:8], refs[8:]
    sens_ref, _, out_ref, sens_out_ref, window_ref, table_ref, part_ref = rest
    sweep_into(blocks, *ins, out_ref, window_ref, table_ref)
    per = out_ref.shape[0] // 5
    nodes = per // blocks
    for k in range(3):
        total = None
        for a in range(5):
            row = (3 * a + k) * per
            term = out_ref[a * per : (a + 1) * per, :] * sens_ref[row : row + per, :]
            total = term if total is None else total + term
        part_ref[k * per : (k + 1) * per, :] = total
    for block in range(blocks):
        total = None
        for node in range(nodes):
            term = part_ref[pl.ds(block * nodes + node, 3, stride=per), :]
            total = term if total is None else total + term
        sens_out_ref[pl.ds(block, 3, stride=blocks), :] = total


def pieces(value, count):
    found = []
    for _ in range(count):
        piece = value.astype(jnp.bfloat16).astype(jnp.float32)
        found.append(piece)
        value = value - piece
    return found


def distance_factors(points, left):
    count = points.shape[1]
    scaled = (points - 0.5) * (1.0 / SUPPORT_RADIUS)
    scaled = jnp.concatenate([scaled, jnp.zeros((5, count), jnp.float32)], axis=0)
    norm = jnp.sum(scaled * scaled, axis=0, keepdims=True)
    norms = pieces(jnp.broadcast_to(norm, (8, count)), 3)
    row = lax.broadcasted_iota(jnp.int32, (8, count), 0)
    norm_block = jnp.zeros((8, count), jnp.float32)
    for place in range(3):
        norm_block = jnp.where(row == place, norms[place], norm_block)
    ones_block = jnp.where(row < 3, 1.0, 0.0)
    first, second, third = pieces(scaled, 3)
    if left:
        dims = [first, first, second, second, first, third]
        dims = [-2.0 * part for part in dims]
        blocks = dims + [norm_block, ones_block]
    else:
        dims = [first, second, first, second, third, first]
        blocks = dims + [ones_block, norm_block]
    return jnp.concatenate(blocks, axis=0)


def wendland_kernel(first_cell, left_ref, right_ref, _, kernel_ref):
    cells, owned = kernel_ref.shape[0] // 2, kernel_ref.shape[1]
    tile, wide = min(128, cells), min(256, owned)

    def squares(row, lane):
        left = left_ref[first_cell + row : first_cell + row + tile, :]
        right = right_ref[:, lane : lane + wide]
        return jnp.dot(left, right, preferred_element_type=jnp.float32)

    places = [(row, lane) for lane in range(0, owned, wide) for row in range(0, cells, tile)]
    following = squares(*places[0])
    for at, (row, lane) in enumerate(places):
        squared = jnp.maximum(following, 1e-30)
        if at + 1 < len(places):
            following = squares(*places[at + 1])
        near = jnp.maximum(1.0 - squared * lax.rsqrt(squared), 0.0)
        power = near * near
        kernel = power * power * (1.25 - near)
        first = kernel.astype(jnp.bfloat16)
        rest = (kernel - first.astype(jnp.float32)).astype(jnp.bfloat16)
        here = slice(lane, lane + wide)
        kernel_ref[row : row + tile, here] = first
        kernel_ref[cells + row : cells + row + tile, here] = rest


def far_wendland_kernel(
    first_cell, left_ref, right_ref, after, adjoint_ref, low_ref, *rest
):
    kernel_ref, one_hot_ref, result_ref, sem = rest
    copy = pltpu.make_async_copy(adjoint_ref, result_ref, sem)
    copy.start()
    owned = low_ref.shape[1]
    write_one_hot(low_ref, one_hot_ref, low_ref.shape[0] - one_hot_ref.shape[0] // owned)
    wendland_kernel(first_cell, left_ref, right_ref, after, kernel_ref)
    copy.wait()


def control_kernel(scale, *refs):
    *sens_refs, near_ref, far_ref = refs[:-4]
    spread_ref, near_hot, far_hot, out_ref = refs[-4:]
    blocks = sens_refs[0].shape[0] // 3
    half = near_ref.shape[0] // 2
    groups = FFD // LANES
    total = sens_refs[0][...]
    for ref in sens_refs[1:]:
        total = total + ref[...]
    total = total * scale

    def halves(value):
        first = value.astype(jnp.bfloat16)
        rest = (value - first.astype(jnp.float32)).astype(jnp.bfloat16)
        return first, rest

    row = lax.broadcasted_iota(jnp.int32, (8, LANES), 0)
    wide = []
    for block in range(blocks):
        sens = jnp.zeros((8, LANES), jnp.float32)
        for k in range(3):
            sens = jnp.where(row == k, total[k * blocks + block : k * blocks + block + 1], sens)
        first = sens.astype(jnp.bfloat16).astype(jnp.float32)
        wide.append(jnp.concatenate([first, sens - first], axis=0))
    sens = jnp.concatenate(wide, axis=1).astype(jnp.bfloat16)
    grad = None
    for part, ref in ((sens[:, :half], near_ref), (sens[:, half:], far_ref)):
        both = jnp.concatenate([part, part], axis=1)
        term = jnp.dot(both, ref[...], preferred_element_type=jnp.float32)
        grad = term if grad is None else grad + term
    grad = grad[:8] + grad[8:]
    row = lax.broadcasted_iota(jnp.int32, (16, grad.shape[1]), 0)
    wide = jnp.zeros(row.shape, jnp.float32)
    for k in range(3):
        mine = jnp.logical_and(row >= k * groups, row < (k + 1) * groups)
        wide = jnp.where(mine, grad[k : k + 1], wide)
    grad = wide
    owned = grad.shape[1]
    result = None
    places = [
        (ref, first) for ref in (near_hot, far_hot) for first in range(0, ref.shape[0], owned)
    ]
    for j, (ref, first) in enumerate(places):
        term = jnp.dot(
            jnp.concatenate(halves(grad * spread_ref[j * 16 : (j + 1) * 16, :]), axis=0),
            ref[first : first + owned, :],
            preferred_element_type=jnp.float32,
        )
        result = term if result is None else result + term
    result = result[:16] + result[16:]
    out_ref[...] = result[: 3 * groups]


def tree(values):
    while len(values) > 1:
        values = [sum(values[i : i + 2]) for i in range(0, len(values), 2)]
    return values[0]


def add_kernel(*refs):
    refs[-1][...] = tree([ref[...] for ref in refs[:-1]])


def finish_kernel(*refs):
    total, out_ref = tree([ref[...] for ref in refs[:-1]]), refs[-1]
    groups = out_ref.shape[1] // LANES
    for k in range(3):
        for group in range(groups):
            row = k * groups + group
            out_ref[k : k + 1, group * LANES : (group + 1) * LANES] = total[row : row + 1]


def sum_rounds():
    lines, nodes, cores = (lax.axis_size(axis) for axis in SUM_AXES)
    if any(size & (size - 1) for size in (lines, nodes, cores)):
        return None
    near = [cores >> 1 >> i for i in range(cores.bit_length() - 1)]
    node_bits = [cores << i for i in range(nodes.bit_length() - 1)]
    line_bits = [cores * nodes << i for i in range(lines.bit_length() - 1)]
    bits = near + line_bits[:2] + node_bits[:1] + line_bits[2:] + node_bits[1:]
    rounds = []
    for first in range(0, len(bits), 2):
        masks = bits[first : first + 2]
        if len(masks) == 2:
            both = masks[0] | masks[1]
            masks = masks + [both] if first else [masks[1], both, masks[0]]
        rounds.append([mask | (cores - 1) for mask in masks] if first else masks)
    return rounds


def exchanged(value, masks):
    peers = lax.axis_size(SUM_AXES)
    return [value] + [
        lax.ppermute(value, SUM_AXES, [(i, i ^ mask) for i in range(peers)]) for mask in masks
    ]


def body(
    adjoint_start,
    adjoint_rhs,
    off_blocks,
    diag_inverse,
    neighbours,
    node_weights,
    sens_blocks,
    cell_points,
    base_points,
    ffd_index,
    ffd_weight,
):
    nodes, _, cells = adjoint_start.shape
    faces = off_blocks.shape[1]
    blocks = cells // LANES
    per = blocks * nodes
    slots = ffd_index.shape[1]
    far_slots = max(1, slots * 3 // 8)
    owned = base_points.shape[1] // lax.axis_size("nodes")
    peers = lax.axis_size(CELL_AXES)
    cores = lax.axis_size("sub")
    node_peers = lax.axis_size("nodes")
    f32, i32, bf16 = jnp.float32, jnp.int32, jnp.bfloat16

    def shape(dims, dtype=f32):
        return jax.ShapeDtypeStruct(dims, dtype)

    def cost(flops, moved):
        return pl.CostEstimate(flops=flops, bytes_accessed=moved, transcendentals=0)

    def swaps(array):
        close = lax.ppermute(array, CELL_AXES, [(i, i ^ 1) for i in range(peers)])
        pairs = []
        for i in range(peers):
            line, core = divmod(i, cores)
            for node in range(node_peers):
                j, beside = (i + 1 if i % 2 else i - 1), node
                if not 0 <= j < peers:
                    j, beside = i, (node ^ 1 if node_peers % 2 == 0 else node)
                to_line, to_core = divmod(j, cores)
                pairs.append(
                    (
                        (line * node_peers + node) * cores + core,
                        (to_line * node_peers + beside) * cores + to_core,
                    )
                )
        return lax.ppermute(array, SUM_AXES, pairs), close

    adjoint = rows_of(adjoint_start)
    far, close = swaps(adjoint)
    prepared = pl.pallas_call(
        functools.partial(prepare_kernel, nodes),
        out_shape=(
            shape((faces * 25 * per, LANES)),
            shape((25 * per, LANES)),
            shape((5 * per, LANES)),
            shape((15 * per, LANES)),
            shape((faces * per, LANES), i32),
            shape((faces * per, LANES), i32),
            shape((slots * 16, owned)),
            shape((slots, owned)),
            shape(((slots - far_slots) * owned, LANES), bf16),
            shape((5 * per, LANES)),
            shape((cells, FACTOR_ROWS), bf16),
            shape((FACTOR_ROWS, owned), bf16),
        ),
        in_specs=[HBM] * 11,
        out_specs=(VMEM,) * 12,
        scratch_shapes=[
            pltpu.VMEM((faces * 25 * per, LANES), bf16),
            pltpu.VMEM((15 * per, LANES), bf16),
            pltpu.VMEM((faces, cells), i32),
            pltpu.SMEM((nodes,), f32),
            pltpu.VMEM((slots, owned), i32),
            pltpu.VMEM((slots, owned), f32),
            pltpu.VMEM((3, cells), f32),
            pltpu.VMEM((3, owned), f32),
            pltpu.SemaphoreType.DMA((11,)),
        ],
        compiler_params=PARAMS,
        cost_estimate=cost(10**9, 10**7),
        name="prepare",
    )(
        *in_hbm(
            rows_of(off_blocks.reshape(nodes, faces * 25, cells)),
            rows_of(diag_inverse),
            rows_of(adjoint_rhs),
            rows_of(sens_blocks),
            neighbours,
            node_weights,
            ffd_index.T,
            ffd_weight.T,
            adjoint,
            cell_points,
            base_points,
        )
    )
    off, inverse, rhs, sens, lane, step, spread, low, near_hot, adjoint, left, right = prepared
    scratch = [
        pltpu.VMEM((3 * 5 * per, LANES), f32),
        pltpu.VMEM((max(8 // nodes - 1, 1) * 3 * 5 * per, LANES), f32),
    ]
    sweep_cost = cost(2 * 10 * 35 * cells, 4 * faces * 25 * per * LANES)

    for _ in range(SWEEPS - 1):
        adjoint = pl.pallas_call(
            functools.partial(sweep_kernel, blocks),
            out_shape=shape((5 * per, LANES)),
            in_specs=[VMEM] * 8,
            out_specs=VMEM,
            scratch_shapes=scratch,
            compiler_params=PARAMS,
            cost_estimate=sweep_cost,
            name="sweep",
        )(far, close, adjoint, rhs, off, inverse, lane, step)
        far, close = swaps(adjoint)

    half = cells * 5 // 8 // LANES * LANES
    wendland_cost = cost(10**9, 10**7)
    near_shape = shape((2 * half, owned), bf16)
    far_shape = shape((2 * (cells - half), owned), bf16)
    near_kernel = pl.pallas_call(
        functools.partial(wendland_kernel, 0),
        out_shape=near_shape,
        in_specs=[VMEM] * 3,
        out_specs=VMEM,
        compiler_params=PARAMS,
        cost_estimate=wendland_cost,
        name="near_wendland",
    )(left, right, adjoint)
    adjoint, part_sens = pl.pallas_call(
        functools.partial(last_sweep_kernel, blocks),
        out_shape=(shape((5 * per, LANES)), shape((3 * blocks, LANES))),
        in_specs=[VMEM] * 9 + [pl.BlockSpec(memory_space=pl.ANY)],
        out_specs=(VMEM, VMEM),
        scratch_shapes=scratch + [pltpu.VMEM((3 * per, LANES), f32)],
        compiler_params=PARAMS,
        cost_estimate=sweep_cost,
        name="last_sweep",
    )(far, close, adjoint, rhs, off, inverse, lane, step, sens, near_kernel)

    all_sens = [part_sens]
    for shift in range(1, node_peers):
        ring = [(i, (i + shift) % node_peers) for i in range(node_peers)]
        all_sens.append(lax.ppermute(part_sens, "nodes", ring))
    hot_shape = shape((far_slots * owned, LANES), bf16)
    far_kernel, far_hot, adjoint = pl.pallas_call(
        functools.partial(far_wendland_kernel, half),
        out_shape=(far_shape, hot_shape, shape((5 * per, LANES))),
        in_specs=[VMEM] * 5,
        out_specs=(VMEM, VMEM, HBM),
        scratch_shapes=[pltpu.SemaphoreType.DMA],
        compiler_params=PARAMS,
        cost_estimate=wendland_cost,
        name="far_wendland",
    )(left, right, part_sens, adjoint, low)
    scale = 4.0 / math.sqrt(cells * peers)
    rows = 3 * FFD // LANES
    partial = pl.pallas_call(
        functools.partial(control_kernel, scale),
        out_shape=shape((rows, LANES)),
        in_specs=[VMEM] * (len(all_sens) + 5),
        out_specs=VMEM,
        compiler_params=PARAMS,
        name="control",
    )(*all_sens, near_kernel, far_kernel, spread, near_hot, far_hot)
    rounds = sum_rounds()
    terms = [partial] if rounds else [lax.psum(partial, SUM_AXES)]
    for masks in rounds or ():
        if len(terms) > 1:
            partial = pl.pallas_call(
                add_kernel, out_shape=shape((rows, LANES)), name="add", compiler_params=PARAMS
            )(*terms)
        terms = exchanged(partial, masks)
    control_grad = pl.pallas_call(
        finish_kernel, out_shape=shape((3, FFD)), name="finish", compiler_params=PARAMS
    )(*terms)
    return (from_rows(adjoint, nodes, cells), control_grad)


def solution(mesh):
    return jax.shard_map(
        body,
        mesh=mesh,
        in_specs=(
            P("nodes", None, ("groups", "cells", "sub")),
            P("nodes", None, ("groups", "cells", "sub")),
            P("nodes", None, None, ("groups", "cells", "sub")),
            P("nodes", None, ("groups", "cells", "sub")),
            P(None, ("cells", "sub")),
            P("nodes"),
            P("nodes", None, ("groups", "cells", "sub")),
            P(None, ("cells", "sub")),
            P(),
            P(),
            P(),
        ),
        out_specs=(P("nodes", None, ("groups", "cells", "sub")), P("groups", None)),
        check_vma=False,
    )
```

```python
import functools
import math

import jax
import jax.numpy as jnp
from jax import lax
from jax.experimental import pallas as pl
from jax.experimental.pallas import tpu as pltpu
from jax.sharding import PartitionSpec as P

SWEEPS = 2
FFD = 512
SUPPORT_RADIUS = 0.3
LANES = 128
CELL_AXES = ("cells", "sub")
SUM_AXES = ("cells", "nodes", "sub")
FACTOR_ROWS = 64
PARAMS = pltpu.CompilerParams(vmem_limit_bytes=24 * 1024 * 1024)
VMEM = pl.BlockSpec(memory_space=pltpu.VMEM)
HBM = pl.BlockSpec(memory_space=pltpu.HBM)


def rows_of(array):
    nodes, rows, cells = array.shape
    blocks = cells // LANES
    split = array.reshape(nodes, rows, blocks, LANES)
    return split.transpose(1, 2, 0, 3).reshape(rows * blocks * nodes, LANES)


def from_rows(array, nodes, cells):
    blocks = cells // LANES
    split = array.reshape(-1, blocks, nodes, LANES)
    return split.transpose(2, 0, 1, 3).reshape(nodes, -1, cells)


def in_hbm(*arrays):
    return [pltpu.with_memory_space_constraint(array, pltpu.HBM) for array in arrays]


def write_one_hot(low_ref, one_hot_ref, first_slot):
    owned = low_ref.shape[1]
    piece = min(512, owned)
    lane = lax.broadcasted_iota(jnp.int32, (piece, LANES), 1).astype(jnp.float32)
    lane = lane.astype(jnp.bfloat16)
    for first in range(0, owned, piece):
        low = low_ref[:, first : first + piece].T.astype(jnp.bfloat16)
        for j in range(one_hot_ref.shape[0] // owned):
            column = low[:, first_slot + j : first_slot + j + 1]
            hit = jnp.broadcast_to(column, (piece, LANES)) == lane
            one_hot_ref[j * owned + first : j * owned + first + piece, :] = jnp.where(
                hit, jnp.bfloat16(1.0), jnp.bfloat16(0.0)
            )


def prepare_kernel(
    nodes,
    off_in,
    inverse_in,
    rhs_in,
    sens_in,
    neigh_in,
    weight_in,
    index_in,
    spread_in,
    start_in,
    cell_in,
    base_in,
    off_ref,
    inverse_ref,
    rhs_ref,
    sens_ref,
    lane_ref,
    step_ref,
    spread_ref,
    low_ref,
    one_hot_ref,
    start_ref,
    left_ref,
    right_ref,
    off_buf,
    sens_buf,
    neigh_buf,
    weight_buf,
    index_buf,
    spread_buf,
    cell_buf,
    base_buf,
    sems,
):
    slots, owned = index_buf.shape
    start = pl.multiple_of(lax.axis_index("nodes") * owned, LANES)
    mine = pl.ds(start, owned)
    pairs = (
        (neigh_in, neigh_buf),
        (index_in.at[:, mine], index_buf),
        (spread_in.at[:, mine], spread_buf),
        (cell_in, cell_buf),
        (base_in.at[:, mine], base_buf),
        (off_in, off_buf),
        (weight_in, weight_buf),
        (sens_in, sens_buf),
        (inverse_in, inverse_ref),
        (rhs_in, rhs_ref),
        (start_in, start_ref),
    )
    copies = [pltpu.make_async_copy(a, b, sems.at[i]) for i, (a, b) in enumerate(pairs)]
    for copy in copies:
        copy.start()

    faces, cells = neigh_buf.shape
    blocks = cells // LANES
    per = blocks * nodes
    first_cell = lax.axis_index(CELL_AXES) * cells
    copies[0].wait()
    for block in range(blocks):
        index = neigh_buf[:, block * LANES : (block + 1) * LANES]
        local = index - first_cell + cells
        lane = jnp.bitwise_and(local, LANES - 1)
        step = jnp.right_shift(local, 7) - block
        step = jnp.where(index >= 0, step, -1)
        for node in range(nodes):
            rows = pl.ds(block * nodes + node, faces, stride=per)
            lane_ref[rows, :] = lane
            step_ref[rows, :] = step

    copies[1].wait()
    copies[2].wait()
    groups = FFD // LANES
    piece = min(512, owned)
    for first in range(0, owned, piece):
        here = slice(first, first + piece)
        high = jnp.right_shift(index_buf[:, here], 7)
        part = lax.broadcasted_iota(jnp.int32, (16, piece), 0)
        part = jnp.where(part < 3 * groups, lax.rem(part, groups), -1)
        for j in range(slots):
            spread_ref[j * 16 : (j + 1) * 16, here] = jnp.where(
                high[j : j + 1] == part, spread_buf[j : j + 1, here], 0.0
            )

    low_ref[...] = jnp.bitwise_and(index_buf[...], LANES - 1).astype(jnp.float32)
    write_one_hot(low_ref, one_hot_ref, 0)

    copies[3].wait()
    left_ref[...] = distance_factors(cell_buf[...], True).T.astype(jnp.bfloat16)
    copies[4].wait()
    right_ref[...] = distance_factors(base_buf[...], False).astype(jnp.bfloat16)

    copies[5].wait()
    off_ref[...] = off_buf[...].astype(jnp.float32)
    copies[6].wait()
    copies[7].wait()
    row_node = lax.rem(lax.broadcasted_iota(jnp.int32, (per, LANES), 0), nodes)
    weights = jnp.zeros((per, LANES), jnp.float32)
    for node in range(nodes):
        weights = jnp.where(row_node == node, weight_buf[node], weights)
    for row in range(0, sens_buf.shape[0], per):
        here = slice(row, row + per)
        sens_ref[here, :] = sens_buf[here, :].astype(jnp.float32) * weights
    for copy in copies[8:]:
        copy.wait()


def take_lanes(table, lanes):
    numbers = lax.GatherDimensionNumbers(
        offset_dims=(),
        collapsed_slice_dims=(1,),
        start_index_map=(1,),
        operand_batching_dims=(0,),
        start_indices_batching_dims=(0,),
    )
    return lax.gather(
        table,
        lanes[..., None],
        numbers,
        slice_sizes=(1, 1),
        mode=lax.GatherScatterMode.PROMISE_IN_BOUNDS,
    )


def sweep_into(
    blocks, far_ref, close_ref, own_ref, rhs_ref, off_ref, inverse_ref, lane_ref, step_ref,
    out_ref, window_ref, table_ref,
):
    per = rhs_ref.shape[0] // 5
    nodes = per // blocks
    faces = lane_ref.shape[0] // per
    odd = lax.rem(lax.axis_index(CELL_AXES), 2)
    place = pl.multiple_of((1 - odd) * 2 * per, 8)
    other = pl.multiple_of(odd * 2 * per, 8)
    width = 3 * per
    for b in range(5):
        rows = slice(b * per, (b + 1) * per)
        base = b * width
        window_ref[pl.ds(base + place, per), :] = close_ref[rows, :]
        window_ref[base + per : base + 2 * per, :] = own_ref[rows, :]
        window_ref[pl.ds(base + other, per), :] = far_ref[rows, :]
    for shift in range(1, 8 // nodes):
        for b in range(5):
            for tile in range(0, width - 8, 8):
                to = ((shift - 1) * 5 + b) * width + tile
                table_ref[to : to + 8, :] = window_ref[
                    pl.ds(b * width + tile + shift * nodes, 8), :
                ]
    for half in range(0, per, 8):
        remaining = [rhs_ref[a * per + half : a * per + half + 8, :] for a in range(5)]
        for f in range(faces):
            lanes = lane_ref[f * per + half : f * per + half + 8, :]
            dist = step_ref[f * per + half : f * per + half + 8, :]
            beside = [jnp.zeros((8, LANES), jnp.float32)] * 5
            for d in range(2 * blocks + 1):
                here = dist == d
                first = half + d * nodes
                for b in range(5):
                    shift, at = first % 8 // nodes, b * width + first // 8 * 8
                    if shift:
                        at = at + (shift - 1) * 5 * width
                        table = table_ref[at : at + 8, :]
                    else:
                        table = window_ref[at : at + 8, :]
                    beside[b] = jnp.where(here, take_lanes(table, lanes), beside[b])
            for a in range(5):
                for b in range(5):
                    row = (f * 25 + 5 * a + b) * per + half
                    remaining[a] = remaining[a] - off_ref[row : row + 8, :] * beside[b]
        for a in range(5):
            total = None
            for b in range(5):
                row = (5 * a + b) * per + half
                term = inverse_ref[row : row + 8, :] * remaining[b]
                total = term if total is None else total + term
            out_ref[a * per + half : a * per + half + 8, :] = total


def sweep_kernel(blocks, *refs):
    sweep_into(blocks, *refs)


def last_sweep_kernel(blocks, *refs):
    ins, rest = refs[:8], refs[8:]
    sens_ref, _, out_ref, sens_out_ref, window_ref, table_ref, part_ref = rest
    sweep_into(blocks, *ins, out_ref, window_ref, table_ref)
    per = out_ref.shape[0] // 5
    nodes = per // blocks
    for k in range(3):
        total = None
        for a in range(5):
            row = (3 * a + k) * per
            term = out_ref[a * per : (a + 1) * per, :] * sens_ref[row : row + per, :]
            total = term if total is None else total + term
        part_ref[k * per : (k + 1) * per, :] = total
    for block in range(blocks):
        total = None
        for node in range(nodes):
            term = part_ref[pl.ds(block * nodes + node, 3, stride=per), :]
            total = term if total is None else total + term
        sens_out_ref[pl.ds(block, 3, stride=blocks), :] = total


def pieces(value, count):
    found = []
    for _ in range(count):
        piece = value.astype(jnp.bfloat16).astype(jnp.float32)
        found.append(piece)
        value = value - piece
    return found


def distance_factors(points, left):
    count = points.shape[1]
    scaled = (points - 0.5) * (1.0 / SUPPORT_RADIUS)
    scaled = jnp.concatenate([scaled, jnp.zeros((5, count), jnp.float32)], axis=0)
    norm = jnp.sum(scaled * scaled, axis=0, keepdims=True)
    norms = pieces(jnp.broadcast_to(norm, (8, count)), 3)
    row = lax.broadcasted_iota(jnp.int32, (8, count), 0)
    norm_block = jnp.zeros((8, count), jnp.float32)
    for place in range(3):
        norm_block = jnp.where(row == place, norms[place], norm_block)
    ones_block = jnp.where(row < 3, 1.0, 0.0)
    first, second, third = pieces(scaled, 3)
    if left:
        dims = [first, first, second, second, first, third]
        dims = [-2.0 * part for part in dims]
        blocks = dims + [norm_block, ones_block]
    else:
        dims = [first, second, first, second, third, first]
        blocks = dims + [ones_block, norm_block]
    return jnp.concatenate(blocks, axis=0)


def wendland_blocks(first_cell, left_ref, right_ref, cells, store):
    owned = right_ref.shape[1]
    tile, wide = min(128, cells), min(256, owned)

    def squares(row, lane):
        left = left_ref[first_cell + row : first_cell + row + tile, :]
        right = right_ref[:, lane : lane + wide]
        return jnp.dot(left, right, preferred_element_type=jnp.float32)

    places = [(row, lane) for lane in range(0, owned, wide) for row in range(0, cells, tile)]
    following = squares(*places[0])
    for at, (row, lane) in enumerate(places):
        squared = jnp.maximum(following, 1e-30)
        if at + 1 < len(places):
            following = squares(*places[at + 1])
        near = jnp.maximum(1.0 - squared * lax.rsqrt(squared), 0.0)
        power = near * near
        store(slice(row, row + tile), slice(lane, lane + wide), power * power * (1.25 - near))


def near_wendland_kernel(left_ref, right_ref, _, kernel_ref):
    cells = kernel_ref.shape[0] // 2

    def store(rows, lanes, kernel):
        first = kernel.astype(jnp.bfloat16)
        rest = (kernel - first.astype(jnp.float32)).astype(jnp.bfloat16)
        kernel_ref[rows, lanes] = first
        kernel_ref[cells + rows.start : cells + rows.stop, lanes] = rest

    wendland_blocks(0, left_ref, right_ref, cells, store)


def far_wendland_kernel(
    left_ref, right_ref, _, adjoint_ref, low_ref, kernel_ref, one_hot_ref, result_ref, sem
):
    copy = pltpu.make_async_copy(adjoint_ref, result_ref, sem)
    copy.start()
    owned = low_ref.shape[1]
    write_one_hot(low_ref, one_hot_ref, low_ref.shape[0] - one_hot_ref.shape[0] // owned)
    cells = kernel_ref.shape[0]

    def store(rows, lanes, kernel):
        kernel_ref[rows, lanes] = kernel

    wendland_blocks(left_ref.shape[0] - cells, left_ref, right_ref, cells, store)
    copy.wait()


def control_kernel(scale, *refs):
    *sens_refs, near_ref, far_ref = refs[:-5]
    spread_ref, near_hot, far_hot, out_ref, column_ref = refs[-5:]
    blocks = sens_refs[0].shape[0] // 3
    half = near_ref.shape[0] // 2
    far, owned = far_ref.shape
    groups = FFD // LANES
    total = sens_refs[0][...]
    for ref in sens_refs[1:]:
        total = total + ref[...]
    total = total * scale

    def halves(value):
        first = value.astype(jnp.bfloat16)
        rest = (value - first.astype(jnp.float32)).astype(jnp.bfloat16)
        return first, rest

    columns = total.T
    for k in range(3):
        for block in range(half // LANES, blocks):
            to = k * far + block * LANES - half
            column = columns[:, k * blocks + block : k * blocks + block + 1]
            column_ref[to : to + LANES, :] = jnp.broadcast_to(column, (LANES, LANES))

    row = lax.broadcasted_iota(jnp.int32, (8, LANES), 0)
    wide = []
    for block in range(half // LANES):
        sens = jnp.zeros((8, LANES), jnp.float32)
        for k in range(3):
            sens = jnp.where(row == k, total[k * blocks + block : k * blocks + block + 1], sens)
        first = sens.astype(jnp.bfloat16).astype(jnp.float32)
        wide.append(jnp.concatenate([first, sens - first], axis=0))
    sens = jnp.concatenate(wide, axis=1).astype(jnp.bfloat16)
    both = jnp.concatenate([sens, sens], axis=1)
    grad = jnp.dot(both, near_ref[...], preferred_element_type=jnp.float32)

    span = min(4 * LANES, owned)
    parts = []
    for first in range(0, owned, span):
        sums = [None] * 3
        for at in range(0, far, 8):
            kernel = far_ref[at : at + 8, first : first + span]
            for k in range(3):
                column = column_ref[k * far + at : k * far + at + 8, :]
                term = kernel * jnp.concatenate([column] * (span // LANES), axis=1)
                sums[k] = term if sums[k] is None else sums[k] + term
        parts.append([jnp.sum(value, axis=0, keepdims=True) for value in sums])
    grad = grad[:8] + grad[8:]
    row = lax.broadcasted_iota(jnp.int32, (16, owned), 0)
    wide = jnp.zeros(row.shape, jnp.float32)
    for k in range(3):
        mine = jnp.logical_and(row >= k * groups, row < (k + 1) * groups)
        part = jnp.concatenate([sums[k] for sums in parts], axis=1)
        wide = jnp.where(mine, grad[k : k + 1] + part, wide)
    grad = wide
    result = None
    places = [
        (ref, first) for ref in (near_hot, far_hot) for first in range(0, ref.shape[0], owned)
    ]
    for j, (ref, first) in enumerate(places):
        term = jnp.dot(
            jnp.concatenate(halves(grad * spread_ref[j * 16 : (j + 1) * 16, :]), axis=0),
            ref[first : first + owned, :],
            preferred_element_type=jnp.float32,
        )
        result = term if result is None else result + term
    result = result[:16] + result[16:]
    out_ref[...] = result[: 3 * groups]


def tree(values):
    while len(values) > 1:
        values = [sum(values[i : i + 2]) for i in range(0, len(values), 2)]
    return values[0]


def add_kernel(*refs):
    refs[-1][...] = tree([ref[...] for ref in refs[:-1]])


def finish_kernel(*refs):
    total, out_ref = tree([ref[...] for ref in refs[:-1]]), refs[-1]
    groups = out_ref.shape[1] // LANES
    for k in range(3):
        for group in range(groups):
            row = k * groups + group
            out_ref[k : k + 1, group * LANES : (group + 1) * LANES] = total[row : row + 1]


def sum_rounds():
    lines, nodes, cores = (lax.axis_size(axis) for axis in SUM_AXES)
    if any(size & (size - 1) for size in (lines, nodes, cores)):
        return None
    near = [cores >> 1 >> i for i in range(cores.bit_length() - 1)]
    node_bits = [cores << i for i in range(nodes.bit_length() - 1)]
    line_bits = [cores * nodes << i for i in range(lines.bit_length() - 1)]
    bits = near + line_bits[:2] + node_bits[:1] + line_bits[2:] + node_bits[1:]
    rounds = []
    for first in range(0, len(bits), 2):
        masks = bits[first : first + 2]
        if len(masks) == 2:
            masks = masks + [masks[0] | masks[1]]
        rounds.append([mask | (cores - 1) for mask in masks] if first else masks)
    return rounds


def exchanged(value, masks):
    peers = lax.axis_size(SUM_AXES)
    return [value] + [
        lax.ppermute(value, SUM_AXES, [(i, i ^ mask) for i in range(peers)]) for mask in masks
    ]


def body(
    adjoint_start,
    adjoint_rhs,
    off_blocks,
    diag_inverse,
    neighbours,
    node_weights,
    sens_blocks,
    cell_points,
    base_points,
    ffd_index,
    ffd_weight,
):
    nodes, _, cells = adjoint_start.shape
    faces = off_blocks.shape[1]
    blocks = cells // LANES
    per = blocks * nodes
    slots = ffd_index.shape[1]
    far_slots = slots // 2
    owned = base_points.shape[1] // lax.axis_size("nodes")
    peers = lax.axis_size(CELL_AXES)
    cores = lax.axis_size("sub")
    node_peers = lax.axis_size("nodes")
    f32, i32, bf16 = jnp.float32, jnp.int32, jnp.bfloat16

    def shape(dims, dtype=f32):
        return jax.ShapeDtypeStruct(dims, dtype)

    def cost(flops, moved):
        return pl.CostEstimate(flops=flops, bytes_accessed=moved, transcendentals=0)

    def swaps(array):
        close = lax.ppermute(array, CELL_AXES, [(i, i ^ 1) for i in range(peers)])
        pairs = []
        for i in range(peers):
            line, core = divmod(i, cores)
            for node in range(node_peers):
                j, beside = (i + 1 if i % 2 else i - 1), node
                if not 0 <= j < peers:
                    j, beside = i, (node ^ 1 if node_peers % 2 == 0 else node)
                to_line, to_core = divmod(j, cores)
                pairs.append(
                    (
                        (line * node_peers + node) * cores + core,
                        (to_line * node_peers + beside) * cores + to_core,
                    )
                )
        return lax.ppermute(array, SUM_AXES, pairs), close

    adjoint = rows_of(adjoint_start)
    far, close = swaps(adjoint)
    prepared = pl.pallas_call(
        functools.partial(prepare_kernel, nodes),
        out_shape=(
            shape((faces * 25 * per, LANES)),
            shape((25 * per, LANES)),
            shape((5 * per, LANES)),
            shape((15 * per, LANES)),
            shape((faces * per, LANES), i32),
            shape((faces * per, LANES), i32),
            shape((slots * 16, owned)),
            shape((slots, owned)),
            shape(((slots - far_slots) * owned, LANES), bf16),
            shape((5 * per, LANES)),
            shape((cells, FACTOR_ROWS), bf16),
            shape((FACTOR_ROWS, owned), bf16),
        ),
        in_specs=[HBM] * 11,
        out_specs=(VMEM,) * 12,
        scratch_shapes=[
            pltpu.VMEM((faces * 25 * per, LANES), bf16),
            pltpu.VMEM((15 * per, LANES), bf16),
            pltpu.VMEM((faces, cells), i32),
            pltpu.SMEM((nodes,), f32),
            pltpu.VMEM((slots, owned), i32),
            pltpu.VMEM((slots, owned), f32),
            pltpu.VMEM((3, cells), f32),
            pltpu.VMEM((3, owned), f32),
            pltpu.SemaphoreType.DMA((11,)),
        ],
        compiler_params=PARAMS,
        cost_estimate=cost(10**9, 10**7),
        name="prepare",
    )(
        *in_hbm(
            rows_of(off_blocks.reshape(nodes, faces * 25, cells)),
            rows_of(diag_inverse),
            rows_of(adjoint_rhs),
            rows_of(sens_blocks),
            neighbours,
            node_weights,
            ffd_index.T,
            ffd_weight.T,
            adjoint,
            cell_points,
            base_points,
        )
    )
    off, inverse, rhs, sens, lane, step, spread, low, near_hot, adjoint, left, right = prepared
    scratch = [
        pltpu.VMEM((3 * 5 * per, LANES), f32),
        pltpu.VMEM((max(8 // nodes - 1, 1) * 3 * 5 * per, LANES), f32),
    ]
    sweep_cost = cost(2 * 10 * 35 * cells, 4 * faces * 25 * per * LANES)

    for _ in range(SWEEPS - 1):
        adjoint = pl.pallas_call(
            functools.partial(sweep_kernel, blocks),
            out_shape=shape((5 * per, LANES)),
            in_specs=[VMEM] * 8,
            out_specs=VMEM,
            scratch_shapes=scratch,
            compiler_params=PARAMS,
            cost_estimate=sweep_cost,
            name="sweep",
        )(far, close, adjoint, rhs, off, inverse, lane, step)
        far, close = swaps(adjoint)

    half = cells // 2 // LANES * LANES
    wendland_cost = cost(10**9, 10**7)
    near_shape = shape((2 * half, owned), bf16)
    far_shape = shape((cells - half, owned))
    near_kernel = pl.pallas_call(
        near_wendland_kernel,
        out_shape=near_shape,
        in_specs=[VMEM] * 3,
        out_specs=VMEM,
        compiler_params=PARAMS,
        cost_estimate=wendland_cost,
        name="near_wendland",
    )(left, right, adjoint)
    adjoint, part_sens = pl.pallas_call(
        functools.partial(last_sweep_kernel, blocks),
        out_shape=(shape((5 * per, LANES)), shape((3 * blocks, LANES))),
        in_specs=[VMEM] * 9 + [pl.BlockSpec(memory_space=pl.ANY)],
        out_specs=(VMEM, VMEM),
        scratch_shapes=scratch + [pltpu.VMEM((3 * per, LANES), f32)],
        compiler_params=PARAMS,
        cost_estimate=sweep_cost,
        name="last_sweep",
    )(far, close, adjoint, rhs, off, inverse, lane, step, sens, near_kernel)

    all_sens = [part_sens]
    for shift in range(1, node_peers):
        ring = [(i, (i + shift) % node_peers) for i in range(node_peers)]
        all_sens.append(lax.ppermute(part_sens, "nodes", ring))
    hot_shape = shape((far_slots * owned, LANES), bf16)
    far_kernel, far_hot, adjoint = pl.pallas_call(
        far_wendland_kernel,
        out_shape=(far_shape, hot_shape, shape((5 * per, LANES))),
        in_specs=[VMEM] * 5,
        out_specs=(VMEM, VMEM, HBM),
        scratch_shapes=[pltpu.SemaphoreType.DMA],
        compiler_params=PARAMS,
        cost_estimate=wendland_cost,
        name="far_wendland",
    )(left, right, part_sens, adjoint, low)
    scale = 4.0 / math.sqrt(cells * peers)
    rows = 3 * FFD // LANES
    partial = pl.pallas_call(
        functools.partial(control_kernel, scale),
        out_shape=shape((rows, LANES)),
        in_specs=[VMEM] * (len(all_sens) + 5),
        out_specs=VMEM,
        scratch_shapes=[pltpu.VMEM((3 * (cells - half), LANES), f32)],
        compiler_params=PARAMS,
        name="control",
    )(*all_sens, near_kernel, far_kernel, spread, near_hot, far_hot)
    rounds = sum_rounds()
    terms = [partial] if rounds else [lax.psum(partial, SUM_AXES)]
    for masks in rounds or ():
        if len(terms) > 1:
            partial = pl.pallas_call(
                add_kernel, out_shape=shape((rows, LANES)), name="add", compiler_params=PARAMS
            )(*terms)
        terms = exchanged(partial, masks)
    control_grad = pl.pallas_call(
        finish_kernel, out_shape=shape((3, FFD)), name="finish", compiler_params=PARAMS
    )(*terms)
    return (from_rows(adjoint, nodes, cells), control_grad)


def solution(mesh):
    return jax.shard_map(
        body,
        mesh=mesh,
        in_specs=(
            P("nodes", None, ("groups", "cells", "sub")),
            P("nodes", None, ("groups", "cells", "sub")),
            P("nodes", None, None, ("groups", "cells", "sub")),
            P("nodes", None, ("groups", "cells", "sub")),
            P(None, ("cells", "sub")),
            P("nodes"),
            P("nodes", None, ("groups", "cells", "sub")),
            P(None, ("cells", "sub")),
            P(),
            P(),
            P(),
        ),
        out_specs=(P("nodes", None, ("groups", "cells", "sub")), P("groups", None)),
        check_vma=False,
    )
```

```python
import functools
import math

import jax
import jax.numpy as jnp
from jax import lax
from jax.experimental import pallas as pl
from jax.experimental.pallas import tpu as pltpu
from jax.sharding import PartitionSpec as P

SWEEPS = 2
FFD = 512
SUPPORT_RADIUS = 0.3
LANES = 128
CELL_AXES = ("cells", "sub")
SUM_AXES = ("cells", "nodes", "sub")
FACTOR_ROWS = 64
PARAMS = pltpu.CompilerParams(vmem_limit_bytes=24 * 1024 * 1024)
VMEM = pl.BlockSpec(memory_space=pltpu.VMEM)
HBM = pl.BlockSpec(memory_space=pltpu.HBM)


def rows_of(array):
    nodes, rows, cells = array.shape
    blocks = cells // LANES
    split = array.reshape(nodes, rows, blocks, LANES)
    return split.transpose(1, 2, 0, 3).reshape(rows * blocks * nodes, LANES)


def from_rows(array, nodes, cells):
    blocks = cells // LANES
    split = array.reshape(-1, blocks, nodes, LANES)
    return split.transpose(2, 0, 1, 3).reshape(nodes, -1, cells)


def in_hbm(*arrays):
    return [pltpu.with_memory_space_constraint(array, pltpu.HBM) for array in arrays]


def one_hot_steps(low_ref, one_hot_ref, first_slot):
    owned = low_ref.shape[1]
    piece = min(512, owned)

    def step(first, j):
        lane = lax.broadcasted_iota(jnp.int32, (piece, LANES), 1).astype(jnp.float32)
        lane = lane.astype(jnp.bfloat16)
        low = low_ref[:, first : first + piece].T.astype(jnp.bfloat16)
        column = low[:, first_slot + j : first_slot + j + 1]
        hit = jnp.broadcast_to(column, (piece, LANES)) == lane
        one_hot_ref[j * owned + first : j * owned + first + piece, :] = jnp.where(
            hit, jnp.bfloat16(1.0), jnp.bfloat16(0.0)
        )

    return [
        functools.partial(step, first, j)
        for first in range(0, owned, piece)
        for j in range(one_hot_ref.shape[0] // owned)
    ]


def prepare_kernel(
    nodes,
    off_in,
    inverse_in,
    rhs_in,
    sens_in,
    neigh_in,
    weight_in,
    index_in,
    spread_in,
    start_in,
    cell_in,
    base_in,
    off_ref,
    inverse_ref,
    rhs_ref,
    sens_ref,
    lane_ref,
    step_ref,
    spread_ref,
    low_ref,
    start_ref,
    left_ref,
    right_ref,
    kernel_ref,
    off_buf,
    sens_buf,
    neigh_buf,
    weight_buf,
    index_buf,
    spread_buf,
    cell_buf,
    base_buf,
    sems,
):
    slots, owned = index_buf.shape
    start = pl.multiple_of(lax.axis_index("nodes") * owned, LANES)
    mine = pl.ds(start, owned)
    pairs = (
        (neigh_in, neigh_buf),
        (index_in.at[:, mine], index_buf),
        (spread_in.at[:, mine], spread_buf),
        (cell_in, cell_buf),
        (base_in.at[:, mine], base_buf),
        (off_in, off_buf),
        (weight_in, weight_buf),
        (sens_in, sens_buf),
        (inverse_in, inverse_ref),
        (rhs_in, rhs_ref),
        (start_in, start_ref),
    )
    copies = [pltpu.make_async_copy(a, b, sems.at[i]) for i, (a, b) in enumerate(pairs)]
    for copy in copies:
        copy.start()

    faces, cells = neigh_buf.shape
    blocks = cells // LANES
    per = blocks * nodes
    first_cell = lax.axis_index(CELL_AXES) * cells
    copies[0].wait()
    for block in range(blocks):
        index = neigh_buf[:, block * LANES : (block + 1) * LANES]
        local = index - first_cell + cells
        lane = jnp.bitwise_and(local, LANES - 1)
        step = jnp.right_shift(local, 7) - block
        step = jnp.where(index >= 0, step, -1)
        for node in range(nodes):
            rows = pl.ds(block * nodes + node, faces, stride=per)
            lane_ref[rows, :] = lane
            step_ref[rows, :] = step

    copies[1].wait()
    copies[2].wait()
    groups = FFD // LANES
    piece = min(512, owned)
    for first in range(0, owned, piece):
        here = slice(first, first + piece)
        high = jnp.right_shift(index_buf[:, here], 7)
        part = lax.broadcasted_iota(jnp.int32, (16, piece), 0)
        part = jnp.where(part < 3 * groups, lax.rem(part, groups), -1)
        for j in range(slots):
            spread_ref[j * 16 : (j + 1) * 16, here] = jnp.where(
                high[j : j + 1] == part, spread_buf[j : j + 1, here], 0.0
            )

    low_ref[...] = jnp.bitwise_and(index_buf[...], LANES - 1).astype(jnp.float32)

    copies[3].wait()
    left_ref[...] = distance_factors(cell_buf[...], True).T.astype(jnp.bfloat16)
    copies[4].wait()
    right_ref[...] = distance_factors(base_buf[...], False).astype(jnp.bfloat16)
    wendland_blocks(0, left_ref, right_ref, kernel_ref)

    copies[5].wait()
    off_ref[...] = off_buf[...].astype(jnp.float32)
    copies[6].wait()
    copies[7].wait()
    row_node = lax.rem(lax.broadcasted_iota(jnp.int32, (per, LANES), 0), nodes)
    weights = jnp.zeros((per, LANES), jnp.float32)
    for node in range(nodes):
        weights = jnp.where(row_node == node, weight_buf[node], weights)
    for row in range(0, sens_buf.shape[0], per):
        here = slice(row, row + per)
        sens_ref[here, :] = sens_buf[here, :].astype(jnp.float32) * weights
    for copy in copies[8:]:
        copy.wait()


def take_lanes(table, lanes):
    numbers = lax.GatherDimensionNumbers(
        offset_dims=(),
        collapsed_slice_dims=(1,),
        start_index_map=(1,),
        operand_batching_dims=(0,),
        start_indices_batching_dims=(0,),
    )
    return lax.gather(
        table,
        lanes[..., None],
        numbers,
        slice_sizes=(1, 1),
        mode=lax.GatherScatterMode.PROMISE_IN_BOUNDS,
    )


def sweep_into(
    blocks, far_ref, close_ref, own_ref, rhs_ref, off_ref, inverse_ref, lane_ref, step_ref,
    out_ref, window_ref, table_ref,
):
    per = rhs_ref.shape[0] // 5
    nodes = per // blocks
    faces = lane_ref.shape[0] // per
    odd = lax.rem(lax.axis_index(CELL_AXES), 2)
    place = pl.multiple_of((1 - odd) * 2 * per, 8)
    other = pl.multiple_of(odd * 2 * per, 8)
    width = 3 * per
    for b in range(5):
        rows = slice(b * per, (b + 1) * per)
        base = b * width
        window_ref[pl.ds(base + place, per), :] = close_ref[rows, :]
        window_ref[base + per : base + 2 * per, :] = own_ref[rows, :]
        window_ref[pl.ds(base + other, per), :] = far_ref[rows, :]
    for shift in range(1, 8 // nodes):
        for b in range(5):
            for tile in range(0, width - 8, 8):
                to = ((shift - 1) * 5 + b) * width + tile
                table_ref[to : to + 8, :] = window_ref[
                    pl.ds(b * width + tile + shift * nodes, 8), :
                ]
    for half in range(0, per, 8):
        remaining = [rhs_ref[a * per + half : a * per + half + 8, :] for a in range(5)]
        for f in range(faces):
            lanes = lane_ref[f * per + half : f * per + half + 8, :]
            dist = step_ref[f * per + half : f * per + half + 8, :]
            beside = [jnp.zeros((8, LANES), jnp.float32)] * 5
            for d in range(2 * blocks + 1):
                here = dist == d
                first = half + d * nodes
                for b in range(5):
                    shift, at = first % 8 // nodes, b * width + first // 8 * 8
                    if shift:
                        at = at + (shift - 1) * 5 * width
                        table = table_ref[at : at + 8, :]
                    else:
                        table = window_ref[at : at + 8, :]
                    beside[b] = jnp.where(here, take_lanes(table, lanes), beside[b])
            for a in range(5):
                for b in range(5):
                    row = (f * 25 + 5 * a + b) * per + half
                    remaining[a] = remaining[a] - off_ref[row : row + 8, :] * beside[b]
        for a in range(5):
            total = None
            for b in range(5):
                row = (5 * a + b) * per + half
                term = inverse_ref[row : row + 8, :] * remaining[b]
                total = term if total is None else total + term
            out_ref[a * per + half : a * per + half + 8, :] = total


def sweep_kernel(blocks, *refs):
    sweep_into(blocks, *refs)


def last_sweep_kernel(blocks, *refs):
    ins, rest = refs[:8], refs[8:]
    sens_ref, _, out_ref, sens_out_ref, window_ref, table_ref, part_ref = rest
    sweep_into(blocks, *ins, out_ref, window_ref, table_ref)
    per = out_ref.shape[0] // 5
    nodes = per // blocks
    for k in range(3):
        total = None
        for a in range(5):
            row = (3 * a + k) * per
            term = out_ref[a * per : (a + 1) * per, :] * sens_ref[row : row + per, :]
            total = term if total is None else total + term
        part_ref[k * per : (k + 1) * per, :] = total
    for block in range(blocks):
        total = None
        for node in range(nodes):
            term = part_ref[pl.ds(block * nodes + node, 3, stride=per), :]
            total = term if total is None else total + term
        sens_out_ref[pl.ds(block, 3, stride=blocks), :] = total


def pieces(value, count):
    found = []
    for _ in range(count):
        piece = value.astype(jnp.bfloat16).astype(jnp.float32)
        found.append(piece)
        value = value - piece
    return found


def distance_factors(points, left):
    count = points.shape[1]
    scaled = (points - 0.5) * (1.0 / SUPPORT_RADIUS)
    scaled = jnp.concatenate([scaled, jnp.zeros((5, count), jnp.float32)], axis=0)
    norm = jnp.sum(scaled * scaled, axis=0, keepdims=True)
    norms = pieces(jnp.broadcast_to(norm, (8, count)), 3)
    row = lax.broadcasted_iota(jnp.int32, (8, count), 0)
    norm_block = jnp.zeros((8, count), jnp.float32)
    for place in range(3):
        norm_block = jnp.where(row == place, norms[place], norm_block)
    ones_block = jnp.where(row < 3, 1.0, 0.0)
    first, second, third = pieces(scaled, 3)
    if left:
        dims = [first, first, second, second, first, third]
        dims = [-2.0 * part for part in dims]
        blocks = dims + [norm_block, ones_block]
    else:
        dims = [first, second, first, second, third, first]
        blocks = dims + [ones_block, norm_block]
    return jnp.concatenate(blocks, axis=0)


def wendland_blocks(first_cell, left_ref, right_ref, kernel_ref, steps=()):
    cells, owned = kernel_ref.shape[0] // 2, kernel_ref.shape[1]
    tile, wide = min(128, cells), min(256, owned)

    def squares(row, lane):
        left = left_ref[first_cell + row : first_cell + row + tile, :]
        right = right_ref[:, lane : lane + wide]
        return jnp.dot(left, right, preferred_element_type=jnp.float32)

    places = [(row, lane) for lane in range(0, owned, wide) for row in range(0, cells, tile)]
    following = squares(*places[0])
    done = 0
    for at, (row, lane) in enumerate(places):
        squared = jnp.maximum(following, 1e-30)
        if at + 1 < len(places):
            following = squares(*places[at + 1])
        while done * len(places) < len(steps) * (at + 1):
            steps[done]()
            done += 1
        near = jnp.maximum(1.0 - squared * lax.rsqrt(squared), 0.0)
        power = near * near
        kernel = power * power * (1.25 - near)
        first = kernel.astype(jnp.bfloat16)
        rest = (kernel - first.astype(jnp.float32)).astype(jnp.bfloat16)
        here = slice(lane, lane + wide)
        kernel_ref[row : row + tile, here] = first
        kernel_ref[cells + row : cells + row + tile, here] = rest


def near_wendland_kernel(first_cell, left_ref, right_ref, low_ref, _, kernel_ref, one_hot_ref):
    steps = one_hot_steps(low_ref, one_hot_ref, 0)
    wendland_blocks(first_cell, left_ref, right_ref, kernel_ref, steps)


def far_wendland_kernel(first_cell, left_ref, right_ref, low_ref, _, adjoint_ref, *rest):
    kernel_ref, one_hot_ref, result_ref, sem = rest
    copy = pltpu.make_async_copy(adjoint_ref, result_ref, sem)
    copy.start()
    first_slot = low_ref.shape[0] - one_hot_ref.shape[0] // low_ref.shape[1]
    steps = one_hot_steps(low_ref, one_hot_ref, first_slot)
    wendland_blocks(first_cell, left_ref, right_ref, kernel_ref, steps)
    copy.wait()


def control_kernel(scale, *refs):
    *sens_refs, first_ref, near_ref, far_ref = refs[:-4]
    spread_ref, near_hot, far_hot, out_ref = refs[-4:]
    blocks = sens_refs[0].shape[0] // 3
    groups = FFD // LANES
    total = sens_refs[0][...]
    for ref in sens_refs[1:]:
        total = total + ref[...]
    total = total * scale

    def halves(value):
        first = value.astype(jnp.bfloat16)
        rest = (value - first.astype(jnp.float32)).astype(jnp.bfloat16)
        return first, rest

    row = lax.broadcasted_iota(jnp.int32, (8, LANES), 0)
    wide = []
    for block in range(blocks):
        sens = jnp.zeros((8, LANES), jnp.float32)
        for k in range(3):
            sens = jnp.where(row == k, total[k * blocks + block : k * blocks + block + 1], sens)
        first = sens.astype(jnp.bfloat16).astype(jnp.float32)
        wide.append(jnp.concatenate([first, sens - first], axis=0))
    sens = jnp.concatenate(wide, axis=1).astype(jnp.bfloat16)
    grad = None
    cell = 0
    for ref in (first_ref, near_ref, far_ref):
        part = sens[:, cell : cell + ref.shape[0] // 2]
        cell += ref.shape[0] // 2
        both = jnp.concatenate([part, part], axis=1)
        term = jnp.dot(both, ref[...], preferred_element_type=jnp.float32)
        grad = term if grad is None else grad + term
    grad = grad[:8] + grad[8:]
    row = lax.broadcasted_iota(jnp.int32, (16, grad.shape[1]), 0)
    wide = jnp.zeros(row.shape, jnp.float32)
    for k in range(3):
        mine = jnp.logical_and(row >= k * groups, row < (k + 1) * groups)
        wide = jnp.where(mine, grad[k : k + 1], wide)
    grad = wide
    owned = grad.shape[1]
    result = None
    places = [
        (ref, first) for ref in (near_hot, far_hot) for first in range(0, ref.shape[0], owned)
    ]
    for j, (ref, first) in enumerate(places):
        term = jnp.dot(
            jnp.concatenate(halves(grad * spread_ref[j * 16 : (j + 1) * 16, :]), axis=0),
            ref[first : first + owned, :],
            preferred_element_type=jnp.float32,
        )
        result = term if result is None else result + term
    result = result[:16] + result[16:]
    out_ref[...] = result[: 3 * groups]


def tree(values):
    while len(values) > 1:
        values = [sum(values[i : i + 2]) for i in range(0, len(values), 2)]
    return values[0]


def add_kernel(*refs):
    refs[-1][...] = tree([ref[...] for ref in refs[:-1]])


def finish_kernel(*refs):
    total, out_ref = tree([ref[...] for ref in refs[:-1]]), refs[-1]
    groups = out_ref.shape[1] // LANES
    for k in range(3):
        for group in range(groups):
            row = k * groups + group
            out_ref[k : k + 1, group * LANES : (group + 1) * LANES] = total[row : row + 1]


def sum_rounds():
    lines, nodes, cores = (lax.axis_size(axis) for axis in SUM_AXES)
    if any(size & (size - 1) for size in (lines, nodes, cores)):
        return None
    near = [cores >> 1 >> i for i in range(cores.bit_length() - 1)]
    node_bits = [cores << i for i in range(nodes.bit_length() - 1)]
    line_bits = [cores * nodes << i for i in range(lines.bit_length() - 1)]
    bits = near + line_bits[:2] + node_bits[:1] + line_bits[2:] + node_bits[1:]
    rounds = []
    for first in range(0, len(bits), 2):
        masks = bits[first : first + 2]
        if len(masks) == 2:
            masks = masks + [masks[0] | masks[1]]
        rounds.append([mask | (cores - 1) for mask in masks] if first else masks)
    return rounds


def exchanged(value, masks):
    peers = lax.axis_size(SUM_AXES)
    return [value] + [
        lax.ppermute(value, SUM_AXES, [(i, i ^ mask) for i in range(peers)]) for mask in masks
    ]


def body(
    adjoint_start,
    adjoint_rhs,
    off_blocks,
    diag_inverse,
    neighbours,
    node_weights,
    sens_blocks,
    cell_points,
    base_points,
    ffd_index,
    ffd_weight,
):
    nodes, _, cells = adjoint_start.shape
    faces = off_blocks.shape[1]
    blocks = cells // LANES
    per = blocks * nodes
    slots = ffd_index.shape[1]
    far_slots = slots // 2
    parts = [cells // 8, cells // 2]
    parts.append(cells - sum(parts))
    owned = base_points.shape[1] // lax.axis_size("nodes")
    peers = lax.axis_size(CELL_AXES)
    cores = lax.axis_size("sub")
    node_peers = lax.axis_size("nodes")
    f32, i32, bf16 = jnp.float32, jnp.int32, jnp.bfloat16

    def shape(dims, dtype=f32):
        return jax.ShapeDtypeStruct(dims, dtype)

    def cost(flops, moved):
        return pl.CostEstimate(flops=flops, bytes_accessed=moved, transcendentals=0)

    def swaps(array):
        close = lax.ppermute(array, CELL_AXES, [(i, i ^ 1) for i in range(peers)])
        pairs = []
        for i in range(peers):
            line, core = divmod(i, cores)
            for node in range(node_peers):
                j, beside = (i + 1 if i % 2 else i - 1), node
                if not 0 <= j < peers:
                    j, beside = i, (node ^ 1 if node_peers % 2 == 0 else node)
                to_line, to_core = divmod(j, cores)
                pairs.append(
                    (
                        (line * node_peers + node) * cores + core,
                        (to_line * node_peers + beside) * cores + to_core,
                    )
                )
        return lax.ppermute(array, SUM_AXES, pairs), close

    adjoint = rows_of(adjoint_start)
    far, close = swaps(adjoint)
    prepared = pl.pallas_call(
        functools.partial(prepare_kernel, nodes),
        out_shape=(
            shape((faces * 25 * per, LANES)),
            shape((25 * per, LANES)),
            shape((5 * per, LANES)),
            shape((15 * per, LANES)),
            shape((faces * per, LANES), i32),
            shape((faces * per, LANES), i32),
            shape((slots * 16, owned)),
            shape((slots, owned)),
            shape((5 * per, LANES)),
            shape((cells, FACTOR_ROWS), bf16),
            shape((FACTOR_ROWS, owned), bf16),
            shape((2 * parts[0], owned), bf16),
        ),
        in_specs=[HBM] * 11,
        out_specs=(VMEM,) * 12,
        scratch_shapes=[
            pltpu.VMEM((faces * 25 * per, LANES), bf16),
            pltpu.VMEM((15 * per, LANES), bf16),
            pltpu.VMEM((faces, cells), i32),
            pltpu.SMEM((nodes,), f32),
            pltpu.VMEM((slots, owned), i32),
            pltpu.VMEM((slots, owned), f32),
            pltpu.VMEM((3, cells), f32),
            pltpu.VMEM((3, owned), f32),
            pltpu.SemaphoreType.DMA((11,)),
        ],
        compiler_params=PARAMS,
        cost_estimate=cost(10**9, 10**7),
        name="prepare",
    )(
        *in_hbm(
            rows_of(off_blocks.reshape(nodes, faces * 25, cells)),
            rows_of(diag_inverse),
            rows_of(adjoint_rhs),
            rows_of(sens_blocks),
            neighbours,
            node_weights,
            ffd_index.T,
            ffd_weight.T,
            adjoint,
            cell_points,
            base_points,
        )
    )
    off, inverse, rhs, sens, lane, step, spread, low, adjoint, left, right, first_kernel = prepared
    scratch = [
        pltpu.VMEM((3 * 5 * per, LANES), f32),
        pltpu.VMEM((max(8 // nodes - 1, 1) * 3 * 5 * per, LANES), f32),
    ]
    sweep_cost = cost(2 * 10 * 35 * cells, 4 * faces * 25 * per * LANES)

    for _ in range(SWEEPS - 1):
        adjoint = pl.pallas_call(
            functools.partial(sweep_kernel, blocks),
            out_shape=shape((5 * per, LANES)),
            in_specs=[VMEM] * 8,
            out_specs=VMEM,
            scratch_shapes=scratch,
            compiler_params=PARAMS,
            cost_estimate=sweep_cost,
            name="sweep",
        )(far, close, adjoint, rhs, off, inverse, lane, step)
        far, close = swaps(adjoint)

    wendland_cost = cost(10**9, 10**7)
    near_kernel, near_hot = pl.pallas_call(
        functools.partial(near_wendland_kernel, parts[0]),
        out_shape=(
            shape((2 * parts[1], owned), bf16),
            shape(((slots - far_slots) * owned, LANES), bf16),
        ),
        in_specs=[VMEM] * 4,
        out_specs=(VMEM, VMEM),
        compiler_params=PARAMS,
        cost_estimate=wendland_cost,
        name="near_wendland",
    )(left, right, low, adjoint)
    adjoint, part_sens = pl.pallas_call(
        functools.partial(last_sweep_kernel, blocks),
        out_shape=(shape((5 * per, LANES)), shape((3 * blocks, LANES))),
        in_specs=[VMEM] * 9 + [pl.BlockSpec(memory_space=pl.ANY)],
        out_specs=(VMEM, VMEM),
        scratch_shapes=scratch + [pltpu.VMEM((3 * per, LANES), f32)],
        compiler_params=PARAMS,
        cost_estimate=sweep_cost,
        name="last_sweep",
    )(far, close, adjoint, rhs, off, inverse, lane, step, sens, near_kernel)

    all_sens = [part_sens]
    for shift in range(1, node_peers):
        ring = [(i, (i + shift) % node_peers) for i in range(node_peers)]
        all_sens.append(lax.ppermute(part_sens, "nodes", ring))
    far_kernel, far_hot, adjoint = pl.pallas_call(
        functools.partial(far_wendland_kernel, parts[0] + parts[1]),
        out_shape=(
            shape((2 * parts[2], owned), bf16),
            shape((far_slots * owned, LANES), bf16),
            shape((5 * per, LANES)),
        ),
        in_specs=[VMEM] * 5,
        out_specs=(VMEM, VMEM, HBM),
        scratch_shapes=[pltpu.SemaphoreType.DMA],
        compiler_params=PARAMS,
        cost_estimate=wendland_cost,
        name="far_wendland",
    )(left, right, low, part_sens, adjoint)
    scale = 4.0 / math.sqrt(cells * peers)
    rows = 3 * FFD // LANES
    partial = pl.pallas_call(
        functools.partial(control_kernel, scale),
        out_shape=shape((rows, LANES)),
        in_specs=[VMEM] * (len(all_sens) + 6),
        out_specs=VMEM,
        compiler_params=PARAMS,
        name="control",
    )(*all_sens, first_kernel, near_kernel, far_kernel, spread, near_hot, far_hot)
    rounds = sum_rounds()
    terms = [partial] if rounds else [lax.psum(partial, SUM_AXES)]
    for masks in rounds or ():
        if len(terms) > 1:
            partial = pl.pallas_call(
                add_kernel, out_shape=shape((rows, LANES)), name="add", compiler_params=PARAMS
            )(*terms)
        terms = exchanged(partial, masks)
    control_grad = pl.pallas_call(
        finish_kernel, out_shape=shape((3, FFD)), name="finish", compiler_params=PARAMS
    )(*terms)
    return (from_rows(adjoint, nodes, cells), control_grad)


def solution(mesh):
    return jax.shard_map(
        body,
        mesh=mesh,
        in_specs=(
            P("nodes", None, ("groups", "cells", "sub")),
            P("nodes", None, ("groups", "cells", "sub")),
            P("nodes", None, None, ("groups", "cells", "sub")),
            P("nodes", None, ("groups", "cells", "sub")),
            P(None, ("cells", "sub")),
            P("nodes"),
            P("nodes", None, ("groups", "cells", "sub")),
            P(None, ("cells", "sub")),
            P(),
            P(),
            P(),
        ),
        out_specs=(P("nodes", None, ("groups", "cells", "sub")), P("groups", None)),
        check_vma=False,
    )
```

```python
import functools
import math

import jax
import jax.numpy as jnp
from jax import lax
from jax.experimental import pallas as pl
from jax.experimental.pallas import tpu as pltpu
from jax.sharding import PartitionSpec as P

SWEEPS = 2
FFD = 512
SUPPORT_RADIUS = 0.3
LANES = 128
CELL_AXES = ("cells", "sub")
SUM_AXES = ("cells", "nodes", "sub")
FACTOR_ROWS = 64
PARAMS = pltpu.CompilerParams(vmem_limit_bytes=24 * 1024 * 1024)
VMEM = pl.BlockSpec(memory_space=pltpu.VMEM)
HBM = pl.BlockSpec(memory_space=pltpu.HBM)


def rows_of(array):
    nodes, rows, cells = array.shape
    blocks = cells // LANES
    split = array.reshape(nodes, rows, blocks, LANES)
    return split.transpose(1, 2, 0, 3).reshape(rows * blocks * nodes, LANES)


def from_rows(array, nodes, cells):
    blocks = cells // LANES
    split = array.reshape(-1, blocks, nodes, LANES)
    return split.transpose(2, 0, 1, 3).reshape(nodes, -1, cells)


def in_hbm(*arrays):
    return [pltpu.with_memory_space_constraint(array, pltpu.HBM) for array in arrays]


def write_one_hot(low_ref, one_hot_ref, first_slot):
    owned = low_ref.shape[1]
    piece = min(512, owned)
    lane = lax.broadcasted_iota(jnp.int32, (piece, LANES), 1).astype(jnp.float32)
    lane = lane.astype(jnp.bfloat16)
    for first in range(0, owned, piece):
        low = low_ref[:, first : first + piece].T.astype(jnp.bfloat16)
        for j in range(one_hot_ref.shape[0] // owned):
            column = low[:, first_slot + j : first_slot + j + 1]
            hit = jnp.broadcast_to(column, (piece, LANES)) == lane
            one_hot_ref[j * owned + first : j * owned + first + piece, :] = jnp.where(
                hit, jnp.bfloat16(1.0), jnp.bfloat16(0.0)
            )


def prepare_kernel(
    nodes,
    off_in,
    inverse_in,
    rhs_in,
    sens_in,
    neigh_in,
    weight_in,
    index_in,
    spread_in,
    start_in,
    cell_in,
    base_in,
    off_ref,
    inverse_ref,
    rhs_ref,
    sens_ref,
    lane_ref,
    step_ref,
    spread_ref,
    low_ref,
    one_hot_ref,
    start_ref,
    left_ref,
    right_ref,
    off_buf,
    sens_buf,
    neigh_buf,
    weight_buf,
    index_buf,
    spread_buf,
    cell_buf,
    base_buf,
    sems,
):
    slots, owned = index_buf.shape
    start = pl.multiple_of(lax.axis_index("nodes") * owned, LANES)
    mine = pl.ds(start, owned)
    pairs = (
        (neigh_in, neigh_buf),
        (index_in.at[:, mine], index_buf),
        (spread_in.at[:, mine], spread_buf),
        (cell_in, cell_buf),
        (base_in.at[:, mine], base_buf),
        (off_in, off_buf),
        (weight_in, weight_buf),
        (sens_in, sens_buf),
        (inverse_in, inverse_ref),
        (rhs_in, rhs_ref),
        (start_in, start_ref),
    )
    copies = [pltpu.make_async_copy(a, b, sems.at[i]) for i, (a, b) in enumerate(pairs)]
    for copy in copies:
        copy.start()

    faces, cells = neigh_buf.shape
    blocks = cells // LANES
    per = blocks * nodes
    first_cell = lax.axis_index(CELL_AXES) * cells
    copies[0].wait()
    for block in range(blocks):
        index = neigh_buf[:, block * LANES : (block + 1) * LANES]
        local = index - first_cell + cells
        lane = jnp.bitwise_and(local, LANES - 1)
        step = jnp.right_shift(local, 7) - block
        step = jnp.where(index >= 0, step, -1)
        for node in range(nodes):
            rows = pl.ds(block * nodes + node, faces, stride=per)
            lane_ref[rows, :] = lane
            step_ref[rows, :] = step

    copies[1].wait()
    copies[2].wait()
    groups = FFD // LANES
    piece = min(512, owned)
    for first in range(0, owned, piece):
        here = slice(first, first + piece)
        high = jnp.right_shift(index_buf[:, here], 7)
        part = lax.broadcasted_iota(jnp.int32, (16, piece), 0)
        part = jnp.where(part < 3 * groups, lax.rem(part, groups), -1)
        for j in range(slots):
            spread_ref[j * 16 : (j + 1) * 16, here] = jnp.where(
                high[j : j + 1] == part, spread_buf[j : j + 1, here], 0.0
            )

    low_ref[...] = jnp.bitwise_and(index_buf[...], LANES - 1).astype(jnp.float32)
    write_one_hot(low_ref, one_hot_ref, 0)

    copies[3].wait()
    left_ref[...] = distance_factors(cell_buf[...], True).T.astype(jnp.bfloat16)
    copies[4].wait()
    right_ref[...] = distance_factors(base_buf[...], False).astype(jnp.bfloat16)

    copies[5].wait()
    off_ref[...] = off_buf[...].astype(jnp.float32)
    copies[6].wait()
    copies[7].wait()
    row_node = lax.rem(lax.broadcasted_iota(jnp.int32, (per, LANES), 0), nodes)
    weights = jnp.zeros((per, LANES), jnp.float32)
    for node in range(nodes):
        weights = jnp.where(row_node == node, weight_buf[node], weights)
    for row in range(0, sens_buf.shape[0], per):
        here = slice(row, row + per)
        sens_ref[here, :] = sens_buf[here, :].astype(jnp.float32) * weights
    for copy in copies[8:]:
        copy.wait()


def take_lanes(table, lanes):
    numbers = lax.GatherDimensionNumbers(
        offset_dims=(),
        collapsed_slice_dims=(1,),
        start_index_map=(1,),
        operand_batching_dims=(0,),
        start_indices_batching_dims=(0,),
    )
    return lax.gather(
        table,
        lanes[..., None],
        numbers,
        slice_sizes=(1, 1),
        mode=lax.GatherScatterMode.PROMISE_IN_BOUNDS,
    )


def sweep_into(
    blocks, first_ref, second_ref, own_ref, rhs_ref, off_ref, inverse_ref, lane_ref, step_ref,
    out_ref, window_ref, table_ref,
):
    per = rhs_ref.shape[0] // 5
    nodes = per // blocks
    faces = lane_ref.shape[0] // per
    odd = lax.rem(lax.axis_index(CELL_AXES), 2)
    place = pl.multiple_of((1 - odd) * 2 * per, 8)
    other = pl.multiple_of(odd * 2 * per, 8)
    width = 3 * per
    for b in range(5):
        rows = slice(b * per, (b + 1) * per)
        base = b * width
        window_ref[pl.ds(base + place, per), :] = first_ref[rows, :]
        window_ref[base + per : base + 2 * per, :] = own_ref[rows, :]
        window_ref[pl.ds(base + other, per), :] = second_ref[rows, :]
    for shift in range(1, 8 // nodes):
        for b in range(5):
            for tile in range(0, width - 8, 8):
                to = ((shift - 1) * 5 + b) * width + tile
                table_ref[to : to + 8, :] = window_ref[
                    pl.ds(b * width + tile + shift * nodes, 8), :
                ]
    for half in range(0, per, 8):
        remaining = [rhs_ref[a * per + half : a * per + half + 8, :] for a in range(5)]
        for f in range(faces):
            lanes = lane_ref[f * per + half : f * per + half + 8, :]
            dist = step_ref[f * per + half : f * per + half + 8, :]
            beside = [jnp.zeros((8, LANES), jnp.float32)] * 5
            for d in range(2 * blocks + 1):
                here = dist == d
                first = half + d * nodes
                for b in range(5):
                    shift, at = first % 8 // nodes, b * width + first // 8 * 8
                    if shift:
                        at = at + (shift - 1) * 5 * width
                        table = table_ref[at : at + 8, :]
                    else:
                        table = window_ref[at : at + 8, :]
                    beside[b] = jnp.where(here, take_lanes(table, lanes), beside[b])
            for a in range(5):
                for b in range(5):
                    row = (f * 25 + 5 * a + b) * per + half
                    remaining[a] = remaining[a] - off_ref[row : row + 8, :] * beside[b]
        for a in range(5):
            total = None
            for b in range(5):
                row = (5 * a + b) * per + half
                term = inverse_ref[row : row + 8, :] * remaining[b]
                total = term if total is None else total + term
            out_ref[a * per + half : a * per + half + 8, :] = total


def sweep_kernel(blocks, *refs):
    sweep_into(blocks, *refs)


def last_sweep_kernel(blocks, *refs):
    ins, rest = refs[:8], refs[8:]
    sens_ref, _, out_ref, sens_out_ref, window_ref, table_ref, part_ref = rest
    sweep_into(blocks, *ins, out_ref, window_ref, table_ref)
    per = out_ref.shape[0] // 5
    nodes = per // blocks
    for k in range(3):
        total = None
        for a in range(5):
            row = (3 * a + k) * per
            term = out_ref[a * per : (a + 1) * per, :] * sens_ref[row : row + per, :]
            total = term if total is None else total + term
        part_ref[k * per : (k + 1) * per, :] = total
    for block in range(blocks):
        total = None
        for node in range(nodes):
            term = part_ref[pl.ds(block * nodes + node, 3, stride=per), :]
            total = term if total is None else total + term
        sens_out_ref[pl.ds(block, 3, stride=blocks), :] = total


def pieces(value, count):
    found = []
    for _ in range(count):
        piece = value.astype(jnp.bfloat16).astype(jnp.float32)
        found.append(piece)
        value = value - piece
    return found


def distance_factors(points, left):
    count = points.shape[1]
    scaled = (points - 0.5) * (1.0 / SUPPORT_RADIUS)
    scaled = jnp.concatenate([scaled, jnp.zeros((5, count), jnp.float32)], axis=0)
    norm = jnp.sum(scaled * scaled, axis=0, keepdims=True)
    norms = pieces(jnp.broadcast_to(norm, (8, count)), 3)
    row = lax.broadcasted_iota(jnp.int32, (8, count), 0)
    norm_block = jnp.zeros((8, count), jnp.float32)
    for place in range(3):
        norm_block = jnp.where(row == place, norms[place], norm_block)
    ones_block = jnp.where(row < 3, 1.0, 0.0)
    first, second, third = pieces(scaled, 3)
    if left:
        dims = [first, first, second, second, first, third]
        dims = [-2.0 * part for part in dims]
        blocks = dims + [norm_block, ones_block]
    else:
        dims = [first, second, first, second, third, first]
        blocks = dims + [ones_block, norm_block]
    return jnp.concatenate(blocks, axis=0)


def wendland_kernel(first_cell, left_ref, right_ref, _, kernel_ref):
    cells, owned = kernel_ref.shape[0] // 2, kernel_ref.shape[1]
    tile, wide = min(128, cells), min(256, owned)

    def squares(row, lane):
        left = left_ref[first_cell + row : first_cell + row + tile, :]
        right = right_ref[:, lane : lane + wide]
        return jnp.dot(left, right, preferred_element_type=jnp.float32)

    places = [(row, lane) for lane in range(0, owned, wide) for row in range(0, cells, tile)]
    following = squares(*places[0])
    for at, (row, lane) in enumerate(places):
        squared = jnp.maximum(following, 1e-30)
        if at + 1 < len(places):
            following = squares(*places[at + 1])
        near = jnp.maximum(1.0 - jnp.exp(0.5 * jnp.log(squared)), 0.0)
        power = near * near
        kernel = power * power * (1.25 - near)
        first = kernel.astype(jnp.bfloat16)
        rest = (kernel - first.astype(jnp.float32)).astype(jnp.bfloat16)
        here = slice(lane, lane + wide)
        kernel_ref[row : row + tile, here] = first
        kernel_ref[cells + row : cells + row + tile, here] = rest


def far_wendland_kernel(
    first_cell, left_ref, right_ref, after, adjoint_ref, low_ref, *rest
):
    kernel_ref, one_hot_ref, result_ref, sem = rest
    copy = pltpu.make_async_copy(adjoint_ref, result_ref, sem)
    copy.start()
    owned = low_ref.shape[1]
    write_one_hot(low_ref, one_hot_ref, low_ref.shape[0] - one_hot_ref.shape[0] // owned)
    wendland_kernel(first_cell, left_ref, right_ref, after, kernel_ref)
    copy.wait()


def control_kernel(scale, *refs):
    *sens_refs, near_ref, far_ref = refs[:-4]
    spread_ref, near_hot, far_hot, out_ref = refs[-4:]
    blocks = sens_refs[0].shape[0] // 3
    half = near_ref.shape[0] // 2
    groups = FFD // LANES
    total = sens_refs[0][...]
    for ref in sens_refs[1:]:
        total = total + ref[...]
    total = total * scale

    def halves(value):
        first = value.astype(jnp.bfloat16)
        rest = (value - first.astype(jnp.float32)).astype(jnp.bfloat16)
        return first, rest

    row = lax.broadcasted_iota(jnp.int32, (8, LANES), 0)
    wide = []
    for block in range(blocks):
        sens = jnp.zeros((8, LANES), jnp.float32)
        for k in range(3):
            sens = jnp.where(row == k, total[k * blocks + block : k * blocks + block + 1], sens)
        first = sens.astype(jnp.bfloat16).astype(jnp.float32)
        wide.append(jnp.concatenate([first, sens - first], axis=0))
    sens = jnp.concatenate(wide, axis=1).astype(jnp.bfloat16)
    grad = None
    for part, ref in ((sens[:, :half], near_ref), (sens[:, half:], far_ref)):
        both = jnp.concatenate([part, part], axis=1)
        term = jnp.dot(both, ref[...], preferred_element_type=jnp.float32)
        grad = term if grad is None else grad + term
    grad = grad[:8] + grad[8:]
    row = lax.broadcasted_iota(jnp.int32, (16, grad.shape[1]), 0)
    wide = jnp.zeros(row.shape, jnp.float32)
    for k in range(3):
        mine = jnp.logical_and(row >= k * groups, row < (k + 1) * groups)
        wide = jnp.where(mine, grad[k : k + 1], wide)
    grad = wide
    owned = grad.shape[1]
    result = None
    places = [
        (ref, first) for ref in (near_hot, far_hot) for first in range(0, ref.shape[0], owned)
    ]
    for j, (ref, first) in enumerate(places):
        term = jnp.dot(
            jnp.concatenate(halves(grad * spread_ref[j * 16 : (j + 1) * 16, :]), axis=0),
            ref[first : first + owned, :],
            preferred_element_type=jnp.float32,
        )
        result = term if result is None else result + term
    result = result[:16] + result[16:]
    out_ref[...] = result[: 3 * groups]


def tree(values):
    while len(values) > 1:
        values = [sum(values[i : i + 2]) for i in range(0, len(values), 2)]
    return values[0]


def add_kernel(*refs):
    refs[-1][...] = tree([ref[...] for ref in refs[:-1]])


def finish_kernel(*refs):
    total, out_ref = tree([ref[...] for ref in refs[:-1]]), refs[-1]
    groups = out_ref.shape[1] // LANES
    for k in range(3):
        for group in range(groups):
            row = k * groups + group
            out_ref[k : k + 1, group * LANES : (group + 1) * LANES] = total[row : row + 1]


def sum_rounds():
    lines, nodes, cores = (lax.axis_size(axis) for axis in SUM_AXES)
    if any(size & (size - 1) for size in (lines, nodes, cores)):
        return None
    near = [cores >> 1 >> i for i in range(cores.bit_length() - 1)]
    node_bits = [cores << i for i in range(nodes.bit_length() - 1)]
    line_bits = [cores * nodes << i for i in range(lines.bit_length() - 1)]
    bits = near + line_bits[:2] + node_bits[:1] + line_bits[2:] + node_bits[1:]
    rounds = []
    for first in range(0, len(bits), 2):
        masks = bits[first : first + 2]
        if len(masks) == 2:
            masks = masks + [masks[0] | masks[1]]
        rounds.append([mask | (cores - 1) for mask in masks] if first else masks)
    return rounds


def exchanged(value, masks):
    peers = lax.axis_size(SUM_AXES)
    return [value] + [
        lax.ppermute(value, SUM_AXES, [(i, i ^ mask) for i in range(peers)]) for mask in masks
    ]


def body(
    adjoint_start,
    adjoint_rhs,
    off_blocks,
    diag_inverse,
    neighbours,
    node_weights,
    sens_blocks,
    cell_points,
    base_points,
    ffd_index,
    ffd_weight,
):
    nodes, _, cells = adjoint_start.shape
    faces = off_blocks.shape[1]
    blocks = cells // LANES
    per = blocks * nodes
    slots = ffd_index.shape[1]
    far_slots = max(1, slots * 3 // 8)
    owned = base_points.shape[1] // lax.axis_size("nodes")
    peers = lax.axis_size(CELL_AXES)
    cores = lax.axis_size("sub")
    node_peers = lax.axis_size("nodes")
    f32, i32, bf16 = jnp.float32, jnp.int32, jnp.bfloat16

    def shape(dims, dtype=f32):
        return jax.ShapeDtypeStruct(dims, dtype)

    def cost(flops, moved):
        return pl.CostEstimate(flops=flops, bytes_accessed=moved, transcendentals=0)

    def swaps(array):
        close = lax.ppermute(array, CELL_AXES, [(i, i ^ 1) for i in range(peers)])
        pairs = []
        for i in range(peers):
            line, core = divmod(i, cores)
            for node in range(node_peers):
                j, beside = (i + 1 if i % 2 else i - 1), node
                if not 0 <= j < peers:
                    j, beside = i, (node ^ 1 if node_peers % 2 == 0 else node)
                to_line, to_core = divmod(j, cores)
                pairs.append(
                    (
                        (line * node_peers + node) * cores + core,
                        (to_line * node_peers + beside) * cores + to_core,
                    )
                )
        return lax.ppermute(array, SUM_AXES, pairs), close

    adjoint = rows_of(adjoint_start)
    far, close = swaps(adjoint)
    prepared = pl.pallas_call(
        functools.partial(prepare_kernel, nodes),
        out_shape=(
            shape((faces * 25 * per, LANES)),
            shape((25 * per, LANES)),
            shape((5 * per, LANES)),
            shape((15 * per, LANES)),
            shape((faces * per, LANES), i32),
            shape((faces * per, LANES), i32),
            shape((slots * 16, owned)),
            shape((slots, owned)),
            shape(((slots - far_slots) * owned, LANES), bf16),
            shape((5 * per, LANES)),
            shape((cells, FACTOR_ROWS), bf16),
            shape((FACTOR_ROWS, owned), bf16),
        ),
        in_specs=[HBM] * 11,
        out_specs=(VMEM,) * 12,
        scratch_shapes=[
            pltpu.VMEM((faces * 25 * per, LANES), bf16),
            pltpu.VMEM((15 * per, LANES), bf16),
            pltpu.VMEM((faces, cells), i32),
            pltpu.SMEM((nodes,), f32),
            pltpu.VMEM((slots, owned), i32),
            pltpu.VMEM((slots, owned), f32),
            pltpu.VMEM((3, cells), f32),
            pltpu.VMEM((3, owned), f32),
            pltpu.SemaphoreType.DMA((11,)),
        ],
        compiler_params=PARAMS,
        cost_estimate=cost(10**9, 10**7),
        name="prepare",
    )(
        *in_hbm(
            rows_of(off_blocks.reshape(nodes, faces * 25, cells)),
            rows_of(diag_inverse),
            rows_of(adjoint_rhs),
            rows_of(sens_blocks),
            neighbours,
            node_weights,
            ffd_index.T,
            ffd_weight.T,
            adjoint,
            cell_points,
            base_points,
        )
    )
    off, inverse, rhs, sens, lane, step, spread, low, near_hot, adjoint, left, right = prepared
    scratch = [
        pltpu.VMEM((3 * 5 * per, LANES), f32),
        pltpu.VMEM((max(8 // nodes - 1, 1) * 3 * 5 * per, LANES), f32),
    ]
    sweep_cost = cost(2 * 10 * 35 * cells, 4 * faces * 25 * per * LANES)

    for _ in range(SWEEPS - 1):
        adjoint = pl.pallas_call(
            functools.partial(sweep_kernel, blocks),
            out_shape=shape((5 * per, LANES)),
            in_specs=[VMEM] * 8,
            out_specs=VMEM,
            scratch_shapes=scratch,
            compiler_params=PARAMS,
            cost_estimate=sweep_cost,
            name="sweep",
        )(close, far, adjoint, rhs, off, inverse, lane, step)
        far, close = swaps(adjoint)

    half = cells * 5 // 8 // LANES * LANES
    wendland_cost = cost(10**9, 10**7)
    near_shape = shape((2 * half, owned), bf16)
    far_shape = shape((2 * (cells - half), owned), bf16)
    near_kernel = pl.pallas_call(
        functools.partial(wendland_kernel, 0),
        out_shape=near_shape,
        in_specs=[VMEM] * 3,
        out_specs=VMEM,
        compiler_params=PARAMS,
        cost_estimate=wendland_cost,
        name="near_wendland",
    )(left, right, adjoint)
    adjoint, part_sens = pl.pallas_call(
        functools.partial(last_sweep_kernel, blocks),
        out_shape=(shape((5 * per, LANES)), shape((3 * blocks, LANES))),
        in_specs=[VMEM] * 9 + [pl.BlockSpec(memory_space=pl.ANY)],
        out_specs=(VMEM, VMEM),
        scratch_shapes=scratch + [pltpu.VMEM((3 * per, LANES), f32)],
        compiler_params=PARAMS,
        cost_estimate=sweep_cost,
        name="last_sweep",
    )(close, far, adjoint, rhs, off, inverse, lane, step, sens, near_kernel)

    all_sens = [part_sens]
    for shift in range(1, node_peers):
        ring = [(i, (i + shift) % node_peers) for i in range(node_peers)]
        all_sens.append(lax.ppermute(part_sens, "nodes", ring))
    hot_shape = shape((far_slots * owned, LANES), bf16)
    far_kernel, far_hot, adjoint = pl.pallas_call(
        functools.partial(far_wendland_kernel, half),
        out_shape=(far_shape, hot_shape, shape((5 * per, LANES))),
        in_specs=[VMEM] * 5,
        out_specs=(VMEM, VMEM, HBM),
        scratch_shapes=[pltpu.SemaphoreType.DMA],
        compiler_params=PARAMS,
        cost_estimate=wendland_cost,
        name="far_wendland",
    )(left, right, part_sens, adjoint, low)
    scale = 4.0 / math.sqrt(cells * peers)
    rows = 3 * FFD // LANES
    partial = pl.pallas_call(
        functools.partial(control_kernel, scale),
        out_shape=shape((rows, LANES)),
        in_specs=[VMEM] * (len(all_sens) + 5),
        out_specs=VMEM,
        compiler_params=PARAMS,
        name="control",
    )(*all_sens, near_kernel, far_kernel, spread, near_hot, far_hot)
    rounds = sum_rounds()
    terms = [partial] if rounds else [lax.psum(partial, SUM_AXES)]
    for masks in rounds or ():
        if len(terms) > 1:
            partial = pl.pallas_call(
                add_kernel, out_shape=shape((rows, LANES)), name="add", compiler_params=PARAMS
            )(*terms)
        terms = exchanged(partial, masks)
    control_grad = pl.pallas_call(
        finish_kernel, out_shape=shape((3, FFD)), name="finish", compiler_params=PARAMS
    )(*terms)
    return (from_rows(adjoint, nodes, cells), control_grad)


def solution(mesh):
    return jax.shard_map(
        body,
        mesh=mesh,
        in_specs=(
            P("nodes", None, ("groups", "cells", "sub")),
            P("nodes", None, ("groups", "cells", "sub")),
            P("nodes", None, None, ("groups", "cells", "sub")),
            P("nodes", None, ("groups", "cells", "sub")),
            P(None, ("cells", "sub")),
            P("nodes"),
            P("nodes", None, ("groups", "cells", "sub")),
            P(None, ("cells", "sub")),
            P(),
            P(),
            P(),
        ),
        out_specs=(P("nodes", None, ("groups", "cells", "sub")), P("groups", None)),
        check_vma=False,
    )
```

```python
import functools
import math

import jax
import jax.numpy as jnp
from jax import lax
from jax.experimental import pallas as pl
from jax.experimental.pallas import tpu as pltpu
from jax.sharding import PartitionSpec as P

FFD = 512
SUPPORT_RADIUS = 0.3
LANES = 128
CELL_AXES = ("cells", "sub")
SUM_AXES = ("cells", "nodes", "sub")
FACTOR_ROWS = 64
PARAMS = pltpu.CompilerParams(vmem_limit_bytes=24 * 1024 * 1024)
VMEM = pl.BlockSpec(memory_space=pltpu.VMEM)
HBM = pl.BlockSpec(memory_space=pltpu.HBM)


def rows_of(array):
    nodes, rows, cells = array.shape
    blocks = cells // LANES
    split = array.reshape(nodes, rows, blocks, LANES)
    return split.transpose(1, 2, 0, 3).reshape(rows * blocks * nodes, LANES)


def from_rows(array, nodes, cells):
    blocks = cells // LANES
    split = array.reshape(-1, blocks, nodes, LANES)
    return split.transpose(2, 0, 1, 3).reshape(nodes, -1, cells)


def in_hbm(*arrays):
    return [pltpu.with_memory_space_constraint(array, pltpu.HBM) for array in arrays]


def write_one_hot(low_ref, one_hot_ref, first_slot):
    owned = low_ref.shape[1]
    piece = min(512, owned)
    lane = lax.broadcasted_iota(jnp.int32, (piece, LANES), 1).astype(jnp.float32)
    lane = lane.astype(jnp.bfloat16)
    for first in range(0, owned, piece):
        low = low_ref[:, first : first + piece].T.astype(jnp.bfloat16)
        for j in range(one_hot_ref.shape[0] // owned):
            column = low[:, first_slot + j : first_slot + j + 1]
            hit = jnp.broadcast_to(column, (piece, LANES)) == lane
            one_hot_ref[j * owned + first : j * owned + first + piece, :] = jnp.where(
                hit, jnp.bfloat16(1.0), jnp.bfloat16(0.0)
            )


def prepare_kernel(
    nodes,
    off_in,
    inverse_in,
    rhs_in,
    sens_in,
    neigh_in,
    weight_in,
    index_in,
    spread_in,
    start_in,
    cell_in,
    base_in,
    off_ref,
    inverse_ref,
    rhs_ref,
    sens_ref,
    lane_ref,
    step_ref,
    spread_ref,
    low_ref,
    one_hot_ref,
    start_ref,
    left_ref,
    right_ref,
    off_buf,
    sens_buf,
    neigh_buf,
    weight_buf,
    index_buf,
    spread_buf,
    cell_buf,
    base_buf,
    sems,
):
    slots, owned = index_buf.shape
    start = pl.multiple_of(lax.axis_index("nodes") * owned, LANES)
    mine = pl.ds(start, owned)
    pairs = (
        (neigh_in, neigh_buf),
        (index_in.at[:, mine], index_buf),
        (spread_in.at[:, mine], spread_buf),
        (cell_in, cell_buf),
        (base_in.at[:, mine], base_buf),
        (off_in, off_buf),
        (weight_in, weight_buf),
        (sens_in, sens_buf),
        (inverse_in, inverse_ref),
        (rhs_in, rhs_ref),
        (start_in, start_ref),
    )
    copies = [pltpu.make_async_copy(a, b, sems.at[i]) for i, (a, b) in enumerate(pairs)]
    for copy in copies:
        copy.start()

    faces, cells = neigh_buf.shape
    blocks = cells // LANES
    per = blocks * nodes
    first_cell = lax.axis_index(CELL_AXES) * cells
    copies[0].wait()
    for block in range(blocks):
        index = neigh_buf[:, block * LANES : (block + 1) * LANES]
        local = index - first_cell + cells
        lane = jnp.bitwise_and(local, LANES - 1)
        step = jnp.right_shift(local, 7) - block
        step = jnp.where(index >= 0, step, -1)
        for node in range(nodes):
            rows = pl.ds(block * nodes + node, faces, stride=per)
            lane_ref[rows, :] = lane
            step_ref[rows, :] = step

    copies[1].wait()
    copies[2].wait()
    groups = FFD // LANES
    piece = min(512, owned)
    for first in range(0, owned, piece):
        here = slice(first, first + piece)
        high = jnp.right_shift(index_buf[:, here], 7)
        part = lax.broadcasted_iota(jnp.int32, (16, piece), 0)
        part = jnp.where(part < 3 * groups, lax.rem(part, groups), -1)
        for j in range(slots):
            spread_ref[j * 16 : (j + 1) * 16, here] = jnp.where(
                high[j : j + 1] == part, spread_buf[j : j + 1, here], 0.0
            )

    low_ref[...] = jnp.bitwise_and(index_buf[...], LANES - 1).astype(jnp.float32)
    write_one_hot(low_ref, one_hot_ref, 0)

    copies[3].wait()
    left_ref[...] = distance_factors(cell_buf[...], True).T.astype(jnp.bfloat16)
    copies[4].wait()
    right_ref[...] = distance_factors(base_buf[...], False).astype(jnp.bfloat16)

    copies[5].wait()
    off_ref[...] = off_buf[...].astype(jnp.float32)
    copies[6].wait()
    copies[7].wait()
    row_node = lax.rem(lax.broadcasted_iota(jnp.int32, (per, LANES), 0), nodes)
    weights = jnp.zeros((per, LANES), jnp.float32)
    for node in range(nodes):
        weights = jnp.where(row_node == node, weight_buf[node], weights)
    for row in range(0, sens_buf.shape[0], per):
        here = slice(row, row + per)
        sens_ref[here, :] = sens_buf[here, :].astype(jnp.float32) * weights
    for copy in copies[8:]:
        copy.wait()


def take_lanes(table, lanes):
    numbers = lax.GatherDimensionNumbers(
        offset_dims=(),
        collapsed_slice_dims=(1,),
        start_index_map=(1,),
        operand_batching_dims=(0,),
        start_indices_batching_dims=(0,),
    )
    return lax.gather(
        table,
        lanes[..., None],
        numbers,
        slice_sizes=(1, 1),
        mode=lax.GatherScatterMode.PROMISE_IN_BOUNDS,
    )


def sweep_into(
    blocks, first_ref, second_ref, own_ref, rhs_ref, off_ref, inverse_ref, lane_ref, step_ref,
    first_cell, left_ref, right_ref, out_ref, kernel_ref, window_ref, table_ref,
):
    places, squares = wendland_places(first_cell, left_ref, right_ref, kernel_ref)
    per = rhs_ref.shape[0] // 5
    nodes = per // blocks
    faces = lane_ref.shape[0] // per
    odd = lax.rem(lax.axis_index(CELL_AXES), 2)
    place = pl.multiple_of((1 - odd) * 2 * per, 8)
    other = pl.multiple_of(odd * 2 * per, 8)
    width = 3 * per
    for b in range(5):
        rows = slice(b * per, (b + 1) * per)
        base = b * width
        window_ref[pl.ds(base + place, per), :] = first_ref[rows, :]
        window_ref[base + per : base + 2 * per, :] = own_ref[rows, :]
        window_ref[pl.ds(base + other, per), :] = second_ref[rows, :]
    for shift in range(1, 8 // nodes):
        for b in range(5):
            for tile in range(0, width - 8, 8):
                to = ((shift - 1) * 5 + b) * width + tile
                table_ref[to : to + 8, :] = window_ref[
                    pl.ds(b * width + tile + shift * nodes, 8), :
                ]
    for half in range(0, per, 8):
        remaining = [rhs_ref[a * per + half : a * per + half + 8, :] for a in range(5)]
        for f in range(faces):
            lanes = lane_ref[f * per + half : f * per + half + 8, :]
            dist = step_ref[f * per + half : f * per + half + 8, :]
            beside = [jnp.zeros((8, LANES), jnp.float32)] * 5
            squared = None
            if places:
                row, lane = places.pop(0)
                squared = squares(row, lane)
            for d in range(2 * blocks + 1):
                here = dist == d
                first = half + d * nodes
                for b in range(5):
                    shift, at = first % 8 // nodes, b * width + first // 8 * 8
                    if shift:
                        at = at + (shift - 1) * 5 * width
                        table = table_ref[at : at + 8, :]
                    else:
                        table = window_ref[at : at + 8, :]
                    beside[b] = jnp.where(here, take_lanes(table, lanes), beside[b])
                if squared is not None and d % 2 and d // 2 * 16 < squared.shape[0]:
                    at = d // 2 * 16
                    wendland_store(squared[at : at + 16], kernel_ref, row + at, lane)
            for a in range(5):
                for b in range(5):
                    at = (f * 25 + 5 * a + b) * per + half
                    remaining[a] = remaining[a] - off_ref[at : at + 8, :] * beside[b]
        for a in range(5):
            total = None
            for b in range(5):
                row = (5 * a + b) * per + half
                term = inverse_ref[row : row + 8, :] * remaining[b]
                total = term if total is None else total + term
            out_ref[a * per + half : a * per + half + 8, :] = total
    while places:
        row, lane = places.pop(0)
        wendland_store(squares(row, lane), kernel_ref, row, lane)


def sweep_kernel(blocks, first_cell, *refs):
    sweep_into(blocks, *refs[:8], first_cell, *refs[8:])


def last_sweep_kernel(blocks, first_cell, *refs):
    ins, (left_ref, right_ref, sens_ref, _, *outs) = refs[:8], refs[8:]
    out_ref, kernel_ref, sens_out_ref, window_ref, table_ref, part_ref = outs
    sweep_into(
        blocks, *ins, first_cell, left_ref, right_ref, out_ref, kernel_ref, window_ref, table_ref
    )
    per = out_ref.shape[0] // 5
    nodes = per // blocks
    for k in range(3):
        total = None
        for a in range(5):
            row = (3 * a + k) * per
            term = out_ref[a * per : (a + 1) * per, :] * sens_ref[row : row + per, :]
            total = term if total is None else total + term
        part_ref[k * per : (k + 1) * per, :] = total
    for block in range(blocks):
        total = None
        for node in range(nodes):
            term = part_ref[pl.ds(block * nodes + node, 3, stride=per), :]
            total = term if total is None else total + term
        sens_out_ref[pl.ds(block, 3, stride=blocks), :] = total


def pieces(value, count):
    found = []
    for _ in range(count):
        piece = value.astype(jnp.bfloat16).astype(jnp.float32)
        found.append(piece)
        value = value - piece
    return found


def distance_factors(points, left):
    count = points.shape[1]
    scaled = (points - 0.5) * (1.0 / SUPPORT_RADIUS)
    scaled = jnp.concatenate([scaled, jnp.zeros((5, count), jnp.float32)], axis=0)
    norm = jnp.sum(scaled * scaled, axis=0, keepdims=True)
    norms = pieces(jnp.broadcast_to(norm, (8, count)), 3)
    row = lax.broadcasted_iota(jnp.int32, (8, count), 0)
    norm_block = jnp.zeros((8, count), jnp.float32)
    for place in range(3):
        norm_block = jnp.where(row == place, norms[place], norm_block)
    ones_block = jnp.where(row < 3, 1.0, 0.0)
    first, second, third = pieces(scaled, 3)
    if left:
        dims = [first, first, second, second, first, third]
        dims = [-2.0 * part for part in dims]
        blocks = dims + [norm_block, ones_block]
    else:
        dims = [first, second, first, second, third, first]
        blocks = dims + [ones_block, norm_block]
    return jnp.concatenate(blocks, axis=0)


def wendland_store(squared, kernel_ref, row, lane):
    squared = jnp.maximum(squared, 1e-30)
    near = jnp.maximum(1.0 - squared * lax.rsqrt(squared), 0.0)
    power = near * near
    kernel = power * power * (1.25 - near)
    first = kernel.astype(jnp.bfloat16)
    rest = (kernel - first.astype(jnp.float32)).astype(jnp.bfloat16)
    cells = kernel_ref.shape[0] // 2
    here = slice(lane, lane + squared.shape[1])
    kernel_ref[row : row + squared.shape[0], here] = first
    kernel_ref[cells + row : cells + row + squared.shape[0], here] = rest


def wendland_places(first_cell, left_ref, right_ref, kernel_ref):
    cells, owned = kernel_ref.shape[0] // 2, kernel_ref.shape[1]
    tile, wide = min(128, cells), min(256, owned)

    def squares(row, lane):
        left = left_ref[first_cell + row : first_cell + row + tile, :]
        right = right_ref[:, lane : lane + wide]
        return jnp.dot(left, right, preferred_element_type=jnp.float32)

    places = [(row, lane) for lane in range(0, owned, wide) for row in range(0, cells, tile)]
    return places, squares


def wendland_kernel(first_cell, left_ref, right_ref, _, kernel_ref):
    places, squares = wendland_places(first_cell, left_ref, right_ref, kernel_ref)
    following = squares(*places[0])
    for at, (row, lane) in enumerate(places):
        squared = following
        if at + 1 < len(places):
            following = squares(*places[at + 1])
        wendland_store(squared, kernel_ref, row, lane)


def far_wendland_kernel(
    first_cell, left_ref, right_ref, after, adjoint_ref, low_ref, *rest
):
    kernel_ref, one_hot_ref, result_ref, sem = rest
    copy = pltpu.make_async_copy(adjoint_ref, result_ref, sem)
    copy.start()
    owned = low_ref.shape[1]
    write_one_hot(low_ref, one_hot_ref, low_ref.shape[0] - one_hot_ref.shape[0] // owned)
    wendland_kernel(first_cell, left_ref, right_ref, after, kernel_ref)
    copy.wait()


def control_kernel(scale, *refs):
    *sens_refs, first_ref, near_ref, third_ref, far_ref = refs[:-4]
    spread_ref, near_hot, far_hot, out_ref = refs[-4:]
    blocks = sens_refs[0].shape[0] // 3
    groups = FFD // LANES
    total = sens_refs[0][...]
    for ref in sens_refs[1:]:
        total = total + ref[...]
    total = total * scale

    def halves(value):
        first = value.astype(jnp.bfloat16)
        rest = (value - first.astype(jnp.float32)).astype(jnp.bfloat16)
        return first, rest

    row = lax.broadcasted_iota(jnp.int32, (8, LANES), 0)
    wide = []
    for block in range(blocks):
        sens = jnp.zeros((8, LANES), jnp.float32)
        for k in range(3):
            sens = jnp.where(row == k, total[k * blocks + block : k * blocks + block + 1], sens)
        first = sens.astype(jnp.bfloat16).astype(jnp.float32)
        wide.append(jnp.concatenate([first, sens - first], axis=0))
    sens = jnp.concatenate(wide, axis=1).astype(jnp.bfloat16)
    grad = None
    cell = 0
    for ref in (first_ref, near_ref, third_ref, far_ref):
        part = sens[:, cell : cell + ref.shape[0] // 2]
        cell += ref.shape[0] // 2
        both = jnp.concatenate([part, part], axis=1)
        term = jnp.dot(both, ref[...], preferred_element_type=jnp.float32)
        grad = term if grad is None else grad + term
    grad = grad[:8] + grad[8:]
    row = lax.broadcasted_iota(jnp.int32, (16, grad.shape[1]), 0)
    wide = jnp.zeros(row.shape, jnp.float32)
    for k in range(3):
        mine = jnp.logical_and(row >= k * groups, row < (k + 1) * groups)
        wide = jnp.where(mine, grad[k : k + 1], wide)
    grad = wide
    owned = grad.shape[1]
    result = None
    places = [
        (ref, first) for ref in (near_hot, far_hot) for first in range(0, ref.shape[0], owned)
    ]
    for j, (ref, first) in enumerate(places):
        term = jnp.dot(
            jnp.concatenate(halves(grad * spread_ref[j * 16 : (j + 1) * 16, :]), axis=0),
            ref[first : first + owned, :],
            preferred_element_type=jnp.float32,
        )
        result = term if result is None else result + term
    result = result[:16] + result[16:]
    out_ref[...] = result[: 3 * groups]


def tree(values):
    while len(values) > 1:
        values = [sum(values[i : i + 2]) for i in range(0, len(values), 2)]
    return values[0]


def add_kernel(*refs):
    refs[-1][...] = tree([ref[...] for ref in refs[:-1]])


def finish_kernel(*refs):
    total, out_ref = tree([ref[...] for ref in refs[:-1]]), refs[-1]
    groups = out_ref.shape[1] // LANES
    for k in range(3):
        for group in range(groups):
            row = k * groups + group
            out_ref[k : k + 1, group * LANES : (group + 1) * LANES] = total[row : row + 1]


def sum_rounds():
    lines, nodes, cores = (lax.axis_size(axis) for axis in SUM_AXES)
    if any(size & (size - 1) for size in (lines, nodes, cores)):
        return None
    near = [cores >> 1 >> i for i in range(cores.bit_length() - 1)]
    node_bits = [cores << i for i in range(nodes.bit_length() - 1)]
    line_bits = [cores * nodes << i for i in range(lines.bit_length() - 1)]
    bits = near + line_bits[:2] + node_bits[:1] + line_bits[2:] + node_bits[1:]
    rounds = []
    for first in range(0, len(bits), 2):
        masks = bits[first : first + 2]
        if len(masks) == 2:
            masks = masks + [masks[0] | masks[1]]
        rounds.append([mask | (cores - 1) for mask in masks] if first else masks)
    return rounds


def exchanged(value, masks):
    peers = lax.axis_size(SUM_AXES)
    return [value] + [
        lax.ppermute(value, SUM_AXES, [(i, i ^ mask) for i in range(peers)]) for mask in masks
    ]


def body(
    adjoint_start,
    adjoint_rhs,
    off_blocks,
    diag_inverse,
    neighbours,
    node_weights,
    sens_blocks,
    cell_points,
    base_points,
    ffd_index,
    ffd_weight,
):
    nodes, _, cells = adjoint_start.shape
    faces = off_blocks.shape[1]
    blocks = cells // LANES
    per = blocks * nodes
    slots = ffd_index.shape[1]
    far_slots = slots // 2
    parts = [cells // 8, cells // 2, cells // 8]
    parts.append(cells - sum(parts))
    firsts = [sum(parts[:i]) for i in range(4)]
    owned = base_points.shape[1] // lax.axis_size("nodes")
    peers = lax.axis_size(CELL_AXES)
    cores = lax.axis_size("sub")
    node_peers = lax.axis_size("nodes")
    f32, i32, bf16 = jnp.float32, jnp.int32, jnp.bfloat16

    def shape(dims, dtype=f32):
        return jax.ShapeDtypeStruct(dims, dtype)

    def cost(flops, moved):
        return pl.CostEstimate(flops=flops, bytes_accessed=moved, transcendentals=0)

    def swaps(array):
        close = lax.ppermute(array, CELL_AXES, [(i, i ^ 1) for i in range(peers)])
        pairs = []
        for i in range(peers):
            line, core = divmod(i, cores)
            for node in range(node_peers):
                j, beside = (i + 1 if i % 2 else i - 1), node
                if not 0 <= j < peers:
                    j, beside = i, (node ^ 1 if node_peers % 2 == 0 else node)
                to_line, to_core = divmod(j, cores)
                pairs.append(
                    (
                        (line * node_peers + node) * cores + core,
                        (to_line * node_peers + beside) * cores + to_core,
                    )
                )
        return lax.ppermute(array, SUM_AXES, pairs), close

    adjoint = rows_of(adjoint_start)
    far, close = swaps(adjoint)
    prepared = pl.pallas_call(
        functools.partial(prepare_kernel, nodes),
        out_shape=(
            shape((faces * 25 * per, LANES)),
            shape((25 * per, LANES)),
            shape((5 * per, LANES)),
            shape((15 * per, LANES)),
            shape((faces * per, LANES), i32),
            shape((faces * per, LANES), i32),
            shape((slots * 16, owned)),
            shape((slots, owned)),
            shape(((slots - far_slots) * owned, LANES), bf16),
            shape((5 * per, LANES)),
            shape((cells, FACTOR_ROWS), bf16),
            shape((FACTOR_ROWS, owned), bf16),
        ),
        in_specs=[HBM] * 11,
        out_specs=(VMEM,) * 12,
        scratch_shapes=[
            pltpu.VMEM((faces * 25 * per, LANES), bf16),
            pltpu.VMEM((15 * per, LANES), bf16),
            pltpu.VMEM((faces, cells), i32),
            pltpu.SMEM((nodes,), f32),
            pltpu.VMEM((slots, owned), i32),
            pltpu.VMEM((slots, owned), f32),
            pltpu.VMEM((3, cells), f32),
            pltpu.VMEM((3, owned), f32),
            pltpu.SemaphoreType.DMA((11,)),
        ],
        compiler_params=PARAMS,
        cost_estimate=cost(10**9, 10**7),
        name="prepare",
    )(
        *in_hbm(
            rows_of(off_blocks.reshape(nodes, faces * 25, cells)),
            rows_of(diag_inverse),
            rows_of(adjoint_rhs),
            rows_of(sens_blocks),
            neighbours,
            node_weights,
            ffd_index.T,
            ffd_weight.T,
            adjoint,
            cell_points,
            base_points,
        )
    )
    off, inverse, rhs, sens, lane, step, spread, low, near_hot, adjoint, left, right = prepared
    scratch = [
        pltpu.VMEM((3 * 5 * per, LANES), f32),
        pltpu.VMEM((max(8 // nodes - 1, 1) * 3 * 5 * per, LANES), f32),
    ]
    sweep_cost = cost(2 * 10 * 35 * cells, 4 * faces * 25 * per * LANES)

    kernel_shapes = [shape((2 * count, owned), bf16) for count in parts]
    adjoint, first_kernel = pl.pallas_call(
        functools.partial(sweep_kernel, blocks, firsts[0]),
        out_shape=(shape((5 * per, LANES)), kernel_shapes[0]),
        in_specs=[VMEM] * 10,
        out_specs=(VMEM, VMEM),
        scratch_shapes=scratch,
        compiler_params=PARAMS,
        cost_estimate=sweep_cost,
        name="sweep",
    )(close, far, adjoint, rhs, off, inverse, lane, step, left, right)
    far, close = swaps(adjoint)

    wendland_cost = cost(10**9, 10**7)
    near_kernel = pl.pallas_call(
        functools.partial(wendland_kernel, firsts[1]),
        out_shape=kernel_shapes[1],
        in_specs=[VMEM] * 3,
        out_specs=VMEM,
        compiler_params=PARAMS,
        cost_estimate=wendland_cost,
        name="near_wendland",
    )(left, right, adjoint)
    adjoint, third_kernel, part_sens = pl.pallas_call(
        functools.partial(last_sweep_kernel, blocks, firsts[2]),
        out_shape=(shape((5 * per, LANES)), kernel_shapes[2], shape((3 * blocks, LANES))),
        in_specs=[VMEM] * 11 + [pl.BlockSpec(memory_space=pl.ANY)],
        out_specs=(VMEM, VMEM, VMEM),
        scratch_shapes=scratch + [pltpu.VMEM((3 * per, LANES), f32)],
        compiler_params=PARAMS,
        cost_estimate=sweep_cost,
        name="last_sweep",
    )(close, far, adjoint, rhs, off, inverse, lane, step, left, right, sens, near_kernel)

    all_sens = [part_sens]
    for shift in range(1, node_peers):
        ring = [(i, (i + shift) % node_peers) for i in range(node_peers)]
        all_sens.append(lax.ppermute(part_sens, "nodes", ring))
    hot_shape = shape((far_slots * owned, LANES), bf16)
    far_kernel, far_hot, adjoint = pl.pallas_call(
        functools.partial(far_wendland_kernel, firsts[3]),
        out_shape=(kernel_shapes[3], hot_shape, shape((5 * per, LANES))),
        in_specs=[VMEM] * 5,
        out_specs=(VMEM, VMEM, HBM),
        scratch_shapes=[pltpu.SemaphoreType.DMA],
        compiler_params=PARAMS,
        cost_estimate=wendland_cost,
        name="far_wendland",
    )(left, right, part_sens, adjoint, low)
    scale = 4.0 / math.sqrt(cells * peers)
    rows = 3 * FFD // LANES
    partial = pl.pallas_call(
        functools.partial(control_kernel, scale),
        out_shape=shape((rows, LANES)),
        in_specs=[VMEM] * (len(all_sens) + 7),
        out_specs=VMEM,
        compiler_params=PARAMS,
        name="control",
    )(*all_sens, first_kernel, near_kernel, third_kernel, far_kernel, spread, near_hot, far_hot)
    rounds = sum_rounds()
    terms = [partial] if rounds else [lax.psum(partial, SUM_AXES)]
    for masks in rounds or ():
        if len(terms) > 1:
            partial = pl.pallas_call(
                add_kernel, out_shape=shape((rows, LANES)), name="add", compiler_params=PARAMS
            )(*terms)
        terms = exchanged(partial, masks)
    control_grad = pl.pallas_call(
        finish_kernel, out_shape=shape((3, FFD)), name="finish", compiler_params=PARAMS
    )(*terms)
    return (from_rows(adjoint, nodes, cells), control_grad)


def solution(mesh):
    return jax.shard_map(
        body,
        mesh=mesh,
        in_specs=(
            P("nodes", None, ("groups", "cells", "sub")),
            P("nodes", None, ("groups", "cells", "sub")),
            P("nodes", None, None, ("groups", "cells", "sub")),
            P("nodes", None, ("groups", "cells", "sub")),
            P(None, ("cells", "sub")),
            P("nodes"),
            P("nodes", None, ("groups", "cells", "sub")),
            P(None, ("cells", "sub")),
            P(),
            P(),
            P(),
        ),
        out_specs=(P("nodes", None, ("groups", "cells", "sub")), P("groups", None)),
        check_vma=False,
    )
```

```python
import functools
import math

import jax
import jax.numpy as jnp
from jax import lax
from jax.experimental import pallas as pl
from jax.experimental.pallas import tpu as pltpu
from jax.sharding import PartitionSpec as P

FFD = 512
SUPPORT_RADIUS = 0.3
LANES = 128
CELL_AXES = ("cells", "sub")
SUM_AXES = ("cells", "nodes", "sub")
FACTOR_ROWS = 64
PARAMS = pltpu.CompilerParams(vmem_limit_bytes=24 * 1024 * 1024)
VMEM = pl.BlockSpec(memory_space=pltpu.VMEM)
HBM = pl.BlockSpec(memory_space=pltpu.HBM)


def rows_of(array):
    nodes, rows, cells = array.shape
    blocks = cells // LANES
    split = array.reshape(nodes, rows, blocks, LANES)
    return split.transpose(1, 2, 0, 3).reshape(rows * blocks * nodes, LANES)


def from_rows(array, nodes, cells):
    blocks = cells // LANES
    split = array.reshape(-1, blocks, nodes, LANES)
    return split.transpose(2, 0, 1, 3).reshape(nodes, -1, cells)


def in_hbm(*arrays):
    return [pltpu.with_memory_space_constraint(array, pltpu.HBM) for array in arrays]


def write_one_hot(low_ref, one_hot_ref, first_slot):
    owned = low_ref.shape[1]
    piece = min(512, owned)
    lane = lax.broadcasted_iota(jnp.int32, (piece, LANES), 1).astype(jnp.float32)
    lane = lane.astype(jnp.bfloat16)
    for first in range(0, owned, piece):
        low = low_ref[:, first : first + piece].T.astype(jnp.bfloat16)
        for j in range(one_hot_ref.shape[0] // owned):
            column = low[:, first_slot + j : first_slot + j + 1]
            hit = jnp.broadcast_to(column, (piece, LANES)) == lane
            one_hot_ref[j * owned + first : j * owned + first + piece, :] = jnp.where(
                hit, jnp.bfloat16(1.0), jnp.bfloat16(0.0)
            )


def prepare_kernel(
    nodes,
    off_in,
    inverse_in,
    rhs_in,
    sens_in,
    neigh_in,
    weight_in,
    index_in,
    spread_in,
    start_in,
    cell_in,
    base_in,
    off_ref,
    inverse_ref,
    rhs_ref,
    sens_ref,
    lane_ref,
    step_ref,
    spread_ref,
    low_ref,
    one_hot_ref,
    start_ref,
    left_ref,
    right_ref,
    off_buf,
    sens_buf,
    neigh_buf,
    weight_buf,
    index_buf,
    spread_buf,
    cell_buf,
    base_buf,
    sems,
):
    slots, owned = index_buf.shape
    start = pl.multiple_of(lax.axis_index("nodes") * owned, LANES)
    mine = pl.ds(start, owned)
    pairs = (
        (neigh_in, neigh_buf),
        (index_in.at[:, mine], index_buf),
        (spread_in.at[:, mine], spread_buf),
        (cell_in, cell_buf),
        (base_in.at[:, mine], base_buf),
        (off_in, off_buf),
        (weight_in, weight_buf),
        (sens_in, sens_buf),
        (inverse_in, inverse_ref),
        (rhs_in, rhs_ref),
        (start_in, start_ref),
    )
    copies = [pltpu.make_async_copy(a, b, sems.at[i]) for i, (a, b) in enumerate(pairs)]
    for copy in copies:
        copy.start()

    faces, cells = neigh_buf.shape
    blocks = cells // LANES
    per = blocks * nodes
    first_cell = lax.axis_index(CELL_AXES) * cells
    copies[0].wait()
    for block in range(blocks):
        index = neigh_buf[:, block * LANES : (block + 1) * LANES]
        local = index - first_cell + cells
        lane = jnp.bitwise_and(local, LANES - 1)
        step = jnp.right_shift(local, 7) - block
        step = jnp.where(index >= 0, step, -1)
        for node in range(nodes):
            rows = pl.ds(block * nodes + node, faces, stride=per)
            lane_ref[rows, :] = lane
            step_ref[rows, :] = step

    copies[1].wait()
    copies[2].wait()
    groups = FFD // LANES
    piece = min(512, owned)
    for first in range(0, owned, piece):
        here = slice(first, first + piece)
        high = jnp.right_shift(index_buf[:, here], 7)
        part = lax.broadcasted_iota(jnp.int32, (16, piece), 0)
        part = jnp.where(part < 3 * groups, lax.rem(part, groups), -1)
        for j in range(slots):
            spread_ref[j * 16 : (j + 1) * 16, here] = jnp.where(
                high[j : j + 1] == part, spread_buf[j : j + 1, here], 0.0
            )

    low_ref[...] = jnp.bitwise_and(index_buf[...], LANES - 1).astype(jnp.float32)
    write_one_hot(low_ref, one_hot_ref, 0)

    copies[3].wait()
    left_ref[...] = distance_factors(cell_buf[...], True).T.astype(jnp.bfloat16)
    copies[4].wait()
    right_ref[...] = distance_factors(base_buf[...], False).astype(jnp.bfloat16)

    copies[5].wait()
    off_ref[...] = off_buf[...].astype(jnp.float32)
    copies[6].wait()
    copies[7].wait()
    row_node = lax.rem(lax.broadcasted_iota(jnp.int32, (per, LANES), 0), nodes)
    weights = jnp.zeros((per, LANES), jnp.float32)
    for node in range(nodes):
        weights = jnp.where(row_node == node, weight_buf[node], weights)
    for row in range(0, sens_buf.shape[0], per):
        here = slice(row, row + per)
        sens_ref[here, :] = sens_buf[here, :].astype(jnp.float32) * weights
    for copy in copies[8:]:
        copy.wait()


def take_lanes(table, lanes):
    numbers = lax.GatherDimensionNumbers(
        offset_dims=(),
        collapsed_slice_dims=(1,),
        start_index_map=(1,),
        operand_batching_dims=(0,),
        start_indices_batching_dims=(0,),
    )
    return lax.gather(
        table,
        lanes[..., None],
        numbers,
        slice_sizes=(1, 1),
        mode=lax.GatherScatterMode.PROMISE_IN_BOUNDS,
    )


def sweep_into(
    blocks, far_ref, close_ref, own_ref, rhs_ref, off_ref, inverse_ref, lane_ref, step_ref,
    first_cell, left_ref, right_ref, out_ref, kernel_ref, window_ref, table_ref,
):
    places, squares = wendland_places(first_cell, left_ref, right_ref, kernel_ref)
    per = rhs_ref.shape[0] // 5
    nodes = per // blocks
    faces = lane_ref.shape[0] // per
    odd = lax.rem(lax.axis_index(CELL_AXES), 2)
    place = pl.multiple_of((1 - odd) * 2 * per, 8)
    other = pl.multiple_of(odd * 2 * per, 8)
    width = 3 * per
    for b in range(5):
        rows = slice(b * per, (b + 1) * per)
        base = b * width
        window_ref[pl.ds(base + place, per), :] = close_ref[rows, :]
        window_ref[base + per : base + 2 * per, :] = own_ref[rows, :]
        window_ref[pl.ds(base + other, per), :] = far_ref[rows, :]
    for shift in range(1, 8 // nodes):
        for b in range(5):
            for tile in range(0, width - 8, 8):
                to = ((shift - 1) * 5 + b) * width + tile
                table_ref[to : to + 8, :] = window_ref[
                    pl.ds(b * width + tile + shift * nodes, 8), :
                ]
    for half in range(0, per, 8):
        remaining = [rhs_ref[a * per + half : a * per + half + 8, :] for a in range(5)]
        for f in range(faces):
            lanes = lane_ref[f * per + half : f * per + half + 8, :]
            dist = step_ref[f * per + half : f * per + half + 8, :]
            beside = [jnp.zeros((8, LANES), jnp.float32)] * 5
            squared = None
            if places:
                row, lane = places.pop(0)
                squared = squares(row, lane)
            for d in range(2 * blocks + 1):
                here = dist == d
                first = half + d * nodes
                for b in range(5):
                    shift, at = first % 8 // nodes, b * width + first // 8 * 8
                    if shift:
                        at = at + (shift - 1) * 5 * width
                        table = table_ref[at : at + 8, :]
                    else:
                        table = window_ref[at : at + 8, :]
                    beside[b] = jnp.where(here, take_lanes(table, lanes), beside[b])
                if squared is not None and d % 2 and d // 2 * 16 < squared.shape[0]:
                    at = d // 2 * 16
                    wendland_store(squared[at : at + 16], kernel_ref, row + at, lane)
            for a in range(5):
                for b in range(5):
                    at = (f * 25 + 5 * a + b) * per + half
                    remaining[a] = remaining[a] - off_ref[at : at + 8, :] * beside[b]
        for a in range(5):
            total = None
            for b in range(5):
                row = (5 * a + b) * per + half
                term = inverse_ref[row : row + 8, :] * remaining[b]
                total = term if total is None else total + term
            out_ref[a * per + half : a * per + half + 8, :] = total
    while places:
        row, lane = places.pop(0)
        wendland_store(squares(row, lane), kernel_ref, row, lane)


def sweep_kernel(blocks, first_cell, *refs):
    sweep_into(blocks, *refs[:8], first_cell, *refs[8:])


def last_sweep_kernel(blocks, first_cell, *refs):
    ins, (left_ref, right_ref, sens_ref, _, *outs) = refs[:8], refs[8:]
    out_ref, kernel_ref, sens_out_ref, window_ref, table_ref, part_ref = outs
    sweep_into(
        blocks, *ins, first_cell, left_ref, right_ref, out_ref, kernel_ref, window_ref, table_ref
    )
    per = out_ref.shape[0] // 5
    nodes = per // blocks
    for k in range(3):
        total = None
        for a in range(5):
            row = (3 * a + k) * per
            term = out_ref[a * per : (a + 1) * per, :] * sens_ref[row : row + per, :]
            total = term if total is None else total + term
        part_ref[k * per : (k + 1) * per, :] = total
    for block in range(blocks):
        total = None
        for node in range(nodes):
            term = part_ref[pl.ds(block * nodes + node, 3, stride=per), :]
            total = term if total is None else total + term
        sens_out_ref[pl.ds(block, 3, stride=blocks), :] = total


def pieces(value, count):
    found = []
    for _ in range(count):
        piece = value.astype(jnp.bfloat16).astype(jnp.float32)
        found.append(piece)
        value = value - piece
    return found


def distance_factors(points, left):
    count = points.shape[1]
    scaled = (points - 0.5) * (1.0 / SUPPORT_RADIUS)
    scaled = jnp.concatenate([scaled, jnp.zeros((5, count), jnp.float32)], axis=0)
    norm = jnp.sum(scaled * scaled, axis=0, keepdims=True)
    norms = pieces(jnp.broadcast_to(norm, (8, count)), 3)
    row = lax.broadcasted_iota(jnp.int32, (8, count), 0)
    norm_block = jnp.zeros((8, count), jnp.float32)
    for place in range(3):
        norm_block = jnp.where(row == place, norms[place], norm_block)
    ones_block = jnp.where(row < 3, 1.0, 0.0)
    first, second, third = pieces(scaled, 3)
    if left:
        dims = [first, first, second, second, first, third]
        dims = [-2.0 * part for part in dims]
        blocks = dims + [norm_block, ones_block]
    else:
        dims = [first, second, first, second, third, first]
        blocks = dims + [ones_block, norm_block]
    return jnp.concatenate(blocks, axis=0)


def wendland_store(squared, kernel_ref, row, lane):
    squared = jnp.maximum(squared, 1e-30)
    near = jnp.maximum(1.0 - squared * lax.rsqrt(squared), 0.0)
    power = near * near
    kernel = power * power * (1.25 - near)
    first = kernel.astype(jnp.bfloat16)
    rest = (kernel - first.astype(jnp.float32)).astype(jnp.bfloat16)
    cells = kernel_ref.shape[0] // 2
    here = slice(lane, lane + squared.shape[1])
    kernel_ref[row : row + squared.shape[0], here] = first
    kernel_ref[cells + row : cells + row + squared.shape[0], here] = rest


def wendland_places(first_cell, left_ref, right_ref, kernel_ref):
    cells, owned = kernel_ref.shape[0] // 2, kernel_ref.shape[1]
    tile, wide = min(128, cells), min(256, owned)

    def squares(row, lane):
        left = left_ref[first_cell + row : first_cell + row + tile, :]
        right = right_ref[:, lane : lane + wide]
        return jnp.dot(left, right, preferred_element_type=jnp.float32)

    places = [(row, lane) for lane in range(0, owned, wide) for row in range(0, cells, tile)]
    return places, squares


def wendland_kernel(first_cell, left_ref, right_ref, _, kernel_ref):
    places, squares = wendland_places(first_cell, left_ref, right_ref, kernel_ref)
    following = squares(*places[0])
    for at, (row, lane) in enumerate(places):
        squared = following
        if at + 1 < len(places):
            following = squares(*places[at + 1])
        wendland_store(squared, kernel_ref, row, lane)


def far_wendland_kernel(
    first_cell, left_ref, right_ref, after, adjoint_ref, low_ref, *rest
):
    kernel_ref, one_hot_ref, result_ref, sem = rest
    copy = pltpu.make_async_copy(adjoint_ref, result_ref, sem)
    copy.start()
    owned = low_ref.shape[1]
    write_one_hot(low_ref, one_hot_ref, low_ref.shape[0] - one_hot_ref.shape[0] // owned)
    wendland_kernel(first_cell, left_ref, right_ref, after, kernel_ref)
    copy.wait()


def control_kernel(scale, *refs):
    *sens_refs, first_ref, near_ref, third_ref, far_ref = refs[:-4]
    spread_ref, near_hot, far_hot, out_ref = refs[-4:]
    blocks = sens_refs[0].shape[0] // 3
    groups = FFD // LANES
    total = sens_refs[0][...]
    for ref in sens_refs[1:]:
        total = total + ref[...]
    total = total * scale

    def halves(value):
        first = value.astype(jnp.bfloat16)
        rest = (value - first.astype(jnp.float32)).astype(jnp.bfloat16)
        return first, rest

    row = lax.broadcasted_iota(jnp.int32, (8, LANES), 0)
    wide = []
    for block in range(blocks):
        sens = jnp.zeros((8, LANES), jnp.float32)
        for k in range(3):
            sens = jnp.where(row == k, total[k * blocks + block : k * blocks + block + 1], sens)
        first = sens.astype(jnp.bfloat16).astype(jnp.float32)
        wide.append(jnp.concatenate([first, sens - first], axis=0))
    sens = jnp.concatenate(wide, axis=1).astype(jnp.bfloat16)
    grad = None
    cell = 0
    for ref in (first_ref, near_ref, third_ref, far_ref):
        part = sens[:, cell : cell + ref.shape[0] // 2]
        cell += ref.shape[0] // 2
        both = jnp.concatenate([part, part], axis=1)
        term = jnp.dot(both, ref[...], preferred_element_type=jnp.float32)
        grad = term if grad is None else grad + term
    grad = grad[:8] + grad[8:]
    row = lax.broadcasted_iota(jnp.int32, (16, grad.shape[1]), 0)
    wide = jnp.zeros(row.shape, jnp.float32)
    for k in range(3):
        mine = jnp.logical_and(row >= k * groups, row < (k + 1) * groups)
        wide = jnp.where(mine, grad[k : k + 1], wide)
    grad = wide
    owned = grad.shape[1]
    result = None
    places = [
        (ref, first) for ref in (near_hot, far_hot) for first in range(0, ref.shape[0], owned)
    ]
    for j, (ref, first) in enumerate(places):
        term = jnp.dot(
            jnp.concatenate(halves(grad * spread_ref[j * 16 : (j + 1) * 16, :]), axis=0),
            ref[first : first + owned, :],
            preferred_element_type=jnp.float32,
        )
        result = term if result is None else result + term
    result = result[:16] + result[16:]
    out_ref[...] = result[: 3 * groups]


def tree(values):
    while len(values) > 1:
        values = [sum(values[i : i + 2]) for i in range(0, len(values), 2)]
    return values[0]


def add_kernel(*refs):
    refs[-1][...] = tree([ref[...] for ref in refs[:-1]])


def finish_kernel(*refs):
    total, out_ref = tree([ref[...] for ref in refs[:-1]]), refs[-1]
    groups = out_ref.shape[1] // LANES
    for k in range(3):
        for group in range(groups):
            row = k * groups + group
            out_ref[k : k + 1, group * LANES : (group + 1) * LANES] = total[row : row + 1]


def sum_rounds():
    lines, nodes, cores = (lax.axis_size(axis) for axis in SUM_AXES)
    if any(size & (size - 1) for size in (lines, nodes, cores)):
        return None
    near = [cores >> 1 >> i for i in range(cores.bit_length() - 1)]
    node_bits = [cores << i for i in range(nodes.bit_length() - 1)]
    line_bits = [cores * nodes << i for i in range(lines.bit_length() - 1)]
    bits = near + line_bits[:2] + node_bits[:1] + line_bits[2:] + node_bits[1:]
    rounds = []
    for first in range(0, len(bits), 2):
        masks = bits[first : first + 2]
        if len(masks) == 2:
            masks = masks + [masks[0] | masks[1]]
        rounds.append([mask | (cores - 1) for mask in masks] if first else masks)
    return rounds


def exchanged(value, masks):
    peers = lax.axis_size(SUM_AXES)
    return [value] + [
        lax.ppermute(value, SUM_AXES, [(i, i ^ mask) for i in range(peers)]) for mask in masks
    ]


def body(
    adjoint_start,
    adjoint_rhs,
    off_blocks,
    diag_inverse,
    neighbours,
    node_weights,
    sens_blocks,
    cell_points,
    base_points,
    ffd_index,
    ffd_weight,
):
    nodes, _, cells = adjoint_start.shape
    faces = off_blocks.shape[1]
    blocks = cells // LANES
    per = blocks * nodes
    slots = ffd_index.shape[1]
    far_slots = slots // 2
    parts = [cells // 8, cells * 3 // 8, cells // 8]
    parts.append(cells - sum(parts))
    firsts = [sum(parts[:i]) for i in range(4)]
    owned = base_points.shape[1] // lax.axis_size("nodes")
    peers = lax.axis_size(CELL_AXES)
    cores = lax.axis_size("sub")
    node_peers = lax.axis_size("nodes")
    f32, i32, bf16 = jnp.float32, jnp.int32, jnp.bfloat16

    def shape(dims, dtype=f32):
        return jax.ShapeDtypeStruct(dims, dtype)

    def cost(flops, moved):
        return pl.CostEstimate(flops=flops, bytes_accessed=moved, transcendentals=0)

    def swaps(array):
        close = lax.ppermute(array, CELL_AXES, [(i, i ^ 1) for i in range(peers)])
        pairs = []
        for i in range(peers):
            line, core = divmod(i, cores)
            for node in range(node_peers):
                j, beside = (i + 1 if i % 2 else i - 1), node
                if not 0 <= j < peers:
                    j, beside = i, (node ^ 1 if node_peers % 2 == 0 else node)
                to_line, to_core = divmod(j, cores)
                pairs.append(
                    (
                        (line * node_peers + node) * cores + core,
                        (to_line * node_peers + beside) * cores + to_core,
                    )
                )
        return lax.ppermute(array, SUM_AXES, pairs), close

    adjoint = rows_of(adjoint_start)
    far, close = swaps(adjoint)
    prepared = pl.pallas_call(
        functools.partial(prepare_kernel, nodes),
        out_shape=(
            shape((faces * 25 * per, LANES)),
            shape((25 * per, LANES)),
            shape((5 * per, LANES)),
            shape((15 * per, LANES)),
            shape((faces * per, LANES), i32),
            shape((faces * per, LANES), i32),
            shape((slots * 16, owned)),
            shape((slots, owned)),
            shape(((slots - far_slots) * owned, LANES), bf16),
            shape((5 * per, LANES)),
            shape((cells, FACTOR_ROWS), bf16),
            shape((FACTOR_ROWS, owned), bf16),
        ),
        in_specs=[HBM] * 11,
        out_specs=(VMEM,) * 12,
        scratch_shapes=[
            pltpu.VMEM((faces * 25 * per, LANES), bf16),
            pltpu.VMEM((15 * per, LANES), bf16),
            pltpu.VMEM((faces, cells), i32),
            pltpu.SMEM((nodes,), f32),
            pltpu.VMEM((slots, owned), i32),
            pltpu.VMEM((slots, owned), f32),
            pltpu.VMEM((3, cells), f32),
            pltpu.VMEM((3, owned), f32),
            pltpu.SemaphoreType.DMA((11,)),
        ],
        compiler_params=PARAMS,
        cost_estimate=cost(10**9, 10**7),
        name="prepare",
    )(
        *in_hbm(
            rows_of(off_blocks.reshape(nodes, faces * 25, cells)),
            rows_of(diag_inverse),
            rows_of(adjoint_rhs),
            rows_of(sens_blocks),
            neighbours,
            node_weights,
            ffd_index.T,
            ffd_weight.T,
            adjoint,
            cell_points,
            base_points,
        )
    )
    off, inverse, rhs, sens, lane, step, spread, low, near_hot, adjoint, left, right = prepared
    scratch = [
        pltpu.VMEM((3 * 5 * per, LANES), f32),
        pltpu.VMEM((max(8 // nodes - 1, 1) * 3 * 5 * per, LANES), f32),
    ]
    sweep_cost = cost(2 * 10 * 35 * cells, 4 * faces * 25 * per * LANES)

    kernel_shapes = [shape((2 * count, owned), bf16) for count in parts]
    adjoint, first_kernel = pl.pallas_call(
        functools.partial(sweep_kernel, blocks, firsts[0]),
        out_shape=(shape((5 * per, LANES)), kernel_shapes[0]),
        in_specs=[VMEM] * 10,
        out_specs=(VMEM, VMEM),
        scratch_shapes=scratch,
        compiler_params=PARAMS,
        cost_estimate=sweep_cost,
        name="sweep",
    )(far, close, adjoint, rhs, off, inverse, lane, step, left, right)
    far, close = swaps(adjoint)

    wendland_cost = cost(10**9, 10**7)
    near_kernel = pl.pallas_call(
        functools.partial(wendland_kernel, firsts[1]),
        out_shape=kernel_shapes[1],
        in_specs=[VMEM] * 3,
        out_specs=VMEM,
        compiler_params=PARAMS,
        cost_estimate=wendland_cost,
        name="near_wendland",
    )(left, right, adjoint)
    adjoint, third_kernel, part_sens = pl.pallas_call(
        functools.partial(last_sweep_kernel, blocks, firsts[2]),
        out_shape=(shape((5 * per, LANES)), kernel_shapes[2], shape((3 * blocks, LANES))),
        in_specs=[VMEM] * 11 + [pl.BlockSpec(memory_space=pl.ANY)],
        out_specs=(VMEM, VMEM, VMEM),
        scratch_shapes=scratch + [pltpu.VMEM((3 * per, LANES), f32)],
        compiler_params=PARAMS,
        cost_estimate=sweep_cost,
        name="last_sweep",
    )(far, close, adjoint, rhs, off, inverse, lane, step, left, right, sens, near_kernel)

    all_sens = [part_sens]
    for shift in range(1, node_peers):
        ring = [(i, (i + shift) % node_peers) for i in range(node_peers)]
        all_sens.append(lax.ppermute(part_sens, "nodes", ring))
    hot_shape = shape((far_slots * owned, LANES), bf16)
    far_kernel, far_hot, adjoint = pl.pallas_call(
        functools.partial(far_wendland_kernel, firsts[3]),
        out_shape=(kernel_shapes[3], hot_shape, shape((5 * per, LANES))),
        in_specs=[VMEM] * 5,
        out_specs=(VMEM, VMEM, HBM),
        scratch_shapes=[pltpu.SemaphoreType.DMA],
        compiler_params=PARAMS,
        cost_estimate=wendland_cost,
        name="far_wendland",
    )(left, right, part_sens, adjoint, low)
    scale = 4.0 / math.sqrt(cells * peers)
    rows = 3 * FFD // LANES
    partial = pl.pallas_call(
        functools.partial(control_kernel, scale),
        out_shape=shape((rows, LANES)),
        in_specs=[VMEM] * (len(all_sens) + 7),
        out_specs=VMEM,
        compiler_params=PARAMS,
        name="control",
    )(*all_sens, first_kernel, near_kernel, third_kernel, far_kernel, spread, near_hot, far_hot)
    rounds = sum_rounds()
    terms = [partial] if rounds else [lax.psum(partial, SUM_AXES)]
    for masks in rounds or ():
        if len(terms) > 1:
            partial = pl.pallas_call(
                add_kernel, out_shape=shape((rows, LANES)), name="add", compiler_params=PARAMS
            )(*terms)
        terms = exchanged(partial, masks)
    control_grad = pl.pallas_call(
        finish_kernel, out_shape=shape((3, FFD)), name="finish", compiler_params=PARAMS
    )(*terms)
    return (from_rows(adjoint, nodes, cells), control_grad)


def solution(mesh):
    return jax.shard_map(
        body,
        mesh=mesh,
        in_specs=(
            P("nodes", None, ("groups", "cells", "sub")),
            P("nodes", None, ("groups", "cells", "sub")),
            P("nodes", None, None, ("groups", "cells", "sub")),
            P("nodes", None, ("groups", "cells", "sub")),
            P(None, ("cells", "sub")),
            P("nodes"),
            P("nodes", None, ("groups", "cells", "sub")),
            P(None, ("cells", "sub")),
            P(),
            P(),
            P(),
        ),
        out_specs=(P("nodes", None, ("groups", "cells", "sub")), P("groups", None)),
        check_vma=False,
    )
```

```python
import functools
import math

import jax
import jax.numpy as jnp
from jax import lax
from jax.experimental import pallas as pl
from jax.experimental.pallas import tpu as pltpu
from jax.sharding import PartitionSpec as P

SWEEPS = 2
FFD = 512
SUPPORT_RADIUS = 0.3
LANES = 128
CELL_AXES = ("cells", "sub")
SUM_AXES = ("cells", "nodes", "sub")
FACTOR_ROWS = 64
PARAMS = pltpu.CompilerParams(vmem_limit_bytes=24 * 1024 * 1024)
VMEM = pl.BlockSpec(memory_space=pltpu.VMEM)
HBM = pl.BlockSpec(memory_space=pltpu.HBM)


def rows_of(array):
    nodes, rows, cells = array.shape
    blocks = cells // LANES
    split = array.reshape(nodes, rows, blocks, LANES)
    return split.transpose(1, 2, 0, 3).reshape(rows * blocks * nodes, LANES)


def from_rows(array, nodes, cells):
    blocks = cells // LANES
    split = array.reshape(-1, blocks, nodes, LANES)
    return split.transpose(2, 0, 1, 3).reshape(nodes, -1, cells)


def in_hbm(*arrays):
    return [pltpu.with_memory_space_constraint(array, pltpu.HBM) for array in arrays]


def write_one_hot(low_ref, one_hot_ref, first_slot):
    owned = low_ref.shape[1]
    piece = min(512, owned)
    lane = lax.broadcasted_iota(jnp.int32, (piece, LANES), 1).astype(jnp.float32)
    lane = lane.astype(jnp.bfloat16)
    for first in range(0, owned, piece):
        low = low_ref[:, first : first + piece].T.astype(jnp.bfloat16)
        for j in range(one_hot_ref.shape[0] // owned):
            column = low[:, first_slot + j : first_slot + j + 1]
            hit = jnp.broadcast_to(column, (piece, LANES)) == lane
            one_hot_ref[j * owned + first : j * owned + first + piece, :] = jnp.where(
                hit, jnp.bfloat16(1.0), jnp.bfloat16(0.0)
            )


def prepare_kernel(
    nodes,
    off_in,
    inverse_in,
    rhs_in,
    sens_in,
    neigh_in,
    weight_in,
    index_in,
    spread_in,
    start_in,
    cell_in,
    base_in,
    off_ref,
    inverse_ref,
    rhs_ref,
    sens_ref,
    lane_ref,
    step_ref,
    spread_ref,
    low_ref,
    one_hot_ref,
    start_ref,
    left_ref,
    right_ref,
    off_buf,
    sens_buf,
    neigh_buf,
    weight_buf,
    index_buf,
    spread_buf,
    cell_buf,
    base_buf,
    sems,
):
    slots, owned = index_buf.shape
    start = pl.multiple_of(lax.axis_index("nodes") * owned, LANES)
    mine = pl.ds(start, owned)
    pairs = (
        (neigh_in, neigh_buf),
        (index_in.at[:, mine], index_buf),
        (spread_in.at[:, mine], spread_buf),
        (cell_in, cell_buf),
        (base_in.at[:, mine], base_buf),
        (off_in, off_buf),
        (weight_in, weight_buf),
        (sens_in, sens_buf),
        (inverse_in, inverse_ref),
        (rhs_in, rhs_ref),
        (start_in, start_ref),
    )
    copies = [pltpu.make_async_copy(a, b, sems.at[i]) for i, (a, b) in enumerate(pairs)]
    for copy in copies:
        copy.start()

    faces, cells = neigh_buf.shape
    blocks = cells // LANES
    per = blocks * nodes
    first_cell = lax.axis_index(CELL_AXES) * cells
    copies[0].wait()
    for block in range(blocks):
        index = neigh_buf[:, block * LANES : (block + 1) * LANES]
        local = index - first_cell + cells
        lane = jnp.bitwise_and(local, LANES - 1)
        step = jnp.right_shift(local, 7) - block
        step = jnp.where(index >= 0, step, -1)
        for node in range(nodes):
            rows = pl.ds(block * nodes + node, faces, stride=per)
            lane_ref[rows, :] = lane
            step_ref[rows, :] = step

    copies[1].wait()
    copies[2].wait()
    groups = FFD // LANES
    piece = min(512, owned)
    for first in range(0, owned, piece):
        here = slice(first, first + piece)
        high = jnp.right_shift(index_buf[:, here], 7)
        part = lax.broadcasted_iota(jnp.int32, (16, piece), 0)
        part = jnp.where(part < 3 * groups, lax.rem(part, groups), -1)
        for j in range(slots):
            spread_ref[j * 16 : (j + 1) * 16, here] = jnp.where(
                high[j : j + 1] == part, spread_buf[j : j + 1, here], 0.0
            )

    low_ref[...] = jnp.bitwise_and(index_buf[...], LANES - 1).astype(jnp.float32)
    write_one_hot(low_ref, one_hot_ref, 0)

    copies[3].wait()
    left_ref[...] = distance_factors(cell_buf[...], True).T.astype(jnp.bfloat16)
    copies[4].wait()
    right_ref[...] = distance_factors(base_buf[...], False).astype(jnp.bfloat16)

    copies[5].wait()
    off_ref[...] = off_buf[...].astype(jnp.float32)
    copies[6].wait()
    copies[7].wait()
    row_node = lax.rem(lax.broadcasted_iota(jnp.int32, (per, LANES), 0), nodes)
    weights = jnp.zeros((per, LANES), jnp.float32)
    for node in range(nodes):
        weights = jnp.where(row_node == node, weight_buf[node], weights)
    for row in range(0, sens_buf.shape[0], per):
        here = slice(row, row + per)
        sens_ref[here, :] = sens_buf[here, :].astype(jnp.float32) * weights
    for copy in copies[8:]:
        copy.wait()


def take_lanes(table, lanes):
    numbers = lax.GatherDimensionNumbers(
        offset_dims=(),
        collapsed_slice_dims=(1,),
        start_index_map=(1,),
        operand_batching_dims=(0,),
        start_indices_batching_dims=(0,),
    )
    return lax.gather(
        table,
        lanes[..., None],
        numbers,
        slice_sizes=(1, 1),
        mode=lax.GatherScatterMode.PROMISE_IN_BOUNDS,
    )


def sweep_into(
    blocks, first_ref, second_ref, own_ref, rhs_ref, off_ref, inverse_ref, lane_ref, step_ref,
    out_ref, window_ref, table_ref,
):
    per = rhs_ref.shape[0] // 5
    nodes = per // blocks
    faces = lane_ref.shape[0] // per
    odd = lax.rem(lax.axis_index(CELL_AXES), 2)
    place = pl.multiple_of((1 - odd) * 2 * per, 8)
    other = pl.multiple_of(odd * 2 * per, 8)
    width = 3 * per
    for b in range(5):
        rows = slice(b * per, (b + 1) * per)
        base = b * width
        window_ref[pl.ds(base + place, per), :] = first_ref[rows, :]
        window_ref[base + per : base + 2 * per, :] = own_ref[rows, :]
        window_ref[pl.ds(base + other, per), :] = second_ref[rows, :]
    for shift in range(1, 8 // nodes):
        for b in range(5):
            for tile in range(0, width - 8, 8):
                to = ((shift - 1) * 5 + b) * width + tile
                table_ref[to : to + 8, :] = window_ref[
                    pl.ds(b * width + tile + shift * nodes, 8), :
                ]
    for half in range(0, per, 8):
        remaining = [rhs_ref[a * per + half : a * per + half + 8, :] for a in range(5)]
        for f in range(faces):
            lanes = lane_ref[f * per + half : f * per + half + 8, :]
            dist = step_ref[f * per + half : f * per + half + 8, :]
            beside = [jnp.zeros((8, LANES), jnp.float32)] * 5
            for d in range(2 * blocks + 1):
                here = dist == d
                first = half + d * nodes
                for b in range(5):
                    shift, at = first % 8 // nodes, b * width + first // 8 * 8
                    if shift:
                        at = at + (shift - 1) * 5 * width
                        table = table_ref[at : at + 8, :]
                    else:
                        table = window_ref[at : at + 8, :]
                    beside[b] = jnp.where(here, take_lanes(table, lanes), beside[b])
            for a in range(5):
                for b in range(5):
                    row = (f * 25 + 5 * a + b) * per + half
                    remaining[a] = remaining[a] - off_ref[row : row + 8, :] * beside[b]
        for a in range(5):
            total = None
            for b in range(5):
                row = (5 * a + b) * per + half
                term = inverse_ref[row : row + 8, :] * remaining[b]
                total = term if total is None else total + term
            out_ref[a * per + half : a * per + half + 8, :] = total


def sweep_kernel(blocks, *refs):
    sweep_into(blocks, *refs)


def last_sweep_kernel(blocks, *refs):
    ins, rest = refs[:8], refs[8:]
    sens_ref, _, out_ref, sens_out_ref, window_ref, table_ref, part_ref = rest
    sweep_into(blocks, *ins, out_ref, window_ref, table_ref)
    per = out_ref.shape[0] // 5
    nodes = per // blocks
    for k in range(3):
        total = None
        for a in range(5):
            row = (3 * a + k) * per
            term = out_ref[a * per : (a + 1) * per, :] * sens_ref[row : row + per, :]
            total = term if total is None else total + term
        part_ref[k * per : (k + 1) * per, :] = total
    for block in range(blocks):
        total = None
        for node in range(nodes):
            term = part_ref[pl.ds(block * nodes + node, 3, stride=per), :]
            total = term if total is None else total + term
        sens_out_ref[pl.ds(block, 3, stride=blocks), :] = total


def pieces(value, count):
    found = []
    for _ in range(count):
        piece = value.astype(jnp.bfloat16).astype(jnp.float32)
        found.append(piece)
        value = value - piece
    return found


def distance_factors(points, left):
    count = points.shape[1]
    scaled = (points - 0.5) * (1.0 / SUPPORT_RADIUS)
    scaled = jnp.concatenate([scaled, jnp.zeros((5, count), jnp.float32)], axis=0)
    norm = jnp.sum(scaled * scaled, axis=0, keepdims=True)
    norms = pieces(jnp.broadcast_to(norm, (8, count)), 3)
    row = lax.broadcasted_iota(jnp.int32, (8, count), 0)
    norm_block = jnp.zeros((8, count), jnp.float32)
    for place in range(3):
        norm_block = jnp.where(row == place, norms[place], norm_block)
    ones_block = jnp.where(row < 3, 1.0, 0.0)
    first, second, third = pieces(scaled, 3)
    if left:
        dims = [first, first, second, second, first, third]
        dims = [-2.0 * part for part in dims]
        blocks = dims + [norm_block, ones_block]
    else:
        dims = [first, second, first, second, third, first]
        blocks = dims + [ones_block, norm_block]
    return jnp.concatenate(blocks, axis=0)


def wendland_kernel(first_cell, left_ref, right_ref, _, kernel_ref):
    cells, owned = kernel_ref.shape[0] // 2, kernel_ref.shape[1]
    tile, wide = min(128, cells), min(256, owned)

    def squares(row, lane):
        left = left_ref[first_cell + row : first_cell + row + tile, :]
        right = right_ref[:, lane : lane + wide]
        return jnp.dot(left, right, preferred_element_type=jnp.float32)

    places = [(row, lane) for lane in range(0, owned, wide) for row in range(0, cells, tile)]
    following = squares(*places[0])
    for at, (row, lane) in enumerate(places):
        squared = jnp.maximum(following, 1e-30)
        if at + 1 < len(places):
            following = squares(*places[at + 1])
        near = jnp.maximum(1.0 - squared * lax.rsqrt(squared), 0.0)
        power = near * near
        kernel = power * power * (1.25 - near)
        first = kernel.astype(jnp.bfloat16)
        rest = (kernel - first.astype(jnp.float32)).astype(jnp.bfloat16)
        here = slice(lane, lane + wide)
        kernel_ref[row : row + tile, here] = first
        kernel_ref[cells + row : cells + row + tile, here] = rest


def far_wendland_kernel(
    first_cell, left_ref, right_ref, after, adjoint_ref, low_ref, *rest
):
    kernel_ref, one_hot_ref, result_ref, sem = rest
    copy = pltpu.make_async_copy(adjoint_ref, result_ref, sem)
    copy.start()
    owned = low_ref.shape[1]
    write_one_hot(low_ref, one_hot_ref, low_ref.shape[0] - one_hot_ref.shape[0] // owned)
    wendland_kernel(first_cell, left_ref, right_ref, after, kernel_ref)
    copy.wait()


def control_kernel(scale, *refs):
    *sens_refs, near_ref, far_ref = refs[:-4]
    spread_ref, near_hot, far_hot, out_ref = refs[-4:]
    blocks = sens_refs[0].shape[0] // 3
    half = near_ref.shape[0] // 2
    groups = FFD // LANES
    total = sens_refs[0][...]
    for ref in sens_refs[1:]:
        total = total + ref[...]
    total = total * scale

    def halves(value):
        first = value.astype(jnp.bfloat16)
        rest = (value - first.astype(jnp.float32)).astype(jnp.bfloat16)
        return first, rest

    row = lax.broadcasted_iota(jnp.int32, (8, LANES), 0)
    wide = []
    for block in range(blocks):
        sens = jnp.zeros((8, LANES), jnp.float32)
        for k in range(3):
            sens = jnp.where(row == k, total[k * blocks + block : k * blocks + block + 1], sens)
        first = sens.astype(jnp.bfloat16).astype(jnp.float32)
        wide.append(jnp.concatenate([first, sens - first], axis=0))
    sens = jnp.concatenate(wide, axis=1).astype(jnp.bfloat16)
    grad = None
    for part, ref in ((sens[:, :half], near_ref), (sens[:, half:], far_ref)):
        both = jnp.concatenate([part, part], axis=1)
        term = jnp.dot(both, ref[...], preferred_element_type=jnp.float32)
        grad = term if grad is None else grad + term
    grad = grad[:8] + grad[8:]
    row = lax.broadcasted_iota(jnp.int32, (16, grad.shape[1]), 0)
    wide = jnp.zeros(row.shape, jnp.float32)
    for k in range(3):
        mine = jnp.logical_and(row >= k * groups, row < (k + 1) * groups)
        wide = jnp.where(mine, grad[k : k + 1], wide)
    grad = wide
    owned = grad.shape[1]
    result = None
    places = [
        (ref, first) for ref in (near_hot, far_hot) for first in range(0, ref.shape[0], owned)
    ]
    for j, (ref, first) in enumerate(places):
        term = jnp.dot(
            jnp.concatenate(halves(grad * spread_ref[j * 16 : (j + 1) * 16, :]), axis=0),
            ref[first : first + owned, :],
            preferred_element_type=jnp.float32,
        )
        result = term if result is None else result + term
    result = result[:16] + result[16:]
    out_ref[...] = result[: 3 * groups]


def tree(values):
    while len(values) > 1:
        values = [sum(values[i : i + 2]) for i in range(0, len(values), 2)]
    return values[0]


def add_kernel(*refs):
    refs[-1][...] = tree([ref[...] for ref in refs[:-1]])


def finish_kernel(*refs):
    total, out_ref = tree([ref[...] for ref in refs[:-1]]), refs[-1]
    groups = out_ref.shape[1] // LANES
    for k in range(3):
        for group in range(groups):
            row = k * groups + group
            out_ref[k : k + 1, group * LANES : (group + 1) * LANES] = total[row : row + 1]


def sum_rounds():
    lines, nodes, cores = (lax.axis_size(axis) for axis in SUM_AXES)
    if any(size & (size - 1) for size in (lines, nodes, cores)):
        return None
    near = [cores >> 1 >> i for i in range(cores.bit_length() - 1)]
    node_bits = [cores << i for i in range(nodes.bit_length() - 1)]
    line_bits = [cores * nodes << i for i in range(lines.bit_length() - 1)]
    bits = near + line_bits[:2] + node_bits[:1] + line_bits[2:] + node_bits[1:]
    rounds = []
    for first in range(0, len(bits), 2):
        masks = bits[first : first + 2]
        if len(masks) == 2:
            masks = masks + [masks[0] | masks[1]]
        rounds.append([mask | (cores - 1) for mask in masks] if first else masks)
    return rounds


def exchanged(value, masks):
    peers = lax.axis_size(SUM_AXES)
    return [value] + [
        lax.ppermute(value, SUM_AXES, [(i, i ^ mask) for i in range(peers)]) for mask in masks
    ]


def body(
    adjoint_start,
    adjoint_rhs,
    off_blocks,
    diag_inverse,
    neighbours,
    node_weights,
    sens_blocks,
    cell_points,
    base_points,
    ffd_index,
    ffd_weight,
):
    nodes, _, cells = adjoint_start.shape
    faces = off_blocks.shape[1]
    blocks = cells // LANES
    per = blocks * nodes
    slots = ffd_index.shape[1]
    far_slots = slots // 2
    owned = base_points.shape[1] // lax.axis_size("nodes")
    peers = lax.axis_size(CELL_AXES)
    cores = lax.axis_size("sub")
    node_peers = lax.axis_size("nodes")
    f32, i32, bf16 = jnp.float32, jnp.int32, jnp.bfloat16

    def shape(dims, dtype=f32):
        return jax.ShapeDtypeStruct(dims, dtype)

    def cost(flops, moved):
        return pl.CostEstimate(flops=flops, bytes_accessed=moved, transcendentals=0)

    def swaps(array):
        close = lax.ppermute(array, CELL_AXES, [(i, i ^ 1) for i in range(peers)])
        pairs = []
        for i in range(peers):
            line, core = divmod(i, cores)
            for node in range(node_peers):
                j, beside = (i + 1 if i % 2 else i - 1), node
                if not 0 <= j < peers:
                    j, beside = i, (node ^ 1 if node_peers % 2 == 0 else node)
                to_line, to_core = divmod(j, cores)
                pairs.append(
                    (
                        (line * node_peers + node) * cores + core,
                        (to_line * node_peers + beside) * cores + to_core,
                    )
                )
        return lax.ppermute(array, SUM_AXES, pairs), close

    adjoint = rows_of(adjoint_start)
    far, close = swaps(adjoint)
    prepared = pl.pallas_call(
        functools.partial(prepare_kernel, nodes),
        out_shape=(
            shape((faces * 25 * per, LANES)),
            shape((25 * per, LANES)),
            shape((5 * per, LANES)),
            shape((15 * per, LANES)),
            shape((faces * per, LANES), i32),
            shape((faces * per, LANES), i32),
            shape((slots * 16, owned)),
            shape((slots, owned)),
            shape(((slots - far_slots) * owned, LANES), bf16),
            shape((5 * per, LANES)),
            shape((cells, FACTOR_ROWS), bf16),
            shape((FACTOR_ROWS, owned), bf16),
        ),
        in_specs=[HBM] * 11,
        out_specs=(VMEM,) * 12,
        scratch_shapes=[
            pltpu.VMEM((faces * 25 * per, LANES), bf16),
            pltpu.VMEM((15 * per, LANES), bf16),
            pltpu.VMEM((faces, cells), i32),
            pltpu.SMEM((nodes,), f32),
            pltpu.VMEM((slots, owned), i32),
            pltpu.VMEM((slots, owned), f32),
            pltpu.VMEM((3, cells), f32),
            pltpu.VMEM((3, owned), f32),
            pltpu.SemaphoreType.DMA((11,)),
        ],
        compiler_params=PARAMS,
        cost_estimate=cost(10**9, 10**7),
        name="prepare",
    )(
        *in_hbm(
            rows_of(off_blocks.reshape(nodes, faces * 25, cells)),
            rows_of(diag_inverse),
            rows_of(adjoint_rhs),
            rows_of(sens_blocks),
            neighbours,
            node_weights,
            ffd_index.T,
            ffd_weight.T,
            adjoint,
            cell_points,
            base_points,
        )
    )
    off, inverse, rhs, sens, lane, step, spread, low, near_hot, adjoint, left, right = prepared
    scratch = [
        pltpu.VMEM((3 * 5 * per, LANES), f32),
        pltpu.VMEM((max(8 // nodes - 1, 1) * 3 * 5 * per, LANES), f32),
    ]
    sweep_cost = cost(2 * 10 * 35 * cells, 4 * faces * 25 * per * LANES)

    for _ in range(SWEEPS - 1):
        adjoint = pl.pallas_call(
            functools.partial(sweep_kernel, blocks),
            out_shape=shape((5 * per, LANES)),
            in_specs=[VMEM] * 8,
            out_specs=VMEM,
            scratch_shapes=scratch,
            compiler_params=PARAMS,
            cost_estimate=sweep_cost,
            name="sweep",
        )(close, far, adjoint, rhs, off, inverse, lane, step)
        far, close = swaps(adjoint)

    half = cells * 5 // 8 // LANES * LANES
    wendland_cost = cost(10**9, 10**7)
    near_shape = shape((2 * half, owned), bf16)
    far_shape = shape((2 * (cells - half), owned), bf16)
    near_kernel = pl.pallas_call(
        functools.partial(wendland_kernel, 0),
        out_shape=near_shape,
        in_specs=[VMEM] * 3,
        out_specs=VMEM,
        compiler_params=PARAMS,
        cost_estimate=wendland_cost,
        name="near_wendland",
    )(left, right, adjoint)
    adjoint, part_sens = pl.pallas_call(
        functools.partial(last_sweep_kernel, blocks),
        out_shape=(shape((5 * per, LANES)), shape((3 * blocks, LANES))),
        in_specs=[VMEM] * 9 + [pl.BlockSpec(memory_space=pl.ANY)],
        out_specs=(VMEM, VMEM),
        scratch_shapes=scratch + [pltpu.VMEM((3 * per, LANES), f32)],
        compiler_params=PARAMS,
        cost_estimate=sweep_cost,
        name="last_sweep",
    )(close, far, adjoint, rhs, off, inverse, lane, step, sens, near_kernel)

    all_sens = [part_sens]
    for shift in range(1, node_peers):
        ring = [(i, (i + shift) % node_peers) for i in range(node_peers)]
        all_sens.append(lax.ppermute(part_sens, "nodes", ring))
    hot_shape = shape((far_slots * owned, LANES), bf16)
    far_kernel, far_hot, adjoint = pl.pallas_call(
        functools.partial(far_wendland_kernel, half),
        out_shape=(far_shape, hot_shape, shape((5 * per, LANES))),
        in_specs=[VMEM] * 5,
        out_specs=(VMEM, VMEM, HBM),
        scratch_shapes=[pltpu.SemaphoreType.DMA],
        compiler_params=PARAMS,
        cost_estimate=wendland_cost,
        name="far_wendland",
    )(left, right, part_sens, adjoint, low)
    scale = 4.0 / math.sqrt(cells * peers)
    rows = 3 * FFD // LANES
    partial = pl.pallas_call(
        functools.partial(control_kernel, scale),
        out_shape=shape((rows, LANES)),
        in_specs=[VMEM] * (len(all_sens) + 5),
        out_specs=VMEM,
        compiler_params=PARAMS,
        name="control",
    )(*all_sens, near_kernel, far_kernel, spread, near_hot, far_hot)
    rounds = sum_rounds()
    terms = [partial] if rounds else [lax.psum(partial, SUM_AXES)]
    for masks in rounds or ():
        if len(terms) > 1:
            partial = pl.pallas_call(
                add_kernel, out_shape=shape((rows, LANES)), name="add", compiler_params=PARAMS
            )(*terms)
        terms = exchanged(partial, masks)
    control_grad = pl.pallas_call(
        finish_kernel, out_shape=shape((3, FFD)), name="finish", compiler_params=PARAMS
    )(*terms)
    return (from_rows(adjoint, nodes, cells), control_grad)


def solution(mesh):
    return jax.shard_map(
        body,
        mesh=mesh,
        in_specs=(
            P("nodes", None, ("groups", "cells", "sub")),
            P("nodes", None, ("groups", "cells", "sub")),
            P("nodes", None, None, ("groups", "cells", "sub")),
            P("nodes", None, ("groups", "cells", "sub")),
            P(None, ("cells", "sub")),
            P("nodes"),
            P("nodes", None, ("groups", "cells", "sub")),
            P(None, ("cells", "sub")),
            P(),
            P(),
            P(),
        ),
        out_specs=(P("nodes", None, ("groups", "cells", "sub")), P("groups", None)),
        check_vma=False,
    )
```

```python
import functools
import math

import jax
import jax.numpy as jnp
from jax import lax
from jax.experimental import pallas as pl
from jax.experimental.pallas import tpu as pltpu
from jax.sharding import PartitionSpec as P

SWEEPS = 2
FFD = 512
SUPPORT_RADIUS = 0.3
LANES = 128
CELL_AXES = ("cells", "sub")
SUM_AXES = ("cells", "nodes", "sub")
FACTOR_ROWS = 64
PARAMS = pltpu.CompilerParams(vmem_limit_bytes=24 * 1024 * 1024)
VMEM = pl.BlockSpec(memory_space=pltpu.VMEM)
HBM = pl.BlockSpec(memory_space=pltpu.HBM)


def rows_of(array):
    nodes, rows, cells = array.shape
    blocks = cells // LANES
    split = array.reshape(nodes, rows, blocks, LANES)
    return split.transpose(1, 2, 0, 3).reshape(rows * blocks * nodes, LANES)


def from_rows(array, nodes, cells):
    blocks = cells // LANES
    split = array.reshape(-1, blocks, nodes, LANES)
    return split.transpose(2, 0, 1, 3).reshape(nodes, -1, cells)


def in_hbm(*arrays):
    return [pltpu.with_memory_space_constraint(array, pltpu.HBM) for array in arrays]


def write_one_hot(low_ref, one_hot_ref, first_slot):
    owned = low_ref.shape[1]
    piece = min(512, owned)
    lane = lax.broadcasted_iota(jnp.int32, (piece, LANES), 1).astype(jnp.float32)
    lane = lane.astype(jnp.bfloat16)
    for first in range(0, owned, piece):
        low = low_ref[:, first : first + piece].T.astype(jnp.bfloat16)
        for j in range(one_hot_ref.shape[0] // owned):
            column = low[:, first_slot + j : first_slot + j + 1]
            hit = jnp.broadcast_to(column, (piece, LANES)) == lane
            one_hot_ref[j * owned + first : j * owned + first + piece, :] = jnp.where(
                hit, jnp.bfloat16(1.0), jnp.bfloat16(0.0)
            )


def prepare_kernel(
    nodes,
    off_in,
    inverse_in,
    rhs_in,
    sens_in,
    neigh_in,
    weight_in,
    index_in,
    spread_in,
    start_in,
    cell_in,
    base_in,
    off_ref,
    inverse_ref,
    rhs_ref,
    sens_ref,
    lane_ref,
    step_ref,
    spread_ref,
    low_ref,
    one_hot_ref,
    start_ref,
    left_ref,
    right_ref,
    off_buf,
    sens_buf,
    neigh_buf,
    weight_buf,
    index_buf,
    spread_buf,
    cell_buf,
    base_buf,
    sems,
):
    slots, owned = index_buf.shape
    start = pl.multiple_of(lax.axis_index("nodes") * owned, LANES)
    mine = pl.ds(start, owned)
    pairs = (
        (neigh_in, neigh_buf),
        (index_in.at[:, mine], index_buf),
        (spread_in.at[:, mine], spread_buf),
        (cell_in, cell_buf),
        (base_in.at[:, mine], base_buf),
        (off_in, off_buf),
        (weight_in, weight_buf),
        (sens_in, sens_buf),
        (inverse_in, inverse_ref),
        (rhs_in, rhs_ref),
        (start_in, start_ref),
    )
    copies = [pltpu.make_async_copy(a, b, sems.at[i]) for i, (a, b) in enumerate(pairs)]
    for copy in copies:
        copy.start()

    faces, cells = neigh_buf.shape
    blocks = cells // LANES
    per = blocks * nodes
    first_cell = lax.axis_index(CELL_AXES) * cells
    copies[0].wait()
    for block in range(blocks):
        index = neigh_buf[:, block * LANES : (block + 1) * LANES]
        local = index - first_cell + cells
        lane = jnp.bitwise_and(local, LANES - 1)
        step = jnp.right_shift(local, 7) - block
        step = jnp.where(index >= 0, step, -1)
        for node in range(nodes):
            rows = pl.ds(block * nodes + node, faces, stride=per)
            lane_ref[rows, :] = lane
            step_ref[rows, :] = step

    copies[1].wait()
    copies[2].wait()
    groups = FFD // LANES
    piece = min(512, owned)
    for first in range(0, owned, piece):
        here = slice(first, first + piece)
        high = jnp.right_shift(index_buf[:, here], 7)
        part = lax.broadcasted_iota(jnp.int32, (16, piece), 0)
        part = jnp.where(part < 3 * groups, lax.rem(part, groups), -1)
        for j in range(slots):
            spread_ref[j * 16 : (j + 1) * 16, here] = jnp.where(
                high[j : j + 1] == part, spread_buf[j : j + 1, here], 0.0
            )

    low_ref[...] = jnp.bitwise_and(index_buf[...], LANES - 1).astype(jnp.float32)
    write_one_hot(low_ref, one_hot_ref, 0)

    copies[3].wait()
    left_ref[...] = distance_factors(cell_buf[...], True).T.astype(jnp.bfloat16)
    copies[4].wait()
    right_ref[...] = distance_factors(base_buf[...], False).astype(jnp.bfloat16)

    copies[5].wait()
    off_ref[...] = off_buf[...].astype(jnp.float32)
    copies[6].wait()
    copies[7].wait()
    row_node = lax.rem(lax.broadcasted_iota(jnp.int32, (per, LANES), 0), nodes)
    weights = jnp.zeros((per, LANES), jnp.float32)
    for node in range(nodes):
        weights = jnp.where(row_node == node, weight_buf[node], weights)
    for row in range(0, sens_buf.shape[0], per):
        here = slice(row, row + per)
        sens_ref[here, :] = sens_buf[here, :].astype(jnp.float32) * weights
    for copy in copies[8:]:
        copy.wait()


def take_lanes(table, lanes):
    numbers = lax.GatherDimensionNumbers(
        offset_dims=(),
        collapsed_slice_dims=(1,),
        start_index_map=(1,),
        operand_batching_dims=(0,),
        start_indices_batching_dims=(0,),
    )
    return lax.gather(
        table,
        lanes[..., None],
        numbers,
        slice_sizes=(1, 1),
        mode=lax.GatherScatterMode.PROMISE_IN_BOUNDS,
    )


def sweep_into(
    blocks, first_ref, second_ref, own_ref, rhs_ref, off_ref, inverse_ref, lane_ref, step_ref,
    out_ref, window_ref, table_ref,
):
    per = rhs_ref.shape[0] // 5
    nodes = per // blocks
    faces = lane_ref.shape[0] // per
    odd = lax.rem(lax.axis_index(CELL_AXES), 2)
    place = pl.multiple_of((1 - odd) * 2 * per, 8)
    other = pl.multiple_of(odd * 2 * per, 8)
    width = 3 * per
    for b in range(5):
        rows = slice(b * per, (b + 1) * per)
        base = b * width
        window_ref[pl.ds(base + place, per), :] = first_ref[rows, :]
        window_ref[base + per : base + 2 * per, :] = own_ref[rows, :]
        window_ref[pl.ds(base + other, per), :] = second_ref[rows, :]
    for shift in range(1, 8 // nodes):
        for b in range(5):
            for tile in range(0, width - 8, 8):
                to = ((shift - 1) * 5 + b) * width + tile
                table_ref[to : to + 8, :] = window_ref[
                    pl.ds(b * width + tile + shift * nodes, 8), :
                ]
    for half in range(0, per, 8):
        remaining = [rhs_ref[a * per + half : a * per + half + 8, :] for a in range(5)]
        for f in range(faces):
            lanes = lane_ref[f * per + half : f * per + half + 8, :]
            dist = step_ref[f * per + half : f * per + half + 8, :]
            beside = [jnp.zeros((8, LANES), jnp.float32)] * 5
            for d in range(2 * blocks + 1):
                here = dist == d
                first = half + d * nodes
                for b in range(5):
                    shift, at = first % 8 // nodes, b * width + first // 8 * 8
                    if shift:
                        at = at + (shift - 1) * 5 * width
                        table = table_ref[at : at + 8, :]
                    else:
                        table = window_ref[at : at + 8, :]
                    beside[b] = jnp.where(here, take_lanes(table, lanes), beside[b])
            for a in range(5):
                for b in range(5):
                    row = (f * 25 + 5 * a + b) * per + half
                    remaining[a] = remaining[a] - off_ref[row : row + 8, :] * beside[b]
        for a in range(5):
            total = None
            for b in range(5):
                row = (5 * a + b) * per + half
                term = inverse_ref[row : row + 8, :] * remaining[b]
                total = term if total is None else total + term
            out_ref[a * per + half : a * per + half + 8, :] = total


def sweep_kernel(blocks, far_ref, close_ref, *refs):
    sweep_into(blocks, close_ref, far_ref, *refs)


def last_sweep_kernel(blocks, *refs):
    ins, rest = refs[:8], refs[8:]
    sens_ref, _, out_ref, sens_out_ref, window_ref, table_ref, part_ref = rest
    sweep_into(blocks, *ins, out_ref, window_ref, table_ref)
    per = out_ref.shape[0] // 5
    nodes = per // blocks
    for k in range(3):
        total = None
        for a in range(5):
            row = (3 * a + k) * per
            term = out_ref[a * per : (a + 1) * per, :] * sens_ref[row : row + per, :]
            total = term if total is None else total + term
        part_ref[k * per : (k + 1) * per, :] = total
    for block in range(blocks):
        total = None
        for node in range(nodes):
            term = part_ref[pl.ds(block * nodes + node, 3, stride=per), :]
            total = term if total is None else total + term
        sens_out_ref[pl.ds(block, 3, stride=blocks), :] = total


def pieces(value, count):
    found = []
    for _ in range(count):
        piece = value.astype(jnp.bfloat16).astype(jnp.float32)
        found.append(piece)
        value = value - piece
    return found


def distance_factors(points, left):
    count = points.shape[1]
    scaled = (points - 0.5) * (1.0 / SUPPORT_RADIUS)
    scaled = jnp.concatenate([scaled, jnp.zeros((5, count), jnp.float32)], axis=0)
    norm = jnp.sum(scaled * scaled, axis=0, keepdims=True)
    norms = pieces(jnp.broadcast_to(norm, (8, count)), 3)
    row = lax.broadcasted_iota(jnp.int32, (8, count), 0)
    norm_block = jnp.zeros((8, count), jnp.float32)
    for place in range(3):
        norm_block = jnp.where(row == place, norms[place], norm_block)
    ones_block = jnp.where(row < 3, 1.0, 0.0)
    first, second, third = pieces(scaled, 3)
    if left:
        dims = [first, first, second, second, first, third]
        dims = [-2.0 * part for part in dims]
        blocks = dims + [norm_block, ones_block]
    else:
        dims = [first, second, first, second, third, first]
        blocks = dims + [ones_block, norm_block]
    return jnp.concatenate(blocks, axis=0)


def wendland_kernel(first_cell, left_ref, right_ref, _, kernel_ref):
    cells, owned = kernel_ref.shape[0] // 2, kernel_ref.shape[1]
    tile, wide = min(128, cells), min(256, owned)

    def squares(row, lane):
        left = left_ref[first_cell + row : first_cell + row + tile, :]
        right = right_ref[:, lane : lane + wide]
        return jnp.dot(left, right, preferred_element_type=jnp.float32)

    places = [(row, lane) for lane in range(0, owned, wide) for row in range(0, cells, tile)]
    following = squares(*places[0])
    for at, (row, lane) in enumerate(places):
        squared = jnp.maximum(following, 1e-30)
        if at + 1 < len(places):
            following = squares(*places[at + 1])
        near = jnp.maximum(1.0 - squared * lax.rsqrt(squared), 0.0)
        power = near * near
        kernel = power * power * (1.25 - near)
        first = kernel.astype(jnp.bfloat16)
        rest = (kernel - first.astype(jnp.float32)).astype(jnp.bfloat16)
        here = slice(lane, lane + wide)
        kernel_ref[row : row + tile, here] = first
        kernel_ref[cells + row : cells + row + tile, here] = rest


def far_wendland_kernel(
    first_cell, left_ref, right_ref, after, adjoint_ref, low_ref, *rest
):
    kernel_ref, one_hot_ref, result_ref, sem = rest
    copy = pltpu.make_async_copy(adjoint_ref, result_ref, sem)
    copy.start()
    owned = low_ref.shape[1]
    write_one_hot(low_ref, one_hot_ref, low_ref.shape[0] - one_hot_ref.shape[0] // owned)
    wendland_kernel(first_cell, left_ref, right_ref, after, kernel_ref)
    copy.wait()


def control_kernel(scale, *refs):
    *sens_refs, near_ref, far_ref = refs[:-4]
    spread_ref, near_hot, far_hot, out_ref = refs[-4:]
    blocks = sens_refs[0].shape[0] // 3
    half = near_ref.shape[0] // 2
    groups = FFD // LANES
    total = sens_refs[0][...]
    for ref in sens_refs[1:]:
        total = total + ref[...]
    total = total * scale

    def halves(value):
        first = value.astype(jnp.bfloat16)
        rest = (value - first.astype(jnp.float32)).astype(jnp.bfloat16)
        return first, rest

    row = lax.broadcasted_iota(jnp.int32, (8, LANES), 0)
    wide = []
    for block in range(blocks):
        sens = jnp.zeros((8, LANES), jnp.float32)
        for k in range(3):
            sens = jnp.where(row == k, total[k * blocks + block : k * blocks + block + 1], sens)
        first = sens.astype(jnp.bfloat16).astype(jnp.float32)
        wide.append(jnp.concatenate([first, sens - first], axis=0))
    sens = jnp.concatenate(wide, axis=1).astype(jnp.bfloat16)
    grad = None
    for part, ref in ((sens[:, :half], near_ref), (sens[:, half:], far_ref)):
        both = jnp.concatenate([part, part], axis=1)
        term = jnp.dot(both, ref[...], preferred_element_type=jnp.float32)
        grad = term if grad is None else grad + term
    grad = grad[:8] + grad[8:]
    row = lax.broadcasted_iota(jnp.int32, (16, grad.shape[1]), 0)
    wide = jnp.zeros(row.shape, jnp.float32)
    for k in range(3):
        mine = jnp.logical_and(row >= k * groups, row < (k + 1) * groups)
        wide = jnp.where(mine, grad[k : k + 1], wide)
    grad = wide
    owned = grad.shape[1]
    result = None
    places = [
        (ref, first) for ref in (near_hot, far_hot) for first in range(0, ref.shape[0], owned)
    ]
    for j, (ref, first) in enumerate(places):
        term = jnp.dot(
            jnp.concatenate(halves(grad * spread_ref[j * 16 : (j + 1) * 16, :]), axis=0),
            ref[first : first + owned, :],
            preferred_element_type=jnp.float32,
        )
        result = term if result is None else result + term
    result = result[:16] + result[16:]
    out_ref[...] = result[: 3 * groups]


def tree(values):
    while len(values) > 1:
        values = [sum(values[i : i + 2]) for i in range(0, len(values), 2)]
    return values[0]


def add_kernel(*refs):
    refs[-1][...] = tree([ref[...] for ref in refs[:-1]])


def finish_kernel(*refs):
    total, out_ref = tree([ref[...] for ref in refs[:-1]]), refs[-1]
    groups = out_ref.shape[1] // LANES
    for k in range(3):
        for group in range(groups):
            row = k * groups + group
            out_ref[k : k + 1, group * LANES : (group + 1) * LANES] = total[row : row + 1]


def sum_rounds():
    lines, nodes, cores = (lax.axis_size(axis) for axis in SUM_AXES)
    if any(size & (size - 1) for size in (lines, nodes, cores)):
        return None
    near = [cores >> 1 >> i for i in range(cores.bit_length() - 1)]
    node_bits = [cores << i for i in range(nodes.bit_length() - 1)]
    line_bits = [cores * nodes << i for i in range(lines.bit_length() - 1)]
    bits = near + line_bits[:2] + node_bits[:1] + line_bits[2:] + node_bits[1:]
    rounds = []
    for first in range(0, len(bits), 2):
        masks = bits[first : first + 2]
        if len(masks) == 2:
            masks = masks + [masks[0] | masks[1]]
        rounds.append([mask | (cores - 1) for mask in masks] if first else masks)
    return rounds


def exchanged(value, masks):
    peers = lax.axis_size(SUM_AXES)
    return [value] + [
        lax.ppermute(value, SUM_AXES, [(i, i ^ mask) for i in range(peers)]) for mask in masks
    ]


def body(
    adjoint_start,
    adjoint_rhs,
    off_blocks,
    diag_inverse,
    neighbours,
    node_weights,
    sens_blocks,
    cell_points,
    base_points,
    ffd_index,
    ffd_weight,
):
    nodes, _, cells = adjoint_start.shape
    faces = off_blocks.shape[1]
    blocks = cells // LANES
    per = blocks * nodes
    slots = ffd_index.shape[1]
    far_slots = slots // 2
    owned = base_points.shape[1] // lax.axis_size("nodes")
    peers = lax.axis_size(CELL_AXES)
    cores = lax.axis_size("sub")
    node_peers = lax.axis_size("nodes")
    f32, i32, bf16 = jnp.float32, jnp.int32, jnp.bfloat16

    def shape(dims, dtype=f32):
        return jax.ShapeDtypeStruct(dims, dtype)

    def cost(flops, moved):
        return pl.CostEstimate(flops=flops, bytes_accessed=moved, transcendentals=0)

    def swaps(array):
        close = lax.ppermute(array, CELL_AXES, [(i, i ^ 1) for i in range(peers)])
        pairs = []
        for i in range(peers):
            line, core = divmod(i, cores)
            for node in range(node_peers):
                j, beside = (i + 1 if i % 2 else i - 1), node
                if not 0 <= j < peers:
                    j, beside = i, (node ^ 1 if node_peers % 2 == 0 else node)
                to_line, to_core = divmod(j, cores)
                pairs.append(
                    (
                        (line * node_peers + node) * cores + core,
                        (to_line * node_peers + beside) * cores + to_core,
                    )
                )
        return lax.ppermute(array, SUM_AXES, pairs), close

    adjoint = rows_of(adjoint_start)
    far, close = swaps(adjoint)
    prepared = pl.pallas_call(
        functools.partial(prepare_kernel, nodes),
        out_shape=(
            shape((faces * 25 * per, LANES)),
            shape((25 * per, LANES)),
            shape((5 * per, LANES)),
            shape((15 * per, LANES)),
            shape((faces * per, LANES), i32),
            shape((faces * per, LANES), i32),
            shape((slots * 16, owned)),
            shape((slots, owned)),
            shape(((slots - far_slots) * owned, LANES), bf16),
            shape((5 * per, LANES)),
            shape((cells, FACTOR_ROWS), bf16),
            shape((FACTOR_ROWS, owned), bf16),
        ),
        in_specs=[HBM] * 11,
        out_specs=(VMEM,) * 12,
        scratch_shapes=[
            pltpu.VMEM((faces * 25 * per, LANES), bf16),
            pltpu.VMEM((15 * per, LANES), bf16),
            pltpu.VMEM((faces, cells), i32),
            pltpu.SMEM((nodes,), f32),
            pltpu.VMEM((slots, owned), i32),
            pltpu.VMEM((slots, owned), f32),
            pltpu.VMEM((3, cells), f32),
            pltpu.VMEM((3, owned), f32),
            pltpu.SemaphoreType.DMA((11,)),
        ],
        compiler_params=PARAMS,
        cost_estimate=cost(10**9, 10**7),
        name="prepare",
    )(
        *in_hbm(
            rows_of(off_blocks.reshape(nodes, faces * 25, cells)),
            rows_of(diag_inverse),
            rows_of(adjoint_rhs),
            rows_of(sens_blocks),
            neighbours,
            node_weights,
            ffd_index.T,
            ffd_weight.T,
            adjoint,
            cell_points,
            base_points,
        )
    )
    off, inverse, rhs, sens, lane, step, spread, low, near_hot, adjoint, left, right = prepared
    scratch = [
        pltpu.VMEM((3 * 5 * per, LANES), f32),
        pltpu.VMEM((max(8 // nodes - 1, 1) * 3 * 5 * per, LANES), f32),
    ]
    sweep_cost = cost(2 * 10 * 35 * cells, 4 * faces * 25 * per * LANES)

    for _ in range(SWEEPS - 1):
        adjoint = pl.pallas_call(
            functools.partial(sweep_kernel, blocks),
            out_shape=shape((5 * per, LANES)),
            in_specs=[VMEM] * 8,
            out_specs=VMEM,
            scratch_shapes=scratch,
            compiler_params=PARAMS,
            cost_estimate=sweep_cost,
            name="sweep",
        )(far, close, adjoint, rhs, off, inverse, lane, step)
        far, close = swaps(adjoint)

    half = cells * 5 // 8 // LANES * LANES
    wendland_cost = cost(10**9, 10**7)
    near_shape = shape((2 * half, owned), bf16)
    far_shape = shape((2 * (cells - half), owned), bf16)
    near_kernel = pl.pallas_call(
        functools.partial(wendland_kernel, 0),
        out_shape=near_shape,
        in_specs=[VMEM] * 3,
        out_specs=VMEM,
        compiler_params=PARAMS,
        cost_estimate=wendland_cost,
        name="near_wendland",
    )(left, right, adjoint)
    adjoint, part_sens = pl.pallas_call(
        functools.partial(last_sweep_kernel, blocks),
        out_shape=(shape((5 * per, LANES)), shape((3 * blocks, LANES))),
        in_specs=[VMEM] * 9 + [pl.BlockSpec(memory_space=pl.ANY)],
        out_specs=(VMEM, VMEM),
        scratch_shapes=scratch + [pltpu.VMEM((3 * per, LANES), f32)],
        compiler_params=PARAMS,
        cost_estimate=sweep_cost,
        name="last_sweep",
    )(close, far, adjoint, rhs, off, inverse, lane, step, sens, near_kernel)

    all_sens = [part_sens]
    for shift in range(1, node_peers):
        ring = [(i, (i + shift) % node_peers) for i in range(node_peers)]
        all_sens.append(lax.ppermute(part_sens, "nodes", ring))
    hot_shape = shape((far_slots * owned, LANES), bf16)
    far_kernel, far_hot, adjoint = pl.pallas_call(
        functools.partial(far_wendland_kernel, half),
        out_shape=(far_shape, hot_shape, shape((5 * per, LANES))),
        in_specs=[VMEM] * 5,
        out_specs=(VMEM, VMEM, HBM),
        scratch_shapes=[pltpu.SemaphoreType.DMA],
        compiler_params=PARAMS,
        cost_estimate=wendland_cost,
        name="far_wendland",
    )(left, right, part_sens, adjoint, low)
    scale = 4.0 / math.sqrt(cells * peers)
    rows = 3 * FFD // LANES
    partial = pl.pallas_call(
        functools.partial(control_kernel, scale),
        out_shape=shape((rows, LANES)),
        in_specs=[VMEM] * (len(all_sens) + 5),
        out_specs=VMEM,
        compiler_params=PARAMS,
        name="control",
    )(*all_sens, near_kernel, far_kernel, spread, near_hot, far_hot)
    rounds = sum_rounds()
    terms = [partial] if rounds else [lax.psum(partial, SUM_AXES)]
    for masks in rounds or ():
        if len(terms) > 1:
            partial = pl.pallas_call(
                add_kernel, out_shape=shape((rows, LANES)), name="add", compiler_params=PARAMS
            )(*terms)
        terms = exchanged(partial, masks)
    control_grad = pl.pallas_call(
        finish_kernel, out_shape=shape((3, FFD)), name="finish", compiler_params=PARAMS
    )(*terms)
    return (from_rows(adjoint, nodes, cells), control_grad)


def solution(mesh):
    return jax.shard_map(
        body,
        mesh=mesh,
        in_specs=(
            P("nodes", None, ("groups", "cells", "sub")),
            P("nodes", None, ("groups", "cells", "sub")),
            P("nodes", None, None, ("groups", "cells", "sub")),
            P("nodes", None, ("groups", "cells", "sub")),
            P(None, ("cells", "sub")),
            P("nodes"),
            P("nodes", None, ("groups", "cells", "sub")),
            P(None, ("cells", "sub")),
            P(),
            P(),
            P(),
        ),
        out_specs=(P("nodes", None, ("groups", "cells", "sub")), P("groups", None)),
        check_vma=False,
    )
```

```python
import functools
import math

import jax
import jax.numpy as jnp
from jax import lax
from jax.experimental import pallas as pl
from jax.experimental.pallas import tpu as pltpu
from jax.sharding import PartitionSpec as P

SWEEPS = 2
FFD = 512
SUPPORT_RADIUS = 0.3
LANES = 128
CELL_AXES = ("cells", "sub")
SUM_AXES = ("cells", "nodes", "sub")
FACTOR_ROWS = 64
PARAMS = pltpu.CompilerParams(vmem_limit_bytes=24 * 1024 * 1024)
VMEM = pl.BlockSpec(memory_space=pltpu.VMEM)
HBM = pl.BlockSpec(memory_space=pltpu.HBM)


def rows_of(array):
    nodes, rows, cells = array.shape
    blocks = cells // LANES
    split = array.reshape(nodes, rows, blocks, LANES)
    return split.transpose(1, 2, 0, 3).reshape(rows * blocks * nodes, LANES)


def from_rows(array, nodes, cells):
    blocks = cells // LANES
    split = array.reshape(-1, blocks, nodes, LANES)
    return split.transpose(2, 0, 1, 3).reshape(nodes, -1, cells)


def in_hbm(*arrays):
    return [pltpu.with_memory_space_constraint(array, pltpu.HBM) for array in arrays]


def write_one_hot(low_ref, one_hot_ref, first_slot):
    owned = low_ref.shape[1]
    piece = min(512, owned)
    lane = lax.broadcasted_iota(jnp.int32, (piece, LANES), 1).astype(jnp.float32)
    lane = lane.astype(jnp.bfloat16)
    for first in range(0, owned, piece):
        low = low_ref[:, first : first + piece].T.astype(jnp.bfloat16)
        for j in range(one_hot_ref.shape[0] // owned):
            column = low[:, first_slot + j : first_slot + j + 1]
            hit = jnp.broadcast_to(column, (piece, LANES)) == lane
            one_hot_ref[j * owned + first : j * owned + first + piece, :] = jnp.where(
                hit, jnp.bfloat16(1.0), jnp.bfloat16(0.0)
            )


def prepare_kernel(
    nodes,
    off_in,
    inverse_in,
    rhs_in,
    sens_in,
    neigh_in,
    weight_in,
    index_in,
    spread_in,
    start_in,
    cell_in,
    base_in,
    off_ref,
    inverse_ref,
    rhs_ref,
    sens_ref,
    lane_ref,
    step_ref,
    spread_ref,
    low_ref,
    one_hot_ref,
    start_ref,
    left_ref,
    right_ref,
    off_buf,
    sens_buf,
    neigh_buf,
    weight_buf,
    index_buf,
    spread_buf,
    cell_buf,
    base_buf,
    sems,
):
    slots, owned = index_buf.shape
    start = pl.multiple_of(lax.axis_index("nodes") * owned, LANES)
    mine = pl.ds(start, owned)
    pairs = (
        (neigh_in, neigh_buf),
        (index_in.at[:, mine], index_buf),
        (spread_in.at[:, mine], spread_buf),
        (cell_in, cell_buf),
        (base_in.at[:, mine], base_buf),
        (off_in, off_buf),
        (weight_in, weight_buf),
        (sens_in, sens_buf),
        (inverse_in, inverse_ref),
        (rhs_in, rhs_ref),
        (start_in, start_ref),
    )
    copies = [pltpu.make_async_copy(a, b, sems.at[i]) for i, (a, b) in enumerate(pairs)]
    for copy in copies:
        copy.start()

    faces, cells = neigh_buf.shape
    blocks = cells // LANES
    per = blocks * nodes
    first_cell = lax.axis_index(CELL_AXES) * cells
    copies[0].wait()
    for block in range(blocks):
        index = neigh_buf[:, block * LANES : (block + 1) * LANES]
        local = index - first_cell + cells
        lane = jnp.bitwise_and(local, LANES - 1)
        step = jnp.right_shift(local, 7) - block
        step = jnp.where(index >= 0, step, -1)
        for node in range(nodes):
            rows = pl.ds(block * nodes + node, faces, stride=per)
            lane_ref[rows, :] = lane
            step_ref[rows, :] = step

    copies[1].wait()
    copies[2].wait()
    groups = FFD // LANES
    piece = min(512, owned)
    for first in range(0, owned, piece):
        here = slice(first, first + piece)
        high = jnp.right_shift(index_buf[:, here], 7)
        part = lax.broadcasted_iota(jnp.int32, (16, piece), 0)
        part = jnp.where(part < 3 * groups, lax.rem(part, groups), -1)
        for j in range(slots):
            spread_ref[j * 16 : (j + 1) * 16, here] = jnp.where(
                high[j : j + 1] == part, spread_buf[j : j + 1, here], 0.0
            )

    low_ref[...] = jnp.bitwise_and(index_buf[...], LANES - 1).astype(jnp.float32)
    write_one_hot(low_ref, one_hot_ref, 0)

    copies[3].wait()
    left_ref[...] = distance_factors(cell_buf[...], True).T.astype(jnp.bfloat16)
    copies[4].wait()
    right_ref[...] = distance_factors(base_buf[...], False).astype(jnp.bfloat16)

    copies[5].wait()
    off_ref[...] = off_buf[...].astype(jnp.float32)
    copies[6].wait()
    copies[7].wait()
    row_node = lax.rem(lax.broadcasted_iota(jnp.int32, (per, LANES), 0), nodes)
    weights = jnp.zeros((per, LANES), jnp.float32)
    for node in range(nodes):
        weights = jnp.where(row_node == node, weight_buf[node], weights)
    for row in range(0, sens_buf.shape[0], per):
        here = slice(row, row + per)
        sens_ref[here, :] = sens_buf[here, :].astype(jnp.float32) * weights
    for copy in copies[8:]:
        copy.wait()


def take_lanes(table, lanes):
    numbers = lax.GatherDimensionNumbers(
        offset_dims=(),
        collapsed_slice_dims=(1,),
        start_index_map=(1,),
        operand_batching_dims=(0,),
        start_indices_batching_dims=(0,),
    )
    return lax.gather(
        table,
        lanes[..., None],
        numbers,
        slice_sizes=(1, 1),
        mode=lax.GatherScatterMode.PROMISE_IN_BOUNDS,
    )


def sweep_into(
    blocks, first_ref, second_ref, own_ref, rhs_ref, off_ref, inverse_ref, lane_ref, step_ref,
    out_ref, window_ref, table_ref,
):
    per = rhs_ref.shape[0] // 5
    nodes = per // blocks
    faces = lane_ref.shape[0] // per
    odd = lax.rem(lax.axis_index(CELL_AXES), 2)
    place = pl.multiple_of((1 - odd) * 2 * per, 8)
    other = pl.multiple_of(odd * 2 * per, 8)
    width = 3 * per
    for b in range(5):
        rows = slice(b * per, (b + 1) * per)
        base = b * width
        window_ref[pl.ds(base + place, per), :] = first_ref[rows, :]
        window_ref[base + per : base + 2 * per, :] = own_ref[rows, :]
        window_ref[pl.ds(base + other, per), :] = second_ref[rows, :]
    for shift in range(1, 8 // nodes):
        for b in range(5):
            for tile in range(0, width - 8, 8):
                to = ((shift - 1) * 5 + b) * width + tile
                table_ref[to : to + 8, :] = window_ref[
                    pl.ds(b * width + tile + shift * nodes, 8), :
                ]
    for half in range(0, per, 8):
        remaining = [rhs_ref[a * per + half : a * per + half + 8, :] for a in range(5)]
        for f in range(faces):
            lanes = lane_ref[f * per + half : f * per + half + 8, :]
            dist = step_ref[f * per + half : f * per + half + 8, :]
            beside = [jnp.zeros((8, LANES), jnp.float32)] * 5
            for d in range(2 * blocks + 1):
                here = dist == d
                first = half + d * nodes
                for b in range(5):
                    shift, at = first % 8 // nodes, b * width + first // 8 * 8
                    if shift:
                        at = at + (shift - 1) * 5 * width
                        table = table_ref[at : at + 8, :]
                    else:
                        table = window_ref[at : at + 8, :]
                    beside[b] = jnp.where(here, take_lanes(table, lanes), beside[b])
            for a in range(5):
                for b in range(5):
                    row = (f * 25 + 5 * a + b) * per + half
                    remaining[a] = remaining[a] - off_ref[row : row + 8, :] * beside[b]
        for a in range(5):
            total = None
            for b in range(5):
                row = (5 * a + b) * per + half
                term = inverse_ref[row : row + 8, :] * remaining[b]
                total = term if total is None else total + term
            out_ref[a * per + half : a * per + half + 8, :] = total


def sweep_kernel(blocks, far_ref, close_ref, *refs):
    sweep_into(blocks, close_ref, far_ref, *refs)


def last_sweep_kernel(blocks, *refs):
    ins, rest = refs[:8], refs[8:]
    sens_ref, _, out_ref, sens_out_ref, window_ref, table_ref, part_ref = rest
    sweep_into(blocks, *ins, out_ref, window_ref, table_ref)
    per = out_ref.shape[0] // 5
    nodes = per // blocks
    for k in range(3):
        total = None
        for a in range(5):
            row = (3 * a + k) * per
            term = out_ref[a * per : (a + 1) * per, :] * sens_ref[row : row + per, :]
            total = term if total is None else total + term
        part_ref[k * per : (k + 1) * per, :] = total
    for block in range(blocks):
        total = None
        for node in range(nodes):
            term = part_ref[pl.ds(block * nodes + node, 3, stride=per), :]
            total = term if total is None else total + term
        sens_out_ref[pl.ds(block, 3, stride=blocks), :] = total


def pieces(value, count):
    found = []
    for _ in range(count):
        piece = value.astype(jnp.bfloat16).astype(jnp.float32)
        found.append(piece)
        value = value - piece
    return found


def distance_factors(points, left):
    count = points.shape[1]
    scaled = (points - 0.5) * (1.0 / SUPPORT_RADIUS)
    scaled = jnp.concatenate([scaled, jnp.zeros((5, count), jnp.float32)], axis=0)
    norm = jnp.sum(scaled * scaled, axis=0, keepdims=True)
    norms = pieces(jnp.broadcast_to(norm, (8, count)), 3)
    row = lax.broadcasted_iota(jnp.int32, (8, count), 0)
    norm_block = jnp.zeros((8, count), jnp.float32)
    for place in range(3):
        norm_block = jnp.where(row == place, norms[place], norm_block)
    ones_block = jnp.where(row < 3, 1.0, 0.0)
    first, second, third = pieces(scaled, 3)
    if left:
        dims = [first, first, second, second, first, third]
        dims = [-2.0 * part for part in dims]
        blocks = dims + [norm_block, ones_block]
    else:
        dims = [first, second, first, second, third, first]
        blocks = dims + [ones_block, norm_block]
    return jnp.concatenate(blocks, axis=0)


def wendland_kernel(first_cell, left_ref, right_ref, _, kernel_ref):
    cells, owned = kernel_ref.shape[0] // 2, kernel_ref.shape[1]
    tile, wide = min(128, cells), min(256, owned)

    def squares(row, lane):
        left = left_ref[first_cell + row : first_cell + row + tile, :]
        right = right_ref[:, lane : lane + wide]
        return jnp.dot(left, right, preferred_element_type=jnp.float32)

    places = [(row, lane) for lane in range(0, owned, wide) for row in range(0, cells, tile)]
    following = squares(*places[0])
    for at, (row, lane) in enumerate(places):
        squared = jnp.maximum(following, 1e-30)
        if at + 1 < len(places):
            following = squares(*places[at + 1])
        near = jnp.maximum(1.0 - squared * lax.rsqrt(squared), 0.0)
        power = near * near
        kernel = power * power * (1.25 - near)
        first = kernel.astype(jnp.bfloat16)
        rest = (kernel - first.astype(jnp.float32)).astype(jnp.bfloat16)
        here = slice(lane, lane + wide)
        kernel_ref[row : row + tile, here] = first
        kernel_ref[cells + row : cells + row + tile, here] = rest


def far_wendland_kernel(
    first_cell, left_ref, right_ref, after, adjoint_ref, low_ref, *rest
):
    kernel_ref, one_hot_ref, result_ref, sem = rest
    copy = pltpu.make_async_copy(adjoint_ref, result_ref, sem)
    copy.start()
    owned = low_ref.shape[1]
    write_one_hot(low_ref, one_hot_ref, low_ref.shape[0] - one_hot_ref.shape[0] // owned)
    wendland_kernel(first_cell, left_ref, right_ref, after, kernel_ref)
    copy.wait()


def control_kernel(scale, *refs):
    *sens_refs, near_ref, far_ref = refs[:-4]
    spread_ref, near_hot, far_hot, out_ref = refs[-4:]
    blocks = sens_refs[0].shape[0] // 3
    half = near_ref.shape[0] // 2
    groups = FFD // LANES
    total = sens_refs[0][...]
    for ref in sens_refs[1:]:
        total = total + ref[...]
    total = total * scale

    def halves(value):
        first = value.astype(jnp.bfloat16)
        rest = (value - first.astype(jnp.float32)).astype(jnp.bfloat16)
        return first, rest

    row = lax.broadcasted_iota(jnp.int32, (8, LANES), 0)
    wide = []
    for block in range(blocks):
        sens = jnp.zeros((8, LANES), jnp.float32)
        for k in range(3):
            sens = jnp.where(row == k, total[k * blocks + block : k * blocks + block + 1], sens)
        first = sens.astype(jnp.bfloat16).astype(jnp.float32)
        wide.append(jnp.concatenate([first, sens - first], axis=0))
    sens = jnp.concatenate(wide, axis=1).astype(jnp.bfloat16)
    grad = None
    for part, ref in ((sens[:, :half], near_ref), (sens[:, half:], far_ref)):
        both = jnp.concatenate([part, part], axis=1)
        term = jnp.dot(both, ref[...], preferred_element_type=jnp.float32)
        grad = term if grad is None else grad + term
    grad = grad[:8] + grad[8:]
    row = lax.broadcasted_iota(jnp.int32, (16, grad.shape[1]), 0)
    wide = jnp.zeros(row.shape, jnp.float32)
    for k in range(3):
        mine = jnp.logical_and(row >= k * groups, row < (k + 1) * groups)
        wide = jnp.where(mine, grad[k : k + 1], wide)
    grad = wide
    owned = grad.shape[1]
    result = None
    places = [
        (ref, first) for ref in (near_hot, far_hot) for first in range(0, ref.shape[0], owned)
    ]
    for j, (ref, first) in enumerate(places):
        term = jnp.dot(
            jnp.concatenate(halves(grad * spread_ref[j * 16 : (j + 1) * 16, :]), axis=0),
            ref[first : first + owned, :],
            preferred_element_type=jnp.float32,
        )
        result = term if result is None else result + term
    result = result[:16] + result[16:]
    out_ref[...] = result[: 3 * groups]


def tree(values):
    while len(values) > 1:
        values = [sum(values[i : i + 2]) for i in range(0, len(values), 2)]
    return values[0]


def add_kernel(*refs):
    refs[-1][...] = tree([ref[...] for ref in refs[:-1]])


def finish_kernel(*refs):
    total, out_ref = tree([ref[...] for ref in refs[:-1]]), refs[-1]
    groups = out_ref.shape[1] // LANES
    for k in range(3):
        for group in range(groups):
            row = k * groups + group
            out_ref[k : k + 1, group * LANES : (group + 1) * LANES] = total[row : row + 1]


def sum_rounds():
    lines, nodes, cores = (lax.axis_size(axis) for axis in SUM_AXES)
    if any(size & (size - 1) for size in (lines, nodes, cores)):
        return None
    near = [cores >> 1 >> i for i in range(cores.bit_length() - 1)]
    node_bits = [cores << i for i in range(nodes.bit_length() - 1)]
    line_bits = [cores * nodes << i for i in range(lines.bit_length() - 1)]
    bits = line_bits[1:2] + node_bits[:1] + line_bits[2:] + node_bits[1:]
    rounds = [[bit] for bit in near] + [[bit | (cores - 1)] for bit in line_bits[:1]]
    for first in range(0, len(bits), 2):
        masks = bits[first : first + 2]
        if len(masks) == 2:
            masks = masks + [masks[0] | masks[1]]
        rounds.append([mask | (cores - 1) for mask in masks])
    return rounds


def exchanged(value, masks):
    peers = lax.axis_size(SUM_AXES)
    return [value] + [
        lax.ppermute(value, SUM_AXES, [(i, i ^ mask) for i in range(peers)]) for mask in masks
    ]


def body(
    adjoint_start,
    adjoint_rhs,
    off_blocks,
    diag_inverse,
    neighbours,
    node_weights,
    sens_blocks,
    cell_points,
    base_points,
    ffd_index,
    ffd_weight,
):
    nodes, _, cells = adjoint_start.shape
    faces = off_blocks.shape[1]
    blocks = cells // LANES
    per = blocks * nodes
    slots = ffd_index.shape[1]
    far_slots = slots // 2
    owned = base_points.shape[1] // lax.axis_size("nodes")
    peers = lax.axis_size(CELL_AXES)
    cores = lax.axis_size("sub")
    node_peers = lax.axis_size("nodes")
    f32, i32, bf16 = jnp.float32, jnp.int32, jnp.bfloat16

    def shape(dims, dtype=f32):
        return jax.ShapeDtypeStruct(dims, dtype)

    def cost(flops, moved):
        return pl.CostEstimate(flops=flops, bytes_accessed=moved, transcendentals=0)

    def swaps(array):
        close = lax.ppermute(array, CELL_AXES, [(i, i ^ 1) for i in range(peers)])
        pairs = []
        for i in range(peers):
            line, core = divmod(i, cores)
            for node in range(node_peers):
                j, beside = (i + 1 if i % 2 else i - 1), node
                if not 0 <= j < peers:
                    j, beside = i, (node ^ 1 if node_peers % 2 == 0 else node)
                to_line, to_core = divmod(j, cores)
                pairs.append(
                    (
                        (line * node_peers + node) * cores + core,
                        (to_line * node_peers + beside) * cores + to_core,
                    )
                )
        return lax.ppermute(array, SUM_AXES, pairs), close

    adjoint = rows_of(adjoint_start)
    far, close = swaps(adjoint)
    prepared = pl.pallas_call(
        functools.partial(prepare_kernel, nodes),
        out_shape=(
            shape((faces * 25 * per, LANES)),
            shape((25 * per, LANES)),
            shape((5 * per, LANES)),
            shape((15 * per, LANES)),
            shape((faces * per, LANES), i32),
            shape((faces * per, LANES), i32),
            shape((slots * 16, owned)),
            shape((slots, owned)),
            shape(((slots - far_slots) * owned, LANES), bf16),
            shape((5 * per, LANES)),
            shape((cells, FACTOR_ROWS), bf16),
            shape((FACTOR_ROWS, owned), bf16),
        ),
        in_specs=[HBM] * 11,
        out_specs=(VMEM,) * 12,
        scratch_shapes=[
            pltpu.VMEM((faces * 25 * per, LANES), bf16),
            pltpu.VMEM((15 * per, LANES), bf16),
            pltpu.VMEM((faces, cells), i32),
            pltpu.SMEM((nodes,), f32),
            pltpu.VMEM((slots, owned), i32),
            pltpu.VMEM((slots, owned), f32),
            pltpu.VMEM((3, cells), f32),
            pltpu.VMEM((3, owned), f32),
            pltpu.SemaphoreType.DMA((11,)),
        ],
        compiler_params=PARAMS,
        cost_estimate=cost(10**9, 10**7),
        name="prepare",
    )(
        *in_hbm(
            rows_of(off_blocks.reshape(nodes, faces * 25, cells)),
            rows_of(diag_inverse),
            rows_of(adjoint_rhs),
            rows_of(sens_blocks),
            neighbours,
            node_weights,
            ffd_index.T,
            ffd_weight.T,
            adjoint,
            cell_points,
            base_points,
        )
    )
    off, inverse, rhs, sens, lane, step, spread, low, near_hot, adjoint, left, right = prepared
    scratch = [
        pltpu.VMEM((3 * 5 * per, LANES), f32),
        pltpu.VMEM((max(8 // nodes - 1, 1) * 3 * 5 * per, LANES), f32),
    ]
    sweep_cost = cost(2 * 10 * 35 * cells, 4 * faces * 25 * per * LANES)

    for _ in range(SWEEPS - 1):
        adjoint = pl.pallas_call(
            functools.partial(sweep_kernel, blocks),
            out_shape=shape((5 * per, LANES)),
            in_specs=[VMEM] * 8,
            out_specs=VMEM,
            scratch_shapes=scratch,
            compiler_params=PARAMS,
            cost_estimate=sweep_cost,
            name="sweep",
        )(far, close, adjoint, rhs, off, inverse, lane, step)
        far, close = swaps(adjoint)

    half = cells * 5 // 8 // LANES * LANES
    wendland_cost = cost(10**9, 10**7)
    near_shape = shape((2 * half, owned), bf16)
    far_shape = shape((2 * (cells - half), owned), bf16)
    near_kernel = pl.pallas_call(
        functools.partial(wendland_kernel, 0),
        out_shape=near_shape,
        in_specs=[VMEM] * 3,
        out_specs=VMEM,
        compiler_params=PARAMS,
        cost_estimate=wendland_cost,
        name="near_wendland",
    )(left, right, adjoint)
    adjoint, part_sens = pl.pallas_call(
        functools.partial(last_sweep_kernel, blocks),
        out_shape=(shape((5 * per, LANES)), shape((3 * blocks, LANES))),
        in_specs=[VMEM] * 9 + [pl.BlockSpec(memory_space=pl.ANY)],
        out_specs=(VMEM, VMEM),
        scratch_shapes=scratch + [pltpu.VMEM((3 * per, LANES), f32)],
        compiler_params=PARAMS,
        cost_estimate=sweep_cost,
        name="last_sweep",
    )(close, far, adjoint, rhs, off, inverse, lane, step, sens, near_kernel)

    all_sens = [part_sens]
    for shift in range(1, node_peers):
        ring = [(i, (i + shift) % node_peers) for i in range(node_peers)]
        all_sens.append(lax.ppermute(part_sens, "nodes", ring))
    hot_shape = shape((far_slots * owned, LANES), bf16)
    far_kernel, far_hot, adjoint = pl.pallas_call(
        functools.partial(far_wendland_kernel, half),
        out_shape=(far_shape, hot_shape, shape((5 * per, LANES))),
        in_specs=[VMEM] * 5,
        out_specs=(VMEM, VMEM, HBM),
        scratch_shapes=[pltpu.SemaphoreType.DMA],
        compiler_params=PARAMS,
        cost_estimate=wendland_cost,
        name="far_wendland",
    )(left, right, part_sens, adjoint, low)
    scale = 4.0 / math.sqrt(cells * peers)
    rows = 3 * FFD // LANES
    partial = pl.pallas_call(
        functools.partial(control_kernel, scale),
        out_shape=shape((rows, LANES)),
        in_specs=[VMEM] * (len(all_sens) + 5),
        out_specs=VMEM,
        compiler_params=PARAMS,
        name="control",
    )(*all_sens, near_kernel, far_kernel, spread, near_hot, far_hot)
    rounds = sum_rounds()
    terms = [partial] if rounds else [lax.psum(partial, SUM_AXES)]
    for masks in rounds or ():
        if len(terms) > 1:
            partial = pl.pallas_call(
                add_kernel, out_shape=shape((rows, LANES)), name="add", compiler_params=PARAMS
            )(*terms)
        terms = exchanged(partial, masks)
    control_grad = pl.pallas_call(
        finish_kernel, out_shape=shape((3, FFD)), name="finish", compiler_params=PARAMS
    )(*terms)
    return (from_rows(adjoint, nodes, cells), control_grad)


def solution(mesh):
    return jax.shard_map(
        body,
        mesh=mesh,
        in_specs=(
            P("nodes", None, ("groups", "cells", "sub")),
            P("nodes", None, ("groups", "cells", "sub")),
            P("nodes", None, None, ("groups", "cells", "sub")),
            P("nodes", None, ("groups", "cells", "sub")),
            P(None, ("cells", "sub")),
            P("nodes"),
            P("nodes", None, ("groups", "cells", "sub")),
            P(None, ("cells", "sub")),
            P(),
            P(),
            P(),
        ),
        out_specs=(P("nodes", None, ("groups", "cells", "sub")), P("groups", None)),
        check_vma=False,
    )
```

```python
import functools
import math

import jax
import jax.numpy as jnp
from jax import lax
from jax.experimental import pallas as pl
from jax.experimental.pallas import tpu as pltpu
from jax.sharding import PartitionSpec as P

SWEEPS = 2
FFD = 512
SUPPORT_RADIUS = 0.3
LANES = 128
CELL_AXES = ("cells", "sub")
SUM_AXES = ("cells", "nodes", "sub")
FACTOR_ROWS = 64
PARAMS = pltpu.CompilerParams(vmem_limit_bytes=24 * 1024 * 1024)
VMEM = pl.BlockSpec(memory_space=pltpu.VMEM)
HBM = pl.BlockSpec(memory_space=pltpu.HBM)


def rows_of(array):
    nodes, rows, cells = array.shape
    blocks = cells // LANES
    split = array.reshape(nodes, rows, blocks, LANES)
    return split.transpose(1, 2, 0, 3).reshape(rows * blocks * nodes, LANES)


def from_rows(array, nodes, cells):
    blocks = cells // LANES
    split = array.reshape(-1, blocks, nodes, LANES)
    return split.transpose(2, 0, 1, 3).reshape(nodes, -1, cells)


def in_hbm(*arrays):
    return [pltpu.with_memory_space_constraint(array, pltpu.HBM) for array in arrays]


def write_one_hot(low_ref, one_hot_ref, first_slot):
    owned = low_ref.shape[1]
    piece = min(512, owned)
    lane = lax.broadcasted_iota(jnp.int32, (piece, LANES), 1).astype(jnp.float32)
    lane = lane.astype(jnp.bfloat16)
    for first in range(0, owned, piece):
        low = low_ref[:, first : first + piece].T.astype(jnp.bfloat16)
        for j in range(one_hot_ref.shape[0] // owned):
            column = low[:, first_slot + j : first_slot + j + 1]
            hit = jnp.broadcast_to(column, (piece, LANES)) == lane
            one_hot_ref[j * owned + first : j * owned + first + piece, :] = jnp.where(
                hit, jnp.bfloat16(1.0), jnp.bfloat16(0.0)
            )


def prepare_kernel(
    nodes,
    off_in,
    inverse_in,
    rhs_in,
    sens_in,
    neigh_in,
    weight_in,
    index_in,
    spread_in,
    start_in,
    cell_in,
    base_in,
    off_ref,
    inverse_ref,
    rhs_ref,
    sens_ref,
    lane_ref,
    step_ref,
    spread_ref,
    low_ref,
    one_hot_ref,
    start_ref,
    left_ref,
    right_ref,
    off_buf,
    sens_buf,
    neigh_buf,
    weight_buf,
    index_buf,
    spread_buf,
    cell_buf,
    base_buf,
    sems,
):
    slots, owned = index_buf.shape
    start = pl.multiple_of(lax.axis_index("nodes") * owned, LANES)
    mine = pl.ds(start, owned)
    pairs = (
        (neigh_in, neigh_buf),
        (index_in.at[:, mine], index_buf),
        (spread_in.at[:, mine], spread_buf),
        (cell_in, cell_buf),
        (base_in.at[:, mine], base_buf),
        (off_in, off_buf),
        (weight_in, weight_buf),
        (sens_in, sens_buf),
        (inverse_in, inverse_ref),
        (rhs_in, rhs_ref),
        (start_in, start_ref),
    )
    copies = [pltpu.make_async_copy(a, b, sems.at[i]) for i, (a, b) in enumerate(pairs)]
    for copy in copies:
        copy.start()

    faces, cells = neigh_buf.shape
    blocks = cells // LANES
    per = blocks * nodes
    first_cell = lax.axis_index(CELL_AXES) * cells
    copies[0].wait()
    for block in range(blocks):
        index = neigh_buf[:, block * LANES : (block + 1) * LANES]
        local = index - first_cell + cells
        lane = jnp.bitwise_and(local, LANES - 1)
        step = jnp.right_shift(local, 7) - block
        step = jnp.where(index >= 0, step, -1)
        for node in range(nodes):
            rows = pl.ds(block * nodes + node, faces, stride=per)
            lane_ref[rows, :] = lane
            step_ref[rows, :] = step

    copies[1].wait()
    copies[2].wait()
    groups = FFD // LANES
    piece = min(512, owned)
    for first in range(0, owned, piece):
        here = slice(first, first + piece)
        high = jnp.right_shift(index_buf[:, here], 7)
        part = lax.broadcasted_iota(jnp.int32, (16, piece), 0)
        part = jnp.where(part < 3 * groups, lax.rem(part, groups), -1)
        for j in range(slots):
            spread_ref[j * 16 : (j + 1) * 16, here] = jnp.where(
                high[j : j + 1] == part, spread_buf[j : j + 1, here], 0.0
            )

    low_ref[...] = jnp.bitwise_and(index_buf[...], LANES - 1).astype(jnp.float32)
    write_one_hot(low_ref, one_hot_ref, 0)

    copies[3].wait()
    left_ref[...] = distance_factors(cell_buf[...], True).T.astype(jnp.bfloat16)
    copies[4].wait()
    right_ref[...] = distance_factors(base_buf[...], False).astype(jnp.bfloat16)

    copies[5].wait()
    off_ref[...] = off_buf[...].astype(jnp.float32)
    copies[6].wait()
    copies[7].wait()
    row_node = lax.rem(lax.broadcasted_iota(jnp.int32, (per, LANES), 0), nodes)
    weights = jnp.zeros((per, LANES), jnp.float32)
    for node in range(nodes):
        weights = jnp.where(row_node == node, weight_buf[node], weights)
    for row in range(0, sens_buf.shape[0], per):
        here = slice(row, row + per)
        sens_ref[here, :] = sens_buf[here, :].astype(jnp.float32) * weights
    for copy in copies[8:]:
        copy.wait()


def take_lanes(table, lanes):
    numbers = lax.GatherDimensionNumbers(
        offset_dims=(),
        collapsed_slice_dims=(1,),
        start_index_map=(1,),
        operand_batching_dims=(0,),
        start_indices_batching_dims=(0,),
    )
    return lax.gather(
        table,
        lanes[..., None],
        numbers,
        slice_sizes=(1, 1),
        mode=lax.GatherScatterMode.PROMISE_IN_BOUNDS,
    )


def sweep_into(
    blocks, first_ref, second_ref, own_ref, rhs_ref, off_ref, inverse_ref, lane_ref, step_ref,
    out_ref, window_ref, table_ref,
):
    per = rhs_ref.shape[0] // 5
    nodes = per // blocks
    faces = lane_ref.shape[0] // per
    odd = lax.rem(lax.axis_index(CELL_AXES), 2)
    place = pl.multiple_of((1 - odd) * 2 * per, 8)
    other = pl.multiple_of(odd * 2 * per, 8)
    width = 3 * per
    for b in range(5):
        rows = slice(b * per, (b + 1) * per)
        base = b * width
        window_ref[pl.ds(base + place, per), :] = first_ref[rows, :]
        window_ref[base + per : base + 2 * per, :] = own_ref[rows, :]
        window_ref[pl.ds(base + other, per), :] = second_ref[rows, :]
    for shift in range(1, 8 // nodes):
        for b in range(5):
            for tile in range(0, width - 8, 8):
                to = ((shift - 1) * 5 + b) * width + tile
                table_ref[to : to + 8, :] = window_ref[
                    pl.ds(b * width + tile + shift * nodes, 8), :
                ]
    for half in range(0, per, 8):
        remaining = [rhs_ref[a * per + half : a * per + half + 8, :] for a in range(5)]
        for f in range(faces):
            lanes = lane_ref[f * per + half : f * per + half + 8, :]
            dist = step_ref[f * per + half : f * per + half + 8, :]
            beside = [jnp.zeros((8, LANES), jnp.float32)] * 5
            for d in range(2 * blocks + 1):
                here = dist == d
                first = half + d * nodes
                for b in range(5):
                    shift, at = first % 8 // nodes, b * width + first // 8 * 8
                    if shift:
                        at = at + (shift - 1) * 5 * width
                        table = table_ref[at : at + 8, :]
                    else:
                        table = window_ref[at : at + 8, :]
                    beside[b] = jnp.where(here, take_lanes(table, lanes), beside[b])
            for a in range(5):
                for b in range(5):
                    row = (f * 25 + 5 * a + b) * per + half
                    remaining[a] = remaining[a] - off_ref[row : row + 8, :] * beside[b]
        for a in range(5):
            total = None
            for b in range(5):
                row = (5 * a + b) * per + half
                term = inverse_ref[row : row + 8, :] * remaining[b]
                total = term if total is None else total + term
            out_ref[a * per + half : a * per + half + 8, :] = total


def sweep_kernel(blocks, far_ref, close_ref, *refs):
    sweep_into(blocks, close_ref, far_ref, *refs)


def last_sweep_kernel(blocks, *refs):
    ins, rest = refs[:8], refs[8:]
    sens_ref, _, out_ref, sens_out_ref, window_ref, table_ref, part_ref = rest
    sweep_into(blocks, *ins, out_ref, window_ref, table_ref)
    per = out_ref.shape[0] // 5
    nodes = per // blocks
    for k in range(3):
        total = None
        for a in range(5):
            row = (3 * a + k) * per
            term = out_ref[a * per : (a + 1) * per, :] * sens_ref[row : row + per, :]
            total = term if total is None else total + term
        part_ref[k * per : (k + 1) * per, :] = total
    for block in range(blocks):
        total = None
        for node in range(nodes):
            term = part_ref[pl.ds(block * nodes + node, 3, stride=per), :]
            total = term if total is None else total + term
        sens_out_ref[pl.ds(block, 3, stride=blocks), :] = total


def pieces(value, count):
    found = []
    for _ in range(count):
        piece = value.astype(jnp.bfloat16).astype(jnp.float32)
        found.append(piece)
        value = value - piece
    return found


def distance_factors(points, left):
    count = points.shape[1]
    scaled = (points - 0.5) * (1.0 / SUPPORT_RADIUS)
    scaled = jnp.concatenate([scaled, jnp.zeros((5, count), jnp.float32)], axis=0)
    norm = jnp.sum(scaled * scaled, axis=0, keepdims=True)
    norms = pieces(jnp.broadcast_to(norm, (8, count)), 3)
    row = lax.broadcasted_iota(jnp.int32, (8, count), 0)
    norm_block = jnp.zeros((8, count), jnp.float32)
    for place in range(3):
        norm_block = jnp.where(row == place, norms[place], norm_block)
    ones_block = jnp.where(row < 3, 1.0, 0.0)
    first, second, third = pieces(scaled, 3)
    if left:
        dims = [first, first, second, second, first, third]
        dims = [-2.0 * part for part in dims]
        blocks = dims + [norm_block, ones_block]
    else:
        dims = [first, second, first, second, third, first]
        blocks = dims + [ones_block, norm_block]
    return jnp.concatenate(blocks, axis=0)


def wendland_kernel(first_cell, left_ref, right_ref, _, kernel_ref):
    cells, owned = kernel_ref.shape[0] // 2, kernel_ref.shape[1]
    tile, wide = min(128, cells), min(256, owned)

    def squares(row, lane):
        left = left_ref[first_cell + row : first_cell + row + tile, :]
        right = right_ref[:, lane : lane + wide]
        return jnp.dot(left, right, preferred_element_type=jnp.float32)

    places = [(row, lane) for lane in range(0, owned, wide) for row in range(0, cells, tile)]
    following = squares(*places[0])
    for at, (row, lane) in enumerate(places):
        squared = jnp.maximum(following, 1e-30)
        if at + 1 < len(places):
            following = squares(*places[at + 1])
        near = jnp.maximum(1.0 - squared * lax.rsqrt(squared), 0.0)
        power = near * near
        kernel = power * power * (1.25 - near)
        first = kernel.astype(jnp.bfloat16)
        rest = (kernel - first.astype(jnp.float32)).astype(jnp.bfloat16)
        here = slice(lane, lane + wide)
        kernel_ref[row : row + tile, here] = first
        kernel_ref[cells + row : cells + row + tile, here] = rest


def far_wendland_kernel(
    first_cell, left_ref, right_ref, after, adjoint_ref, low_ref, *rest
):
    kernel_ref, one_hot_ref, result_ref, sem = rest
    copy = pltpu.make_async_copy(adjoint_ref, result_ref, sem)
    copy.start()
    owned = low_ref.shape[1]
    write_one_hot(low_ref, one_hot_ref, low_ref.shape[0] - one_hot_ref.shape[0] // owned)
    wendland_kernel(first_cell, left_ref, right_ref, after, kernel_ref)
    copy.wait()


def control_kernel(scale, *refs):
    *sens_refs, near_ref, far_ref = refs[:-4]
    spread_ref, near_hot, far_hot, out_ref = refs[-4:]
    blocks = sens_refs[0].shape[0] // 3
    half = near_ref.shape[0] // 2
    groups = FFD // LANES
    total = sens_refs[0][...]
    for ref in sens_refs[1:]:
        total = total + ref[...]
    total = total * scale

    def halves(value):
        first = value.astype(jnp.bfloat16)
        rest = (value - first.astype(jnp.float32)).astype(jnp.bfloat16)
        return first, rest

    row = lax.broadcasted_iota(jnp.int32, (8, LANES), 0)
    wide = []
    for block in range(blocks):
        sens = jnp.zeros((8, LANES), jnp.float32)
        for k in range(3):
            sens = jnp.where(row == k, total[k * blocks + block : k * blocks + block + 1], sens)
        first = sens.astype(jnp.bfloat16).astype(jnp.float32)
        wide.append(jnp.concatenate([first, sens - first], axis=0))
    sens = jnp.concatenate(wide, axis=1).astype(jnp.bfloat16)
    grad = None
    for part, ref in ((sens[:, :half], near_ref), (sens[:, half:], far_ref)):
        both = jnp.concatenate([part, part], axis=1)
        term = jnp.dot(both, ref[...], preferred_element_type=jnp.float32)
        grad = term if grad is None else grad + term
    grad = grad[:8] + grad[8:]
    row = lax.broadcasted_iota(jnp.int32, (16, grad.shape[1]), 0)
    wide = jnp.zeros(row.shape, jnp.float32)
    for k in range(3):
        mine = jnp.logical_and(row >= k * groups, row < (k + 1) * groups)
        wide = jnp.where(mine, grad[k : k + 1], wide)
    grad = wide
    owned = grad.shape[1]
    result = None
    places = [
        (ref, first) for ref in (near_hot, far_hot) for first in range(0, ref.shape[0], owned)
    ]
    for j, (ref, first) in enumerate(places):
        term = jnp.dot(
            jnp.concatenate(halves(grad * spread_ref[j * 16 : (j + 1) * 16, :]), axis=0),
            ref[first : first + owned, :],
            preferred_element_type=jnp.float32,
        )
        result = term if result is None else result + term
    result = result[:16] + result[16:]
    out_ref[...] = result[: 3 * groups]


def tree(values):
    while len(values) > 1:
        values = [sum(values[i : i + 2]) for i in range(0, len(values), 2)]
    return values[0]


def add_kernel(*refs):
    refs[-1][...] = tree([ref[...] for ref in refs[:-1]])


def finish_kernel(*refs):
    total, out_ref = tree([ref[...] for ref in refs[:-1]]), refs[-1]
    groups = out_ref.shape[1] // LANES
    for k in range(3):
        for group in range(groups):
            row = k * groups + group
            out_ref[k : k + 1, group * LANES : (group + 1) * LANES] = total[row : row + 1]


def sum_rounds():
    lines, nodes, cores = (lax.axis_size(axis) for axis in SUM_AXES)
    if any(size & (size - 1) for size in (lines, nodes, cores)):
        return None
    near = [cores >> 1 >> i for i in range(cores.bit_length() - 1)]
    node_bits = [cores << i for i in range(nodes.bit_length() - 1)]
    line_bits = [cores * nodes << i for i in range(lines.bit_length() - 1)]
    bits = line_bits[1:2] + node_bits[:1] + line_bits[2:] + node_bits[1:]
    rounds = [[bit] for bit in near] + [[bit | (cores - 1)] for bit in line_bits[:1]]
    for first in range(0, len(bits), 2):
        masks = bits[first : first + 2]
        if len(masks) == 2:
            masks = [masks[0] | masks[1]] + masks
        rounds.append([mask | (cores - 1) for mask in masks])
    return rounds


def exchanged(value, masks):
    peers = lax.axis_size(SUM_AXES)
    return [value] + [
        lax.ppermute(value, SUM_AXES, [(i, i ^ mask) for i in range(peers)]) for mask in masks
    ]


def body(
    adjoint_start,
    adjoint_rhs,
    off_blocks,
    diag_inverse,
    neighbours,
    node_weights,
    sens_blocks,
    cell_points,
    base_points,
    ffd_index,
    ffd_weight,
):
    nodes, _, cells = adjoint_start.shape
    faces = off_blocks.shape[1]
    blocks = cells // LANES
    per = blocks * nodes
    slots = ffd_index.shape[1]
    far_slots = slots // 2
    owned = base_points.shape[1] // lax.axis_size("nodes")
    peers = lax.axis_size(CELL_AXES)
    cores = lax.axis_size("sub")
    node_peers = lax.axis_size("nodes")
    f32, i32, bf16 = jnp.float32, jnp.int32, jnp.bfloat16

    def shape(dims, dtype=f32):
        return jax.ShapeDtypeStruct(dims, dtype)

    def cost(flops, moved):
        return pl.CostEstimate(flops=flops, bytes_accessed=moved, transcendentals=0)

    def swaps(array):
        close = lax.ppermute(array, CELL_AXES, [(i, i ^ 1) for i in range(peers)])
        pairs = []
        for i in range(peers):
            line, core = divmod(i, cores)
            for node in range(node_peers):
                j, beside = (i + 1 if i % 2 else i - 1), node
                if not 0 <= j < peers:
                    j, beside = i, (node ^ 1 if node_peers % 2 == 0 else node)
                to_line, to_core = divmod(j, cores)
                pairs.append(
                    (
                        (line * node_peers + node) * cores + core,
                        (to_line * node_peers + beside) * cores + to_core,
                    )
                )
        return lax.ppermute(array, SUM_AXES, pairs), close

    adjoint = rows_of(adjoint_start)
    far, close = swaps(adjoint)
    prepared = pl.pallas_call(
        functools.partial(prepare_kernel, nodes),
        out_shape=(
            shape((faces * 25 * per, LANES)),
            shape((25 * per, LANES)),
            shape((5 * per, LANES)),
            shape((15 * per, LANES)),
            shape((faces * per, LANES), i32),
            shape((faces * per, LANES), i32),
            shape((slots * 16, owned)),
            shape((slots, owned)),
            shape(((slots - far_slots) * owned, LANES), bf16),
            shape((5 * per, LANES)),
            shape((cells, FACTOR_ROWS), bf16),
            shape((FACTOR_ROWS, owned), bf16),
        ),
        in_specs=[HBM] * 11,
        out_specs=(VMEM,) * 12,
        scratch_shapes=[
            pltpu.VMEM((faces * 25 * per, LANES), bf16),
            pltpu.VMEM((15 * per, LANES), bf16),
            pltpu.VMEM((faces, cells), i32),
            pltpu.SMEM((nodes,), f32),
            pltpu.VMEM((slots, owned), i32),
            pltpu.VMEM((slots, owned), f32),
            pltpu.VMEM((3, cells), f32),
            pltpu.VMEM((3, owned), f32),
            pltpu.SemaphoreType.DMA((11,)),
        ],
        compiler_params=PARAMS,
        cost_estimate=cost(10**9, 10**7),
        name="prepare",
    )(
        *in_hbm(
            rows_of(off_blocks.reshape(nodes, faces * 25, cells)),
            rows_of(diag_inverse),
            rows_of(adjoint_rhs),
            rows_of(sens_blocks),
            neighbours,
            node_weights,
            ffd_index.T,
            ffd_weight.T,
            adjoint,
            cell_points,
            base_points,
        )
    )
    off, inverse, rhs, sens, lane, step, spread, low, near_hot, adjoint, left, right = prepared
    scratch = [
        pltpu.VMEM((3 * 5 * per, LANES), f32),
        pltpu.VMEM((max(8 // nodes - 1, 1) * 3 * 5 * per, LANES), f32),
    ]
    sweep_cost = cost(2 * 10 * 35 * cells, 4 * faces * 25 * per * LANES)

    for _ in range(SWEEPS - 1):
        adjoint = pl.pallas_call(
            functools.partial(sweep_kernel, blocks),
            out_shape=shape((5 * per, LANES)),
            in_specs=[VMEM] * 8,
            out_specs=VMEM,
            scratch_shapes=scratch,
            compiler_params=PARAMS,
            cost_estimate=sweep_cost,
            name="sweep",
        )(far, close, adjoint, rhs, off, inverse, lane, step)
        far, close = swaps(adjoint)

    half = cells * 5 // 8 // LANES * LANES
    wendland_cost = cost(10**9, 10**7)
    near_shape = shape((2 * half, owned), bf16)
    far_shape = shape((2 * (cells - half), owned), bf16)
    near_kernel = pl.pallas_call(
        functools.partial(wendland_kernel, 0),
        out_shape=near_shape,
        in_specs=[VMEM] * 3,
        out_specs=VMEM,
        compiler_params=PARAMS,
        cost_estimate=wendland_cost,
        name="near_wendland",
    )(left, right, adjoint)
    adjoint, part_sens = pl.pallas_call(
        functools.partial(last_sweep_kernel, blocks),
        out_shape=(shape((5 * per, LANES)), shape((3 * blocks, LANES))),
        in_specs=[VMEM] * 9 + [pl.BlockSpec(memory_space=pl.ANY)],
        out_specs=(VMEM, VMEM),
        scratch_shapes=scratch + [pltpu.VMEM((3 * per, LANES), f32)],
        compiler_params=PARAMS,
        cost_estimate=sweep_cost,
        name="last_sweep",
    )(close, far, adjoint, rhs, off, inverse, lane, step, sens, near_kernel)

    all_sens = [part_sens]
    for shift in range(1, node_peers):
        ring = [(i, (i + shift) % node_peers) for i in range(node_peers)]
        all_sens.append(lax.ppermute(part_sens, "nodes", ring))
    hot_shape = shape((far_slots * owned, LANES), bf16)
    far_kernel, far_hot, adjoint = pl.pallas_call(
        functools.partial(far_wendland_kernel, half),
        out_shape=(far_shape, hot_shape, shape((5 * per, LANES))),
        in_specs=[VMEM] * 5,
        out_specs=(VMEM, VMEM, HBM),
        scratch_shapes=[pltpu.SemaphoreType.DMA],
        compiler_params=PARAMS,
        cost_estimate=wendland_cost,
        name="far_wendland",
    )(left, right, part_sens, adjoint, low)
    scale = 4.0 / math.sqrt(cells * peers)
    rows = 3 * FFD // LANES
    partial = pl.pallas_call(
        functools.partial(control_kernel, scale),
        out_shape=shape((rows, LANES)),
        in_specs=[VMEM] * (len(all_sens) + 5),
        out_specs=VMEM,
        compiler_params=PARAMS,
        name="control",
    )(*all_sens, near_kernel, far_kernel, spread, near_hot, far_hot)
    rounds = sum_rounds()
    terms = [partial] if rounds else [lax.psum(partial, SUM_AXES)]
    for masks in rounds or ():
        if len(terms) > 1:
            partial = pl.pallas_call(
                add_kernel, out_shape=shape((rows, LANES)), name="add", compiler_params=PARAMS
            )(*terms)
        terms = exchanged(partial, masks)
    control_grad = pl.pallas_call(
        finish_kernel, out_shape=shape((3, FFD)), name="finish", compiler_params=PARAMS
    )(*terms)
    return (from_rows(adjoint, nodes, cells), control_grad)


def solution(mesh):
    return jax.shard_map(
        body,
        mesh=mesh,
        in_specs=(
            P("nodes", None, ("groups", "cells", "sub")),
            P("nodes", None, ("groups", "cells", "sub")),
            P("nodes", None, None, ("groups", "cells", "sub")),
            P("nodes", None, ("groups", "cells", "sub")),
            P(None, ("cells", "sub")),
            P("nodes"),
            P("nodes", None, ("groups", "cells", "sub")),
            P(None, ("cells", "sub")),
            P(),
            P(),
            P(),
        ),
        out_specs=(P("nodes", None, ("groups", "cells", "sub")), P("groups", None)),
        check_vma=False,
    )
```

```python
import functools
import math

import jax
import jax.numpy as jnp
from jax import lax
from jax.experimental import pallas as pl
from jax.experimental.pallas import tpu as pltpu
from jax.sharding import PartitionSpec as P

SWEEPS = 2
FFD = 512
SUPPORT_RADIUS = 0.3
LANES = 128
CELL_AXES = ("cells", "sub")
SUM_AXES = ("cells", "nodes", "sub")
FACTOR_ROWS = 64
PARAMS = pltpu.CompilerParams(vmem_limit_bytes=24 * 1024 * 1024)
VMEM = pl.BlockSpec(memory_space=pltpu.VMEM)
HBM = pl.BlockSpec(memory_space=pltpu.HBM)


def rows_of(array):
    nodes, rows, cells = array.shape
    blocks = cells // LANES
    split = array.reshape(nodes, rows, blocks, LANES)
    return split.transpose(1, 2, 0, 3).reshape(rows * blocks * nodes, LANES)


def from_rows(array, nodes, cells):
    blocks = cells // LANES
    split = array.reshape(-1, blocks, nodes, LANES)
    return split.transpose(2, 0, 1, 3).reshape(nodes, -1, cells)


def in_hbm(*arrays):
    return [pltpu.with_memory_space_constraint(array, pltpu.HBM) for array in arrays]


def write_one_hot(low_ref, one_hot_ref, first_slot):
    owned = low_ref.shape[1]
    piece = min(512, owned)
    lane = lax.broadcasted_iota(jnp.int32, (piece, LANES), 1).astype(jnp.float32)
    lane = lane.astype(jnp.bfloat16)
    for first in range(0, owned, piece):
        low = low_ref[:, first : first + piece].T.astype(jnp.bfloat16)
        for j in range(one_hot_ref.shape[0] // owned):
            column = low[:, first_slot + j : first_slot + j + 1]
            hit = jnp.broadcast_to(column, (piece, LANES)) == lane
            one_hot_ref[j * owned + first : j * owned + first + piece, :] = jnp.where(
                hit, jnp.bfloat16(1.0), jnp.bfloat16(0.0)
            )


def prepare_kernel(
    nodes,
    off_in,
    inverse_in,
    rhs_in,
    sens_in,
    neigh_in,
    weight_in,
    index_in,
    spread_in,
    start_in,
    cell_in,
    base_in,
    off_ref,
    inverse_ref,
    rhs_ref,
    sens_ref,
    lane_ref,
    step_ref,
    spread_ref,
    low_ref,
    one_hot_ref,
    start_ref,
    left_ref,
    right_ref,
    off_buf,
    sens_buf,
    neigh_buf,
    weight_buf,
    index_buf,
    spread_buf,
    cell_buf,
    base_buf,
    sems,
):
    slots, owned = index_buf.shape
    start = pl.multiple_of(lax.axis_index("nodes") * owned, LANES)
    mine = pl.ds(start, owned)
    pairs = (
        (neigh_in, neigh_buf),
        (index_in.at[:, mine], index_buf),
        (spread_in.at[:, mine], spread_buf),
        (cell_in, cell_buf),
        (base_in.at[:, mine], base_buf),
        (off_in, off_buf),
        (weight_in, weight_buf),
        (sens_in, sens_buf),
        (inverse_in, inverse_ref),
        (rhs_in, rhs_ref),
        (start_in, start_ref),
    )
    copies = [pltpu.make_async_copy(a, b, sems.at[i]) for i, (a, b) in enumerate(pairs)]
    for copy in copies:
        copy.start()

    faces, cells = neigh_buf.shape
    blocks = cells // LANES
    per = blocks * nodes
    first_cell = lax.axis_index(CELL_AXES) * cells
    copies[0].wait()
    for block in range(blocks):
        index = neigh_buf[:, block * LANES : (block + 1) * LANES]
        local = index - first_cell + cells
        lane = jnp.bitwise_and(local, LANES - 1)
        step = jnp.right_shift(local, 7) - block
        step = jnp.where(index >= 0, step, -1)
        for node in range(nodes):
            rows = pl.ds(block * nodes + node, faces, stride=per)
            lane_ref[rows, :] = lane
            step_ref[rows, :] = step

    copies[1].wait()
    copies[2].wait()
    groups = FFD // LANES
    piece = min(512, owned)
    for first in range(0, owned, piece):
        here = slice(first, first + piece)
        high = jnp.right_shift(index_buf[:, here], 7)
        part = lax.broadcasted_iota(jnp.int32, (16, piece), 0)
        part = jnp.where(part < 3 * groups, lax.rem(part, groups), -1)
        for j in range(slots):
            spread_ref[j * 16 : (j + 1) * 16, here] = jnp.where(
                high[j : j + 1] == part, spread_buf[j : j + 1, here], 0.0
            )

    low_ref[...] = jnp.bitwise_and(index_buf[...], LANES - 1).astype(jnp.float32)
    write_one_hot(low_ref, one_hot_ref, 0)

    copies[3].wait()
    left_ref[...] = distance_factors(cell_buf[...], True).T.astype(jnp.bfloat16)
    copies[4].wait()
    right_ref[...] = distance_factors(base_buf[...], False).astype(jnp.bfloat16)

    copies[5].wait()
    off_ref[...] = off_buf[...].astype(jnp.float32)
    copies[6].wait()
    copies[7].wait()
    row_node = lax.rem(lax.broadcasted_iota(jnp.int32, (per, LANES), 0), nodes)
    weights = jnp.zeros((per, LANES), jnp.float32)
    for node in range(nodes):
        weights = jnp.where(row_node == node, weight_buf[node], weights)
    for row in range(0, sens_buf.shape[0], per):
        here = slice(row, row + per)
        sens_ref[here, :] = sens_buf[here, :].astype(jnp.float32) * weights
    for copy in copies[8:]:
        copy.wait()


def take_lanes(table, lanes):
    numbers = lax.GatherDimensionNumbers(
        offset_dims=(),
        collapsed_slice_dims=(1,),
        start_index_map=(1,),
        operand_batching_dims=(0,),
        start_indices_batching_dims=(0,),
    )
    return lax.gather(
        table,
        lanes[..., None],
        numbers,
        slice_sizes=(1, 1),
        mode=lax.GatherScatterMode.PROMISE_IN_BOUNDS,
    )


def sweep_into(
    blocks, first_ref, second_ref, own_ref, rhs_ref, off_ref, inverse_ref, lane_ref, step_ref,
    out_ref, window_ref, table_ref,
):
    per = rhs_ref.shape[0] // 5
    nodes = per // blocks
    faces = lane_ref.shape[0] // per
    odd = lax.rem(lax.axis_index(CELL_AXES), 2)
    place = pl.multiple_of((1 - odd) * 2 * per, 8)
    other = pl.multiple_of(odd * 2 * per, 8)
    width = 3 * per
    for b in range(5):
        rows = slice(b * per, (b + 1) * per)
        base = b * width
        window_ref[pl.ds(base + place, per), :] = first_ref[rows, :]
        window_ref[base + per : base + 2 * per, :] = own_ref[rows, :]
        window_ref[pl.ds(base + other, per), :] = second_ref[rows, :]
    for shift in range(1, 8 // nodes):
        for b in range(5):
            for tile in range(0, width - 8, 8):
                to = ((shift - 1) * 5 + b) * width + tile
                table_ref[to : to + 8, :] = window_ref[
                    pl.ds(b * width + tile + shift * nodes, 8), :
                ]
    for half in range(0, per, 8):
        remaining = [rhs_ref[a * per + half : a * per + half + 8, :] for a in range(5)]
        for f in range(faces):
            lanes = lane_ref[f * per + half : f * per + half + 8, :]
            dist = step_ref[f * per + half : f * per + half + 8, :]
            beside = [jnp.zeros((8, LANES), jnp.float32)] * 5
            for d in range(2 * blocks + 1):
                here = dist == d
                first = half + d * nodes
                for b in range(5):
                    shift, at = first % 8 // nodes, b * width + first // 8 * 8
                    if shift:
                        at = at + (shift - 1) * 5 * width
                        table = table_ref[at : at + 8, :]
                    else:
                        table = window_ref[at : at + 8, :]
                    beside[b] = jnp.where(here, take_lanes(table, lanes), beside[b])
            for a in range(5):
                for b in range(5):
                    row = (f * 25 + 5 * a + b) * per + half
                    remaining[a] = remaining[a] - off_ref[row : row + 8, :] * beside[b]
        for a in range(5):
            total = None
            for b in range(5):
                row = (5 * a + b) * per + half
                term = inverse_ref[row : row + 8, :] * remaining[b]
                total = term if total is None else total + term
            out_ref[a * per + half : a * per + half + 8, :] = total


def sweep_kernel(blocks, far_ref, close_ref, *refs):
    sweep_into(blocks, close_ref, far_ref, *refs)


def last_sweep_kernel(blocks, *refs):
    ins, rest = refs[:8], refs[8:]
    sens_ref, _, out_ref, sens_out_ref, window_ref, table_ref, part_ref = rest
    sweep_into(blocks, *ins, out_ref, window_ref, table_ref)
    per = out_ref.shape[0] // 5
    nodes = per // blocks
    for k in range(3):
        total = None
        for a in range(5):
            row = (3 * a + k) * per
            term = out_ref[a * per : (a + 1) * per, :] * sens_ref[row : row + per, :]
            total = term if total is None else total + term
        part_ref[k * per : (k + 1) * per, :] = total
    for block in range(blocks):
        total = None
        for node in range(nodes):
            term = part_ref[pl.ds(block * nodes + node, 3, stride=per), :]
            total = term if total is None else total + term
        sens_out_ref[pl.ds(block, 3, stride=blocks), :] = total


def pieces(value, count):
    found = []
    for _ in range(count):
        piece = value.astype(jnp.bfloat16).astype(jnp.float32)
        found.append(piece)
        value = value - piece
    return found


def distance_factors(points, left):
    count = points.shape[1]
    scaled = (points - 0.5) * (1.0 / SUPPORT_RADIUS)
    scaled = jnp.concatenate([scaled, jnp.zeros((5, count), jnp.float32)], axis=0)
    norm = jnp.sum(scaled * scaled, axis=0, keepdims=True)
    norms = pieces(jnp.broadcast_to(norm, (8, count)), 3)
    row = lax.broadcasted_iota(jnp.int32, (8, count), 0)
    norm_block = jnp.zeros((8, count), jnp.float32)
    for place in range(3):
        norm_block = jnp.where(row == place, norms[place], norm_block)
    ones_block = jnp.where(row < 3, 1.0, 0.0)
    first, second, third = pieces(scaled, 3)
    if left:
        dims = [first, first, second, second, first, third]
        dims = [-2.0 * part for part in dims]
        blocks = dims + [norm_block, ones_block]
    else:
        dims = [first, second, first, second, third, first]
        blocks = dims + [ones_block, norm_block]
    return jnp.concatenate(blocks, axis=0)


def wendland_kernel(first_cell, left_ref, right_ref, _, kernel_ref):
    cells, owned = kernel_ref.shape[0] // 2, kernel_ref.shape[1]
    tile, wide = min(128, cells), min(256, owned)

    def squares(row, lane):
        left = left_ref[first_cell + row : first_cell + row + tile, :]
        right = right_ref[:, lane : lane + wide]
        return jnp.dot(left, right, preferred_element_type=jnp.float32)

    places = [(row, lane) for lane in range(0, owned, wide) for row in range(0, cells, tile)]
    following = squares(*places[0])
    for at, (row, lane) in enumerate(places):
        squared = jnp.maximum(following, 1e-30)
        if at + 1 < len(places):
            following = squares(*places[at + 1])
        near = jnp.maximum(1.0 - squared * lax.rsqrt(squared), 0.0)
        power = near * near
        kernel = power * power * (1.25 - near)
        first = kernel.astype(jnp.bfloat16)
        rest = (kernel - first.astype(jnp.float32)).astype(jnp.bfloat16)
        here = slice(lane, lane + wide)
        kernel_ref[row : row + tile, here] = first
        kernel_ref[cells + row : cells + row + tile, here] = rest


def far_wendland_kernel(
    first_cell, left_ref, right_ref, after, adjoint_ref, low_ref, *rest
):
    kernel_ref, one_hot_ref, result_ref, sem = rest
    copy = pltpu.make_async_copy(adjoint_ref, result_ref, sem)
    copy.start()
    owned = low_ref.shape[1]
    write_one_hot(low_ref, one_hot_ref, low_ref.shape[0] - one_hot_ref.shape[0] // owned)
    wendland_kernel(first_cell, left_ref, right_ref, after, kernel_ref)
    copy.wait()


def control_kernel(scale, *refs):
    *sens_refs, near_ref, far_ref = refs[:-4]
    spread_ref, near_hot, far_hot, out_ref = refs[-4:]
    blocks = sens_refs[0].shape[0] // 3
    half = near_ref.shape[0] // 2
    groups = FFD // LANES
    total = sens_refs[0][...]
    for ref in sens_refs[1:]:
        total = total + ref[...]
    total = total * scale

    def halves(value):
        first = value.astype(jnp.bfloat16)
        rest = (value - first.astype(jnp.float32)).astype(jnp.bfloat16)
        return first, rest

    row = lax.broadcasted_iota(jnp.int32, (8, LANES), 0)
    wide = []
    for block in range(blocks):
        sens = jnp.zeros((8, LANES), jnp.float32)
        for k in range(3):
            sens = jnp.where(row == k, total[k * blocks + block : k * blocks + block + 1], sens)
        first = sens.astype(jnp.bfloat16).astype(jnp.float32)
        wide.append(jnp.concatenate([first, sens - first], axis=0))
    sens = jnp.concatenate(wide, axis=1).astype(jnp.bfloat16)
    grad = None
    for part, ref in ((sens[:, :half], near_ref), (sens[:, half:], far_ref)):
        both = jnp.concatenate([part, part], axis=1)
        term = jnp.dot(both, ref[...], preferred_element_type=jnp.float32)
        grad = term if grad is None else grad + term
    grad = grad[:8] + grad[8:]
    row = lax.broadcasted_iota(jnp.int32, (16, grad.shape[1]), 0)
    wide = jnp.zeros(row.shape, jnp.float32)
    for k in range(3):
        mine = jnp.logical_and(row >= k * groups, row < (k + 1) * groups)
        wide = jnp.where(mine, grad[k : k + 1], wide)
    grad = wide
    owned = grad.shape[1]
    result = None
    places = [
        (ref, first) for ref in (near_hot, far_hot) for first in range(0, ref.shape[0], owned)
    ]
    for j, (ref, first) in enumerate(places):
        term = jnp.dot(
            jnp.concatenate(halves(grad * spread_ref[j * 16 : (j + 1) * 16, :]), axis=0),
            ref[first : first + owned, :],
            preferred_element_type=jnp.float32,
        )
        result = term if result is None else result + term
    result = result[:16] + result[16:]
    out_ref[...] = result[: 3 * groups]


def tree(values):
    while len(values) > 1:
        values = [sum(values[i : i + 2]) for i in range(0, len(values), 2)]
    return values[0]


def add_kernel(*refs):
    refs[-1][...] = tree([ref[...] for ref in refs[:-1]])


def finish_kernel(*refs):
    total, out_ref = tree([ref[...] for ref in refs[:-1]]), refs[-1]
    groups = out_ref.shape[1] // LANES
    for k in range(3):
        for group in range(groups):
            row = k * groups + group
            out_ref[k : k + 1, group * LANES : (group + 1) * LANES] = total[row : row + 1]


def sum_rounds():
    lines, nodes, cores = (lax.axis_size(axis) for axis in SUM_AXES)
    if any(size & (size - 1) for size in (lines, nodes, cores)):
        return None
    near = [cores >> 1 >> i for i in range(cores.bit_length() - 1)]
    node_bits = [cores << i for i in range(nodes.bit_length() - 1)]
    line_bits = [cores * nodes << i for i in range(lines.bit_length() - 1)]
    bits = line_bits[1:2] + node_bits[:1] + line_bits[2:] + node_bits[1:]
    rounds = [[bit] for bit in near] + [[bit | (cores - 1)] for bit in line_bits[:1]]
    for first in range(0, len(bits), 2):
        masks = bits[first : first + 2]
        if len(masks) == 2:
            masks = [masks[0] | masks[1]] + masks
        rounds.append([mask | (cores - 1) for mask in masks])
    return rounds


def exchanged(value, masks):
    peers = lax.axis_size(SUM_AXES)
    return [value] + [
        lax.ppermute(value, SUM_AXES, [(i, i ^ mask) for i in range(peers)]) for mask in masks
    ]


def body(
    adjoint_start,
    adjoint_rhs,
    off_blocks,
    diag_inverse,
    neighbours,
    node_weights,
    sens_blocks,
    cell_points,
    base_points,
    ffd_index,
    ffd_weight,
):
    nodes, _, cells = adjoint_start.shape
    faces = off_blocks.shape[1]
    blocks = cells // LANES
    per = blocks * nodes
    slots = ffd_index.shape[1]
    far_slots = slots * 5 // 8
    owned = base_points.shape[1] // lax.axis_size("nodes")
    peers = lax.axis_size(CELL_AXES)
    cores = lax.axis_size("sub")
    node_peers = lax.axis_size("nodes")
    f32, i32, bf16 = jnp.float32, jnp.int32, jnp.bfloat16

    def shape(dims, dtype=f32):
        return jax.ShapeDtypeStruct(dims, dtype)

    def cost(flops, moved):
        return pl.CostEstimate(flops=flops, bytes_accessed=moved, transcendentals=0)

    def swaps(array):
        close = lax.ppermute(array, CELL_AXES, [(i, i ^ 1) for i in range(peers)])
        pairs = []
        for i in range(peers):
            line, core = divmod(i, cores)
            for node in range(node_peers):
                j, beside = (i + 1 if i % 2 else i - 1), node
                if not 0 <= j < peers:
                    j, beside = i, (node ^ 1 if node_peers % 2 == 0 else node)
                to_line, to_core = divmod(j, cores)
                pairs.append(
                    (
                        (line * node_peers + node) * cores + core,
                        (to_line * node_peers + beside) * cores + to_core,
                    )
                )
        return lax.ppermute(array, SUM_AXES, pairs), close

    adjoint = rows_of(adjoint_start)
    far, close = swaps(adjoint)
    prepared = pl.pallas_call(
        functools.partial(prepare_kernel, nodes),
        out_shape=(
            shape((faces * 25 * per, LANES)),
            shape((25 * per, LANES)),
            shape((5 * per, LANES)),
            shape((15 * per, LANES)),
            shape((faces * per, LANES), i32),
            shape((faces * per, LANES), i32),
            shape((slots * 16, owned)),
            shape((slots, owned)),
            shape(((slots - far_slots) * owned, LANES), bf16),
            shape((5 * per, LANES)),
            shape((cells, FACTOR_ROWS), bf16),
            shape((FACTOR_ROWS, owned), bf16),
        ),
        in_specs=[HBM] * 11,
        out_specs=(VMEM,) * 12,
        scratch_shapes=[
            pltpu.VMEM((faces * 25 * per, LANES), bf16),
            pltpu.VMEM((15 * per, LANES), bf16),
            pltpu.VMEM((faces, cells), i32),
            pltpu.SMEM((nodes,), f32),
            pltpu.VMEM((slots, owned), i32),
            pltpu.VMEM((slots, owned), f32),
            pltpu.VMEM((3, cells), f32),
            pltpu.VMEM((3, owned), f32),
            pltpu.SemaphoreType.DMA((11,)),
        ],
        compiler_params=PARAMS,
        cost_estimate=cost(10**9, 10**7),
        name="prepare",
    )(
        *in_hbm(
            rows_of(off_blocks.reshape(nodes, faces * 25, cells)),
            rows_of(diag_inverse),
            rows_of(adjoint_rhs),
            rows_of(sens_blocks),
            neighbours,
            node_weights,
            ffd_index.T,
            ffd_weight.T,
            adjoint,
            cell_points,
            base_points,
        )
    )
    off, inverse, rhs, sens, lane, step, spread, low, near_hot, adjoint, left, right = prepared
    scratch = [
        pltpu.VMEM((3 * 5 * per, LANES), f32),
        pltpu.VMEM((max(8 // nodes - 1, 1) * 3 * 5 * per, LANES), f32),
    ]
    sweep_cost = cost(2 * 10 * 35 * cells, 4 * faces * 25 * per * LANES)

    for _ in range(SWEEPS - 1):
        adjoint = pl.pallas_call(
            functools.partial(sweep_kernel, blocks),
            out_shape=shape((5 * per, LANES)),
            in_specs=[VMEM] * 8,
            out_specs=VMEM,
            scratch_shapes=scratch,
            compiler_params=PARAMS,
            cost_estimate=sweep_cost,
            name="sweep",
        )(far, close, adjoint, rhs, off, inverse, lane, step)
        far, close = swaps(adjoint)

    half = cells * 5 // 8 // LANES * LANES
    wendland_cost = cost(10**9, 10**7)
    near_shape = shape((2 * half, owned), bf16)
    far_shape = shape((2 * (cells - half), owned), bf16)
    near_kernel = pl.pallas_call(
        functools.partial(wendland_kernel, 0),
        out_shape=near_shape,
        in_specs=[VMEM] * 3,
        out_specs=VMEM,
        compiler_params=PARAMS,
        cost_estimate=wendland_cost,
        name="near_wendland",
    )(left, right, adjoint)
    adjoint, part_sens = pl.pallas_call(
        functools.partial(last_sweep_kernel, blocks),
        out_shape=(shape((5 * per, LANES)), shape((3 * blocks, LANES))),
        in_specs=[VMEM] * 9 + [pl.BlockSpec(memory_space=pl.ANY)],
        out_specs=(VMEM, VMEM),
        scratch_shapes=scratch + [pltpu.VMEM((3 * per, LANES), f32)],
        compiler_params=PARAMS,
        cost_estimate=sweep_cost,
        name="last_sweep",
    )(close, far, adjoint, rhs, off, inverse, lane, step, sens, near_kernel)

    all_sens = [part_sens]
    for shift in range(1, node_peers):
        ring = [(i, (i + shift) % node_peers) for i in range(node_peers)]
        all_sens.append(lax.ppermute(part_sens, "nodes", ring))
    hot_shape = shape((far_slots * owned, LANES), bf16)
    far_kernel, far_hot, adjoint = pl.pallas_call(
        functools.partial(far_wendland_kernel, half),
        out_shape=(far_shape, hot_shape, shape((5 * per, LANES))),
        in_specs=[VMEM] * 5,
        out_specs=(VMEM, VMEM, HBM),
        scratch_shapes=[pltpu.SemaphoreType.DMA],
        compiler_params=PARAMS,
        cost_estimate=wendland_cost,
        name="far_wendland",
    )(left, right, part_sens, adjoint, low)
    scale = 4.0 / math.sqrt(cells * peers)
    rows = 3 * FFD // LANES
    partial = pl.pallas_call(
        functools.partial(control_kernel, scale),
        out_shape=shape((rows, LANES)),
        in_specs=[VMEM] * (len(all_sens) + 5),
        out_specs=VMEM,
        compiler_params=PARAMS,
        name="control",
    )(*all_sens, near_kernel, far_kernel, spread, near_hot, far_hot)
    rounds = sum_rounds()
    terms = [partial] if rounds else [lax.psum(partial, SUM_AXES)]
    for masks in rounds or ():
        if len(terms) > 1:
            partial = pl.pallas_call(
                add_kernel, out_shape=shape((rows, LANES)), name="add", compiler_params=PARAMS
            )(*terms)
        terms = exchanged(partial, masks)
    control_grad = pl.pallas_call(
        finish_kernel, out_shape=shape((3, FFD)), name="finish", compiler_params=PARAMS
    )(*terms)
    return (from_rows(adjoint, nodes, cells), control_grad)


def solution(mesh):
    return jax.shard_map(
        body,
        mesh=mesh,
        in_specs=(
            P("nodes", None, ("groups", "cells", "sub")),
            P("nodes", None, ("groups", "cells", "sub")),
            P("nodes", None, None, ("groups", "cells", "sub")),
            P("nodes", None, ("groups", "cells", "sub")),
            P(None, ("cells", "sub")),
            P("nodes"),
            P("nodes", None, ("groups", "cells", "sub")),
            P(None, ("cells", "sub")),
            P(),
            P(),
            P(),
        ),
        out_specs=(P("nodes", None, ("groups", "cells", "sub")), P("groups", None)),
        check_vma=False,
    )
```

```python
import functools
import math

import jax
import jax.numpy as jnp
from jax import lax
from jax.experimental import pallas as pl
from jax.experimental.pallas import tpu as pltpu
from jax.sharding import PartitionSpec as P

SWEEPS = 2
FFD = 512
SUPPORT_RADIUS = 0.3
LANES = 128
CELL_AXES = ("cells", "sub")
SUM_AXES = ("cells", "nodes", "sub")
FACTOR_ROWS = 64
PARAMS = pltpu.CompilerParams(vmem_limit_bytes=24 * 1024 * 1024)
VMEM = pl.BlockSpec(memory_space=pltpu.VMEM)
HBM = pl.BlockSpec(memory_space=pltpu.HBM)


def rows_of(array):
    nodes, rows, cells = array.shape
    blocks = cells // LANES
    split = array.reshape(nodes, rows, blocks, LANES)
    return split.transpose(1, 2, 0, 3).reshape(rows * blocks * nodes, LANES)


def from_rows(array, nodes, cells):
    blocks = cells // LANES
    split = array.reshape(-1, blocks, nodes, LANES)
    return split.transpose(2, 0, 1, 3).reshape(nodes, -1, cells)


def in_hbm(*arrays):
    return [pltpu.with_memory_space_constraint(array, pltpu.HBM) for array in arrays]


def write_one_hot(low_ref, one_hot_ref, first_slot):
    owned = low_ref.shape[1]
    piece = min(512, owned)
    lane = lax.broadcasted_iota(jnp.int32, (piece, LANES), 1).astype(jnp.float32)
    lane = lane.astype(jnp.bfloat16)
    for first in range(0, owned, piece):
        low = low_ref[:, first : first + piece].T.astype(jnp.bfloat16)
        for j in range(one_hot_ref.shape[0] // owned):
            column = low[:, first_slot + j : first_slot + j + 1]
            hit = jnp.broadcast_to(column, (piece, LANES)) == lane
            one_hot_ref[j * owned + first : j * owned + first + piece, :] = jnp.where(
                hit, jnp.bfloat16(1.0), jnp.bfloat16(0.0)
            )


def prepare_kernel(
    nodes,
    off_in,
    inverse_in,
    rhs_in,
    sens_in,
    neigh_in,
    weight_in,
    index_in,
    spread_in,
    start_in,
    cell_in,
    base_in,
    off_ref,
    inverse_ref,
    rhs_ref,
    sens_ref,
    lane_ref,
    step_ref,
    spread_ref,
    low_ref,
    one_hot_ref,
    start_ref,
    left_ref,
    right_ref,
    off_buf,
    sens_buf,
    neigh_buf,
    weight_buf,
    index_buf,
    spread_buf,
    cell_buf,
    base_buf,
    sems,
):
    slots, owned = index_buf.shape
    start = pl.multiple_of(lax.axis_index("nodes") * owned, LANES)
    mine = pl.ds(start, owned)
    pairs = (
        (neigh_in, neigh_buf),
        (index_in.at[:, mine], index_buf),
        (spread_in.at[:, mine], spread_buf),
        (cell_in, cell_buf),
        (base_in.at[:, mine], base_buf),
        (off_in, off_buf),
        (weight_in, weight_buf),
        (sens_in, sens_buf),
        (inverse_in, inverse_ref),
        (rhs_in, rhs_ref),
        (start_in, start_ref),
    )
    copies = [pltpu.make_async_copy(a, b, sems.at[i]) for i, (a, b) in enumerate(pairs)]
    for copy in copies:
        copy.start()

    faces, cells = neigh_buf.shape
    blocks = cells // LANES
    per = blocks * nodes
    first_cell = lax.axis_index(CELL_AXES) * cells
    copies[0].wait()
    for block in range(blocks):
        index = neigh_buf[:, block * LANES : (block + 1) * LANES]
        local = index - first_cell + cells
        lane = jnp.bitwise_and(local, LANES - 1)
        step = jnp.right_shift(local, 7) - block
        step = jnp.where(index >= 0, step, -1)
        for node in range(nodes):
            rows = pl.ds(block * nodes + node, faces, stride=per)
            lane_ref[rows, :] = lane
            step_ref[rows, :] = step

    copies[1].wait()
    copies[2].wait()
    groups = FFD // LANES
    piece = min(512, owned)
    for first in range(0, owned, piece):
        here = slice(first, first + piece)
        high = jnp.right_shift(index_buf[:, here], 7)
        part = lax.broadcasted_iota(jnp.int32, (16, piece), 0)
        part = jnp.where(part < 3 * groups, lax.rem(part, groups), -1)
        for j in range(slots):
            spread_ref[j * 16 : (j + 1) * 16, here] = jnp.where(
                high[j : j + 1] == part, spread_buf[j : j + 1, here], 0.0
            )

    low_ref[...] = jnp.bitwise_and(index_buf[...], LANES - 1).astype(jnp.float32)
    write_one_hot(low_ref, one_hot_ref, 0)

    copies[3].wait()
    left_ref[...] = distance_factors(cell_buf[...], True).T.astype(jnp.bfloat16)
    copies[4].wait()
    right_ref[...] = distance_factors(base_buf[...], False).astype(jnp.bfloat16)

    copies[5].wait()
    off_ref[...] = off_buf[...].astype(jnp.float32)
    copies[6].wait()
    copies[7].wait()
    row_node = lax.rem(lax.broadcasted_iota(jnp.int32, (per, LANES), 0), nodes)
    weights = jnp.zeros((per, LANES), jnp.float32)
    for node in range(nodes):
        weights = jnp.where(row_node == node, weight_buf[node], weights)
    for row in range(0, sens_buf.shape[0], per):
        here = slice(row, row + per)
        sens_ref[here, :] = sens_buf[here, :].astype(jnp.float32) * weights
    for copy in copies[8:]:
        copy.wait()


def take_lanes(table, lanes):
    numbers = lax.GatherDimensionNumbers(
        offset_dims=(),
        collapsed_slice_dims=(1,),
        start_index_map=(1,),
        operand_batching_dims=(0,),
        start_indices_batching_dims=(0,),
    )
    return lax.gather(
        table,
        lanes[..., None],
        numbers,
        slice_sizes=(1, 1),
        mode=lax.GatherScatterMode.PROMISE_IN_BOUNDS,
    )


def sweep_into(
    blocks, first_ref, second_ref, own_ref, rhs_ref, off_ref, inverse_ref, lane_ref, step_ref,
    out_ref, window_ref, table_ref,
):
    per = rhs_ref.shape[0] // 5
    nodes = per // blocks
    faces = lane_ref.shape[0] // per
    odd = lax.rem(lax.axis_index(CELL_AXES), 2)
    place = pl.multiple_of((1 - odd) * 2 * per, 8)
    other = pl.multiple_of(odd * 2 * per, 8)
    width = 3 * per
    for b in range(5):
        rows = slice(b * per, (b + 1) * per)
        base = b * width
        window_ref[pl.ds(base + place, per), :] = first_ref[rows, :]
        window_ref[base + per : base + 2 * per, :] = own_ref[rows, :]
        window_ref[pl.ds(base + other, per), :] = second_ref[rows, :]
    for shift in range(1, 8 // nodes):
        for b in range(5):
            for tile in range(0, width - 8, 8):
                to = ((shift - 1) * 5 + b) * width + tile
                table_ref[to : to + 8, :] = window_ref[
                    pl.ds(b * width + tile + shift * nodes, 8), :
                ]
    for half in range(0, per, 8):
        remaining = [rhs_ref[a * per + half : a * per + half + 8, :] for a in range(5)]
        for f in range(faces):
            lanes = lane_ref[f * per + half : f * per + half + 8, :]
            dist = step_ref[f * per + half : f * per + half + 8, :]
            beside = [jnp.zeros((8, LANES), jnp.float32)] * 5
            for d in range(2 * blocks + 1):
                here = dist == d
                first = half + d * nodes
                for b in range(5):
                    shift, at = first % 8 // nodes, b * width + first // 8 * 8
                    if shift:
                        at = at + (shift - 1) * 5 * width
                        table = table_ref[at : at + 8, :]
                    else:
                        table = window_ref[at : at + 8, :]
                    beside[b] = jnp.where(here, take_lanes(table, lanes), beside[b])
            for a in range(5):
                for b in range(5):
                    row = (f * 25 + 5 * a + b) * per + half
                    remaining[a] = remaining[a] - off_ref[row : row + 8, :] * beside[b]
        for a in range(5):
            total = None
            for b in range(5):
                row = (5 * a + b) * per + half
                term = inverse_ref[row : row + 8, :] * remaining[b]
                total = term if total is None else total + term
            out_ref[a * per + half : a * per + half + 8, :] = total


def sweep_kernel(blocks, far_ref, close_ref, *refs):
    sweep_into(blocks, close_ref, far_ref, *refs)


def last_sweep_kernel(blocks, *refs):
    ins, rest = refs[:8], refs[8:]
    sens_ref, _, out_ref, sens_out_ref, window_ref, table_ref, part_ref = rest
    sweep_into(blocks, *ins, out_ref, window_ref, table_ref)
    per = out_ref.shape[0] // 5
    nodes = per // blocks
    for k in range(3):
        total = None
        for a in range(5):
            row = (3 * a + k) * per
            term = out_ref[a * per : (a + 1) * per, :] * sens_ref[row : row + per, :]
            total = term if total is None else total + term
        part_ref[k * per : (k + 1) * per, :] = total
    for block in range(blocks):
        total = None
        for node in range(nodes):
            term = part_ref[pl.ds(block * nodes + node, 3, stride=per), :]
            total = term if total is None else total + term
        sens_out_ref[pl.ds(block, 3, stride=blocks), :] = total


def pieces(value, count):
    found = []
    for _ in range(count):
        piece = value.astype(jnp.bfloat16).astype(jnp.float32)
        found.append(piece)
        value = value - piece
    return found


def distance_factors(points, left):
    count = points.shape[1]
    scaled = (points - 0.5) * (1.0 / SUPPORT_RADIUS)
    scaled = jnp.concatenate([scaled, jnp.zeros((5, count), jnp.float32)], axis=0)
    norm = jnp.sum(scaled * scaled, axis=0, keepdims=True)
    norms = pieces(jnp.broadcast_to(norm, (8, count)), 3)
    row = lax.broadcasted_iota(jnp.int32, (8, count), 0)
    norm_block = jnp.zeros((8, count), jnp.float32)
    for place in range(3):
        norm_block = jnp.where(row == place, norms[place], norm_block)
    ones_block = jnp.where(row < 3, 1.0, 0.0)
    first, second, third = pieces(scaled, 3)
    if left:
        dims = [first, first, second, second, first, third]
        dims = [-2.0 * part for part in dims]
        blocks = dims + [norm_block, ones_block]
    else:
        dims = [first, second, first, second, third, first]
        blocks = dims + [ones_block, norm_block]
    return jnp.concatenate(blocks, axis=0)


def wendland_kernel(first_cell, left_ref, right_ref, _, kernel_ref):
    cells, owned = kernel_ref.shape[0] // 2, kernel_ref.shape[1]
    tile, wide = min(128, cells), min(256, owned)

    def squares(row, lane):
        left = left_ref[first_cell + row : first_cell + row + tile, :]
        right = right_ref[:, lane : lane + wide]
        return jnp.dot(left, right, preferred_element_type=jnp.float32)

    places = [(row, lane) for lane in range(0, owned, wide) for row in range(0, cells, tile)]
    following = squares(*places[0])
    for at, (row, lane) in enumerate(places):
        squared = jnp.maximum(following, 1e-30)
        if at + 1 < len(places):
            following = squares(*places[at + 1])
        near = jnp.maximum(1.0 - squared * lax.rsqrt(squared), 0.0)
        power = near * near
        kernel = power * power * (1.25 - near)
        first = kernel.astype(jnp.bfloat16)
        rest = (kernel - first.astype(jnp.float32)).astype(jnp.bfloat16)
        here = slice(lane, lane + wide)
        kernel_ref[row : row + tile, here] = first
        kernel_ref[cells + row : cells + row + tile, here] = rest


def far_wendland_kernel(
    first_cell, left_ref, right_ref, after, adjoint_ref, low_ref, *rest
):
    kernel_ref, one_hot_ref, result_ref, sem = rest
    copy = pltpu.make_async_copy(adjoint_ref, result_ref, sem)
    copy.start()
    owned = low_ref.shape[1]
    write_one_hot(low_ref, one_hot_ref, low_ref.shape[0] - one_hot_ref.shape[0] // owned)
    wendland_kernel(first_cell, left_ref, right_ref, after, kernel_ref)
    copy.wait()


def control_kernel(scale, *refs):
    *sens_refs, near_ref, far_ref = refs[:-4]
    spread_ref, near_hot, far_hot, out_ref = refs[-4:]
    blocks = sens_refs[0].shape[0] // 3
    half = near_ref.shape[0] // 2
    groups = FFD // LANES
    total = sens_refs[0][...]
    for ref in sens_refs[1:]:
        total = total + ref[...]
    total = total * scale

    def halves(value):
        first = value.astype(jnp.bfloat16)
        rest = (value - first.astype(jnp.float32)).astype(jnp.bfloat16)
        return first, rest

    row = lax.broadcasted_iota(jnp.int32, (8, LANES), 0)
    wide = []
    for block in range(blocks):
        sens = jnp.zeros((8, LANES), jnp.float32)
        for k in range(3):
            sens = jnp.where(row == k, total[k * blocks + block : k * blocks + block + 1], sens)
        first = sens.astype(jnp.bfloat16).astype(jnp.float32)
        wide.append(jnp.concatenate([first, sens - first], axis=0))
    sens = jnp.concatenate(wide, axis=1).astype(jnp.bfloat16)
    operands = [
        (jnp.concatenate([part, part], axis=1), ref)
        for part, ref in ((sens[:, :half], near_ref), (sens[:, half:], far_ref))
    ]
    owned = near_ref.shape[1]
    span = min(256, owned)

    def gradient(here):
        grad = None
        for both, ref in operands:
            term = jnp.dot(both, ref[:, here], preferred_element_type=jnp.float32)
            grad = term if grad is None else grad + term
        return grad[:8] + grad[8:]

    places = [
        (ref, first) for ref in (near_hot, far_hot) for first in range(0, ref.shape[0], owned)
    ]
    row = lax.broadcasted_iota(jnp.int32, (16, span), 0)
    spans = [slice(first, first + span) for first in range(0, owned, span)]
    following = gradient(spans[0])
    result = None
    for at, here in enumerate(spans):
        grad = following
        if at + 1 < len(spans):
            following = gradient(spans[at + 1])
        wide = jnp.zeros((16, span), jnp.float32)
        for k in range(3):
            mine = jnp.logical_and(row >= k * groups, row < (k + 1) * groups)
            wide = jnp.where(mine, grad[k : k + 1], wide)
        for j, (ref, first) in enumerate(places):
            term = jnp.dot(
                jnp.concatenate(halves(wide * spread_ref[j * 16 : (j + 1) * 16, here]), axis=0),
                ref[first + here.start : first + here.stop, :],
                preferred_element_type=jnp.float32,
            )
            result = term if result is None else result + term
    result = result[:16] + result[16:]
    out_ref[...] = result[: 3 * groups]


def tree(values):
    while len(values) > 1:
        values = [sum(values[i : i + 2]) for i in range(0, len(values), 2)]
    return values[0]


def add_kernel(*refs):
    refs[-1][...] = tree([ref[...] for ref in refs[:-1]])


def finish_kernel(*refs):
    total, out_ref = tree([ref[...] for ref in refs[:-1]]), refs[-1]
    groups = out_ref.shape[1] // LANES
    for k in range(3):
        for group in range(groups):
            row = k * groups + group
            out_ref[k : k + 1, group * LANES : (group + 1) * LANES] = total[row : row + 1]


def sum_rounds():
    lines, nodes, cores = (lax.axis_size(axis) for axis in SUM_AXES)
    if any(size & (size - 1) for size in (lines, nodes, cores)):
        return None
    near = [cores >> 1 >> i for i in range(cores.bit_length() - 1)]
    node_bits = [cores << i for i in range(nodes.bit_length() - 1)]
    line_bits = [cores * nodes << i for i in range(lines.bit_length() - 1)]
    bits = line_bits[1:2] + node_bits[:1] + line_bits[2:] + node_bits[1:]
    rounds = [[bit] for bit in near] + [[bit | (cores - 1)] for bit in line_bits[:1]]
    for first in range(0, len(bits), 2):
        masks = bits[first : first + 2]
        if len(masks) == 2:
            masks = [masks[0] | masks[1]] + masks
        rounds.append([mask | (cores - 1) for mask in masks])
    return rounds


def exchanged(value, masks):
    peers = lax.axis_size(SUM_AXES)
    return [value] + [
        lax.ppermute(value, SUM_AXES, [(i, i ^ mask) for i in range(peers)]) for mask in masks
    ]


def body(
    adjoint_start,
    adjoint_rhs,
    off_blocks,
    diag_inverse,
    neighbours,
    node_weights,
    sens_blocks,
    cell_points,
    base_points,
    ffd_index,
    ffd_weight,
):
    nodes, _, cells = adjoint_start.shape
    faces = off_blocks.shape[1]
    blocks = cells // LANES
    per = blocks * nodes
    slots = ffd_index.shape[1]
    far_slots = slots * 5 // 8
    owned = base_points.shape[1] // lax.axis_size("nodes")
    peers = lax.axis_size(CELL_AXES)
    cores = lax.axis_size("sub")
    node_peers = lax.axis_size("nodes")
    f32, i32, bf16 = jnp.float32, jnp.int32, jnp.bfloat16

    def shape(dims, dtype=f32):
        return jax.ShapeDtypeStruct(dims, dtype)

    def cost(flops, moved):
        return pl.CostEstimate(flops=flops, bytes_accessed=moved, transcendentals=0)

    def swaps(array):
        close = lax.ppermute(array, CELL_AXES, [(i, i ^ 1) for i in range(peers)])
        pairs = []
        for i in range(peers):
            line, core = divmod(i, cores)
            for node in range(node_peers):
                j, beside = (i + 1 if i % 2 else i - 1), node
                if not 0 <= j < peers:
                    j, beside = i, (node ^ 1 if node_peers % 2 == 0 else node)
                to_line, to_core = divmod(j, cores)
                pairs.append(
                    (
                        (line * node_peers + node) * cores + core,
                        (to_line * node_peers + beside) * cores + to_core,
                    )
                )
        return lax.ppermute(array, SUM_AXES, pairs), close

    adjoint = rows_of(adjoint_start)
    far, close = swaps(adjoint)
    prepared = pl.pallas_call(
        functools.partial(prepare_kernel, nodes),
        out_shape=(
            shape((faces * 25 * per, LANES)),
            shape((25 * per, LANES)),
            shape((5 * per, LANES)),
            shape((15 * per, LANES)),
            shape((faces * per, LANES), i32),
            shape((faces * per, LANES), i32),
            shape((slots * 16, owned)),
            shape((slots, owned)),
            shape(((slots - far_slots) * owned, LANES), bf16),
            shape((5 * per, LANES)),
            shape((cells, FACTOR_ROWS), bf16),
            shape((FACTOR_ROWS, owned), bf16),
        ),
        in_specs=[HBM] * 11,
        out_specs=(VMEM,) * 12,
        scratch_shapes=[
            pltpu.VMEM((faces * 25 * per, LANES), bf16),
            pltpu.VMEM((15 * per, LANES), bf16),
            pltpu.VMEM((faces, cells), i32),
            pltpu.SMEM((nodes,), f32),
            pltpu.VMEM((slots, owned), i32),
            pltpu.VMEM((slots, owned), f32),
            pltpu.VMEM((3, cells), f32),
            pltpu.VMEM((3, owned), f32),
            pltpu.SemaphoreType.DMA((11,)),
        ],
        compiler_params=PARAMS,
        cost_estimate=cost(10**9, 10**7),
        name="prepare",
    )(
        *in_hbm(
            rows_of(off_blocks.reshape(nodes, faces * 25, cells)),
            rows_of(diag_inverse),
            rows_of(adjoint_rhs),
            rows_of(sens_blocks),
            neighbours,
            node_weights,
            ffd_index.T,
            ffd_weight.T,
            adjoint,
            cell_points,
            base_points,
        )
    )
    off, inverse, rhs, sens, lane, step, spread, low, near_hot, adjoint, left, right = prepared
    scratch = [
        pltpu.VMEM((3 * 5 * per, LANES), f32),
        pltpu.VMEM((max(8 // nodes - 1, 1) * 3 * 5 * per, LANES), f32),
    ]
    sweep_cost = cost(2 * 10 * 35 * cells, 4 * faces * 25 * per * LANES)

    for _ in range(SWEEPS - 1):
        adjoint = pl.pallas_call(
            functools.partial(sweep_kernel, blocks),
            out_shape=shape((5 * per, LANES)),
            in_specs=[VMEM] * 8,
            out_specs=VMEM,
            scratch_shapes=scratch,
            compiler_params=PARAMS,
            cost_estimate=sweep_cost,
            name="sweep",
        )(far, close, adjoint, rhs, off, inverse, lane, step)
        far, close = swaps(adjoint)

    half = cells * 5 // 8 // LANES * LANES
    wendland_cost = cost(10**9, 10**7)
    near_shape = shape((2 * half, owned), bf16)
    far_shape = shape((2 * (cells - half), owned), bf16)
    near_kernel = pl.pallas_call(
        functools.partial(wendland_kernel, 0),
        out_shape=near_shape,
        in_specs=[VMEM] * 3,
        out_specs=VMEM,
        compiler_params=PARAMS,
        cost_estimate=wendland_cost,
        name="near_wendland",
    )(left, right, adjoint)
    adjoint, part_sens = pl.pallas_call(
        functools.partial(last_sweep_kernel, blocks),
        out_shape=(shape((5 * per, LANES)), shape((3 * blocks, LANES))),
        in_specs=[VMEM] * 9 + [pl.BlockSpec(memory_space=pl.ANY)],
        out_specs=(VMEM, VMEM),
        scratch_shapes=scratch + [pltpu.VMEM((3 * per, LANES), f32)],
        compiler_params=PARAMS,
        cost_estimate=sweep_cost,
        name="last_sweep",
    )(close, far, adjoint, rhs, off, inverse, lane, step, sens, near_kernel)

    all_sens = [part_sens]
    for shift in range(1, node_peers):
        ring = [(i, (i + shift) % node_peers) for i in range(node_peers)]
        all_sens.append(lax.ppermute(part_sens, "nodes", ring))
    hot_shape = shape((far_slots * owned, LANES), bf16)
    far_kernel, far_hot, adjoint = pl.pallas_call(
        functools.partial(far_wendland_kernel, half),
        out_shape=(far_shape, hot_shape, shape((5 * per, LANES))),
        in_specs=[VMEM] * 5,
        out_specs=(VMEM, VMEM, HBM),
        scratch_shapes=[pltpu.SemaphoreType.DMA],
        compiler_params=PARAMS,
        cost_estimate=wendland_cost,
        name="far_wendland",
    )(left, right, part_sens, adjoint, low)
    scale = 4.0 / math.sqrt(cells * peers)
    rows = 3 * FFD // LANES
    partial = pl.pallas_call(
        functools.partial(control_kernel, scale),
        out_shape=shape((rows, LANES)),
        in_specs=[VMEM] * (len(all_sens) + 5),
        out_specs=VMEM,
        compiler_params=PARAMS,
        name="control",
    )(*all_sens, near_kernel, far_kernel, spread, near_hot, far_hot)
    rounds = sum_rounds()
    terms = [partial] if rounds else [lax.psum(partial, SUM_AXES)]
    for masks in rounds or ():
        if len(terms) > 1:
            partial = pl.pallas_call(
                add_kernel, out_shape=shape((rows, LANES)), name="add", compiler_params=PARAMS
            )(*terms)
        terms = exchanged(partial, masks)
    control_grad = pl.pallas_call(
        finish_kernel, out_shape=shape((3, FFD)), name="finish", compiler_params=PARAMS
    )(*terms)
    return (from_rows(adjoint, nodes, cells), control_grad)


def solution(mesh):
    return jax.shard_map(
        body,
        mesh=mesh,
        in_specs=(
            P("nodes", None, ("groups", "cells", "sub")),
            P("nodes", None, ("groups", "cells", "sub")),
            P("nodes", None, None, ("groups", "cells", "sub")),
            P("nodes", None, ("groups", "cells", "sub")),
            P(None, ("cells", "sub")),
            P("nodes"),
            P("nodes", None, ("groups", "cells", "sub")),
            P(None, ("cells", "sub")),
            P(),
            P(),
            P(),
        ),
        out_specs=(P("nodes", None, ("groups", "cells", "sub")), P("groups", None)),
        check_vma=False,
    )
```

```python
import functools
import math

import jax
import jax.numpy as jnp
from jax import lax
from jax.experimental import pallas as pl
from jax.experimental.pallas import tpu as pltpu
from jax.sharding import PartitionSpec as P

SWEEPS = 2
FFD = 512
SUPPORT_RADIUS = 0.3
LANES = 128
CELL_AXES = ("cells", "sub")
SUM_AXES = ("cells", "nodes", "sub")
FACTOR_ROWS = 64
PARAMS = pltpu.CompilerParams(vmem_limit_bytes=24 * 1024 * 1024)
VMEM = pl.BlockSpec(memory_space=pltpu.VMEM)
HBM = pl.BlockSpec(memory_space=pltpu.HBM)


def rows_of(array):
    nodes, rows, cells = array.shape
    blocks = cells // LANES
    split = array.reshape(nodes, rows, blocks, LANES)
    return split.transpose(1, 2, 0, 3).reshape(rows * blocks * nodes, LANES)


def from_rows(array, nodes, cells):
    blocks = cells // LANES
    split = array.reshape(-1, blocks, nodes, LANES)
    return split.transpose(2, 0, 1, 3).reshape(nodes, -1, cells)


def in_hbm(*arrays):
    return [pltpu.with_memory_space_constraint(array, pltpu.HBM) for array in arrays]


def write_one_hot(low_ref, one_hot_ref, first_slot):
    owned = low_ref.shape[1]
    piece = min(512, owned)
    lane = lax.broadcasted_iota(jnp.int32, (piece, LANES), 1).astype(jnp.float32)
    lane = lane.astype(jnp.bfloat16)
    for first in range(0, owned, piece):
        low = low_ref[:, first : first + piece].T.astype(jnp.bfloat16)
        for j in range(one_hot_ref.shape[0] // owned):
            column = low[:, first_slot + j : first_slot + j + 1]
            hit = jnp.broadcast_to(column, (piece, LANES)) == lane
            one_hot_ref[j * owned + first : j * owned + first + piece, :] = jnp.where(
                hit, jnp.bfloat16(1.0), jnp.bfloat16(0.0)
            )


def prepare_kernel(
    nodes,
    off_in,
    inverse_in,
    rhs_in,
    sens_in,
    neigh_in,
    weight_in,
    index_in,
    spread_in,
    start_in,
    cell_in,
    base_in,
    off_ref,
    inverse_ref,
    rhs_ref,
    sens_ref,
    lane_ref,
    step_ref,
    spread_ref,
    low_ref,
    one_hot_ref,
    start_ref,
    left_ref,
    right_ref,
    off_buf,
    sens_buf,
    neigh_buf,
    weight_buf,
    index_buf,
    spread_buf,
    cell_buf,
    base_buf,
    sems,
):
    slots, owned = index_buf.shape
    start = pl.multiple_of(lax.axis_index("nodes") * owned, LANES)
    mine = pl.ds(start, owned)
    pairs = (
        (neigh_in, neigh_buf),
        (index_in.at[:, mine], index_buf),
        (spread_in.at[:, mine], spread_buf),
        (cell_in, cell_buf),
        (base_in.at[:, mine], base_buf),
        (off_in, off_buf),
        (weight_in, weight_buf),
        (sens_in, sens_buf),
        (inverse_in, inverse_ref),
        (rhs_in, rhs_ref),
        (start_in, start_ref),
    )
    copies = [pltpu.make_async_copy(a, b, sems.at[i]) for i, (a, b) in enumerate(pairs)]
    for copy in copies:
        copy.start()

    faces, cells = neigh_buf.shape
    blocks = cells // LANES
    per = blocks * nodes
    first_cell = lax.axis_index(CELL_AXES) * cells
    copies[0].wait()
    for block in range(blocks):
        index = neigh_buf[:, block * LANES : (block + 1) * LANES]
        local = index - first_cell + cells
        lane = jnp.bitwise_and(local, LANES - 1)
        step = jnp.right_shift(local, 7) - block
        step = jnp.where(index >= 0, step, -1)
        for node in range(nodes):
            rows = pl.ds(block * nodes + node, faces, stride=per)
            lane_ref[rows, :] = lane
            step_ref[rows, :] = step

    copies[1].wait()
    copies[2].wait()
    groups = FFD // LANES
    piece = min(512, owned)
    for first in range(0, owned, piece):
        here = slice(first, first + piece)
        high = jnp.right_shift(index_buf[:, here], 7)
        part = lax.broadcasted_iota(jnp.int32, (16, piece), 0)
        part = jnp.where(part < 3 * groups, lax.rem(part, groups), -1)
        for j in range(slots):
            spread_ref[j * 16 : (j + 1) * 16, here] = jnp.where(
                high[j : j + 1] == part, spread_buf[j : j + 1, here], 0.0
            )

    low_ref[...] = jnp.bitwise_and(index_buf[...], LANES - 1).astype(jnp.float32)
    write_one_hot(low_ref, one_hot_ref, 0)

    copies[3].wait()
    left_ref[...] = distance_factors(cell_buf[...], True).T.astype(jnp.bfloat16)
    copies[4].wait()
    right_ref[...] = distance_factors(base_buf[...], False).astype(jnp.bfloat16)

    copies[5].wait()
    off_ref[...] = off_buf[...].astype(jnp.float32)
    copies[6].wait()
    copies[7].wait()
    row_node = lax.rem(lax.broadcasted_iota(jnp.int32, (per, LANES), 0), nodes)
    weights = jnp.zeros((per, LANES), jnp.float32)
    for node in range(nodes):
        weights = jnp.where(row_node == node, weight_buf[node], weights)
    for row in range(0, sens_buf.shape[0], per):
        here = slice(row, row + per)
        sens_ref[here, :] = sens_buf[here, :].astype(jnp.float32) * weights
    for copy in copies[8:]:
        copy.wait()


def take_lanes(table, lanes):
    numbers = lax.GatherDimensionNumbers(
        offset_dims=(),
        collapsed_slice_dims=(1,),
        start_index_map=(1,),
        operand_batching_dims=(0,),
        start_indices_batching_dims=(0,),
    )
    return lax.gather(
        table,
        lanes[..., None],
        numbers,
        slice_sizes=(1, 1),
        mode=lax.GatherScatterMode.PROMISE_IN_BOUNDS,
    )


def sweep_into(
    blocks, first_ref, second_ref, own_ref, rhs_ref, off_ref, inverse_ref, lane_ref, step_ref,
    out_ref, window_ref, table_ref,
):
    per = rhs_ref.shape[0] // 5
    nodes = per // blocks
    faces = lane_ref.shape[0] // per
    odd = lax.rem(lax.axis_index(CELL_AXES), 2)
    place = pl.multiple_of((1 - odd) * 2 * per, 8)
    other = pl.multiple_of(odd * 2 * per, 8)
    width = 3 * per
    for b in range(5):
        rows = slice(b * per, (b + 1) * per)
        base = b * width
        window_ref[pl.ds(base + place, per), :] = first_ref[rows, :]
        window_ref[base + per : base + 2 * per, :] = own_ref[rows, :]
        window_ref[pl.ds(base + other, per), :] = second_ref[rows, :]
    for shift in range(1, 8 // nodes):
        for b in range(5):
            for tile in range(0, width - 8, 8):
                to = ((shift - 1) * 5 + b) * width + tile
                table_ref[to : to + 8, :] = window_ref[
                    pl.ds(b * width + tile + shift * nodes, 8), :
                ]
    for half in range(0, per, 8):
        remaining = [rhs_ref[a * per + half : a * per + half + 8, :] for a in range(5)]
        for f in range(faces):
            lanes = lane_ref[f * per + half : f * per + half + 8, :]
            dist = step_ref[f * per + half : f * per + half + 8, :]
            beside = [jnp.zeros((8, LANES), jnp.float32)] * 5
            for d in range(2 * blocks + 1):
                here = dist == d
                first = half + d * nodes
                for b in range(5):
                    shift, at = first % 8 // nodes, b * width + first // 8 * 8
                    if shift:
                        at = at + (shift - 1) * 5 * width
                        table = table_ref[at : at + 8, :]
                    else:
                        table = window_ref[at : at + 8, :]
                    beside[b] = jnp.where(here, take_lanes(table, lanes), beside[b])
            for a in range(5):
                for b in range(5):
                    row = (f * 25 + 5 * a + b) * per + half
                    remaining[a] = remaining[a] - off_ref[row : row + 8, :] * beside[b]
        for a in range(5):
            total = None
            for b in range(5):
                row = (5 * a + b) * per + half
                term = inverse_ref[row : row + 8, :] * remaining[b]
                total = term if total is None else total + term
            out_ref[a * per + half : a * per + half + 8, :] = total


def sweep_kernel(blocks, far_ref, close_ref, *refs):
    sweep_into(blocks, close_ref, far_ref, *refs)


def last_sweep_kernel(blocks, *refs):
    ins, rest = refs[:8], refs[8:]
    sens_ref, _, out_ref, sens_out_ref, window_ref, table_ref, part_ref = rest
    sweep_into(blocks, *ins, out_ref, window_ref, table_ref)
    per = out_ref.shape[0] // 5
    nodes = per // blocks
    for k in range(3):
        total = None
        for a in range(5):
            row = (3 * a + k) * per
            term = out_ref[a * per : (a + 1) * per, :] * sens_ref[row : row + per, :]
            total = term if total is None else total + term
        part_ref[k * per : (k + 1) * per, :] = total
    for block in range(blocks):
        total = None
        for node in range(nodes):
            term = part_ref[pl.ds(block * nodes + node, 3, stride=per), :]
            total = term if total is None else total + term
        sens_out_ref[pl.ds(block, 3, stride=blocks), :] = total


def pieces(value, count):
    found = []
    for _ in range(count):
        piece = value.astype(jnp.bfloat16).astype(jnp.float32)
        found.append(piece)
        value = value - piece
    return found


def distance_factors(points, left):
    count = points.shape[1]
    scaled = (points - 0.5) * (1.0 / SUPPORT_RADIUS)
    scaled = jnp.concatenate([scaled, jnp.zeros((5, count), jnp.float32)], axis=0)
    norm = jnp.sum(scaled * scaled, axis=0, keepdims=True)
    norms = pieces(jnp.broadcast_to(norm, (8, count)), 3)
    row = lax.broadcasted_iota(jnp.int32, (8, count), 0)
    norm_block = jnp.zeros((8, count), jnp.float32)
    for place in range(3):
        norm_block = jnp.where(row == place, norms[place], norm_block)
    ones_block = jnp.where(row < 3, 1.0, 0.0)
    first, second, third = pieces(scaled, 3)
    if left:
        dims = [first, first, second, second, first, third]
        dims = [-2.0 * part for part in dims]
        blocks = dims + [norm_block, ones_block]
    else:
        dims = [first, second, first, second, third, first]
        blocks = dims + [ones_block, norm_block]
    return jnp.concatenate(blocks, axis=0)


def wendland_kernel(first_cell, left_ref, right_ref, _, kernel_ref):
    cells, owned = kernel_ref.shape[0] // 2, kernel_ref.shape[1]
    tile, wide = min(128, cells), min(256, owned)

    def squares(row, lane):
        left = left_ref[first_cell + row : first_cell + row + tile, :]
        right = right_ref[:, lane : lane + wide]
        return jnp.dot(left, right, preferred_element_type=jnp.float32)

    places = [(row, lane) for lane in range(0, owned, wide) for row in range(0, cells, tile)]
    following = squares(*places[0])
    for at, (row, lane) in enumerate(places):
        squared = jnp.maximum(following, 1e-30)
        if at + 1 < len(places):
            following = squares(*places[at + 1])
        near = jnp.maximum(1.0 - squared * lax.rsqrt(squared), 0.0)
        power = near * near
        kernel = power * power * (1.25 - near)
        first = kernel.astype(jnp.bfloat16)
        rest = (kernel - first.astype(jnp.float32)).astype(jnp.bfloat16)
        here = slice(lane, lane + wide)
        kernel_ref[row : row + tile, here] = first
        kernel_ref[cells + row : cells + row + tile, here] = rest


def far_wendland_kernel(
    first_cell, left_ref, right_ref, after, adjoint_ref, low_ref, *rest
):
    kernel_ref, one_hot_ref, result_ref, sem = rest
    copy = pltpu.make_async_copy(adjoint_ref, result_ref, sem)
    copy.start()
    owned = low_ref.shape[1]
    write_one_hot(low_ref, one_hot_ref, low_ref.shape[0] - one_hot_ref.shape[0] // owned)
    wendland_kernel(first_cell, left_ref, right_ref, after, kernel_ref)
    copy.wait()


def control_kernel(scale, *refs):
    *sens_refs, near_ref, far_ref = refs[:-4]
    spread_ref, near_hot, far_hot, out_ref = refs[-4:]
    blocks = sens_refs[0].shape[0] // 3
    half = near_ref.shape[0] // 2
    groups = FFD // LANES
    total = sens_refs[0][...]
    for ref in sens_refs[1:]:
        total = total + ref[...]
    total = total * scale

    def halves(value):
        first = value.astype(jnp.bfloat16)
        rest = (value - first.astype(jnp.float32)).astype(jnp.bfloat16)
        return first, rest

    row = lax.broadcasted_iota(jnp.int32, (8, LANES), 0)
    wide = []
    for block in range(blocks):
        sens = jnp.zeros((8, LANES), jnp.float32)
        for k in range(3):
            sens = jnp.where(row == k, total[k * blocks + block : k * blocks + block + 1], sens)
        first = sens.astype(jnp.bfloat16).astype(jnp.float32)
        wide.append(jnp.concatenate([first, sens - first], axis=0))
    sens = jnp.concatenate(wide, axis=1).astype(jnp.bfloat16)
    grad = None
    for part, ref in ((sens[:, :half], near_ref), (sens[:, half:], far_ref)):
        both = jnp.concatenate([part, part], axis=1)
        term = jnp.dot(both, ref[...], preferred_element_type=jnp.float32)
        grad = term if grad is None else grad + term
    grad = grad[:8] + grad[8:]
    row = lax.broadcasted_iota(jnp.int32, (16, grad.shape[1]), 0)
    wide = jnp.zeros(row.shape, jnp.float32)
    for k in range(3):
        mine = jnp.logical_and(row >= k * groups, row < (k + 1) * groups)
        wide = jnp.where(mine, grad[k : k + 1], wide)
    grad = wide
    owned = grad.shape[1]
    result, slot = None, 0
    for ref in (near_hot, far_hot):
        parts = []
        for _ in range(ref.shape[0] // owned):
            parts.append(halves(grad * spread_ref[slot * 16 : (slot + 1) * 16, :]))
            slot += 1
        parts = [jnp.concatenate(both, axis=1) for both in zip(*parts)]
        term = jnp.dot(
            jnp.concatenate(parts, axis=0), ref[...], preferred_element_type=jnp.float32
        )
        result = term if result is None else result + term
    result = result[:16] + result[16:]
    out_ref[...] = result[: 3 * groups]


def tree(values):
    while len(values) > 1:
        values = [sum(values[i : i + 2]) for i in range(0, len(values), 2)]
    return values[0]


def add_kernel(*refs):
    refs[-1][...] = tree([ref[...] for ref in refs[:-1]])


def finish_kernel(*refs):
    total, out_ref = tree([ref[...] for ref in refs[:-1]]), refs[-1]
    groups = out_ref.shape[1] // LANES
    for k in range(3):
        for group in range(groups):
            row = k * groups + group
            out_ref[k : k + 1, group * LANES : (group + 1) * LANES] = total[row : row + 1]


def sum_rounds():
    lines, nodes, cores = (lax.axis_size(axis) for axis in SUM_AXES)
    if any(size & (size - 1) for size in (lines, nodes, cores)):
        return None
    near = [cores >> 1 >> i for i in range(cores.bit_length() - 1)]
    node_bits = [cores << i for i in range(nodes.bit_length() - 1)]
    line_bits = [cores * nodes << i for i in range(lines.bit_length() - 1)]
    bits = line_bits[1:2] + node_bits[:1] + line_bits[2:] + node_bits[1:]
    rounds = [[bit] for bit in near] + [[bit | (cores - 1)] for bit in line_bits[:1]]
    for first in range(0, len(bits), 2):
        masks = bits[first : first + 2]
        if len(masks) == 2:
            masks = [masks[0] | masks[1]] + masks
        rounds.append([mask | (cores - 1) for mask in masks])
    return rounds


def exchanged(value, masks):
    peers = lax.axis_size(SUM_AXES)
    return [value] + [
        lax.ppermute(value, SUM_AXES, [(i, i ^ mask) for i in range(peers)]) for mask in masks
    ]


def body(
    adjoint_start,
    adjoint_rhs,
    off_blocks,
    diag_inverse,
    neighbours,
    node_weights,
    sens_blocks,
    cell_points,
    base_points,
    ffd_index,
    ffd_weight,
):
    nodes, _, cells = adjoint_start.shape
    faces = off_blocks.shape[1]
    blocks = cells // LANES
    per = blocks * nodes
    slots = ffd_index.shape[1]
    far_slots = slots * 5 // 8
    owned = base_points.shape[1] // lax.axis_size("nodes")
    peers = lax.axis_size(CELL_AXES)
    cores = lax.axis_size("sub")
    node_peers = lax.axis_size("nodes")
    f32, i32, bf16 = jnp.float32, jnp.int32, jnp.bfloat16

    def shape(dims, dtype=f32):
        return jax.ShapeDtypeStruct(dims, dtype)

    def cost(flops, moved):
        return pl.CostEstimate(flops=flops, bytes_accessed=moved, transcendentals=0)

    def swaps(array):
        close = lax.ppermute(array, CELL_AXES, [(i, i ^ 1) for i in range(peers)])
        pairs = []
        for i in range(peers):
            line, core = divmod(i, cores)
            for node in range(node_peers):
                j, beside = (i + 1 if i % 2 else i - 1), node
                if not 0 <= j < peers:
                    j, beside = i, (node ^ 1 if node_peers % 2 == 0 else node)
                to_line, to_core = divmod(j, cores)
                pairs.append(
                    (
                        (line * node_peers + node) * cores + core,
                        (to_line * node_peers + beside) * cores + to_core,
                    )
                )
        return lax.ppermute(array, SUM_AXES, pairs), close

    adjoint = rows_of(adjoint_start)
    far, close = swaps(adjoint)
    prepared = pl.pallas_call(
        functools.partial(prepare_kernel, nodes),
        out_shape=(
            shape((faces * 25 * per, LANES)),
            shape((25 * per, LANES)),
            shape((5 * per, LANES)),
            shape((15 * per, LANES)),
            shape((faces * per, LANES), i32),
            shape((faces * per, LANES), i32),
            shape((slots * 16, owned)),
            shape((slots, owned)),
            shape(((slots - far_slots) * owned, LANES), bf16),
            shape((5 * per, LANES)),
            shape((cells, FACTOR_ROWS), bf16),
            shape((FACTOR_ROWS, owned), bf16),
        ),
        in_specs=[HBM] * 11,
        out_specs=(VMEM,) * 12,
        scratch_shapes=[
            pltpu.VMEM((faces * 25 * per, LANES), bf16),
            pltpu.VMEM((15 * per, LANES), bf16),
            pltpu.VMEM((faces, cells), i32),
            pltpu.SMEM((nodes,), f32),
            pltpu.VMEM((slots, owned), i32),
            pltpu.VMEM((slots, owned), f32),
            pltpu.VMEM((3, cells), f32),
            pltpu.VMEM((3, owned), f32),
            pltpu.SemaphoreType.DMA((11,)),
        ],
        compiler_params=PARAMS,
        cost_estimate=cost(10**9, 10**7),
        name="prepare",
    )(
        *in_hbm(
            rows_of(off_blocks.reshape(nodes, faces * 25, cells)),
            rows_of(diag_inverse),
            rows_of(adjoint_rhs),
            rows_of(sens_blocks),
            neighbours,
            node_weights,
            ffd_index.T,
            ffd_weight.T,
            adjoint,
            cell_points,
            base_points,
        )
    )
    off, inverse, rhs, sens, lane, step, spread, low, near_hot, adjoint, left, right = prepared
    scratch = [
        pltpu.VMEM((3 * 5 * per, LANES), f32),
        pltpu.VMEM((max(8 // nodes - 1, 1) * 3 * 5 * per, LANES), f32),
    ]
    sweep_cost = cost(2 * 10 * 35 * cells, 4 * faces * 25 * per * LANES)

    for _ in range(SWEEPS - 1):
        adjoint = pl.pallas_call(
            functools.partial(sweep_kernel, blocks),
            out_shape=shape((5 * per, LANES)),
            in_specs=[VMEM] * 8,
            out_specs=VMEM,
            scratch_shapes=scratch,
            compiler_params=PARAMS,
            cost_estimate=sweep_cost,
            name="sweep",
        )(far, close, adjoint, rhs, off, inverse, lane, step)
        far, close = swaps(adjoint)

    half = cells * 5 // 8 // LANES * LANES
    wendland_cost = cost(10**9, 10**7)
    near_shape = shape((2 * half, owned), bf16)
    far_shape = shape((2 * (cells - half), owned), bf16)
    near_kernel = pl.pallas_call(
        functools.partial(wendland_kernel, 0),
        out_shape=near_shape,
        in_specs=[VMEM] * 3,
        out_specs=VMEM,
        compiler_params=PARAMS,
        cost_estimate=wendland_cost,
        name="near_wendland",
    )(left, right, adjoint)
    adjoint, part_sens = pl.pallas_call(
        functools.partial(last_sweep_kernel, blocks),
        out_shape=(shape((5 * per, LANES)), shape((3 * blocks, LANES))),
        in_specs=[VMEM] * 9 + [pl.BlockSpec(memory_space=pl.ANY)],
        out_specs=(VMEM, VMEM),
        scratch_shapes=scratch + [pltpu.VMEM((3 * per, LANES), f32)],
        compiler_params=PARAMS,
        cost_estimate=sweep_cost,
        name="last_sweep",
    )(close, far, adjoint, rhs, off, inverse, lane, step, sens, near_kernel)

    all_sens = [part_sens]
    for shift in range(1, node_peers):
        ring = [(i, (i + shift) % node_peers) for i in range(node_peers)]
        all_sens.append(lax.ppermute(part_sens, "nodes", ring))
    hot_shape = shape((far_slots * owned, LANES), bf16)
    far_kernel, far_hot, adjoint = pl.pallas_call(
        functools.partial(far_wendland_kernel, half),
        out_shape=(far_shape, hot_shape, shape((5 * per, LANES))),
        in_specs=[VMEM] * 5,
        out_specs=(VMEM, VMEM, HBM),
        scratch_shapes=[pltpu.SemaphoreType.DMA],
        compiler_params=PARAMS,
        cost_estimate=wendland_cost,
        name="far_wendland",
    )(left, right, part_sens, adjoint, low)
    scale = 4.0 / math.sqrt(cells * peers)
    rows = 3 * FFD // LANES
    partial = pl.pallas_call(
        functools.partial(control_kernel, scale),
        out_shape=shape((rows, LANES)),
        in_specs=[VMEM] * (len(all_sens) + 5),
        out_specs=VMEM,
        compiler_params=PARAMS,
        name="control",
    )(*all_sens, near_kernel, far_kernel, spread, near_hot, far_hot)
    rounds = sum_rounds()
    terms = [partial] if rounds else [lax.psum(partial, SUM_AXES)]
    for masks in rounds or ():
        if len(terms) > 1:
            partial = pl.pallas_call(
                add_kernel, out_shape=shape((rows, LANES)), name="add", compiler_params=PARAMS
            )(*terms)
        terms = exchanged(partial, masks)
    control_grad = pl.pallas_call(
        finish_kernel, out_shape=shape((3, FFD)), name="finish", compiler_params=PARAMS
    )(*terms)
    return (from_rows(adjoint, nodes, cells), control_grad)


def solution(mesh):
    return jax.shard_map(
        body,
        mesh=mesh,
        in_specs=(
            P("nodes", None, ("groups", "cells", "sub")),
            P("nodes", None, ("groups", "cells", "sub")),
            P("nodes", None, None, ("groups", "cells", "sub")),
            P("nodes", None, ("groups", "cells", "sub")),
            P(None, ("cells", "sub")),
            P("nodes"),
            P("nodes", None, ("groups", "cells", "sub")),
            P(None, ("cells", "sub")),
            P(),
            P(),
            P(),
        ),
        out_specs=(P("nodes", None, ("groups", "cells", "sub")), P("groups", None)),
        check_vma=False,
    )
```

```python
import functools
import math

import jax
import jax.numpy as jnp
from jax import lax
from jax.experimental import pallas as pl
from jax.experimental.pallas import tpu as pltpu
from jax.sharding import PartitionSpec as P

SWEEPS = 2
FFD = 512
SUPPORT_RADIUS = 0.3
LANES = 128
CELL_AXES = ("cells", "sub")
SUM_AXES = ("cells", "nodes", "sub")
FACTOR_ROWS = 64
PARAMS = pltpu.CompilerParams(vmem_limit_bytes=24 * 1024 * 1024)
VMEM = pl.BlockSpec(memory_space=pltpu.VMEM)
HBM = pl.BlockSpec(memory_space=pltpu.HBM)


def rows_of(array):
    nodes, rows, cells = array.shape
    blocks = cells // LANES
    split = array.reshape(nodes, rows, blocks, LANES)
    return split.transpose(1, 2, 0, 3).reshape(rows * blocks * nodes, LANES)


def from_rows(array, nodes, cells):
    blocks = cells // LANES
    split = array.reshape(-1, blocks, nodes, LANES)
    return split.transpose(2, 0, 1, 3).reshape(nodes, -1, cells)


def in_hbm(*arrays):
    return [pltpu.with_memory_space_constraint(array, pltpu.HBM) for array in arrays]


def write_one_hot(low_ref, one_hot_ref, first_slot):
    owned = low_ref.shape[1]
    piece = min(512, owned)
    lane = lax.broadcasted_iota(jnp.int32, (piece, LANES), 1).astype(jnp.float32)
    lane = lane.astype(jnp.bfloat16)
    for first in range(0, owned, piece):
        low = low_ref[:, first : first + piece].T.astype(jnp.bfloat16)
        for j in range(one_hot_ref.shape[0] // owned):
            column = low[:, first_slot + j : first_slot + j + 1]
            hit = jnp.broadcast_to(column, (piece, LANES)) == lane
            one_hot_ref[j * owned + first : j * owned + first + piece, :] = jnp.where(
                hit, jnp.bfloat16(1.0), jnp.bfloat16(0.0)
            )


def prepare_kernel(
    nodes,
    off_in,
    inverse_in,
    rhs_in,
    sens_in,
    neigh_in,
    weight_in,
    index_in,
    spread_in,
    start_in,
    cell_in,
    base_in,
    off_ref,
    inverse_ref,
    rhs_ref,
    sens_ref,
    lane_ref,
    step_ref,
    spread_ref,
    low_ref,
    one_hot_ref,
    start_ref,
    left_ref,
    right_ref,
    sens_buf,
    neigh_buf,
    weight_buf,
    index_buf,
    spread_buf,
    cell_buf,
    base_buf,
    sems,
):
    slots, owned = index_buf.shape
    start = pl.multiple_of(lax.axis_index("nodes") * owned, LANES)
    mine = pl.ds(start, owned)
    pairs = (
        (neigh_in, neigh_buf),
        (index_in.at[:, mine], index_buf),
        (spread_in.at[:, mine], spread_buf),
        (cell_in, cell_buf),
        (base_in.at[:, mine], base_buf),
        (off_in, off_ref),
        (weight_in, weight_buf),
        (sens_in, sens_buf),
        (inverse_in, inverse_ref),
        (rhs_in, rhs_ref),
        (start_in, start_ref),
    )
    copies = [pltpu.make_async_copy(a, b, sems.at[i]) for i, (a, b) in enumerate(pairs)]
    for copy in copies:
        copy.start()

    faces, cells = neigh_buf.shape
    blocks = cells // LANES
    per = blocks * nodes
    first_cell = lax.axis_index(CELL_AXES) * cells
    copies[0].wait()
    for block in range(blocks):
        index = neigh_buf[:, block * LANES : (block + 1) * LANES]
        local = index - first_cell + cells
        lane = jnp.bitwise_and(local, LANES - 1)
        step = jnp.right_shift(local, 7) - block
        step = jnp.where(index >= 0, step, -1)
        for node in range(nodes):
            rows = pl.ds(block * nodes + node, faces, stride=per)
            lane_ref[rows, :] = lane
            step_ref[rows, :] = step

    copies[1].wait()
    copies[2].wait()
    groups = FFD // LANES
    piece = min(512, owned)
    for first in range(0, owned, piece):
        here = slice(first, first + piece)
        high = jnp.right_shift(index_buf[:, here], 7)
        part = lax.broadcasted_iota(jnp.int32, (16, piece), 0)
        part = jnp.where(part < 3 * groups, lax.rem(part, groups), -1)
        for j in range(slots):
            spread_ref[j * 16 : (j + 1) * 16, here] = jnp.where(
                high[j : j + 1] == part, spread_buf[j : j + 1, here], 0.0
            )

    low_ref[...] = jnp.bitwise_and(index_buf[...], LANES - 1).astype(jnp.float32)
    write_one_hot(low_ref, one_hot_ref, 0)

    copies[3].wait()
    left_ref[...] = distance_factors(cell_buf[...], True).T.astype(jnp.bfloat16)
    copies[4].wait()
    right_ref[...] = distance_factors(base_buf[...], False).astype(jnp.bfloat16)

    copies[5].wait()
    copies[6].wait()
    copies[7].wait()
    row_node = lax.rem(lax.broadcasted_iota(jnp.int32, (per, LANES), 0), nodes)
    weights = jnp.zeros((per, LANES), jnp.float32)
    for node in range(nodes):
        weights = jnp.where(row_node == node, weight_buf[node], weights)
    for row in range(0, sens_buf.shape[0], per):
        here = slice(row, row + per)
        sens_ref[here, :] = sens_buf[here, :].astype(jnp.float32) * weights
    for copy in copies[8:]:
        copy.wait()


def take_lanes(table, lanes):
    numbers = lax.GatherDimensionNumbers(
        offset_dims=(),
        collapsed_slice_dims=(1,),
        start_index_map=(1,),
        operand_batching_dims=(0,),
        start_indices_batching_dims=(0,),
    )
    return lax.gather(
        table,
        lanes[..., None],
        numbers,
        slice_sizes=(1, 1),
        mode=lax.GatherScatterMode.PROMISE_IN_BOUNDS,
    )


def sweep_into(
    blocks, first_ref, second_ref, own_ref, rhs_ref, off_ref, inverse_ref, lane_ref, step_ref,
    out_ref, window_ref, table_ref,
):
    per = rhs_ref.shape[0] // 5
    nodes = per // blocks
    faces = lane_ref.shape[0] // per
    odd = lax.rem(lax.axis_index(CELL_AXES), 2)
    place = pl.multiple_of((1 - odd) * 2 * per, 8)
    other = pl.multiple_of(odd * 2 * per, 8)
    width = 3 * per
    for b in range(5):
        rows = slice(b * per, (b + 1) * per)
        base = b * width
        window_ref[pl.ds(base + place, per), :] = first_ref[rows, :]
        window_ref[base + per : base + 2 * per, :] = own_ref[rows, :]
        window_ref[pl.ds(base + other, per), :] = second_ref[rows, :]
    for shift in range(1, 8 // nodes):
        for b in range(5):
            for tile in range(0, width - 8, 8):
                to = ((shift - 1) * 5 + b) * width + tile
                table_ref[to : to + 8, :] = window_ref[
                    pl.ds(b * width + tile + shift * nodes, 8), :
                ]
    halves = range(0, per, 8)
    remaining = [
        [rhs_ref[a * per + half : a * per + half + 8, :] for a in range(5)] for half in halves
    ]
    for f in range(faces):
        beside = []
        for half in halves:
            lanes = lane_ref[f * per + half : f * per + half + 8, :]
            dist = step_ref[f * per + half : f * per + half + 8, :]
            found = [jnp.zeros((8, LANES), jnp.float32)] * 5
            for d in range(2 * blocks + 1):
                here = dist == d
                first = half + d * nodes
                for b in range(5):
                    shift, at = first % 8 // nodes, b * width + first // 8 * 8
                    if shift:
                        at = at + (shift - 1) * 5 * width
                        table = table_ref[at : at + 8, :]
                    else:
                        table = window_ref[at : at + 8, :]
                    found[b] = jnp.where(here, take_lanes(table, lanes), found[b])
            beside.append(found)
        for a in range(5):
            for b in range(5):
                row = (f * 25 + 5 * a + b) * per
                block = off_ref[row : row + per, :].astype(jnp.float32)
                for i, half in enumerate(halves):
                    remaining[i][a] = remaining[i][a] - block[half : half + 8] * beside[i][b]
    for i, half in enumerate(halves):
        for a in range(5):
            total = None
            for b in range(5):
                row = (5 * a + b) * per + half
                term = inverse_ref[row : row + 8, :] * remaining[i][b]
                total = term if total is None else total + term
            out_ref[a * per + half : a * per + half + 8, :] = total


def sweep_kernel(blocks, far_ref, close_ref, *refs):
    sweep_into(blocks, close_ref, far_ref, *refs)


def last_sweep_kernel(blocks, *refs):
    ins, rest = refs[:8], refs[8:]
    sens_ref, _, out_ref, sens_out_ref, window_ref, table_ref, part_ref = rest
    sweep_into(blocks, *ins, out_ref, window_ref, table_ref)
    per = out_ref.shape[0] // 5
    nodes = per // blocks
    for k in range(3):
        total = None
        for a in range(5):
            row = (3 * a + k) * per
            term = out_ref[a * per : (a + 1) * per, :] * sens_ref[row : row + per, :]
            total = term if total is None else total + term
        part_ref[k * per : (k + 1) * per, :] = total
    for block in range(blocks):
        total = None
        for node in range(nodes):
            term = part_ref[pl.ds(block * nodes + node, 3, stride=per), :]
            total = term if total is None else total + term
        sens_out_ref[pl.ds(block, 3, stride=blocks), :] = total


def pieces(value, count):
    found = []
    for _ in range(count):
        piece = value.astype(jnp.bfloat16).astype(jnp.float32)
        found.append(piece)
        value = value - piece
    return found


def distance_factors(points, left):
    count = points.shape[1]
    scaled = (points - 0.5) * (1.0 / SUPPORT_RADIUS)
    scaled = jnp.concatenate([scaled, jnp.zeros((5, count), jnp.float32)], axis=0)
    norm = jnp.sum(scaled * scaled, axis=0, keepdims=True)
    norms = pieces(jnp.broadcast_to(norm, (8, count)), 3)
    row = lax.broadcasted_iota(jnp.int32, (8, count), 0)
    norm_block = jnp.zeros((8, count), jnp.float32)
    for place in range(3):
        norm_block = jnp.where(row == place, norms[place], norm_block)
    ones_block = jnp.where(row < 3, 1.0, 0.0)
    first, second, third = pieces(scaled, 3)
    if left:
        dims = [first, first, second, second, first, third]
        dims = [-2.0 * part for part in dims]
        blocks = dims + [norm_block, ones_block]
    else:
        dims = [first, second, first, second, third, first]
        blocks = dims + [ones_block, norm_block]
    return jnp.concatenate(blocks, axis=0)


def wendland_kernel(first_cell, left_ref, right_ref, _, kernel_ref):
    cells, owned = kernel_ref.shape[0] // 2, kernel_ref.shape[1]
    tile, wide = min(128, cells), min(256, owned)

    def squares(row, lane):
        left = left_ref[first_cell + row : first_cell + row + tile, :]
        right = right_ref[:, lane : lane + wide]
        return jnp.dot(left, right, preferred_element_type=jnp.float32)

    places = [(row, lane) for lane in range(0, owned, wide) for row in range(0, cells, tile)]
    following = squares(*places[0])
    for at, (row, lane) in enumerate(places):
        squared = jnp.maximum(following, 1e-30)
        if at + 1 < len(places):
            following = squares(*places[at + 1])
        near = jnp.maximum(1.0 - squared * lax.rsqrt(squared), 0.0)
        power = near * near
        kernel = power * power * (1.25 - near)
        first = kernel.astype(jnp.bfloat16)
        rest = (kernel - first.astype(jnp.float32)).astype(jnp.bfloat16)
        here = slice(lane, lane + wide)
        kernel_ref[row : row + tile, here] = first
        kernel_ref[cells + row : cells + row + tile, here] = rest


def far_wendland_kernel(
    first_cell, left_ref, right_ref, after, adjoint_ref, low_ref, *rest
):
    kernel_ref, one_hot_ref, result_ref, sem = rest
    copy = pltpu.make_async_copy(adjoint_ref, result_ref, sem)
    copy.start()
    owned = low_ref.shape[1]
    write_one_hot(low_ref, one_hot_ref, low_ref.shape[0] - one_hot_ref.shape[0] // owned)
    wendland_kernel(first_cell, left_ref, right_ref, after, kernel_ref)
    copy.wait()


def control_kernel(scale, *refs):
    *sens_refs, near_ref, far_ref = refs[:-4]
    spread_ref, near_hot, far_hot, out_ref = refs[-4:]
    blocks = sens_refs[0].shape[0] // 3
    half = near_ref.shape[0] // 2
    groups = FFD // LANES
    total = sens_refs[0][...]
    for ref in sens_refs[1:]:
        total = total + ref[...]
    total = total * scale

    def halves(value):
        first = value.astype(jnp.bfloat16)
        rest = (value - first.astype(jnp.float32)).astype(jnp.bfloat16)
        return first, rest

    row = lax.broadcasted_iota(jnp.int32, (8, LANES), 0)
    wide = []
    for block in range(blocks):
        sens = jnp.zeros((8, LANES), jnp.float32)
        for k in range(3):
            sens = jnp.where(row == k, total[k * blocks + block : k * blocks + block + 1], sens)
        first = sens.astype(jnp.bfloat16).astype(jnp.float32)
        wide.append(jnp.concatenate([first, sens - first], axis=0))
    sens = jnp.concatenate(wide, axis=1).astype(jnp.bfloat16)
    grad = None
    for part, ref in ((sens[:, :half], near_ref), (sens[:, half:], far_ref)):
        both = jnp.concatenate([part, part], axis=1)
        term = jnp.dot(both, ref[...], preferred_element_type=jnp.float32)
        grad = term if grad is None else grad + term
    grad = grad[:8] + grad[8:]
    row = lax.broadcasted_iota(jnp.int32, (16, grad.shape[1]), 0)
    wide = jnp.zeros(row.shape, jnp.float32)
    for k in range(3):
        mine = jnp.logical_and(row >= k * groups, row < (k + 1) * groups)
        wide = jnp.where(mine, grad[k : k + 1], wide)
    grad = wide
    owned = grad.shape[1]
    result = None
    places = [
        (ref, first) for ref in (near_hot, far_hot) for first in range(0, ref.shape[0], owned)
    ]
    for j, (ref, first) in enumerate(places):
        term = jnp.dot(
            jnp.concatenate(halves(grad * spread_ref[j * 16 : (j + 1) * 16, :]), axis=0),
            ref[first : first + owned, :],
            preferred_element_type=jnp.float32,
        )
        result = term if result is None else result + term
    result = result[:16] + result[16:]
    out_ref[...] = result[: 3 * groups]


def tree(values):
    while len(values) > 1:
        values = [sum(values[i : i + 2]) for i in range(0, len(values), 2)]
    return values[0]


def add_kernel(*refs):
    refs[-1][...] = tree([ref[...] for ref in refs[:-1]])


def finish_kernel(*refs):
    total, out_ref = tree([ref[...] for ref in refs[:-1]]), refs[-1]
    groups = out_ref.shape[1] // LANES
    for k in range(3):
        for group in range(groups):
            row = k * groups + group
            out_ref[k : k + 1, group * LANES : (group + 1) * LANES] = total[row : row + 1]


def sum_rounds():
    lines, nodes, cores = (lax.axis_size(axis) for axis in SUM_AXES)
    if any(size & (size - 1) for size in (lines, nodes, cores)):
        return None
    near = [cores >> 1 >> i for i in range(cores.bit_length() - 1)]
    node_bits = [cores << i for i in range(nodes.bit_length() - 1)]
    line_bits = [cores * nodes << i for i in range(lines.bit_length() - 1)]
    bits = line_bits[1:2] + node_bits[:1] + line_bits[2:] + node_bits[1:]
    rounds = [[bit] for bit in near] + [[bit | (cores - 1)] for bit in line_bits[:1]]
    for first in range(0, len(bits), 2):
        masks = bits[first : first + 2]
        if len(masks) == 2:
            masks = [masks[0] | masks[1]] + masks
        rounds.append([mask | (cores - 1) for mask in masks])
    return rounds


def exchanged(value, masks):
    peers = lax.axis_size(SUM_AXES)
    return [value] + [
        lax.ppermute(value, SUM_AXES, [(i, i ^ mask) for i in range(peers)]) for mask in masks
    ]


def body(
    adjoint_start,
    adjoint_rhs,
    off_blocks,
    diag_inverse,
    neighbours,
    node_weights,
    sens_blocks,
    cell_points,
    base_points,
    ffd_index,
    ffd_weight,
):
    nodes, _, cells = adjoint_start.shape
    faces = off_blocks.shape[1]
    blocks = cells // LANES
    per = blocks * nodes
    slots = ffd_index.shape[1]
    far_slots = slots * 5 // 8
    owned = base_points.shape[1] // lax.axis_size("nodes")
    peers = lax.axis_size(CELL_AXES)
    cores = lax.axis_size("sub")
    node_peers = lax.axis_size("nodes")
    f32, i32, bf16 = jnp.float32, jnp.int32, jnp.bfloat16

    def shape(dims, dtype=f32):
        return jax.ShapeDtypeStruct(dims, dtype)

    def cost(flops, moved):
        return pl.CostEstimate(flops=flops, bytes_accessed=moved, transcendentals=0)

    def swaps(array):
        close = lax.ppermute(array, CELL_AXES, [(i, i ^ 1) for i in range(peers)])
        pairs = []
        for i in range(peers):
            line, core = divmod(i, cores)
            for node in range(node_peers):
                j, beside = (i + 1 if i % 2 else i - 1), node
                if not 0 <= j < peers:
                    j, beside = i, (node ^ 1 if node_peers % 2 == 0 else node)
                to_line, to_core = divmod(j, cores)
                pairs.append(
                    (
                        (line * node_peers + node) * cores + core,
                        (to_line * node_peers + beside) * cores + to_core,
                    )
                )
        return lax.ppermute(array, SUM_AXES, pairs), close

    adjoint = rows_of(adjoint_start)
    far, close = swaps(adjoint)
    prepared = pl.pallas_call(
        functools.partial(prepare_kernel, nodes),
        out_shape=(
            shape((faces * 25 * per, LANES), bf16),
            shape((25 * per, LANES)),
            shape((5 * per, LANES)),
            shape((15 * per, LANES)),
            shape((faces * per, LANES), i32),
            shape((faces * per, LANES), i32),
            shape((slots * 16, owned)),
            shape((slots, owned)),
            shape(((slots - far_slots) * owned, LANES), bf16),
            shape((5 * per, LANES)),
            shape((cells, FACTOR_ROWS), bf16),
            shape((FACTOR_ROWS, owned), bf16),
        ),
        in_specs=[HBM] * 11,
        out_specs=(VMEM,) * 12,
        scratch_shapes=[
            pltpu.VMEM((15 * per, LANES), bf16),
            pltpu.VMEM((faces, cells), i32),
            pltpu.SMEM((nodes,), f32),
            pltpu.VMEM((slots, owned), i32),
            pltpu.VMEM((slots, owned), f32),
            pltpu.VMEM((3, cells), f32),
            pltpu.VMEM((3, owned), f32),
            pltpu.SemaphoreType.DMA((11,)),
        ],
        compiler_params=PARAMS,
        cost_estimate=cost(10**9, 10**7),
        name="prepare",
    )(
        *in_hbm(
            rows_of(off_blocks.reshape(nodes, faces * 25, cells)),
            rows_of(diag_inverse),
            rows_of(adjoint_rhs),
            rows_of(sens_blocks),
            neighbours,
            node_weights,
            ffd_index.T,
            ffd_weight.T,
            adjoint,
            cell_points,
            base_points,
        )
    )
    off, inverse, rhs, sens, lane, step, spread, low, near_hot, adjoint, left, right = prepared
    scratch = [
        pltpu.VMEM((3 * 5 * per, LANES), f32),
        pltpu.VMEM((max(8 // nodes - 1, 1) * 3 * 5 * per, LANES), f32),
    ]
    sweep_cost = cost(2 * 10 * 35 * cells, 4 * faces * 25 * per * LANES)

    for _ in range(SWEEPS - 1):
        adjoint = pl.pallas_call(
            functools.partial(sweep_kernel, blocks),
            out_shape=shape((5 * per, LANES)),
            in_specs=[VMEM] * 8,
            out_specs=VMEM,
            scratch_shapes=scratch,
            compiler_params=PARAMS,
            cost_estimate=sweep_cost,
            name="sweep",
        )(far, close, adjoint, rhs, off, inverse, lane, step)
        far, close = swaps(adjoint)

    half = cells * 5 // 8 // LANES * LANES
    wendland_cost = cost(10**9, 10**7)
    near_shape = shape((2 * half, owned), bf16)
    far_shape = shape((2 * (cells - half), owned), bf16)
    near_kernel = pl.pallas_call(
        functools.partial(wendland_kernel, 0),
        out_shape=near_shape,
        in_specs=[VMEM] * 3,
        out_specs=VMEM,
        compiler_params=PARAMS,
        cost_estimate=wendland_cost,
        name="near_wendland",
    )(left, right, adjoint)
    adjoint, part_sens = pl.pallas_call(
        functools.partial(last_sweep_kernel, blocks),
        out_shape=(shape((5 * per, LANES)), shape((3 * blocks, LANES))),
        in_specs=[VMEM] * 9 + [pl.BlockSpec(memory_space=pl.ANY)],
        out_specs=(VMEM, VMEM),
        scratch_shapes=scratch + [pltpu.VMEM((3 * per, LANES), f32)],
        compiler_params=PARAMS,
        cost_estimate=sweep_cost,
        name="last_sweep",
    )(close, far, adjoint, rhs, off, inverse, lane, step, sens, near_kernel)

    all_sens = [part_sens]
    for shift in range(1, node_peers):
        ring = [(i, (i + shift) % node_peers) for i in range(node_peers)]
        all_sens.append(lax.ppermute(part_sens, "nodes", ring))
    hot_shape = shape((far_slots * owned, LANES), bf16)
    far_kernel, far_hot, adjoint = pl.pallas_call(
        functools.partial(far_wendland_kernel, half),
        out_shape=(far_shape, hot_shape, shape((5 * per, LANES))),
        in_specs=[VMEM] * 5,
        out_specs=(VMEM, VMEM, HBM),
        scratch_shapes=[pltpu.SemaphoreType.DMA],
        compiler_params=PARAMS,
        cost_estimate=wendland_cost,
        name="far_wendland",
    )(left, right, part_sens, adjoint, low)
    scale = 4.0 / math.sqrt(cells * peers)
    rows = 3 * FFD // LANES
    partial = pl.pallas_call(
        functools.partial(control_kernel, scale),
        out_shape=shape((rows, LANES)),
        in_specs=[VMEM] * (len(all_sens) + 5),
        out_specs=VMEM,
        compiler_params=PARAMS,
        name="control",
    )(*all_sens, near_kernel, far_kernel, spread, near_hot, far_hot)
    rounds = sum_rounds()
    terms = [partial] if rounds else [lax.psum(partial, SUM_AXES)]
    for masks in rounds or ():
        if len(terms) > 1:
            partial = pl.pallas_call(
                add_kernel, out_shape=shape((rows, LANES)), name="add", compiler_params=PARAMS
            )(*terms)
        terms = exchanged(partial, masks)
    control_grad = pl.pallas_call(
        finish_kernel, out_shape=shape((3, FFD)), name="finish", compiler_params=PARAMS
    )(*terms)
    return (from_rows(adjoint, nodes, cells), control_grad)


def solution(mesh):
    return jax.shard_map(
        body,
        mesh=mesh,
        in_specs=(
            P("nodes", None, ("groups", "cells", "sub")),
            P("nodes", None, ("groups", "cells", "sub")),
            P("nodes", None, None, ("groups", "cells", "sub")),
            P("nodes", None, ("groups", "cells", "sub")),
            P(None, ("cells", "sub")),
            P("nodes"),
            P("nodes", None, ("groups", "cells", "sub")),
            P(None, ("cells", "sub")),
            P(),
            P(),
            P(),
        ),
        out_specs=(P("nodes", None, ("groups", "cells", "sub")), P("groups", None)),
        check_vma=False,
    )
```

```python
import functools
import math

import jax
import jax.numpy as jnp
from jax import lax
from jax.experimental import pallas as pl
from jax.experimental.pallas import tpu as pltpu
from jax.sharding import PartitionSpec as P

SWEEPS = 2
FFD = 512
SUPPORT_RADIUS = 0.3
LANES = 128
CELL_AXES = ("cells", "sub")
SUM_AXES = ("cells", "nodes", "sub")
FACTOR_ROWS = 64
PARAMS = pltpu.CompilerParams(vmem_limit_bytes=24 * 1024 * 1024)
VMEM = pl.BlockSpec(memory_space=pltpu.VMEM)
HBM = pl.BlockSpec(memory_space=pltpu.HBM)


def rows_of(array):
    nodes, rows, cells = array.shape
    blocks = cells // LANES
    split = array.reshape(nodes, rows, blocks, LANES)
    return split.transpose(1, 2, 0, 3).reshape(rows * blocks * nodes, LANES)


def from_rows(array, nodes, cells):
    blocks = cells // LANES
    split = array.reshape(-1, blocks, nodes, LANES)
    return split.transpose(2, 0, 1, 3).reshape(nodes, -1, cells)


def in_hbm(*arrays):
    return [pltpu.with_memory_space_constraint(array, pltpu.HBM) for array in arrays]


def write_one_hot(low_ref, one_hot_ref, first_slot):
    owned = low_ref.shape[1]
    piece = min(512, owned)
    lane = lax.broadcasted_iota(jnp.int32, (piece, LANES), 1).astype(jnp.float32)
    lane = lane.astype(jnp.bfloat16)
    for first in range(0, owned, piece):
        low = low_ref[:, first : first + piece].T.astype(jnp.bfloat16)
        for j in range(one_hot_ref.shape[0] // owned):
            column = low[:, first_slot + j : first_slot + j + 1]
            hit = jnp.broadcast_to(column, (piece, LANES)) == lane
            one_hot_ref[j * owned + first : j * owned + first + piece, :] = jnp.where(
                hit, jnp.bfloat16(1.0), jnp.bfloat16(0.0)
            )


def prepare_kernel(
    nodes,
    off_in,
    inverse_in,
    rhs_in,
    sens_in,
    neigh_in,
    weight_in,
    index_in,
    spread_in,
    start_in,
    cell_in,
    base_in,
    off_ref,
    inverse_ref,
    rhs_ref,
    sens_ref,
    lane_ref,
    step_ref,
    spread_ref,
    low_ref,
    one_hot_ref,
    start_ref,
    left_ref,
    right_ref,
    off_buf,
    sens_buf,
    neigh_buf,
    weight_buf,
    index_buf,
    spread_buf,
    cell_buf,
    base_buf,
    sems,
):
    slots, owned = index_buf.shape
    start = pl.multiple_of(lax.axis_index("nodes") * owned, LANES)
    mine = pl.ds(start, owned)
    pairs = (
        (neigh_in, neigh_buf),
        (index_in.at[:, mine], index_buf),
        (spread_in.at[:, mine], spread_buf),
        (cell_in, cell_buf),
        (base_in.at[:, mine], base_buf),
        (off_in, off_buf),
        (weight_in, weight_buf),
        (sens_in, sens_buf),
        (inverse_in, inverse_ref),
        (rhs_in, rhs_ref),
        (start_in, start_ref),
    )
    copies = [pltpu.make_async_copy(a, b, sems.at[i]) for i, (a, b) in enumerate(pairs)]
    for copy in copies:
        copy.start()

    faces, cells = neigh_buf.shape
    blocks = cells // LANES
    per = blocks * nodes
    first_cell = lax.axis_index(CELL_AXES) * cells
    copies[0].wait()
    for block in range(blocks):
        index = neigh_buf[:, block * LANES : (block + 1) * LANES]
        local = index - first_cell + cells
        lane = jnp.bitwise_and(local, LANES - 1)
        step = jnp.right_shift(local, 7) - block
        step = jnp.where(index >= 0, step, -1)
        for node in range(nodes):
            rows = pl.ds(block * nodes + node, faces, stride=per)
            lane_ref[rows, :] = lane
            step_ref[rows, :] = step

    copies[1].wait()
    copies[2].wait()
    groups = FFD // LANES
    piece = min(512, owned)
    for first in range(0, owned, piece):
        here = slice(first, first + piece)
        high = jnp.right_shift(index_buf[:, here], 7)
        part = lax.broadcasted_iota(jnp.int32, (16, piece), 0)
        part = jnp.where(part < 3 * groups, lax.rem(part, groups), -1)
        for j in range(slots):
            spread_ref[j * 16 : (j + 1) * 16, here] = jnp.where(
                high[j : j + 1] == part, spread_buf[j : j + 1, here], 0.0
            )

    low_ref[...] = jnp.bitwise_and(index_buf[...], LANES - 1).astype(jnp.float32)
    write_one_hot(low_ref, one_hot_ref, 0)

    copies[3].wait()
    left_ref[...] = distance_factors(cell_buf[...], True).T.astype(jnp.bfloat16)
    copies[4].wait()
    right_ref[...] = distance_factors(base_buf[...], False).astype(jnp.bfloat16)

    copies[5].wait()
    off_ref[...] = off_buf[...].astype(jnp.float32)
    copies[6].wait()
    copies[7].wait()
    row_node = lax.rem(lax.broadcasted_iota(jnp.int32, (per, LANES), 0), nodes)
    weights = jnp.zeros((per, LANES), jnp.float32)
    for node in range(nodes):
        weights = jnp.where(row_node == node, weight_buf[node], weights)
    for row in range(0, sens_buf.shape[0], per):
        here = slice(row, row + per)
        sens_ref[here, :] = sens_buf[here, :].astype(jnp.float32) * weights
    for copy in copies[8:]:
        copy.wait()


def take_lanes(table, lanes):
    numbers = lax.GatherDimensionNumbers(
        offset_dims=(),
        collapsed_slice_dims=(1,),
        start_index_map=(1,),
        operand_batching_dims=(0,),
        start_indices_batching_dims=(0,),
    )
    return lax.gather(
        table,
        lanes[..., None],
        numbers,
        slice_sizes=(1, 1),
        mode=lax.GatherScatterMode.PROMISE_IN_BOUNDS,
    )


def sweep_into(
    blocks, first_ref, second_ref, own_ref, rhs_ref, off_ref, inverse_ref, lane_ref, step_ref,
    out_ref, window_ref, table_ref,
):
    per = rhs_ref.shape[0] // 5
    nodes = per // blocks
    faces = lane_ref.shape[0] // per
    odd = lax.rem(lax.axis_index(CELL_AXES), 2)
    place = pl.multiple_of((1 - odd) * 2 * per, 8)
    other = pl.multiple_of(odd * 2 * per, 8)
    width = 3 * per
    for b in range(5):
        rows = slice(b * per, (b + 1) * per)
        base = b * width
        window_ref[pl.ds(base + place, per), :] = first_ref[rows, :]
        window_ref[base + per : base + 2 * per, :] = own_ref[rows, :]
        window_ref[pl.ds(base + other, per), :] = second_ref[rows, :]
    for shift in range(1, 8 // nodes):
        for b in range(5):
            for tile in range(0, width - 8, 8):
                to = ((shift - 1) * 5 + b) * width + tile
                table_ref[to : to + 8, :] = window_ref[
                    pl.ds(b * width + tile + shift * nodes, 8), :
                ]
    for half in range(0, per, 8):
        remaining = [rhs_ref[a * per + half : a * per + half + 8, :] for a in range(5)]
        for f in range(faces):
            lanes = lane_ref[f * per + half : f * per + half + 8, :]
            dist = step_ref[f * per + half : f * per + half + 8, :]
            beside = [jnp.zeros((8, LANES), jnp.float32)] * 5
            for d in range(2 * blocks + 1):
                here = dist == d
                first = half + d * nodes
                for b in range(5):
                    shift, at = first % 8 // nodes, b * width + first // 8 * 8
                    if shift:
                        at = at + (shift - 1) * 5 * width
                        table = table_ref[at : at + 8, :]
                    else:
                        table = window_ref[at : at + 8, :]
                    beside[b] = jnp.where(here, take_lanes(table, lanes), beside[b])
            for a in range(5):
                for b in range(5):
                    row = (f * 25 + 5 * a + b) * per + half
                    remaining[a] = remaining[a] - off_ref[row : row + 8, :] * beside[b]
        for a in range(5):
            total = None
            for b in range(5):
                row = (5 * a + b) * per + half
                term = inverse_ref[row : row + 8, :] * remaining[b]
                total = term if total is None else total + term
            out_ref[a * per + half : a * per + half + 8, :] = total


def sweep_kernel(blocks, far_ref, close_ref, *refs):
    sweep_into(blocks, close_ref, far_ref, *refs)


def last_sweep_kernel(blocks, *refs):
    ins, rest = refs[:8], refs[8:]
    sens_ref, _, out_ref, sens_out_ref, window_ref, table_ref, part_ref = rest
    sweep_into(blocks, *ins, out_ref, window_ref, table_ref)
    per = out_ref.shape[0] // 5
    nodes = per // blocks
    for k in range(3):
        total = None
        for a in range(5):
            row = (3 * a + k) * per
            term = out_ref[a * per : (a + 1) * per, :] * sens_ref[row : row + per, :]
            total = term if total is None else total + term
        part_ref[k * per : (k + 1) * per, :] = total
    for block in range(blocks):
        total = None
        for node in range(nodes):
            term = part_ref[pl.ds(block * nodes + node, 3, stride=per), :]
            total = term if total is None else total + term
        sens_out_ref[pl.ds(block, 3, stride=blocks), :] = total


def pieces(value, count):
    found = []
    for _ in range(count):
        piece = value.astype(jnp.bfloat16).astype(jnp.float32)
        found.append(piece)
        value = value - piece
    return found


def distance_factors(points, left):
    count = points.shape[1]
    scaled = (points - 0.5) * (1.0 / SUPPORT_RADIUS)
    scaled = jnp.concatenate([scaled, jnp.zeros((5, count), jnp.float32)], axis=0)
    norm = jnp.sum(scaled * scaled, axis=0, keepdims=True)
    norms = pieces(jnp.broadcast_to(norm, (8, count)), 3)
    row = lax.broadcasted_iota(jnp.int32, (8, count), 0)
    norm_block = jnp.zeros((8, count), jnp.float32)
    for place in range(3):
        norm_block = jnp.where(row == place, norms[place], norm_block)
    ones_block = jnp.where(row < 3, 1.0, 0.0)
    first, second, third = pieces(scaled, 3)
    if left:
        dims = [first, first, second, second, first, third]
        dims = [-2.0 * part for part in dims]
        blocks = dims + [norm_block, ones_block]
    else:
        dims = [first, second, first, second, third, first]
        blocks = dims + [ones_block, norm_block]
    return jnp.concatenate(blocks, axis=0)


def wendland_kernel(first_cell, left_ref, right_ref, _, kernel_ref):
    cells, owned = kernel_ref.shape[0] // 2, kernel_ref.shape[1]
    tile, wide = min(128, cells), min(256, owned)

    def squares(row, lane):
        left = left_ref[first_cell + row : first_cell + row + tile, :]
        right = right_ref[:, lane : lane + wide]
        return jnp.dot(left, right, preferred_element_type=jnp.float32)

    places = [(row, lane) for lane in range(0, owned, wide) for row in range(0, cells, tile)]
    following = squares(*places[0])
    for at, (row, lane) in enumerate(places):
        squared = jnp.maximum(following, 1e-30)
        if at + 1 < len(places):
            following = squares(*places[at + 1])
        near = jnp.maximum(1.0 - squared * lax.rsqrt(squared), 0.0)
        power = near * near
        kernel = power * power * (1.25 - near)
        first = kernel.astype(jnp.bfloat16)
        rest = (kernel - first.astype(jnp.float32)).astype(jnp.bfloat16)
        here = slice(lane, lane + wide)
        kernel_ref[row : row + tile, here] = first
        kernel_ref[cells + row : cells + row + tile, here] = rest


def far_wendland_kernel(
    first_cell, left_ref, right_ref, after, adjoint_ref, low_ref, *rest
):
    kernel_ref, one_hot_ref, result_ref, sem = rest
    copy = pltpu.make_async_copy(adjoint_ref, result_ref, sem)
    copy.start()
    owned = low_ref.shape[1]
    write_one_hot(low_ref, one_hot_ref, low_ref.shape[0] - one_hot_ref.shape[0] // owned)
    wendland_kernel(first_cell, left_ref, right_ref, after, kernel_ref)
    copy.wait()


def control_kernel(scale, *refs):
    *sens_refs, near_ref, far_ref = refs[:-4]
    spread_ref, near_hot, far_hot, out_ref = refs[-4:]
    blocks = sens_refs[0].shape[0] // 3
    half = near_ref.shape[0] // 2
    groups = FFD // LANES
    total = sens_refs[0][...]
    for ref in sens_refs[1:]:
        total = total + ref[...]
    total = total * scale

    def halves(value):
        first = value.astype(jnp.bfloat16)
        rest = (value - first.astype(jnp.float32)).astype(jnp.bfloat16)
        return first, rest

    row = lax.broadcasted_iota(jnp.int32, (8, LANES), 0)
    wide = []
    for block in range(blocks):
        sens = jnp.zeros((8, LANES), jnp.float32)
        for k in range(3):
            sens = jnp.where(row == k, total[k * blocks + block : k * blocks + block + 1], sens)
        first = sens.astype(jnp.bfloat16).astype(jnp.float32)
        wide.append(jnp.concatenate([first, sens - first], axis=0))
    sens = jnp.concatenate(wide, axis=1).astype(jnp.bfloat16)
    grad = None
    for part, ref in ((sens[:, :half], near_ref), (sens[:, half:], far_ref)):
        both = jnp.concatenate([part, part], axis=1)
        term = jnp.dot(both, ref[...], preferred_element_type=jnp.float32)
        grad = term if grad is None else grad + term
    grad = grad[:8] + grad[8:]
    row = lax.broadcasted_iota(jnp.int32, (16, grad.shape[1]), 0)
    wide = jnp.zeros(row.shape, jnp.float32)
    for k in range(3):
        mine = jnp.logical_and(row >= k * groups, row < (k + 1) * groups)
        wide = jnp.where(mine, grad[k : k + 1], wide)
    grad = wide
    owned = grad.shape[1]
    result = None
    places = [
        (ref, first) for ref in (near_hot, far_hot) for first in range(0, ref.shape[0], owned)
    ]
    for j, (ref, first) in enumerate(places):
        term = jnp.dot(
            jnp.concatenate(halves(grad * spread_ref[j * 16 : (j + 1) * 16, :]), axis=0),
            ref[first : first + owned, :],
            preferred_element_type=jnp.float32,
        )
        result = term if result is None else result + term
    result = result[:16] + result[16:]
    out_ref[...] = result[: 3 * groups]


def tree(values):
    while len(values) > 1:
        values = [sum(values[i : i + 2]) for i in range(0, len(values), 2)]
    return values[0]


def add_kernel(*refs):
    refs[-1][...] = tree([ref[...] for ref in refs[:-1]])


def finish_kernel(*refs):
    total, out_ref = tree([ref[...] for ref in refs[:-1]]), refs[-1]
    groups = out_ref.shape[1] // LANES
    for k in range(3):
        for group in range(groups):
            row = k * groups + group
            out_ref[k : k + 1, group * LANES : (group + 1) * LANES] = total[row : row + 1]


def sum_rounds():
    lines, nodes, cores = (lax.axis_size(axis) for axis in SUM_AXES)
    if any(size & (size - 1) for size in (lines, nodes, cores)):
        return None
    near = [cores >> 1 >> i for i in range(cores.bit_length() - 1)]
    node_bits = [cores << i for i in range(nodes.bit_length() - 1)]
    line_bits = [cores * nodes << i for i in range(lines.bit_length() - 1)]
    bits = line_bits[:1] + node_bits[:1] + line_bits[2:] + node_bits[1:]
    rounds = [[bit] for bit in near] + [[bit | (cores - 1)] for bit in line_bits[1:2]]
    for first in range(0, len(bits), 2):
        masks = bits[first : first + 2]
        if len(masks) == 2:
            masks = [masks[0] | masks[1]] + masks
        rounds.append([mask | (cores - 1) for mask in masks])
    return rounds


def exchanged(value, masks):
    peers = lax.axis_size(SUM_AXES)
    return [value] + [
        lax.ppermute(value, SUM_AXES, [(i, i ^ mask) for i in range(peers)]) for mask in masks
    ]


def body(
    adjoint_start,
    adjoint_rhs,
    off_blocks,
    diag_inverse,
    neighbours,
    node_weights,
    sens_blocks,
    cell_points,
    base_points,
    ffd_index,
    ffd_weight,
):
    nodes, _, cells = adjoint_start.shape
    faces = off_blocks.shape[1]
    blocks = cells // LANES
    per = blocks * nodes
    slots = ffd_index.shape[1]
    far_slots = slots * 5 // 8
    owned = base_points.shape[1] // lax.axis_size("nodes")
    peers = lax.axis_size(CELL_AXES)
    cores = lax.axis_size("sub")
    node_peers = lax.axis_size("nodes")
    f32, i32, bf16 = jnp.float32, jnp.int32, jnp.bfloat16

    def shape(dims, dtype=f32):
        return jax.ShapeDtypeStruct(dims, dtype)

    def cost(flops, moved):
        return pl.CostEstimate(flops=flops, bytes_accessed=moved, transcendentals=0)

    def swaps(array):
        close = lax.ppermute(array, CELL_AXES, [(i, i ^ 1) for i in range(peers)])
        pairs = []
        for i in range(peers):
            line, core = divmod(i, cores)
            for node in range(node_peers):
                j, beside = (i + 1 if i % 2 else i - 1), node
                if not 0 <= j < peers:
                    j, beside = i, (node ^ 1 if node_peers % 2 == 0 else node)
                to_line, to_core = divmod(j, cores)
                pairs.append(
                    (
                        (line * node_peers + node) * cores + core,
                        (to_line * node_peers + beside) * cores + to_core,
                    )
                )
        return lax.ppermute(array, SUM_AXES, pairs), close

    adjoint = rows_of(adjoint_start)
    far, close = swaps(adjoint)
    prepared = pl.pallas_call(
        functools.partial(prepare_kernel, nodes),
        out_shape=(
            shape((faces * 25 * per, LANES)),
            shape((25 * per, LANES)),
            shape((5 * per, LANES)),
            shape((15 * per, LANES)),
            shape((faces * per, LANES), i32),
            shape((faces * per, LANES), i32),
            shape((slots * 16, owned)),
            shape((slots, owned)),
            shape(((slots - far_slots) * owned, LANES), bf16),
            shape((5 * per, LANES)),
            shape((cells, FACTOR_ROWS), bf16),
            shape((FACTOR_ROWS, owned), bf16),
        ),
        in_specs=[HBM] * 11,
        out_specs=(VMEM,) * 12,
        scratch_shapes=[
            pltpu.VMEM((faces * 25 * per, LANES), bf16),
            pltpu.VMEM((15 * per, LANES), bf16),
            pltpu.VMEM((faces, cells), i32),
            pltpu.SMEM((nodes,), f32),
            pltpu.VMEM((slots, owned), i32),
            pltpu.VMEM((slots, owned), f32),
            pltpu.VMEM((3, cells), f32),
            pltpu.VMEM((3, owned), f32),
            pltpu.SemaphoreType.DMA((11,)),
        ],
        compiler_params=PARAMS,
        cost_estimate=cost(10**9, 10**7),
        name="prepare",
    )(
        *in_hbm(
            rows_of(off_blocks.reshape(nodes, faces * 25, cells)),
            rows_of(diag_inverse),
            rows_of(adjoint_rhs),
            rows_of(sens_blocks),
            neighbours,
            node_weights,
            ffd_index.T,
            ffd_weight.T,
            adjoint,
            cell_points,
            base_points,
        )
    )
    off, inverse, rhs, sens, lane, step, spread, low, near_hot, adjoint, left, right = prepared
    scratch = [
        pltpu.VMEM((3 * 5 * per, LANES), f32),
        pltpu.VMEM((max(8 // nodes - 1, 1) * 3 * 5 * per, LANES), f32),
    ]
    sweep_cost = cost(2 * 10 * 35 * cells, 4 * faces * 25 * per * LANES)

    for _ in range(SWEEPS - 1):
        adjoint = pl.pallas_call(
            functools.partial(sweep_kernel, blocks),
            out_shape=shape((5 * per, LANES)),
            in_specs=[VMEM] * 8,
            out_specs=VMEM,
            scratch_shapes=scratch,
            compiler_params=PARAMS,
            cost_estimate=sweep_cost,
            name="sweep",
        )(far, close, adjoint, rhs, off, inverse, lane, step)
        far, close = swaps(adjoint)

    half = cells * 5 // 8 // LANES * LANES
    wendland_cost = cost(10**9, 10**7)
    near_shape = shape((2 * half, owned), bf16)
    far_shape = shape((2 * (cells - half), owned), bf16)
    near_kernel = pl.pallas_call(
        functools.partial(wendland_kernel, 0),
        out_shape=near_shape,
        in_specs=[VMEM] * 3,
        out_specs=VMEM,
        compiler_params=PARAMS,
        cost_estimate=wendland_cost,
        name="near_wendland",
    )(left, right, adjoint)
    adjoint, part_sens = pl.pallas_call(
        functools.partial(last_sweep_kernel, blocks),
        out_shape=(shape((5 * per, LANES)), shape((3 * blocks, LANES))),
        in_specs=[VMEM] * 9 + [pl.BlockSpec(memory_space=pl.ANY)],
        out_specs=(VMEM, VMEM),
        scratch_shapes=scratch + [pltpu.VMEM((3 * per, LANES), f32)],
        compiler_params=PARAMS,
        cost_estimate=sweep_cost,
        name="last_sweep",
    )(close, far, adjoint, rhs, off, inverse, lane, step, sens, near_kernel)

    all_sens = [part_sens]
    for shift in range(1, node_peers):
        ring = [(i, (i + shift) % node_peers) for i in range(node_peers)]
        all_sens.append(lax.ppermute(part_sens, "nodes", ring))
    hot_shape = shape((far_slots * owned, LANES), bf16)
    far_kernel, far_hot, adjoint = pl.pallas_call(
        functools.partial(far_wendland_kernel, half),
        out_shape=(far_shape, hot_shape, shape((5 * per, LANES))),
        in_specs=[VMEM] * 5,
        out_specs=(VMEM, VMEM, HBM),
        scratch_shapes=[pltpu.SemaphoreType.DMA],
        compiler_params=PARAMS,
        cost_estimate=wendland_cost,
        name="far_wendland",
    )(left, right, part_sens, adjoint, low)
    scale = 4.0 / math.sqrt(cells * peers)
    rows = 3 * FFD // LANES
    partial = pl.pallas_call(
        functools.partial(control_kernel, scale),
        out_shape=shape((rows, LANES)),
        in_specs=[VMEM] * (len(all_sens) + 5),
        out_specs=VMEM,
        compiler_params=PARAMS,
        name="control",
    )(*all_sens, near_kernel, far_kernel, spread, near_hot, far_hot)
    rounds = sum_rounds()
    terms = [partial] if rounds else [lax.psum(partial, SUM_AXES)]
    for masks in rounds or ():
        if len(terms) > 1:
            partial = pl.pallas_call(
                add_kernel, out_shape=shape((rows, LANES)), name="add", compiler_params=PARAMS
            )(*terms)
        terms = exchanged(partial, masks)
    control_grad = pl.pallas_call(
        finish_kernel, out_shape=shape((3, FFD)), name="finish", compiler_params=PARAMS
    )(*terms)
    return (from_rows(adjoint, nodes, cells), control_grad)


def solution(mesh):
    return jax.shard_map(
        body,
        mesh=mesh,
        in_specs=(
            P("nodes", None, ("groups", "cells", "sub")),
            P("nodes", None, ("groups", "cells", "sub")),
            P("nodes", None, None, ("groups", "cells", "sub")),
            P("nodes", None, ("groups", "cells", "sub")),
            P(None, ("cells", "sub")),
            P("nodes"),
            P("nodes", None, ("groups", "cells", "sub")),
            P(None, ("cells", "sub")),
            P(),
            P(),
            P(),
        ),
        out_specs=(P("nodes", None, ("groups", "cells", "sub")), P("groups", None)),
        check_vma=False,
    )
```

```python
import functools
import math

import jax
import jax.numpy as jnp
from jax import lax
from jax.experimental import pallas as pl
from jax.experimental.pallas import tpu as pltpu
from jax.sharding import PartitionSpec as P

SWEEPS = 2
FFD = 512
SUPPORT_RADIUS = 0.3
LANES = 128
CELL_AXES = ("cells", "sub")
SUM_AXES = ("cells", "nodes", "sub")
FACTOR_ROWS = 64
PARAMS = pltpu.CompilerParams(vmem_limit_bytes=24 * 1024 * 1024)
VMEM = pl.BlockSpec(memory_space=pltpu.VMEM)
HBM = pl.BlockSpec(memory_space=pltpu.HBM)


def rows_of(array):
    nodes, rows, cells = array.shape
    blocks = cells // LANES
    split = array.reshape(nodes, rows, blocks, LANES)
    return split.transpose(1, 2, 0, 3).reshape(rows * blocks * nodes, LANES)


def from_rows(array, nodes, cells):
    blocks = cells // LANES
    split = array.reshape(-1, blocks, nodes, LANES)
    return split.transpose(2, 0, 1, 3).reshape(nodes, -1, cells)


def in_hbm(*arrays):
    return [pltpu.with_memory_space_constraint(array, pltpu.HBM) for array in arrays]


def write_one_hot(low_ref, one_hot_ref, first_slot):
    owned = low_ref.shape[1]
    piece = min(512, owned)
    lane = lax.broadcasted_iota(jnp.int32, (piece, LANES), 1).astype(jnp.float32)
    lane = lane.astype(jnp.bfloat16)
    for first in range(0, owned, piece):
        low = low_ref[:, first : first + piece].T.astype(jnp.bfloat16)
        for j in range(one_hot_ref.shape[0] // owned):
            column = low[:, first_slot + j : first_slot + j + 1]
            hit = jnp.broadcast_to(column, (piece, LANES)) == lane
            one_hot_ref[j * owned + first : j * owned + first + piece, :] = jnp.where(
                hit, jnp.bfloat16(1.0), jnp.bfloat16(0.0)
            )


def prepare_kernel(
    nodes,
    off_in,
    inverse_in,
    rhs_in,
    sens_in,
    neigh_in,
    weight_in,
    index_in,
    spread_in,
    start_in,
    cell_in,
    base_in,
    off_ref,
    inverse_ref,
    rhs_ref,
    sens_ref,
    lane_ref,
    step_ref,
    spread_ref,
    low_ref,
    one_hot_ref,
    start_ref,
    left_ref,
    right_ref,
    off_buf,
    sens_buf,
    neigh_buf,
    weight_buf,
    index_buf,
    spread_buf,
    cell_buf,
    base_buf,
    sems,
):
    slots, owned = index_buf.shape
    start = pl.multiple_of(lax.axis_index("nodes") * owned, LANES)
    mine = pl.ds(start, owned)
    pairs = (
        (neigh_in, neigh_buf),
        (index_in.at[:, mine], index_buf),
        (spread_in.at[:, mine], spread_buf),
        (cell_in, cell_buf),
        (base_in.at[:, mine], base_buf),
        (off_in, off_buf),
        (weight_in, weight_buf),
        (sens_in, sens_buf),
        (inverse_in, inverse_ref),
        (rhs_in, rhs_ref),
        (start_in, start_ref),
    )
    copies = [pltpu.make_async_copy(a, b, sems.at[i]) for i, (a, b) in enumerate(pairs)]
    for copy in copies:
        copy.start()

    faces, cells = neigh_buf.shape
    blocks = cells // LANES
    per = blocks * nodes
    first_cell = lax.axis_index(CELL_AXES) * cells
    copies[0].wait()
    for block in range(blocks):
        index = neigh_buf[:, block * LANES : (block + 1) * LANES]
        local = index - first_cell + cells
        lane = jnp.bitwise_and(local, LANES - 1)
        step = jnp.right_shift(local, 7) - block
        step = jnp.where(index >= 0, step, -1)
        for node in range(nodes):
            rows = pl.ds(block * nodes + node, faces, stride=per)
            lane_ref[rows, :] = lane
            step_ref[rows, :] = step

    copies[1].wait()
    copies[2].wait()
    groups = FFD // LANES
    piece = min(512, owned)
    for first in range(0, owned, piece):
        here = slice(first, first + piece)
        high = jnp.right_shift(index_buf[:, here], 7)
        part = lax.broadcasted_iota(jnp.int32, (16, piece), 0)
        part = jnp.where(part < 3 * groups, lax.rem(part, groups), -1)
        for j in range(slots):
            spread_ref[j * 16 : (j + 1) * 16, here] = jnp.where(
                high[j : j + 1] == part, spread_buf[j : j + 1, here], 0.0
            )

    low_ref[...] = jnp.bitwise_and(index_buf[...], LANES - 1).astype(jnp.float32)
    write_one_hot(low_ref, one_hot_ref, 0)

    copies[3].wait()
    left_ref[...] = distance_factors(cell_buf[...], True).T.astype(jnp.bfloat16)
    copies[4].wait()
    right_ref[...] = distance_factors(base_buf[...], False).astype(jnp.bfloat16)

    copies[5].wait()
    off_ref[...] = off_buf[...].astype(jnp.float32)
    copies[6].wait()
    copies[7].wait()
    row_node = lax.rem(lax.broadcasted_iota(jnp.int32, (per, LANES), 0), nodes)
    weights = jnp.zeros((per, LANES), jnp.float32)
    for node in range(nodes):
        weights = jnp.where(row_node == node, weight_buf[node], weights)
    for row in range(0, sens_buf.shape[0], per):
        here = slice(row, row + per)
        sens_ref[here, :] = sens_buf[here, :].astype(jnp.float32) * weights
    for copy in copies[8:]:
        copy.wait()


def take_lanes(table, lanes):
    numbers = lax.GatherDimensionNumbers(
        offset_dims=(),
        collapsed_slice_dims=(1,),
        start_index_map=(1,),
        operand_batching_dims=(0,),
        start_indices_batching_dims=(0,),
    )
    return lax.gather(
        table,
        lanes[..., None],
        numbers,
        slice_sizes=(1, 1),
        mode=lax.GatherScatterMode.PROMISE_IN_BOUNDS,
    )


def sweep_into(
    blocks, first_ref, second_ref, own_ref, rhs_ref, off_ref, inverse_ref, lane_ref, step_ref,
    out_ref, window_ref, table_ref,
):
    per = rhs_ref.shape[0] // 5
    nodes = per // blocks
    faces = lane_ref.shape[0] // per
    odd = lax.rem(lax.axis_index(CELL_AXES), 2)
    place = pl.multiple_of((1 - odd) * 2 * per, 8)
    other = pl.multiple_of(odd * 2 * per, 8)
    width = 3 * per
    for b in range(5):
        rows = slice(b * per, (b + 1) * per)
        base = b * width
        window_ref[pl.ds(base + place, per), :] = first_ref[rows, :]
        window_ref[base + per : base + 2 * per, :] = own_ref[rows, :]
        window_ref[pl.ds(base + other, per), :] = second_ref[rows, :]
    for shift in range(1, 8 // nodes):
        for b in range(5):
            for tile in range(0, width - 8, 8):
                to = ((shift - 1) * 5 + b) * width + tile
                table_ref[to : to + 8, :] = window_ref[
                    pl.ds(b * width + tile + shift * nodes, 8), :
                ]
    for half in range(0, per, 8):
        remaining = [rhs_ref[a * per + half : a * per + half + 8, :] for a in range(5)]
        for f in range(faces):
            lanes = lane_ref[f * per + half : f * per + half + 8, :]
            dist = step_ref[f * per + half : f * per + half + 8, :]
            beside = [jnp.zeros((8, LANES), jnp.float32)] * 5
            for d in range(2 * blocks + 1):
                here = dist == d
                first = half + d * nodes
                for b in range(5):
                    shift, at = first % 8 // nodes, b * width + first // 8 * 8
                    if shift:
                        at = at + (shift - 1) * 5 * width
                        table = table_ref[at : at + 8, :]
                    else:
                        table = window_ref[at : at + 8, :]
                    beside[b] = jnp.where(here, take_lanes(table, lanes), beside[b])
            for a in range(5):
                for b in range(5):
                    row = (f * 25 + 5 * a + b) * per + half
                    remaining[a] = remaining[a] - off_ref[row : row + 8, :] * beside[b]
        for a in range(5):
            total = None
            for b in range(5):
                row = (5 * a + b) * per + half
                term = inverse_ref[row : row + 8, :] * remaining[b]
                total = term if total is None else total + term
            out_ref[a * per + half : a * per + half + 8, :] = total


def sweep_kernel(blocks, far_ref, close_ref, *refs):
    sweep_into(blocks, close_ref, far_ref, *refs)


def last_sweep_kernel(blocks, *refs):
    ins, rest = refs[:8], refs[8:]
    sens_ref, _, out_ref, sens_out_ref, window_ref, table_ref, part_ref = rest
    sweep_into(blocks, *ins, out_ref, window_ref, table_ref)
    per = out_ref.shape[0] // 5
    nodes = per // blocks
    for k in range(3):
        total = None
        for a in range(5):
            row = (3 * a + k) * per
            term = out_ref[a * per : (a + 1) * per, :] * sens_ref[row : row + per, :]
            total = term if total is None else total + term
        part_ref[k * per : (k + 1) * per, :] = total
    for block in range(blocks):
        total = None
        for node in range(nodes):
            term = part_ref[pl.ds(block * nodes + node, 3, stride=per), :]
            total = term if total is None else total + term
        sens_out_ref[pl.ds(block, 3, stride=blocks), :] = total


def pieces(value, count):
    found = []
    for _ in range(count):
        piece = value.astype(jnp.bfloat16).astype(jnp.float32)
        found.append(piece)
        value = value - piece
    return found


def distance_factors(points, left):
    count = points.shape[1]
    scaled = (points - 0.5) * (1.0 / SUPPORT_RADIUS)
    scaled = jnp.concatenate([scaled, jnp.zeros((5, count), jnp.float32)], axis=0)
    norm = jnp.sum(scaled * scaled, axis=0, keepdims=True)
    norms = pieces(jnp.broadcast_to(norm, (8, count)), 3)
    row = lax.broadcasted_iota(jnp.int32, (8, count), 0)
    norm_block = jnp.zeros((8, count), jnp.float32)
    for place in range(3):
        norm_block = jnp.where(row == place, norms[place], norm_block)
    ones_block = jnp.where(row < 3, 1.0, 0.0)
    first, second, third = pieces(scaled, 3)
    if left:
        dims = [first, first, second, second, first, third]
        dims = [-2.0 * part for part in dims]
        blocks = dims + [norm_block, ones_block]
    else:
        dims = [first, second, first, second, third, first]
        blocks = dims + [ones_block, norm_block]
    return jnp.concatenate(blocks, axis=0)


def wendland_kernel(first_cell, left_ref, right_ref, _, kernel_ref):
    cells, owned = kernel_ref.shape[0] // 2, kernel_ref.shape[1]
    tile, wide = min(128, cells), min(512, owned)

    def squares(row, lane):
        left = left_ref[first_cell + row : first_cell + row + tile, :]
        right = right_ref[:, lane : lane + wide]
        return jnp.dot(left, right, preferred_element_type=jnp.float32)

    places = [(row, lane) for lane in range(0, owned, wide) for row in range(0, cells, tile)]
    following = squares(*places[0])
    for at, (row, lane) in enumerate(places):
        squared = jnp.maximum(following, 1e-30)
        if at + 1 < len(places):
            following = squares(*places[at + 1])
        near = jnp.maximum(1.0 - squared * lax.rsqrt(squared), 0.0)
        power = near * near
        kernel = power * power * (1.25 - near)
        first = kernel.astype(jnp.bfloat16)
        rest = (kernel - first.astype(jnp.float32)).astype(jnp.bfloat16)
        here = slice(lane, lane + wide)
        kernel_ref[row : row + tile, here] = first
        kernel_ref[cells + row : cells + row + tile, here] = rest


def far_wendland_kernel(
    first_cell, left_ref, right_ref, after, adjoint_ref, low_ref, *rest
):
    kernel_ref, one_hot_ref, result_ref, sem = rest
    copy = pltpu.make_async_copy(adjoint_ref, result_ref, sem)
    copy.start()
    owned = low_ref.shape[1]
    write_one_hot(low_ref, one_hot_ref, low_ref.shape[0] - one_hot_ref.shape[0] // owned)
    wendland_kernel(first_cell, left_ref, right_ref, after, kernel_ref)
    copy.wait()


def control_kernel(scale, *refs):
    *sens_refs, near_ref, far_ref = refs[:-4]
    spread_ref, near_hot, far_hot, out_ref = refs[-4:]
    blocks = sens_refs[0].shape[0] // 3
    half = near_ref.shape[0] // 2
    groups = FFD // LANES
    total = sens_refs[0][...]
    for ref in sens_refs[1:]:
        total = total + ref[...]
    total = total * scale

    def halves(value):
        first = value.astype(jnp.bfloat16)
        rest = (value - first.astype(jnp.float32)).astype(jnp.bfloat16)
        return first, rest

    row = lax.broadcasted_iota(jnp.int32, (8, LANES), 0)
    wide = []
    for block in range(blocks):
        sens = jnp.zeros((8, LANES), jnp.float32)
        for k in range(3):
            sens = jnp.where(row == k, total[k * blocks + block : k * blocks + block + 1], sens)
        first = sens.astype(jnp.bfloat16).astype(jnp.float32)
        wide.append(jnp.concatenate([first, sens - first], axis=0))
    sens = jnp.concatenate(wide, axis=1).astype(jnp.bfloat16)
    grad = None
    for part, ref in ((sens[:, :half], near_ref), (sens[:, half:], far_ref)):
        both = jnp.concatenate([part, part], axis=1)
        term = jnp.dot(both, ref[...], preferred_element_type=jnp.float32)
        grad = term if grad is None else grad + term
    grad = grad[:8] + grad[8:]
    row = lax.broadcasted_iota(jnp.int32, (16, grad.shape[1]), 0)
    wide = jnp.zeros(row.shape, jnp.float32)
    for k in range(3):
        mine = jnp.logical_and(row >= k * groups, row < (k + 1) * groups)
        wide = jnp.where(mine, grad[k : k + 1], wide)
    grad = wide
    owned = grad.shape[1]
    result = None
    places = [
        (ref, first) for ref in (near_hot, far_hot) for first in range(0, ref.shape[0], owned)
    ]
    for j, (ref, first) in enumerate(places):
        term = jnp.dot(
            jnp.concatenate(halves(grad * spread_ref[j * 16 : (j + 1) * 16, :]), axis=0),
            ref[first : first + owned, :],
            preferred_element_type=jnp.float32,
        )
        result = term if result is None else result + term
    result = result[:16] + result[16:]
    out_ref[...] = result[: 3 * groups]


def tree(values):
    while len(values) > 1:
        values = [sum(values[i : i + 2]) for i in range(0, len(values), 2)]
    return values[0]


def add_kernel(*refs):
    refs[-1][...] = tree([ref[...] for ref in refs[:-1]])


def finish_kernel(*refs):
    total, out_ref = tree([ref[...] for ref in refs[:-1]]), refs[-1]
    groups = out_ref.shape[1] // LANES
    for k in range(3):
        for group in range(groups):
            row = k * groups + group
            out_ref[k : k + 1, group * LANES : (group + 1) * LANES] = total[row : row + 1]


def sum_rounds():
    lines, nodes, cores = (lax.axis_size(axis) for axis in SUM_AXES)
    if any(size & (size - 1) for size in (lines, nodes, cores)):
        return None
    near = [cores >> 1 >> i for i in range(cores.bit_length() - 1)]
    node_bits = [cores << i for i in range(nodes.bit_length() - 1)]
    line_bits = [cores * nodes << i for i in range(lines.bit_length() - 1)]
    bits = line_bits[1:2] + node_bits[:1] + line_bits[2:] + node_bits[1:]
    rounds = [[bit] for bit in near] + [[bit | (cores - 1)] for bit in line_bits[:1]]
    for first in range(0, len(bits), 2):
        masks = bits[first : first + 2]
        if len(masks) == 2:
            masks = [masks[0] | masks[1]] + masks
        rounds.append([mask | (cores - 1) for mask in masks])
    return rounds


def exchanged(value, masks):
    peers = lax.axis_size(SUM_AXES)
    return [value] + [
        lax.ppermute(value, SUM_AXES, [(i, i ^ mask) for i in range(peers)]) for mask in masks
    ]


def body(
    adjoint_start,
    adjoint_rhs,
    off_blocks,
    diag_inverse,
    neighbours,
    node_weights,
    sens_blocks,
    cell_points,
    base_points,
    ffd_index,
    ffd_weight,
):
    nodes, _, cells = adjoint_start.shape
    faces = off_blocks.shape[1]
    blocks = cells // LANES
    per = blocks * nodes
    slots = ffd_index.shape[1]
    far_slots = slots * 5 // 8
    owned = base_points.shape[1] // lax.axis_size("nodes")
    peers = lax.axis_size(CELL_AXES)
    cores = lax.axis_size("sub")
    node_peers = lax.axis_size("nodes")
    f32, i32, bf16 = jnp.float32, jnp.int32, jnp.bfloat16

    def shape(dims, dtype=f32):
        return jax.ShapeDtypeStruct(dims, dtype)

    def cost(flops, moved):
        return pl.CostEstimate(flops=flops, bytes_accessed=moved, transcendentals=0)

    def swaps(array):
        close = lax.ppermute(array, CELL_AXES, [(i, i ^ 1) for i in range(peers)])
        pairs = []
        for i in range(peers):
            line, core = divmod(i, cores)
            for node in range(node_peers):
                j, beside = (i + 1 if i % 2 else i - 1), node
                if not 0 <= j < peers:
                    j, beside = i, (node ^ 1 if node_peers % 2 == 0 else node)
                to_line, to_core = divmod(j, cores)
                pairs.append(
                    (
                        (line * node_peers + node) * cores + core,
                        (to_line * node_peers + beside) * cores + to_core,
                    )
                )
        return lax.ppermute(array, SUM_AXES, pairs), close

    adjoint = rows_of(adjoint_start)
    far, close = swaps(adjoint)
    prepared = pl.pallas_call(
        functools.partial(prepare_kernel, nodes),
        out_shape=(
            shape((faces * 25 * per, LANES)),
            shape((25 * per, LANES)),
            shape((5 * per, LANES)),
            shape((15 * per, LANES)),
            shape((faces * per, LANES), i32),
            shape((faces * per, LANES), i32),
            shape((slots * 16, owned)),
            shape((slots, owned)),
            shape(((slots - far_slots) * owned, LANES), bf16),
            shape((5 * per, LANES)),
            shape((cells, FACTOR_ROWS), bf16),
            shape((FACTOR_ROWS, owned), bf16),
        ),
        in_specs=[HBM] * 11,
        out_specs=(VMEM,) * 12,
        scratch_shapes=[
            pltpu.VMEM((faces * 25 * per, LANES), bf16),
            pltpu.VMEM((15 * per, LANES), bf16),
            pltpu.VMEM((faces, cells), i32),
            pltpu.SMEM((nodes,), f32),
            pltpu.VMEM((slots, owned), i32),
            pltpu.VMEM((slots, owned), f32),
            pltpu.VMEM((3, cells), f32),
            pltpu.VMEM((3, owned), f32),
            pltpu.SemaphoreType.DMA((11,)),
        ],
        compiler_params=PARAMS,
        cost_estimate=cost(10**9, 10**7),
        name="prepare",
    )(
        *in_hbm(
            rows_of(off_blocks.reshape(nodes, faces * 25, cells)),
            rows_of(diag_inverse),
            rows_of(adjoint_rhs),
            rows_of(sens_blocks),
            neighbours,
            node_weights,
            ffd_index.T,
            ffd_weight.T,
            adjoint,
            cell_points,
            base_points,
        )
    )
    off, inverse, rhs, sens, lane, step, spread, low, near_hot, adjoint, left, right = prepared
    scratch = [
        pltpu.VMEM((3 * 5 * per, LANES), f32),
        pltpu.VMEM((max(8 // nodes - 1, 1) * 3 * 5 * per, LANES), f32),
    ]
    sweep_cost = cost(2 * 10 * 35 * cells, 4 * faces * 25 * per * LANES)

    for _ in range(SWEEPS - 1):
        adjoint = pl.pallas_call(
            functools.partial(sweep_kernel, blocks),
            out_shape=shape((5 * per, LANES)),
            in_specs=[VMEM] * 8,
            out_specs=VMEM,
            scratch_shapes=scratch,
            compiler_params=PARAMS,
            cost_estimate=sweep_cost,
            name="sweep",
        )(far, close, adjoint, rhs, off, inverse, lane, step)
        far, close = swaps(adjoint)

    half = cells * 5 // 8 // LANES * LANES
    wendland_cost = cost(10**9, 10**7)
    near_shape = shape((2 * half, owned), bf16)
    far_shape = shape((2 * (cells - half), owned), bf16)
    near_kernel = pl.pallas_call(
        functools.partial(wendland_kernel, 0),
        out_shape=near_shape,
        in_specs=[VMEM] * 3,
        out_specs=VMEM,
        compiler_params=PARAMS,
        cost_estimate=wendland_cost,
        name="near_wendland",
    )(left, right, adjoint)
    adjoint, part_sens = pl.pallas_call(
        functools.partial(last_sweep_kernel, blocks),
        out_shape=(shape((5 * per, LANES)), shape((3 * blocks, LANES))),
        in_specs=[VMEM] * 9 + [pl.BlockSpec(memory_space=pl.ANY)],
        out_specs=(VMEM, VMEM),
        scratch_shapes=scratch + [pltpu.VMEM((3 * per, LANES), f32)],
        compiler_params=PARAMS,
        cost_estimate=sweep_cost,
        name="last_sweep",
    )(close, far, adjoint, rhs, off, inverse, lane, step, sens, near_kernel)

    all_sens = [part_sens]
    for shift in range(1, node_peers):
        ring = [(i, (i + shift) % node_peers) for i in range(node_peers)]
        all_sens.append(lax.ppermute(part_sens, "nodes", ring))
    hot_shape = shape((far_slots * owned, LANES), bf16)
    far_kernel, far_hot, adjoint = pl.pallas_call(
        functools.partial(far_wendland_kernel, half),
        out_shape=(far_shape, hot_shape, shape((5 * per, LANES))),
        in_specs=[VMEM] * 5,
        out_specs=(VMEM, VMEM, HBM),
        scratch_shapes=[pltpu.SemaphoreType.DMA],
        compiler_params=PARAMS,
        cost_estimate=wendland_cost,
        name="far_wendland",
    )(left, right, part_sens, adjoint, low)
    scale = 4.0 / math.sqrt(cells * peers)
    rows = 3 * FFD // LANES
    partial = pl.pallas_call(
        functools.partial(control_kernel, scale),
        out_shape=shape((rows, LANES)),
        in_specs=[VMEM] * (len(all_sens) + 5),
        out_specs=VMEM,
        compiler_params=PARAMS,
        name="control",
    )(*all_sens, near_kernel, far_kernel, spread, near_hot, far_hot)
    rounds = sum_rounds()
    terms = [partial] if rounds else [lax.psum(partial, SUM_AXES)]
    for masks in rounds or ():
        if len(terms) > 1:
            partial = pl.pallas_call(
                add_kernel, out_shape=shape((rows, LANES)), name="add", compiler_params=PARAMS
            )(*terms)
        terms = exchanged(partial, masks)
    control_grad = pl.pallas_call(
        finish_kernel, out_shape=shape((3, FFD)), name="finish", compiler_params=PARAMS
    )(*terms)
    return (from_rows(adjoint, nodes, cells), control_grad)


def solution(mesh):
    return jax.shard_map(
        body,
        mesh=mesh,
        in_specs=(
            P("nodes", None, ("groups", "cells", "sub")),
            P("nodes", None, ("groups", "cells", "sub")),
            P("nodes", None, None, ("groups", "cells", "sub")),
            P("nodes", None, ("groups", "cells", "sub")),
            P(None, ("cells", "sub")),
            P("nodes"),
            P("nodes", None, ("groups", "cells", "sub")),
            P(None, ("cells", "sub")),
            P(),
            P(),
            P(),
        ),
        out_specs=(P("nodes", None, ("groups", "cells", "sub")), P("groups", None)),
        check_vma=False,
    )
```
